32 devices in a mesh: seq: 8 (over z, y), stream: 4 (over x, core).
Axes of the slice: x: 2, y: 2, z: 4, core: 2. Of those that a mesh axis runs over, the one named last changes fastest.
Arguments:
- resid_in: bfloat16 [4, 4096, 2048], P('stream', 'seq'), may hold values from -6 to 6
- out_grad: bfloat16 [4, 4096, 2048], P('stream', 'seq'), may hold values from -6 to 6
- row_lengths: int32 [4, 16], P('stream'), may hold values from 0 to 4096, as said below
- norm_gain: bfloat16 [2048], P(('seq', 'stream')), may hold values from 0.099609375 to 1.8984375
- in_weight: bfloat16 [2048, 8192], P(('seq', 'stream')), may hold values from -0.125 to 0.125
- conv_weight: bfloat16 [4, 4096], P(None, ('seq', 'stream')), may hold values from -3 to 3
- conv_bias: bfloat16 [4096], P(('seq', 'stream')), may hold values from -3 to 3
- xproj_weight: bfloat16 [4096, 160], P(('seq', 'stream')), may hold values from -0.09375 to 0.09375
- dt_weight: bfloat16 [128, 4096], P(None, ('seq', 'stream')), may hold values from -0.5 to 0.5
- dt_bias: bfloat16 [4096], P(('seq', 'stream')), may hold values from -4.59375 to -3.390625
- a_log: bfloat16 [4096, 16], P(('seq', 'stream')), may hold values from -12 to 1
- skip_gain: bfloat16 [4096], P(('seq', 'stream')), may hold values from 0.5 to 1.5
- out_weight: bfloat16 [4096, 2048], P(('seq', 'stream')), may hold values from -0.09375 to 0.09375
Outputs:
- output: bfloat16 [4, 4096, 2048], P('stream', 'seq')
- in_grad: bfloat16 [4, 4096, 2048], P('stream', 'seq')
- grad_norm_gain: float32 [2048], P(('seq', 'stream'))
- grad_in_weight: float32 [2048, 8192], P(('seq', 'stream'))
- grad_conv_weight: float32 [4, 4096], P(None, ('seq', 'stream'))
- grad_conv_bias: float32 [4096], P(('seq', 'stream'))
- grad_xproj_weight: float32 [4096, 160], P(('seq', 'stream'))
- grad_dt_weight: float32 [128, 4096], P(None, ('seq', 'stream'))
- grad_dt_bias: float32 [4096], P(('seq', 'stream'))
- grad_a_log: float32 [4096, 16], P(('seq', 'stream'))
- grad_skip_gain: float32 [4096], P(('seq', 'stream'))
- grad_out_weight: float32 [4096, 2048], P(('seq', 'stream'))
The draws below stay inside these ranges and needn't reach their ends.
Inputs may be any that keep to these rules, and one draw needn't show every extreme that they name: `row_lengths`: slots hold the documents in order from position 0; unused slots at the end are 0; after the documents fewer than 256 padding positions remain; in one stream a single document fills all 4096 positions.
All inputs are finite; a program needn't handle non-finite values.
Results may differ from the reference program's by a relative error of at most 0.012.
Values may be sent and summed in bfloat16 or wider, within the bound.
A program may use at most 512 MiB of HBM per device.

```python
import math
import jax
import jax.numpy as jnp
from jax import lax

D = 2048
INNER = 4096
RANK = 128
STATE = 16
CONV = 4
MINLEN = 256
STREAMS = 4
LEN = 4096
SLOTS = 16


def draw_row_lengths(key, part):
    key = jax.random.fold_in(key, 5)
    power_key, extra_key, other_key, pad_key, pick_key = jax.random.split(key, 5)
    first_pow = jax.random.randint(power_key, (STREAMS, SLOTS), 0, 6)
    second_pow = jax.random.randint(other_key, (STREAMS, SLOTS), 0, 6)
    powers = jnp.minimum(first_pow, second_pow)
    doubling = jnp.array([1, 2, 4, 8, 16, 32], jnp.int32)
    wished = MINLEN * doubling[powers] + jax.random.randint(extra_key, (STREAMS, SLOTS), 0, MINLEN)
    wished = jnp.minimum(wished, 32 * MINLEN).astype(jnp.int32)
    padding = jax.random.randint(pad_key, (STREAMS, 1), 0, MINLEN)
    reach = jnp.minimum(jnp.cumsum(wished, axis=1), LEN - padding).astype(jnp.int32)
    lengths = reach - jnp.concatenate([jnp.zeros((STREAMS, 1), jnp.int32), reach[:, :-1]], axis=1)
    chosen = jax.random.randint(pick_key, (), 0, STREAMS)
    single = jnp.where(jnp.arange(SLOTS) == 0, LEN, 0).astype(jnp.int32)
    return jnp.where((jnp.arange(STREAMS) == chosen)[:, None], single[None, :], lengths).astype(jnp.int32)


def draw_a_log(key, part):
    key = jax.random.fold_in(key, 9)
    pick_key, slow_key, fast_key = jax.random.split(key, 3)
    share = 0.5
    slow_pick = jax.random.uniform(pick_key, (INNER, STATE)) < share
    slow_vals = jax.random.uniform(slow_key, (INNER, STATE), minval=math.log(2.5), maxval=math.log(50.0)) - math.log(LEN)
    fast_vals = jax.random.uniform(fast_key, (INNER, STATE), minval=math.log(0.5), maxval=math.log(2.0))
    return jnp.where(slow_pick, slow_vals, fast_vals).astype(jnp.bfloat16)


def steps_of(rng, shape, shards, smallest, high):
    def one(axis_at, parts):
        draws = jax.random.uniform(jax.random.fold_in(jax.random.fold_in(rng, 6), axis_at), (parts,), jnp.float32, smallest / len(shards), high / len(shards))
        return jnp.repeat(jnp.exp(draws), shape[axis_at] // parts).reshape((-1,) + (1,) * (len(shape) - axis_at - 1))

    loudness = one(*shards[0])
    for cut in shards[1:]:
        loudness = loudness * one(*cut)
    return loudness


def bell_draw(stream_key, dims, width, most, cuts=(), kind=jnp.bfloat16):
    values = width * jax.random.normal(stream_key, dims, jnp.float32)
    if cuts:
        values = values * steps_of(stream_key, dims, cuts, -0.22, 0.18)
    return jnp.clip(values, -most, most).astype(kind)


def setup_inputs(seed: int = 0) -> dict:
    key_list = jax.random.split(jax.random.key(seed), 14)
    resid_in = bell_draw(key_list[0], (STREAMS, LEN, D), 1.0, 6.0, ((0, 4), (1, 8)))
    out_grad = bell_draw(key_list[1], (STREAMS, LEN, D), 1.0, 6.0, ((0, 4), (1, 8)))
    row_lengths = draw_row_lengths(jax.random.fold_in(key_list[13], 71), 0)
    norm_gain = jnp.clip(1.0 + 0.18 * jax.random.normal(key_list[3], (D,), jnp.float32), 0.099609375, 1.8984375).astype(jnp.bfloat16)
    in_weight = bell_draw(key_list[4], (D, 2 * INNER), D ** -0.5, 0.125, ((0, 32),))
    conv_weight = bell_draw(key_list[5], (CONV, INNER), CONV ** -0.5, 3.0, ((1, 32),))
    conv_bias = bell_draw(key_list[6], (INNER,), 0.5, 3.0, ((0, 32),))
    xproj_weight = bell_draw(key_list[7], (INNER, RANK + 2 * STATE), INNER ** -0.5, 0.09375, ((0, 32),))
    dt_weight = bell_draw(key_list[8], (RANK, INNER), RANK ** -0.5, 0.5, ((1, 32),))
    dt_bias = jnp.clip(-4.59375 + 1.203125 * jax.random.uniform(key_list[9], (INNER,), jnp.float32) ** steps_of(key_list[9], (INNER,), ((0, 32),), -0.2, 0.2), -4.59375, -3.390625).astype(jnp.bfloat16)
    a_log = draw_a_log(jax.random.fold_in(key_list[13], 71), 0)
    skip_gain = jnp.clip(0.5 + 1.0 * jax.random.uniform(key_list[11], (INNER,), jnp.float32) ** steps_of(key_list[11], (INNER,), ((0, 32),), -0.2, 0.2), 0.5, 1.5).astype(jnp.bfloat16)
    out_weight = bell_draw(key_list[12], (INNER, D), INNER ** -0.5, 0.09375, ((0, 32),))
    return {"resid_in": resid_in, "out_grad": out_grad, "row_lengths": row_lengths, "norm_gain": norm_gain, "in_weight": in_weight, "conv_weight": conv_weight, "conv_bias": conv_bias, "xproj_weight": xproj_weight, "dt_weight": dt_weight, "dt_bias": dt_bias, "a_log": a_log, "skip_gain": skip_gain, "out_weight": out_weight}


EPSILON = 1e-05
HIGHEST = lax.Precision.HIGHEST

@jax.custom_vjp
def low(v):
    return lax.optimization_barrier(v.astype(jnp.bfloat16)).astype(jnp.float32)

@jax.custom_vjp
def low_back(v):
    return v

def low_keep(v):
    return (low(v), None)

def low_pass(kept, grad):
    return (grad,)

def back_keep(v):
    return (v, None)

def back_low(kept, grad):
    return (low(grad),)
low.defvjp(low_keep, low_pass)
low_back.defvjp(back_keep, back_low)

def product(left_mat, right_mat):
    return jnp.dot(left_mat, right_mat, precision=HIGHEST, preferred_element_type=jnp.float32)

def token_layout(lengths, n_tokens):
    doc_ends = jnp.cumsum(lengths).astype(jnp.int32)
    begins = (doc_ends - lengths).astype(jnp.int32)
    positions = jnp.arange(n_tokens, dtype=jnp.int32)
    live_slot = (lengths > 0)[None, :]
    doc_ids = lax.optimization_barrier(jnp.sum(((begins[None, :] <= positions[:, None]) & live_slot).astype(jnp.int32), axis=1)).astype(jnp.int32)
    start_flags = lax.optimization_barrier(jnp.sum(((begins[None, :] == positions[:, None]) & live_slot).astype(jnp.float32), axis=1))
    valid_mask = (positions < doc_ends[-1]).astype(jnp.float32)
    return (doc_ids, start_flags, valid_mask)

def scan_block(decay_rates, state_now, pieces):

    def one_token(hidden, piece):
        dt_step, act_in, kept_flag, write_in, readout = piece
        hidden = jnp.exp(dt_step[:, None] * decay_rates) * kept_flag * hidden + (dt_step * act_in)[:, None] * write_in[None, :]
        return (hidden, lax.optimization_barrier(jnp.sum(hidden * readout[None, :], axis=1)))
    return lax.scan(one_token, state_now, pieces)

def stream_forward(doc_ids, start_flags, valid_mask, residual, norm_gain, in_weight, conv_weight, conv_bias, xproj_weight, dt_weight, dt_bias, a_log, skip_gain, out_weight):
    n_tokens = residual.shape[0]
    inv_rms = lax.rsqrt(lax.optimization_barrier(jnp.mean(residual * residual, axis=-1, keepdims=True)) + EPSILON)
    normed_in = low(residual * inv_rms * norm_gain[None, :])
    mixed_in = low_back(product(normed_in, in_weight))
    conv_in = mixed_in[:, :INNER]
    gate_in = mixed_in[:, INNER:]
    padded_in = jnp.concatenate([jnp.zeros((CONV - 1, INNER), jnp.float32), conv_in], axis=0)
    padded_ids = jnp.concatenate([jnp.full((CONV - 1,), -1, jnp.int32), doc_ids.astype(jnp.int32)])
    conv_out = conv_bias[None, :]
    for tap_index in range(CONV):
        matches = (padded_ids[tap_index:tap_index + n_tokens] == doc_ids).astype(jnp.float32)[:, None]
        conv_out = conv_out + conv_weight[tap_index][None, :] * padded_in[tap_index:tap_index + n_tokens] * matches
    activated = low(jax.nn.silu(conv_out))
    projected = low_back(product(activated, xproj_weight))
    low_rank = low(projected[:, :RANK])
    write_in = projected[:, RANK:RANK + STATE]
    readout = projected[:, RANK + STATE:]
    dt_step = jax.nn.softplus(low_back(product(low_rank, dt_weight)) + dt_bias[None, :])
    decay_rates = -jnp.exp(a_log)
    block_len = math.gcd(n_tokens, 64)
    blocks = n_tokens // block_len
    pieces = (dt_step.reshape(blocks, block_len, INNER), activated.reshape(blocks, block_len, INNER), (1.0 - start_flags).reshape(blocks, block_len), write_in.reshape(blocks, block_len, STATE), readout.reshape(blocks, block_len, STATE))
    walk_block = jax.checkpoint(scan_block)

    def visit_block(state_now, piece):
        return walk_block(decay_rates, state_now, piece)
    final_state, scanned = lax.scan(visit_block, jnp.zeros((INNER, STATE), jnp.float32), pieces)
    ssm_out = scanned.reshape(n_tokens, INNER) + skip_gain[None, :] * activated
    gated = low(ssm_out * jax.nn.silu(gate_in) * valid_mask[:, None])
    return residual + product(gated, out_weight)

def reference(resid_in, out_grad, row_lengths, norm_gain, in_weight, conv_weight, conv_bias, xproj_weight, dt_weight, dt_bias, a_log, skip_gain, out_weight):
    weights = tuple((weight_arr.astype(jnp.float32) for weight_arr in (norm_gain, in_weight, conv_weight, conv_bias, xproj_weight, dt_weight, dt_bias, a_log, skip_gain, out_weight)))
    n_tokens = resid_in.shape[1]

    def per_stream(totals, pieces):
        residual, cotangent, lengths = pieces
        doc_ids, start_flags, valid_mask = token_layout(lengths, n_tokens)

        def forward(resid_now, *params):
            return stream_forward(doc_ids, start_flags, valid_mask, resid_now, *params)
        result, pull_back = jax.vjp(forward, residual.astype(jnp.float32), *weights)
        grads = pull_back(cotangent.astype(jnp.float32))
        totals = tuple((running + fresh for running, fresh in zip(totals, grads[1:])))
        return (totals, (result.astype(jnp.bfloat16), grads[0].astype(jnp.bfloat16)))
    zeros_start = tuple((jnp.zeros_like(weight_arr) for weight_arr in weights))
    totals, (outputs, in_grads) = lax.scan(per_stream, zeros_start, (resid_in, out_grad, row_lengths))
    return (outputs, in_grads, totals[0], totals[1], totals[2], totals[3], totals[4], totals[5], totals[6], totals[7], totals[8], totals[9])
```

```python
import jax
import jax.numpy as jnp
from jax import lax
from jax.experimental import pallas as pl
from jax.experimental.pallas import tpu as pltpu
from jax.sharding import PartitionSpec as P

CONV = 4
EPSILON = 1e-05
AXES = ("seq", "stream")
RESET = 1e30
GROUP = 16
LN2 = 0.6931471805599453
NT = (((1,), (1,)), ((), ()))

def fwd_end_body(dte_ref, dtx_ref, wide_ref, rate_ref, end_ref):
    n_tok = dte_ref.shape[0]
    n = rate_ref.shape[0]
    rate = rate_ref[...]

    def group(g, h):
        for p in range(GROUP):
            t = g * GROUP + p
            w = wide_ref[pl.ds(t * n, n), :]
            w = jnp.concatenate([w] * (rate.shape[1] // w.shape[1]), axis=1)
            h = jnp.exp2(dte_ref[pl.ds(t, 1), :] * rate) * h + dtx_ref[pl.ds(t, 1), :] * w
        return h

    end_ref[...] = lax.fori_loop(0, n_tok // GROUP, group, jnp.zeros_like(rate))

def fwd_end(dte, dtx, wide, rate, width=512):
    n_tok, chans = dte.shape
    n = rate.shape[0]
    return pl.pallas_call(
        fwd_end_body, grid=(chans // width,),
        in_specs=[pl.BlockSpec((n_tok, width), lambda c: (0, c)), pl.BlockSpec((n_tok, width), lambda c: (0, c)),
                  pl.BlockSpec(wide.shape, lambda c: (0, 0)), pl.BlockSpec((n, width), lambda c: (0, c))],
        out_specs=pl.BlockSpec((n, width), lambda c: (0, c)),
        out_shape=jax.ShapeDtypeStruct((n, chans), jnp.float32),
        compiler_params=pltpu.CompilerParams(vmem_limit_bytes=48 << 20), name="fwd_end",
    )(dte, dtx, wide, rate)

def bwd_end_body(dte_ref, grad_ref, wide_ref, rate_ref, end_ref):
    n_tok = dte_ref.shape[0]
    n = rate_ref.shape[0]
    rate = rate_ref[...]
    groups = n_tok // GROUP

    def group(k, g):
        for p in reversed(range(GROUP)):
            t = (groups - 1 - k) * GROUP + p
            w = wide_ref[pl.ds(t * n, n), :]
            w = jnp.concatenate([w] * (rate.shape[1] // w.shape[1]), axis=1)
            g = jnp.exp2(dte_ref[pl.ds(t, 1), :] * rate) * (g + grad_ref[pl.ds(t, 1), :] * w)
        return g

    end_ref[...] = lax.fori_loop(0, groups, group, jnp.zeros_like(rate))

def bwd_end(dte, grad, wide, rate, width=512):
    n_tok, chans = dte.shape
    n = rate.shape[0]
    return pl.pallas_call(
        bwd_end_body, grid=(chans // width,),
        in_specs=[pl.BlockSpec((n_tok, width), lambda c: (0, c)), pl.BlockSpec((n_tok, width), lambda c: (0, c)),
                  pl.BlockSpec(wide.shape, lambda c: (0, 0)), pl.BlockSpec((n, width), lambda c: (0, c))],
        out_specs=pl.BlockSpec((n, width), lambda c: (0, c)),
        out_shape=jax.ShapeDtypeStruct((n, chans), jnp.float32),
        compiler_params=pltpu.CompilerParams(vmem_limit_bytes=48 << 20), name="bwd_end",
    )(dte, grad, wide, rate)

def fwd_full_body(dte_ref, dtx_ref, wide_ref, read_ref, rate_ref, start_ref, y_ref, hist_ref, h_ref):
    block = dte_ref.shape[0]
    n = rate_ref.shape[0]
    span = GROUP * n
    at = pl.program_id(1)
    rate = rate_ref[...]

    @pl.when(at == 0)
    def _():
        h_ref[...] = start_ref[...]

    h0 = h_ref[...]
    hist_ref[pl.ds(0, n), :] = h0.astype(jnp.bfloat16)

    def group(g, h):
        for p in range(GROUP):
            t = g * GROUP + p
            w = wide_ref[pl.ds((at * block + t) * n, n), :]
            w = jnp.concatenate([w] * (rate.shape[1] // w.shape[1]), axis=1)
            h = jnp.exp2(dte_ref[pl.ds(t, 1), :] * rate) * h + dtx_ref[pl.ds(t, 1), :] * w
            hist_ref[pl.ds((t + 1) * n, n), :] = h.astype(jnp.bfloat16)
        y_ref[pl.ds(g * GROUP, GROUP), :] = jnp.dot(
            read_ref[pl.ds(g * GROUP, GROUP), :], hist_ref[pl.ds(n + g * span, span), :],
            preferred_element_type=jnp.float32)
        return h

    h_ref[...] = lax.fori_loop(0, block // GROUP, group, h0)

def fwd_full(dte, dtx, wide, read, rate, start, width=1024, block=128):
    n_tok, chans = dte.shape
    n = rate.shape[0]
    blocks = n_tok // block
    return pl.pallas_call(
        fwd_full_body, grid=(chans // width, blocks),
        in_specs=[pl.BlockSpec((block, width), lambda c, t: (t, c)), pl.BlockSpec((block, width), lambda c, t: (t, c)),
                  pl.BlockSpec(wide.shape, lambda c, t: (0, 0)),
                  pl.BlockSpec((block, read.shape[1]), lambda c, t: (t, 0)),
                  pl.BlockSpec((n, width), lambda c, t: (0, c)), pl.BlockSpec((n, width), lambda c, t: (0, c))],
        out_specs=[pl.BlockSpec((block, width), lambda c, t: (t, c)),
                   pl.BlockSpec(((block + 1) * n, width), lambda c, t: (t, c))],
        out_shape=[jax.ShapeDtypeStruct((n_tok, chans), jnp.float32),
                   jax.ShapeDtypeStruct((blocks * (block + 1) * n, chans), jnp.bfloat16)],
        scratch_shapes=[pltpu.VMEM((n, width), jnp.float32)],
        compiler_params=pltpu.CompilerParams(vmem_limit_bytes=56 << 20), name="fwd_full",
    )(dte, dtx, wide, read, rate, start)

def bwd_full_body(dte_ref, dtx_ref, grad_ref, hist_ref, wide_ref, write_ref, ones_ref, rate_ref, start_ref,
                  s1_ref, s2_ref, grate_ref, dw_ref, dr_ref, g_ref, adj_ref, r_ref):
    block = dte_ref.shape[0]
    n = rate_ref.shape[0]
    span = GROUP * n
    blocks = pl.num_programs(1)
    step = pl.program_id(1)
    at = blocks - 1 - step
    rate = rate_ref[...]
    groups = block // GROUP
    bf = jnp.bfloat16

    @pl.when(step == 0)
    def _():
        g_ref[...] = start_ref[...]
        grate_ref[...] = jnp.zeros_like(grate_ref)

    @pl.when((step == 0) & (pl.program_id(0) == 0))
    def _():
        dw_ref[...] = jnp.zeros_like(dw_ref)
        dr_ref[...] = jnp.zeros_like(dr_ref)

    def group(k, g):
        q = groups - 1 - k
        for p in reversed(range(GROUP)):
            t = q * GROUP + p
            w = wide_ref[pl.ds((at * block + t) * n, n), :]
            w = jnp.concatenate([w] * (rate.shape[1] // w.shape[1]), axis=1)
            lam = dte_ref[pl.ds(t, 1), :] * rate
            adj = g + grad_ref[pl.ds(t, 1), :] * w
            g = jnp.exp2(lam) * adj
            adj_ref[pl.ds(p * n, n), :] = adj.astype(bf)
            r_ref[pl.ds(p * n, n), :] = g.astype(bf) * hist_ref[pl.ds(t * n, n), :] * lam.astype(bf)
        rows = pl.ds(q * GROUP, GROUP)
        adj_all = adj_ref[...]
        s1_ref[rows, :] = jnp.dot(write_ref[rows, :], adj_all, preferred_element_type=jnp.float32)
        sums = jnp.dot(ones_ref[...], r_ref[...], preferred_element_type=jnp.float32)
        s2_ref[rows, :] = sums[:GROUP]
        grate_ref[...] += sums[GROUP:]
        whole = pl.ds(at * block + q * GROUP, GROUP)
        dw_ref[whole, :] += lax.dot_general(dtx_ref[rows, :].astype(bf), adj_all, NT, preferred_element_type=jnp.float32)
        dr_ref[whole, :] += lax.dot_general(grad_ref[rows, :].astype(bf), hist_ref[pl.ds(n + q * span, span), :], NT,
                                            preferred_element_type=jnp.float32)
        return g

    g_ref[...] = lax.fori_loop(0, groups, group, g_ref[...])

def bwd_full(dte, dtx, grad, hist, wide, write, rate, start, width=1024, block=128):
    n_tok, chans = dte.shape
    n = rate.shape[0]
    blocks = n_tok // block
    span = GROUP * n
    col = jnp.arange(span)
    ones = jnp.concatenate([(col // n)[None, :] == jnp.arange(GROUP)[:, None], (col % n)[None, :] == jnp.arange(n)[:, None]]).astype(jnp.bfloat16)
    tok = lambda c, t: (blocks - 1 - t, c)
    return pl.pallas_call(
        bwd_full_body, grid=(chans // width, blocks),
        in_specs=[pl.BlockSpec((block, width), tok), pl.BlockSpec((block, width), tok), pl.BlockSpec((block, width), tok),
                  pl.BlockSpec(((block + 1) * n, width), tok),
                  pl.BlockSpec(wide.shape, lambda c, t: (0, 0)),
                  pl.BlockSpec((block, span), lambda c, t: (blocks - 1 - t, 0)),
                  pl.BlockSpec(ones.shape, lambda c, t: (0, 0)),
                  pl.BlockSpec((n, width), lambda c, t: (0, c)), pl.BlockSpec((n, width), lambda c, t: (0, c))],
        out_specs=[pl.BlockSpec((block, width), tok), pl.BlockSpec((block, width), tok),
                   pl.BlockSpec((n, width), lambda c, t: (0, c)),
                   pl.BlockSpec((n_tok, span), lambda c, t: (0, 0)), pl.BlockSpec((n_tok, span), lambda c, t: (0, 0))],
        out_shape=[jax.ShapeDtypeStruct((n_tok, chans), jnp.float32), jax.ShapeDtypeStruct((n_tok, chans), jnp.float32),
                   jax.ShapeDtypeStruct((n, chans), jnp.float32),
                   jax.ShapeDtypeStruct((n_tok, span), jnp.float32), jax.ShapeDtypeStruct((n_tok, span), jnp.float32)],
        scratch_shapes=[pltpu.VMEM((n, width), jnp.float32), pltpu.VMEM((span, width), jnp.bfloat16), pltpu.VMEM((span, width), jnp.bfloat16)],
        compiler_params=pltpu.CompilerParams(vmem_limit_bytes=56 << 20), name="bwd_full",
    )(dte, dtx, grad, hist, wide, write, ones, rate, start)

def widen(v):
    return jnp.broadcast_to(v.reshape(-1)[:, None], (v.size, 128))

def diag_rows(v):
    T, n = v.shape
    sel = (jnp.arange(T)[:, None] % GROUP == jnp.arange(GROUP)[None, :])
    return jnp.where(sel[:, :, None], v[:, None, :], 0).reshape(T, GROUP * n).astype(jnp.bfloat16)

def undiag(d, n):
    T = d.shape[0]
    sel = (jnp.arange(T)[:, None] % GROUP == jnp.arange(GROUP)[None, :])
    return jnp.sum(jnp.where(sel[:, :, None], d.reshape(T, GROUP, n), 0), axis=1)


def passed_along(block, axis, distance):
    devices = range(lax.axis_size(axis))
    route = [(i - distance, i) for i in devices if i - distance in devices]
    return lax.ppermute(block, axis, route)


def silu_slope(values_in):
    sigmoid_v = jax.nn.sigmoid(values_in)
    return sigmoid_v * (1.0 + values_in * (1.0 - sigmoid_v))


def norm_rows(residual, norm_scale):
    inv_rms = lax.rsqrt(jnp.mean(residual * residual, axis=-1, keepdims=True) + EPSILON)
    return residual * inv_rms * norm_scale[None, :]


def token_layout(lengths, first_pos, n_tokens):
    doc_ends = jnp.cumsum(lengths)
    begins = doc_ends - lengths
    positions = first_pos + jnp.arange(n_tokens, dtype=jnp.int32)
    live_slot = (lengths > 0)[None, :]
    doc_ids = jnp.sum(((begins[None, :] <= positions[:, None]) & live_slot).astype(jnp.int32), axis=1)
    start_flags = jnp.sum(((begins[None, :] == positions[:, None]) & live_slot).astype(jnp.float32), axis=1)
    valid_mask = (positions < doc_ends[-1]).astype(jnp.float32)
    return (doc_ids, start_flags, valid_mask)


def contract_rows(left_mat, right_mat):
    return lax.dot_general(left_mat, right_mat, (((0,), (0,)), ((), ())), preferred_element_type=jnp.float32)


def contract_cols(left_mat, right_mat):
    return lax.dot_general(left_mat, right_mat, NT, preferred_element_type=jnp.float32)


def carried(ends, step_sum, rate, backward):
    high = step_sum.astype(jnp.bfloat16)
    low = (step_sum - high.astype(jnp.float32)).astype(jnp.bfloat16)
    n = ends.shape[0]
    sent = jnp.concatenate([ends.astype(jnp.bfloat16), high[None], low[None]], axis=0)
    gathered = lax.all_gather(sent, "seq")
    count = lax.axis_size("seq")
    place = lax.axis_index("seq")
    state = jnp.zeros_like(ends)
    for step in range(count - 1):
        source = count - 1 - step if backward else step
        block = gathered[source].astype(jnp.float32)
        joined = jnp.exp2((block[n] + block[n + 1])[None, :] * rate) * state + block[:n]
        state = jnp.where(source > place if backward else source < place, joined, state)
    return state


def local(resid_in, out_grad, row_lengths, norm_gain, in_weight, conv_weight, conv_bias, xproj_weight, dt_weight,
          dt_bias, a_log, skip_gain, out_weight):
    bf, f32 = jnp.bfloat16, jnp.float32
    own_chans = conv_bias.shape[0]
    own_feats = norm_gain.shape[0]
    rank_dim = dt_weight.shape[0]
    state_dim = a_log.shape[1]
    proj_dim = xproj_weight.shape[1]
    half = in_weight.shape[1] // 2
    in_conv = lax.all_gather(in_weight[:, :half], AXES, axis=0, tiled=True)
    packed = jnp.concatenate(
        [xproj_weight, dt_weight.T, a_log, conv_weight.T, conv_bias[:, None], dt_bias[:, None], skip_gain[:, None],
         jnp.pad(norm_gain, (0, own_chans - own_feats))[:, None]], axis=1)
    packed = lax.all_gather(packed, AXES, axis=0, tiled=True)
    in_gate = lax.all_gather(in_weight[:, half:], AXES, axis=0, tiled=True)
    out_full = lax.all_gather(out_weight, AXES, axis=0, tiled=True)
    at = 0
    xproj_full = packed[:, :proj_dim]
    at = proj_dim
    dtw_cols = packed[:, at : at + rank_dim]
    at += rank_dim
    log_rates = packed[:, at : at + state_dim].astype(f32).T
    at += state_dim
    conv_taps = packed[:, at : at + CONV].astype(f32).T
    at += CONV
    conv_shift, dt_shift, skip_vec = (packed[:, at + i].astype(f32) for i in range(3))
    norm_scale = packed[:, at + 3].reshape(-1, own_chans)[:, :own_feats].reshape(-1).astype(f32)
    rate = -jnp.exp(log_rates) / LN2

    residual = resid_in[0].astype(f32)
    n_tokens = residual.shape[0]
    rim_width = CONV - 1
    first_pos = lax.axis_index("seq") * n_tokens
    doc_ids, start_flags, valid_mask = token_layout(row_lengths[0], first_pos - rim_width, n_tokens + 2 * rim_width)
    own_ids = doc_ids[rim_width : rim_width + n_tokens]
    starts = start_flags[rim_width : rim_width + n_tokens]
    valid_mask = valid_mask[rim_width : rim_width + n_tokens]
    normed_f, norm_pull = jax.vjp(norm_rows, residual, norm_scale)
    normed_in = normed_f.astype(bf)
    conv_in = jnp.dot(normed_in, in_conv, preferred_element_type=f32)
    gate_in = jnp.dot(normed_in, in_gate, preferred_element_type=f32)
    earlier_rows = passed_along(conv_in[n_tokens - rim_width :].astype(bf), "seq", 1).astype(f32)
    padded_in = jnp.concatenate([earlier_rows, conv_in], axis=0)
    matches = [(doc_ids[tap : tap + n_tokens] == own_ids).astype(f32)[:, None] for tap in range(CONV)]
    conv_out = conv_shift[None, :]
    for tap in range(CONV):
        conv_out = conv_out + conv_taps[tap][None, :] * padded_in[tap : tap + n_tokens] * matches[tap]
    activated = jax.nn.silu(conv_out).astype(bf)
    act_float = activated.astype(f32)
    projected = jnp.dot(activated, xproj_full, preferred_element_type=f32)
    low_rank = projected[:, :rank_dim].astype(bf)
    write_in = projected[:, rank_dim : rank_dim + state_dim]
    readout = projected[:, rank_dim + state_dim :]
    dt_pre = contract_cols(low_rank, dtw_cols) + dt_shift[None, :]
    dt_step = jax.nn.softplus(dt_pre)
    dt_reset = jnp.where(starts[:, None] > 0, RESET, dt_step)
    dt_act = dt_step * act_float
    write_wide, read_wide = widen(write_in), widen(readout)
    write_diag, read_diag = diag_rows(write_in), diag_rows(readout)

    step_sum = jnp.sum(dt_reset, axis=0)
    ends = fwd_end(dt_reset, dt_act, write_wide, rate)
    start_state = carried(ends, step_sum, rate, False)
    scanned, history = fwd_full(dt_reset, dt_act, write_wide, read_diag, rate, start_state)
    ssm_out = scanned + skip_vec[None, :] * act_float
    gate_act = jax.nn.silu(gate_in)
    gated = (ssm_out * gate_act * valid_mask[:, None]).astype(bf)
    output = (residual + jnp.dot(gated, out_full, preferred_element_type=f32)).astype(bf)
    cotangent = out_grad[0]
    d_gated = contract_cols(cotangent, out_full)
    g_out = lax.psum_scatter(contract_rows(gated, cotangent).astype(bf), AXES, scatter_dimension=0, tiled=True)
    d_masked = d_gated * valid_mask[:, None]
    d_ssm = d_masked * gate_act
    d_gate = (d_masked * ssm_out * silu_slope(gate_in)).astype(bf)
    g_in_gate = lax.psum_scatter(contract_rows(normed_in, d_gate).astype(bf), AXES, scatter_dimension=0, tiled=True)
    d_normed_gate = contract_cols(d_gate, in_gate)
    g_skip = jnp.sum(d_ssm * act_float, axis=0)
    back_ends = bwd_end(dt_reset, d_ssm, read_wide, rate)
    later_sum = carried(back_ends, step_sum, rate, True)
    sum_write, sum_rate, g_log, d_write, d_read = bwd_full(
        dt_reset, dt_act, d_ssm, history, read_wide, write_diag, rate, later_sum)
    d_write, d_read = undiag(d_write, state_dim), undiag(d_read, state_dim)
    g_log = g_log * LN2
    per_step = jnp.where(dt_step > 1e-30, sum_rate * LN2 / jnp.maximum(dt_step, 1e-30), 0.0)
    d_step = per_step + act_float * sum_write
    d_pre = d_step * jax.nn.sigmoid(dt_pre)
    g_dt_bias = jnp.sum(d_pre, axis=0)
    d_pre_low = d_pre.astype(bf)
    g_dt = contract_rows(d_pre_low, low_rank)
    d_low = jnp.dot(d_pre_low, dtw_cols, preferred_element_type=f32)
    d_proj = jnp.concatenate([d_low, d_write, d_read], axis=1).astype(bf)
    g_xproj = contract_rows(activated, d_proj)
    d_act = dt_step * sum_write + skip_vec[None, :] * d_ssm + contract_cols(d_proj, xproj_full)
    d_conv = d_act * silu_slope(conv_out)
    g_conv_bias = jnp.sum(d_conv, axis=0)
    g_conv = jnp.stack(
        [jnp.sum(d_conv * padded_in[tap : tap + n_tokens] * matches[tap], axis=0) for tap in range(CONV)], axis=1)
    later_rows = passed_along(d_conv[:rim_width].astype(bf), "seq", -1).astype(f32)
    d_ext = jnp.concatenate([d_conv, later_rows], axis=0)
    d_conv_in = jnp.zeros_like(d_conv)
    for tap in range(CONV):
        offset = rim_width - tap
        match_back = (doc_ids[rim_width + offset : rim_width + offset + n_tokens] == own_ids).astype(f32)[:, None]
        d_conv_in = d_conv_in + conv_taps[tap][None, :] * d_ext[offset : offset + n_tokens] * match_back
    d_conv_in = d_conv_in.astype(bf)
    g_in_conv = lax.psum_scatter(contract_rows(normed_in, d_conv_in).astype(bf), AXES, scatter_dimension=0, tiled=True)
    d_normed = contract_cols(d_conv_in, in_conv) + d_normed_gate
    d_resid, g_gain = norm_pull(d_normed)
    in_grad = (d_resid + cotangent.astype(f32)).astype(bf)
    g_gain = jnp.pad(g_gain.reshape(-1, own_feats), ((0, 0), (0, own_chans - own_feats))).reshape(-1)
    small = jnp.concatenate(
        [g_xproj, g_dt, g_log.T, g_conv, g_conv_bias[:, None], g_dt_bias[:, None], g_skip[:, None], g_gain[:, None]],
        axis=1)
    small = lax.psum_scatter(small, AXES, scatter_dimension=0, tiled=True)
    at = proj_dim + rank_dim
    return (
        output[None],
        in_grad[None],
        small[:own_feats, at + state_dim + CONV + 3],
        jnp.concatenate([g_in_conv, g_in_gate], axis=1).astype(f32),
        small[:, at + state_dim : at + state_dim + CONV].T,
        small[:, at + state_dim + CONV],
        small[:, :proj_dim],
        small[:, proj_dim:at].T,
        small[:, at + state_dim + CONV + 1],
        small[:, at : at + state_dim],
        small[:, at + state_dim + CONV + 2],
        g_out.astype(f32),
    )


def solution(mesh):
    in_specs = (
        P("stream", "seq", None),
        P("stream", "seq", None),
        P("stream", None),
        P(("seq", "stream")),
        P(("seq", "stream"), None),
        P(None, ("seq", "stream")),
        P(("seq", "stream")),
        P(("seq", "stream"), None),
        P(None, ("seq", "stream")),
        P(("seq", "stream")),
        P(("seq", "stream"), None),
        P(("seq", "stream")),
        P(("seq", "stream"), None),
    )
    out_specs = (
        P("stream", "seq", None),
        P("stream", "seq", None),
        P(("seq", "stream")),
        P(("seq", "stream"), None),
        P(None, ("seq", "stream")),
        P(("seq", "stream")),
        P(("seq", "stream"), None),
        P(None, ("seq", "stream")),
        P(("seq", "stream")),
        P(("seq", "stream"), None),
        P(("seq", "stream")),
        P(("seq", "stream"), None),
    )
    return jax.shard_map(local, mesh=mesh, in_specs=in_specs, out_specs=out_specs, check_vma=False)
```

```python
import functools

import jax
import jax.numpy as jnp
from jax import lax
from jax.experimental import pallas as pl
from jax.experimental.pallas import tpu as pltpu
from jax.sharding import PartitionSpec as P

CONV = 4
EPSILON = 1e-05
RESET = 1e30
GROUP = 16
LN2 = 0.6931471805599453
NT = (((1,), (1,)), ((), ()))
VMEM_LIMIT = 56 << 20


def across(rows, width):
    return jnp.concatenate([rows] * (width // rows.shape[1]), axis=1)


def fwd_end_body(dte_ref, dtx_ref, wide_ref, rate_ref, end_ref):
    n, width = rate_ref.shape
    rate = rate_ref[...]

    def group(at, state):
        for place in range(GROUP):
            t = at * GROUP + place
            write = across(wide_ref[pl.ds(t * n, n), :], width)
            state = jnp.exp2(dte_ref[pl.ds(t, 1), :] * rate) * state + dtx_ref[pl.ds(t, 1), :] * write
        return state

    end_ref[...] = lax.fori_loop(0, dte_ref.shape[0] // GROUP, group, jnp.zeros_like(rate))


def bwd_end_body(dte_ref, grad_ref, wide_ref, rate_ref, end_ref):
    n, width = rate_ref.shape
    rate = rate_ref[...]
    groups = dte_ref.shape[0] // GROUP

    def group(step, state):
        for place in reversed(range(GROUP)):
            t = (groups - 1 - step) * GROUP + place
            read = across(wide_ref[pl.ds(t * n, n), :], width)
            state = jnp.exp2(dte_ref[pl.ds(t, 1), :] * rate) * (state + grad_ref[pl.ds(t, 1), :] * read)
        return state

    end_ref[...] = lax.fori_loop(0, groups, group, jnp.zeros_like(rate))


def scan_end(body, dte, other, wide, rate, seqs, width=512):
    tokens, chans = dte.shape
    length = tokens // seqs
    n = rate.shape[0]
    width = min(width, chans)
    work = tokens * chans * n
    return pl.pallas_call(
        body,
        grid=(seqs, chans // width),
        in_specs=[
            pl.BlockSpec((length, width), lambda s, c: (s, c)),
            pl.BlockSpec((length, width), lambda s, c: (s, c)),
            pl.BlockSpec((length * n, wide.shape[1]), lambda s, c: (s, 0)),
            pl.BlockSpec((n, width), lambda s, c: (0, c)),
        ],
        out_specs=pl.BlockSpec((n, width), lambda s, c: (s, c)),
        out_shape=jax.ShapeDtypeStruct((seqs * n, chans), jnp.float32),
        compiler_params=pltpu.CompilerParams(vmem_limit_bytes=VMEM_LIMIT),
        cost_estimate=pl.CostEstimate(flops=4 * work, transcendentals=work, bytes_accessed=8 * tokens * chans),
        name=body.__name__[:7],
    )(dte, other, wide, rate)


def fwd_full_body(dte_ref, dtx_ref, wide_ref, read_ref, rate_ref, start_ref, y_ref, hist_ref, h_ref):
    block = dte_ref.shape[0]
    n, width = rate_ref.shape
    span = GROUP * n
    rate = rate_ref[...]

    @pl.when(pl.program_id(2) == 0)
    def _():
        h_ref[...] = start_ref[...]

    first = h_ref[...]
    hist_ref[pl.ds(0, n), :] = first.astype(jnp.bfloat16)

    def group(at, state):
        for place in range(GROUP):
            t = at * GROUP + place
            write = across(wide_ref[pl.ds(t * n, n), :], width)
            state = jnp.exp2(dte_ref[pl.ds(t, 1), :] * rate) * state + dtx_ref[pl.ds(t, 1), :] * write
            hist_ref[pl.ds((t + 1) * n, n), :] = state.astype(jnp.bfloat16)
        y_ref[pl.ds(at * GROUP, GROUP), :] = jnp.dot(
            read_ref[pl.ds(at * GROUP, GROUP), :],
            hist_ref[pl.ds(n + at * span, span), :],
            preferred_element_type=jnp.float32,
        )
        return state

    h_ref[...] = lax.fori_loop(0, block // GROUP, group, first)


def fwd_full(dte, dtx, wide, read, rate, start, seqs, width=1024, block=128):
    tokens, chans = dte.shape
    n = rate.shape[0]
    width = min(width, chans)
    blocks = tokens // seqs // block
    work = tokens * chans * n
    here = lambda c, s, t: (s * blocks + t, c)
    rows = lambda c, s, t: (s * blocks + t, 0)
    return pl.pallas_call(
        fwd_full_body,
        grid=(chans // width, seqs, blocks),
        in_specs=[
            pl.BlockSpec((block, width), here),
            pl.BlockSpec((block, width), here),
            pl.BlockSpec((block * n, wide.shape[1]), rows),
            pl.BlockSpec((block, read.shape[1]), rows),
            pl.BlockSpec((n, width), lambda c, s, t: (0, c)),
            pl.BlockSpec((n, width), lambda c, s, t: (s, c)),
        ],
        out_specs=[pl.BlockSpec((block, width), here), pl.BlockSpec(((block + 1) * n, width), here)],
        out_shape=[
            jax.ShapeDtypeStruct((tokens, chans), jnp.float32),
            jax.ShapeDtypeStruct((seqs * blocks * (block + 1) * n, chans), jnp.bfloat16),
        ],
        scratch_shapes=[pltpu.VMEM((n, width), jnp.float32)],
        compiler_params=pltpu.CompilerParams(vmem_limit_bytes=VMEM_LIMIT),
        cost_estimate=pl.CostEstimate(flops=8 * work, transcendentals=work, bytes_accessed=2 * work),
        name="fwd_full",
    )(dte, dtx, wide, read, rate, start)


def bwd_full_body(dte_ref, dtx_ref, grad_ref, hist_ref, wide_ref, write_ref, ones_ref, rate_ref, start_ref,
                  s1_ref, s2_ref, grate_ref, dw_ref, dr_ref, g_ref, adj_ref, r_ref):
    block = dte_ref.shape[0]
    n, width = rate_ref.shape
    span = GROUP * n
    rate = rate_ref[...]
    groups = block // GROUP
    bf = jnp.bfloat16

    @pl.when(pl.program_id(2) == 0)
    def _():
        g_ref[...] = start_ref[...]

    @pl.when((pl.program_id(2) == 0) & (pl.program_id(1) == 0))
    def _():
        grate_ref[...] = jnp.zeros_like(grate_ref)

    def group(step, state):
        at = groups - 1 - step
        for place in reversed(range(GROUP)):
            t = at * GROUP + place
            read = across(wide_ref[pl.ds(t * n, n), :], width)
            power = dte_ref[pl.ds(t, 1), :] * rate
            adjoint = state + grad_ref[pl.ds(t, 1), :] * read
            state = jnp.exp2(power) * adjoint
            adj_ref[pl.ds(place * n, n), :] = adjoint.astype(bf)
            r_ref[pl.ds(place * n, n), :] = state.astype(bf) * hist_ref[pl.ds(t * n, n), :] * power.astype(bf)
        rows = pl.ds(at * GROUP, GROUP)
        adj_all = adj_ref[...]
        s1_ref[rows, :] = jnp.dot(write_ref[rows, :], adj_all, preferred_element_type=jnp.float32)
        sums = jnp.dot(ones_ref[...], r_ref[...], preferred_element_type=jnp.float32)
        s2_ref[rows, :] = sums[:GROUP]
        grate_ref[...] += sums[GROUP:]
        dw_ref[rows, :] = lax.dot_general(
            dtx_ref[rows, :].astype(bf), adj_all, NT, preferred_element_type=jnp.float32)
        dr_ref[rows, :] = lax.dot_general(
            grad_ref[rows, :].astype(bf), hist_ref[pl.ds(n + at * span, span), :], NT,
            preferred_element_type=jnp.float32)
        return state

    g_ref[...] = lax.fori_loop(0, groups, group, g_ref[...])


def bwd_full(dte, dtx, grad, hist, wide, write, rate, start, seqs, width=1024, block=128):
    tokens, chans = dte.shape
    n = rate.shape[0]
    width = min(width, chans)
    strips = chans // width
    blocks = tokens // seqs // block
    span = GROUP * n
    work = tokens * chans * n
    column = jnp.arange(span)
    ones = jnp.concatenate(
        [(column // n)[None, :] == jnp.arange(GROUP)[:, None], (column % n)[None, :] == jnp.arange(n)[:, None]]
    ).astype(jnp.bfloat16)
    here = lambda c, s, t: (s * blocks + blocks - 1 - t, c)
    rows = lambda c, s, t: (s * blocks + blocks - 1 - t, 0)
    strip = lambda c, s, t: (c * seqs * blocks + s * blocks + blocks - 1 - t, 0)
    f32 = jnp.float32
    s1, s2, grate, dw, dr = pl.pallas_call(
        bwd_full_body,
        grid=(strips, seqs, blocks),
        in_specs=[
            pl.BlockSpec((block, width), here),
            pl.BlockSpec((block, width), here),
            pl.BlockSpec((block, width), here),
            pl.BlockSpec(((block + 1) * n, width), here),
            pl.BlockSpec((block * n, wide.shape[1]), rows),
            pl.BlockSpec((block, span), rows),
            pl.BlockSpec(ones.shape, lambda c, s, t: (0, 0)),
            pl.BlockSpec((n, width), lambda c, s, t: (0, c)),
            pl.BlockSpec((n, width), lambda c, s, t: (s, c)),
        ],
        out_specs=[
            pl.BlockSpec((block, width), here),
            pl.BlockSpec((block, width), here),
            pl.BlockSpec((n, width), lambda c, s, t: (0, c)),
            pl.BlockSpec((block, span), strip),
            pl.BlockSpec((block, span), strip),
        ],
        out_shape=[
            jax.ShapeDtypeStruct((tokens, chans), f32),
            jax.ShapeDtypeStruct((tokens, chans), f32),
            jax.ShapeDtypeStruct((n, chans), f32),
            jax.ShapeDtypeStruct((strips * tokens, span), f32),
            jax.ShapeDtypeStruct((strips * tokens, span), f32),
        ],
        scratch_shapes=[
            pltpu.VMEM((n, width), f32),
            pltpu.VMEM((span, width), jnp.bfloat16),
            pltpu.VMEM((span, width), jnp.bfloat16),
        ],
        compiler_params=pltpu.CompilerParams(vmem_limit_bytes=VMEM_LIMIT),
        cost_estimate=pl.CostEstimate(flops=14 * work, transcendentals=work, bytes_accessed=2 * work),
        name="bwd_full",
    )(dte, dtx, grad, hist, wide, write, ones, rate, start)
    return s1, s2, grate, diagonal(dw.reshape(strips, tokens, span).sum(0), n), diagonal(
        dr.reshape(strips, tokens, span).sum(0), n)


def widen(values):
    return jnp.broadcast_to(values.reshape(-1)[:, None], (values.size, 128))


def spread(values):
    tokens, n = values.shape
    own = jnp.arange(tokens)[:, None] % GROUP == jnp.arange(GROUP)[None, :]
    return jnp.where(own[:, :, None], values[:, None, :], 0).reshape(tokens, GROUP * n).astype(jnp.bfloat16)


def diagonal(sums, n):
    tokens = sums.shape[0]
    own = jnp.arange(tokens)[:, None] % GROUP == jnp.arange(GROUP)[None, :]
    return jnp.sum(jnp.where(own[:, :, None], sums.reshape(tokens, GROUP, n), 0), axis=1)


MESH = pl.DeviceIdType.MESH


class Grid:
    def __init__(self, axis, size, inner):
        self.axis, self.inner, self.outer = axis, inner, size // inner
        me = lax.axis_index(axis)
        self.row, self.col = me // inner, me % inner

    def device(self, row, col):
        return {self.axis: row * self.inner + col}

    def neighbours(self):
        row, col = self.row, self.col
        found = []
        if self.outer > 1:
            found += [(row > 0, self.device(row - 1, col)), (row < self.outer - 1, self.device(row + 1, col))]
        if self.inner > 1:
            found += [(col > 0, self.device(row, col - 1)), (col < self.inner - 1, self.device(row, col + 1))]
        return found


def greet(grids):
    barrier = pltpu.get_barrier_semaphore()
    count = 0
    for grid in grids:
        for there, device in grid.neighbours():

            @pl.when(there)
            def _(device=device):
                pl.semaphore_signal(barrier, inc=1, device_id=device, device_id_type=MESH)

            count = count + there.astype(jnp.int32)
    pl.semaphore_wait(barrier, count)


def gather_steps(grid, whole_ref, out_ref, send_sem, recv_sem, own_sem, waits, chunk, chunks):
    rows = whole_ref.shape[0]
    part = rows // chunks
    src_ref = whole_ref.at[pl.ds(chunk * part, part)]
    outer, inner = grid.outer, grid.inner
    row, col = grid.row, grid.col

    def place(r, c):
        return pl.ds(pl.multiple_of((r * inner + c) * rows + chunk * part, part), part)

    def send(there, way, r, c, device, source):
        copy = pltpu.make_async_remote_copy(
            src_ref=source, dst_ref=out_ref.at[place(r, c)], send_sem=send_sem.at[way, r * inner + c],
            recv_sem=recv_sem.at[r * inner + c], device_id=device, device_id_type=MESH)

        @pl.when(there)
        def _():
            copy.start()

        waits.append((there, copy))

    def across(there, r, c, source):
        if inner > 1:
            send(there & (c >= col) & (col > 0), 2, r, c, grid.device(row, col - 1), source)
            send(there & (c <= col) & (col < inner - 1), 3, r, c, grid.device(row, col + 1), source)

    def along(there, r, source):
        if outer > 1:
            send(there & (r >= row) & (row > 0), 0, r, col, grid.device(row - 1, col), source)
            send(there & (r <= row) & (row < outer - 1), 1, r, col, grid.device(row + 1, col), source)

    def arrive(there, r, c):
        copy = pltpu.make_async_remote_copy(
            src_ref=src_ref, dst_ref=out_ref.at[place(r, c)], send_sem=send_sem.at[0, 0],
            recv_sem=recv_sem.at[r * inner + c], device_id=grid.device(row, col), device_id_type=MESH)

        @pl.when(there)
        def _():
            copy.wait_recv()

    always = row >= 0
    along(always, row, src_ref)
    across(always, row, col, src_ref)
    own = pltpu.make_async_copy(src_ref, out_ref.at[place(row, col)], own_sem)
    own.start()
    waits.append((None, own))
    for _ in range(chunk + 1):
        yield
    for distance in range(1, outer):
        for r in (row - distance, row + distance):
            there = (r >= 0) & (r < outer)
            arrive(there, r, col)
            along(there, r, out_ref.at[place(r, col)])
            across(there, r, col, out_ref.at[place(r, col)])
        yield
    for step in range(1, inner):
        for distance in range(outer):
            for r in (row - distance, row + distance) if distance else (row,):
                for c in (col - step, col + step):
                    there = (r >= 0) & (r < outer) & (c >= 0) & (c < inner)
                    arrive(there, r, c)
                    if step < inner - 1:
                        across(there, r, c, out_ref.at[place(r, c)])
            yield


def finish(waits):
    for there, copy in waits:
        if there is None:
            copy.wait()
        else:

            @pl.when(there)
            def _(copy=copy):
                copy.wait_send()


def in_turn(runs):
    runs = list(runs)
    while runs:
        left = []
        for run in runs:
            if next(run, run) is not run:
                left.append(run)
        runs = left


def link_gather(arrays, sizes, collective_id):
    count = len(arrays)
    axes = sorted({entry[0] for entry in arrays})

    def kernel(*refs):
        sources, outs, sems = refs[:count], refs[count : 2 * count], refs[2 * count :]
        grids = {axis: Grid(axis, *sizes[axis]) for axis in axes}
        greet([grids[axis] for axis in axes])
        waits = []
        runs = []
        for i, (axis, _, chunks) in enumerate(arrays):
            for chunk in range(chunks):
                runs.append(gather_steps(grids[axis], sources[i], outs[i], *sems[:3], waits, chunk, chunks))
                sems = sems[3:]
        in_turn(runs)
        finish(waits)

    sems = []
    for axis, _, chunks in arrays:
        size = sizes[axis][0]
        sems += [pltpu.SemaphoreType.DMA((4, size)), pltpu.SemaphoreType.DMA((size,)), pltpu.SemaphoreType.DMA] * chunks
    return pl.pallas_call(
        kernel,
        in_specs=[pl.BlockSpec(memory_space=pl.ANY)] * count,
        out_specs=[pl.BlockSpec(memory_space=pl.ANY)] * count,
        out_shape=[
            jax.ShapeDtypeStruct((sizes[axis][0] * a.shape[0], *a.shape[1:]), a.dtype) for axis, a, _ in arrays],
        scratch_shapes=sems,
        compiler_params=pltpu.CompilerParams(collective_id=collective_id, has_side_effects=True),
        name="link_gather",
    )(*[a for _, a, _ in arrays])


def reduce_steps(grid, src_ref, out_ref, acc, inner_buf, outer_buf, sems, waits, chunk, chunks):
    outer, inner = grid.outer, grid.inner
    row, col = grid.row, grid.col
    rows, part = acc.shape[0] // (outer * inner), acc.shape[0] // (outer * inner * chunks)
    piece = min(part, 64)
    load_sem, inner_send, inner_recv, outer_send, outer_recv, out_sem = sems

    def place(r, c):
        return pl.ds(pl.multiple_of((r * inner + c) * rows + chunk * part, part), part)

    def add(r, c, buf):
        start = (r * inner + c) * rows + chunk * part

        @pl.loop(0, part // piece)
        def _(k):
            here = pl.ds(pl.multiple_of(start + k * piece, piece), piece)
            there = pl.ds(pl.multiple_of(k * piece, piece), piece)
            acc[here, :] = (acc[here, :].astype(jnp.float32) + buf[there, :].astype(jnp.float32)).astype(acc.dtype)

    def line(me, size, device, block, buf, send, recv):
        def hop(there, target, onward, slot):
            copy = pltpu.make_async_remote_copy(
                src_ref=acc.at[place(*block(target))], dst_ref=buf.at[slot], send_sem=send.at[target],
                recv_sem=recv.at[slot], device_id=device(onward), device_id_type=MESH)

            @pl.when(there)
            def _():
                copy.start()

            waits.append((there, copy))

        def from_low(target):
            return target if size > 2 else 0

        def from_high(target, owner):
            return jnp.where(target == owner, size, target) if size > 2 else 0

        def up(there, target):
            hop(there & (target > me), target, me + 1, from_low(target))

        def down(there, target):
            hop(there & (target < me), target, me - 1, from_high(target, me - 1))

        def arrive(there, target, slot):
            copy = pltpu.make_async_remote_copy(
                src_ref=acc.at[place(*block(target))], dst_ref=buf.at[slot], send_sem=send.at[target],
                recv_sem=recv.at[slot], device_id=device(me), device_id_type=MESH)

            @pl.when(there)
            def _():
                copy.wait_recv()
                add(*block(target), buf.at[slot])

        def begin(target):
            up(me == 0, target)
            down(me == size - 1, target)

        def go_on(target):
            arrive((me > 0) & (target >= me), target, from_low(target))
            arrive((me < size - 1) & (target <= me), target, from_high(target, me))
            up((me > 0) & (me < size - 1), target)
            down((me > 0) & (me < size - 1), target)

        return begin, go_on

    order = sorted(range(outer), key=lambda k: -abs(2 * k - outer + 1))
    lines = {}
    for r in order:
        loads = []
        for c in range(inner):
            load = pltpu.make_async_copy(src_ref.at[place(r, c)], acc.at[place(r, c)], load_sem.at[r * inner + c])
            load.start()
            loads.append(load)
        lines[r] = (loads, line(
            col, inner, lambda c: grid.device(row, c), lambda t, r=r: (r, t), inner_buf.at[r], inner_send.at[r],
            inner_recv.at[r]))
    for r in order:
        loads, (begin, _) = lines[r]
        for load in loads:
            load.wait()
        if inner > 1:
            for c in range(inner):
                begin(c)
    for _ in range(chunk + 1):
        yield
    begin_outer, go_on_outer = line(
        row, outer, lambda r: grid.device(r, col), lambda t: (t, col), outer_buf, outer_send, outer_recv)
    for r in order:
        if inner > 1:
            for c in range(inner):
                lines[r][1][1](c)
        if outer > 1:
            begin_outer(r)
        yield
    if outer > 1:
        for r in order:
            go_on_outer(r)
            yield
    last = pltpu.make_async_copy(acc.at[place(row, col)], out_ref.at[pl.ds(chunk * part, part)], out_sem)
    last.start()
    waits.append((None, last))


def link_reduce(arrays, sizes, collective_id):
    count = len(arrays)
    axes = sorted({entry[0] for entry in arrays})

    def kernel(*refs):
        sources, outs, scratch = refs[:count], refs[count : 2 * count], refs[2 * count :]
        grids = {axis: Grid(axis, *sizes[axis]) for axis in axes}
        greet([grids[axis] for axis in axes])
        waits = []
        runs = []
        for i, (axis, _, chunks) in enumerate(arrays):
            acc, scratch = scratch[0], scratch[1:]
            for chunk in range(chunks):
                inner_buf, outer_buf, sems, scratch = scratch[0], scratch[1], scratch[2:8], scratch[8:]
                runs.append(
                    reduce_steps(grids[axis], sources[i], outs[i], acc, inner_buf, outer_buf, sems, waits, chunk, chunks))
        in_turn(runs)
        finish(waits)

    scratch, shapes = [], []
    for axis, a, chunks in arrays:
        size, inner = sizes[axis]
        outer = size // inner
        part = a.shape[0] // size // chunks
        slots = [n + 1 if n > 2 else 1 for n in (inner, outer)]
        dma = pltpu.SemaphoreType.DMA
        shapes.append(jax.ShapeDtypeStruct((a.shape[0] // size, a.shape[1]), a.dtype))
        scratch.append(pltpu.VMEM(a.shape, a.dtype))
        for _ in range(chunks):
            scratch += [
                pltpu.VMEM((outer, slots[0], part, a.shape[1]), a.dtype),
                pltpu.VMEM((slots[1], part, a.shape[1]), a.dtype),
                dma((size,)), dma((outer, inner)), dma((outer, slots[0])), dma((outer,)), dma((slots[1],)), dma]
    return pl.pallas_call(
        kernel,
        in_specs=[pl.BlockSpec(memory_space=pl.ANY)] * count,
        out_specs=[pl.BlockSpec(memory_space=pl.ANY)] * count,
        out_shape=shapes,
        scratch_shapes=scratch,
        compiler_params=pltpu.CompilerParams(
            collective_id=collective_id, has_side_effects=True, vmem_limit_bytes=VMEM_LIMIT),
        name="link_reduce",
    )(*[a for _, a, _ in arrays])


def passed_along(block, axis, distance):
    devices = range(lax.axis_size(axis))
    route = [(i - distance, i) for i in devices if i - distance in devices]
    return lax.ppermute(block, axis, route)


def silu_slope(values_in):
    sigmoid_v = jax.nn.sigmoid(values_in)
    return sigmoid_v * (1.0 + values_in * (1.0 - sigmoid_v))


def token_layout(lengths, first_pos, n_tokens):
    doc_ends = jnp.cumsum(lengths)
    begins = doc_ends - lengths
    positions = first_pos + jnp.arange(n_tokens, dtype=jnp.int32)
    live_slot = (lengths > 0)[None, :]
    doc_ids = jnp.sum(((begins[None, :] <= positions[:, None]) & live_slot).astype(jnp.int32), axis=1)
    start_flags = jnp.sum(((begins[None, :] == positions[:, None]) & live_slot).astype(jnp.float32), axis=1)
    valid_mask = (positions < doc_ends[-1]).astype(jnp.float32)
    return (doc_ids, start_flags, valid_mask)


def contract_rows(left_mat, right_mat):
    return lax.dot_general(left_mat, right_mat, (((0,), (0,)), ((), ())), preferred_element_type=jnp.float32)


def contract_cols(left_mat, right_mat):
    return lax.dot_general(left_mat, right_mat, NT, preferred_element_type=jnp.float32)


def padded_rows(array, rows):
    return jnp.pad(array, ((0, -array.shape[0] % rows), (0, 0)))


def shared_sum(partial, sizes, collective_id):
    width = partial.shape[1]
    sent = jnp.pad(partial.astype(jnp.bfloat16), ((0, 0), (0, -width % 128)))
    (terms,) = link_gather([("stream", sent, 2)], sizes, collective_id)
    terms = terms.reshape(-1, *sent.shape)[:, :, :width].astype(jnp.float32)
    return jnp.sum(terms, axis=0)


def carried(ends, step_sum, rate, backward, sizes, collective_id):
    seqs, chans = step_sum.shape
    n = rate.shape[0]
    high = step_sum.astype(jnp.bfloat16)
    low = (step_sum - high.astype(jnp.float32)).astype(jnp.bfloat16)
    sent = padded_rows(jnp.concatenate([ends.astype(jnp.bfloat16), high, low], axis=0), 16)
    (gathered,) = link_gather([("seq", sent, 1)], sizes, collective_id)
    gathered = gathered.reshape(-1, *sent.shape)
    count = lax.axis_size("seq")
    place = lax.axis_index("seq")
    state = jnp.zeros((seqs, n, chans), jnp.float32)
    for step in range(count - 1):
        source = count - 1 - step if backward else step
        block = gathered[source].astype(jnp.float32)
        total = block[seqs * n : seqs * (n + 1)] + block[seqs * (n + 1) : seqs * (n + 2)]
        joined = jnp.exp2(total[:, None, :] * rate[None]) * state + block[: seqs * n].reshape(seqs, n, chans)
        state = jnp.where(source > place if backward else source < place, joined, state)
    return state.reshape(seqs * n, chans)


def local(sizes, resid_in, out_grad, row_lengths, norm_gain, in_weight, conv_weight, conv_bias, xproj_weight, dt_weight,
          dt_bias, a_log, skip_gain, out_weight):
    bf, f32 = jnp.bfloat16, jnp.float32
    seqs = lax.axis_size("stream")
    parts = lax.axis_size("seq")
    own = conv_bias.shape[0]
    own_feats = norm_gain.shape[0]
    chans = own * parts
    rank_dim = dt_weight.shape[0]
    state_dim = a_log.shape[1]
    proj_dim = xproj_weight.shape[1]
    length, feats = resid_in.shape[1:]
    tokens = seqs * length

    gain = norm_gain.astype(f32)
    scaled = (in_weight.astype(f32) * gain[:, None]).astype(bf).reshape(own_feats, 2, parts, seqs, own)
    scaled = scaled.transpose(3, 0, 1, 2, 4).reshape(seqs, own_feats, 2, chans)

    mine = lax.all_to_all(scaled.reshape(seqs * own_feats, 2 * chans), "stream", 0, 0, tiled=True)
    packed = jnp.concatenate(
        [xproj_weight, dt_weight.T, a_log, conv_weight.T, conv_bias[:, None], dt_bias[:, None], skip_gain[:, None]],
        axis=1)
    residual = resid_in[0].astype(f32)
    cotangent = out_grad[0]
    inv_rms = lax.rsqrt(jnp.mean(residual * residual, axis=-1, keepdims=True) + EPSILON)
    unit_own = residual * inv_rms
    slots = row_lengths.shape[1]
    in_conv, packed, unit, lengths = link_gather(
        [("seq", mine[:, :chans], 1), ("seq", jnp.pad(packed, ((0, 0), (0, -packed.shape[1] % 128))), 1),
         ("stream", unit_own.astype(bf), 4), ("stream", jnp.pad(row_lengths, ((0, 7), (0, -slots % 128))), 1)],
        sizes, 1)
    lengths = lengths[::8, :slots]
    in_gate = lax.all_gather(mine[:, chans:], "seq", axis=0, tiled=True)
    out_full = lax.all_gather(out_weight, "seq", axis=0, tiled=True)
    cot_all = lax.all_gather(cotangent, "stream", axis=0, tiled=True)
    xproj_full = packed[:, :proj_dim]
    dtw_cols = packed[:, proj_dim : proj_dim + rank_dim]
    at = proj_dim + rank_dim
    log_rates = packed[:, at : at + state_dim].astype(f32).T
    at += state_dim
    conv_taps = packed[:, at : at + CONV].astype(f32).T
    at += CONV
    conv_shift, dt_shift, skip_vec = (packed[:, at + i].astype(f32) for i in range(3))
    rate = -jnp.exp(log_rates) / LN2

    rim = CONV - 1
    first_pos = lax.axis_index("seq") * length
    doc_ids, start_flags, valid_mask = jax.vmap(
        lambda row: token_layout(row, first_pos - rim, length + 2 * rim))(lengths)
    own_ids = doc_ids[:, rim : rim + length]
    starts = start_flags[:, rim : rim + length].reshape(tokens, 1)
    valid = valid_mask[:, rim : rim + length].reshape(tokens, 1)
    matches = [(doc_ids[:, tap : tap + length] == own_ids).astype(f32)[:, :, None] for tap in range(CONV)]

    conv_in = jnp.dot(unit, in_conv, preferred_element_type=f32).reshape(seqs, length, chans)
    gate_in = jnp.dot(unit, in_gate, preferred_element_type=f32)
    earlier = passed_along(conv_in[:, length - rim :].astype(bf), "seq", 1).astype(f32)
    padded = jnp.concatenate([earlier, conv_in], axis=1)
    conv_out = conv_shift
    for tap in range(CONV):
        conv_out = conv_out + conv_taps[tap] * padded[:, tap : tap + length] * matches[tap]
    activated = jax.nn.silu(conv_out).astype(bf).reshape(tokens, chans)
    act_float = activated.astype(f32)
    projected = shared_sum(jnp.dot(activated, xproj_full, preferred_element_type=f32), sizes, 2)
    low_rank = projected[:, :rank_dim].astype(bf)
    write_in = projected[:, rank_dim : rank_dim + state_dim]
    readout = projected[:, rank_dim + state_dim :]
    dt_pre = contract_cols(low_rank, dtw_cols) + dt_shift
    dt_step = jax.nn.softplus(dt_pre)
    dt_reset = jnp.where(starts > 0, RESET, dt_step)
    dt_act = dt_step * act_float
    write_wide, read_wide = widen(write_in), widen(readout)
    write_diag, read_diag = spread(write_in), spread(readout)

    step_sum = jnp.sum(dt_reset.reshape(seqs, length, chans), axis=1)
    ends = scan_end(fwd_end_body, dt_reset, dt_act, write_wide, rate, seqs)
    start_state = carried(ends, step_sum, rate, False, sizes, 3)
    scanned, history = fwd_full(dt_reset, dt_act, write_wide, read_diag, rate, start_state, seqs)
    ssm_out = scanned + skip_vec * act_float
    gate_act = jax.nn.silu(gate_in)
    gated = (ssm_out * gate_act * valid).astype(bf)
    product = jnp.dot(gated, out_full, preferred_element_type=f32).astype(bf)
    output = (residual + lax.psum_scatter(product, "stream", scatter_dimension=0, tiled=True).astype(f32)).astype(bf)

    d_gated = contract_cols(cot_all, out_full)
    g_out = lax.psum_scatter(contract_rows(gated, cot_all).astype(bf), "seq", scatter_dimension=0, tiled=True)
    d_masked = d_gated * valid
    d_ssm = d_masked * gate_act
    d_gate = (d_masked * ssm_out * silu_slope(gate_in)).astype(bf)
    g_in_gate = lax.psum_scatter(contract_rows(unit, d_gate).astype(bf), "seq", scatter_dimension=0, tiled=True)
    g_skip = jnp.sum(d_ssm * act_float, axis=0)
    back_ends = scan_end(bwd_end_body, dt_reset, d_ssm, read_wide, rate, seqs)
    later_sum = carried(back_ends, step_sum, rate, True, sizes, 4)
    sum_write, sum_rate, g_log, d_write, d_read = bwd_full(
        dt_reset, dt_act, d_ssm, history, read_wide, write_diag, rate, later_sum, seqs)
    per_step = jnp.where(dt_step > 1e-30, sum_rate * LN2 / jnp.maximum(dt_step, 1e-30), 0.0)
    d_step = per_step + act_float * sum_write
    d_pre = d_step * jax.nn.sigmoid(dt_pre)
    g_dt_bias = jnp.sum(d_pre, axis=0)
    d_pre_low = d_pre.astype(bf)
    g_dt = contract_rows(d_pre_low, low_rank)
    d_low = jnp.dot(d_pre_low, dtw_cols, preferred_element_type=f32)
    d_proj = shared_sum(jnp.concatenate([d_low, d_write, d_read], axis=1), sizes, 5).astype(bf)
    g_xproj = contract_rows(activated, d_proj)
    d_act = dt_step * sum_write + skip_vec * d_ssm + contract_cols(d_proj, xproj_full)
    d_conv = d_act.reshape(seqs, length, chans) * silu_slope(conv_out)
    g_conv_bias = jnp.sum(d_conv, axis=(0, 1))
    g_conv = jnp.stack(
        [jnp.sum(d_conv * padded[:, tap : tap + length] * matches[tap], axis=(0, 1)) for tap in range(CONV)], axis=1)
    later = passed_along(d_conv[:, :rim].astype(bf), "seq", -1).astype(f32)
    d_ext = jnp.concatenate([d_conv, later], axis=1)
    d_conv_in = jnp.zeros_like(d_conv)
    for tap in range(CONV):
        offset = rim - tap
        match_back = (doc_ids[:, rim + offset : rim + offset + length] == own_ids).astype(f32)[:, :, None]
        d_conv_in = d_conv_in + conv_taps[tap] * d_ext[:, offset : offset + length] * match_back
    d_conv_in = d_conv_in.astype(bf).reshape(tokens, chans)
    g_in_conv = contract_rows(unit, d_conv_in).astype(bf)
    d_unit = (contract_cols(d_conv_in, in_conv) + contract_cols(d_gate, in_gate)).astype(bf)
    small = jnp.concatenate(
        [g_xproj, g_dt, g_log.T * LN2, g_conv, g_conv_bias[:, None], g_dt_bias[:, None], g_skip[:, None]], axis=1)
    small = jnp.pad(small, ((0, 0), (0, -small.shape[1] % 128))).astype(bf)
    g_in_conv, small, d_unit = link_reduce(
        [("seq", g_in_conv, 1), ("seq", small, 1), ("stream", d_unit, 4)], sizes, 6)
    small = small.astype(f32)
    d_unit = d_unit.astype(f32)
    in_grad = cotangent.astype(f32) + inv_rms * (d_unit - unit_own * jnp.mean(d_unit * unit_own, axis=-1, keepdims=True))

    def in_rows(block):
        shared = lax.all_to_all(block, "stream", 0, 0, tiled=True).reshape(seqs, own_feats, 2 * parts, own)
        return shared.transpose(1, 2, 0, 3).reshape(own_feats, 2 * parts * seqs * own).astype(f32)

    g_unit = in_rows(jnp.stack([g_in_conv, g_in_gate], axis=1).reshape(g_in_conv.shape[0], 2 * chans))
    at = proj_dim + rank_dim
    return (
        output[None],
        in_grad.astype(bf)[None],
        jnp.sum(g_unit * in_weight.astype(f32), axis=1),
        g_unit * gain[:, None],
        small[:, at + state_dim : at + state_dim + CONV].T,
        small[:, at + state_dim + CONV],
        small[:, :proj_dim],
        small[:, proj_dim:at].T,
        small[:, at + state_dim + CONV + 1],
        small[:, at : at + state_dim],
        small[:, at + state_dim + CONV + 2],
        g_out.astype(f32),
    )


def lines_of(mesh):
    devices = mesh.devices
    places = [getattr(device, "coords", None) for device in devices[:, 0]]
    seq = len(places)
    plane = 1
    if all(place is not None for place in places):
        plane = len({tuple(place)[1] for place in places})
    if seq % plane:
        plane = 1
    return {"seq": (seq, plane), "stream": (devices.shape[1], 1 if devices.shape[1] % 2 else 2)}


def solution(mesh):
    in_specs = (
        P("stream", "seq", None),
        P("stream", "seq", None),
        P("stream", None),
        P(("seq", "stream")),
        P(("seq", "stream"), None),
        P(None, ("seq", "stream")),
        P(("seq", "stream")),
        P(("seq", "stream"), None),
        P(None, ("seq", "stream")),
        P(("seq", "stream")),
        P(("seq", "stream"), None),
        P(("seq", "stream")),
        P(("seq", "stream"), None),
    )
    out_specs = (
        P("stream", "seq", None),
        P("stream", "seq", None),
        P(("seq", "stream")),
        P(("seq", "stream"), None),
        P(None, ("seq", "stream")),
        P(("seq", "stream")),
        P(("seq", "stream"), None),
        P(None, ("seq", "stream")),
        P(("seq", "stream")),
        P(("seq", "stream"), None),
        P(("seq", "stream")),
        P(("seq", "stream"), None),
    )
    return jax.shard_map(functools.partial(local, lines_of(mesh)), mesh=mesh, in_specs=in_specs, out_specs=out_specs, check_vma=False)
```

```python
import functools

import jax
import jax.numpy as jnp
from jax import lax
from jax.experimental import pallas as pl
from jax.experimental.pallas import tpu as pltpu
from jax.sharding import PartitionSpec as P

CONV = 4
EPSILON = 1e-05
RESET = 1e30
GROUP = 16
LN2 = 0.6931471805599453
NT = (((1,), (1,)), ((), ()))
VMEM_LIMIT = 56 << 20


def across(slab, place, width):
    return jnp.concatenate([jnp.broadcast_to(slab[:, place : place + 1], (slab.shape[0], 128))] * (width // 128), axis=1)


def decays(dte_ref, rate_ref, at, buf, power_buf=None):
    n = rate_ref.shape[0]
    for place in range(GROUP):
        power = dte_ref[pl.ds(at * GROUP + place, 1), :] * rate_ref[...]
        buf[pl.ds(place * n, n), :] = jnp.exp2(power)
        if power_buf is not None:
            power_buf[pl.ds(place * n, n), :] = power.astype(jnp.bfloat16)


def fwd_end_body(dte_ref, dtx_ref, slab_ref, rate_ref, end_ref, even_ref, odd_ref):
    n, width = rate_ref.shape
    groups = dte_ref.shape[0] // GROUP

    def walk(at, state, decay_ref):
        slab = slab_ref[pl.ds(at * n, n), :]
        for place in range(GROUP):
            write = across(slab, place, width)
            state = decay_ref[pl.ds(place * n, n), :] * state + dtx_ref[pl.ds(at * GROUP + place, 1), :] * write
        return state

    def pair(step, state):
        decays(dte_ref, rate_ref, 2 * step + 1, odd_ref)
        state = walk(2 * step, state, even_ref)
        decays(dte_ref, rate_ref, jnp.minimum(2 * step + 2, groups - 1), even_ref)
        return walk(2 * step + 1, state, odd_ref)

    decays(dte_ref, rate_ref, 0, even_ref)
    end_ref[...] = lax.fori_loop(0, groups // 2, pair, jnp.zeros_like(end_ref))


def bwd_end_body(dte_ref, grad_ref, slab_ref, rate_ref, end_ref, even_ref, odd_ref):
    n, width = rate_ref.shape
    groups = dte_ref.shape[0] // GROUP

    def walk(at, state, decay_ref):
        slab = slab_ref[pl.ds(at * n, n), :]
        for place in reversed(range(GROUP)):
            read = across(slab, place, width)
            state = decay_ref[pl.ds(place * n, n), :] * (state + grad_ref[pl.ds(at * GROUP + place, 1), :] * read)
        return state

    def pair(step, state):
        at = groups - 1 - 2 * step
        decays(dte_ref, rate_ref, at - 1, odd_ref)
        state = walk(at, state, even_ref)
        decays(dte_ref, rate_ref, jnp.maximum(at - 2, 0), even_ref)
        return walk(at - 1, state, odd_ref)

    decays(dte_ref, rate_ref, groups - 1, even_ref)
    end_ref[...] = lax.fori_loop(0, groups // 2, pair, jnp.zeros_like(end_ref))


def scan_end(body, dte, other, slabs, rate, seqs, width=512):
    tokens, chans = dte.shape
    length = tokens // seqs
    n = rate.shape[0]
    width = min(width, chans)
    work = tokens * chans * n
    return pl.pallas_call(
        body,
        grid=(seqs, chans // width),
        in_specs=[
            pl.BlockSpec((length, width), lambda s, c: (s, c)),
            pl.BlockSpec((length, width), lambda s, c: (s, c)),
            pl.BlockSpec((length // GROUP * n, GROUP), lambda s, c: (s, 0)),
            pl.BlockSpec((n, width), lambda s, c: (0, c)),
        ],
        out_specs=pl.BlockSpec((n, width), lambda s, c: (s, c)),
        out_shape=jax.ShapeDtypeStruct((seqs * n, chans), jnp.float32),
        scratch_shapes=[pltpu.VMEM((GROUP * n, width), jnp.float32)] * 2,
        compiler_params=pltpu.CompilerParams(vmem_limit_bytes=VMEM_LIMIT),
        cost_estimate=pl.CostEstimate(flops=4 * work, transcendentals=work, bytes_accessed=8 * tokens * chans),
        name=body.__name__[:7],
    )(dte, other, slabs, rate)


def fwd_full_body(dte_ref, dtx_ref, slab_ref, read_ref, rate_ref, start_ref, y_ref, hist_ref, h_ref, even_ref, odd_ref):
    block = dte_ref.shape[0]
    n, width = rate_ref.shape
    span = GROUP * n
    rate = rate_ref[...]

    @pl.when(pl.program_id(2) == 0)
    def _():
        h_ref[...] = start_ref[...]

    first = h_ref[...]
    hist_ref[pl.ds(0, n), :] = first.astype(jnp.bfloat16)

    def rows_out(at, buf):
        y_ref[pl.ds(at * GROUP, GROUP), :] = jnp.dot(
            read_ref[pl.ds(at * GROUP, GROUP), :], buf[...], preferred_element_type=jnp.float32)

    def group(at, state, buf):
        slab = slab_ref[pl.ds(at * n, n), :]
        for place in range(GROUP):
            t = at * GROUP + place
            write = across(slab, place, width)
            state = jnp.exp2(dte_ref[pl.ds(t, 1), :] * rate) * state + dtx_ref[pl.ds(t, 1), :] * write
            kept = state.astype(jnp.bfloat16)
            hist_ref[pl.ds((t + 1) * n, n), :] = kept
            buf[pl.ds(place * n, n), :] = kept
        return state

    def pair(step, state):
        at = 2 * step
        rows_out(jnp.maximum(at - 1, 0), odd_ref)
        state = group(at, state, even_ref)
        rows_out(at, even_ref)
        return group(at + 1, state, odd_ref)

    h_ref[...] = lax.fori_loop(0, block // GROUP // 2, pair, first)
    rows_out(block // GROUP - 1, odd_ref)


def fwd_full(dte, dtx, slabs, read, rate, start, seqs, width=512, block=256):
    tokens, chans = dte.shape
    n = rate.shape[0]
    width = min(width, chans)
    blocks = tokens // seqs // block
    work = tokens * chans * n
    here = lambda c, s, t: (s * blocks + t, c)
    rows = lambda c, s, t: (s * blocks + t, 0)
    return pl.pallas_call(
        fwd_full_body,
        grid=(chans // width, seqs, blocks),
        in_specs=[
            pl.BlockSpec((block, width), here),
            pl.BlockSpec((block, width), here),
            pl.BlockSpec((block // GROUP * n, GROUP), rows),
            pl.BlockSpec((block, read.shape[1]), rows),
            pl.BlockSpec((n, width), lambda c, s, t: (0, c)),
            pl.BlockSpec((n, width), lambda c, s, t: (s, c)),
        ],
        out_specs=[pl.BlockSpec((block, width), here), pl.BlockSpec(((block + 1) * n, width), here)],
        out_shape=[
            jax.ShapeDtypeStruct((tokens, chans), jnp.float32),
            jax.ShapeDtypeStruct((seqs * blocks * (block + 1) * n, chans), jnp.bfloat16),
        ],
        scratch_shapes=[pltpu.VMEM((n, width), jnp.float32)] + [pltpu.VMEM((GROUP * n, width), jnp.bfloat16)] * 2,
        compiler_params=pltpu.CompilerParams(vmem_limit_bytes=VMEM_LIMIT),
        cost_estimate=pl.CostEstimate(flops=8 * work, transcendentals=work, bytes_accessed=2 * work),
        name="fwd_full",
    )(dte, dtx, slabs, read, rate, start)


def bwd_full_body(dte_ref, dtx_ref, grad_ref, hist_ref, slab_ref, write_ref, ones_ref, rate_ref, start_ref,
                  s1_ref, s2_ref, grate_ref, dw_ref, dr_ref, g_ref, *scratch):
    block = dte_ref.shape[0]
    n, width = rate_ref.shape
    groups = block // GROUP
    bf, f32 = jnp.bfloat16, jnp.float32
    even, odd = scratch[:5], scratch[5:]
    unit = jnp.ones((GROUP, 128), bf)

    @pl.when(pl.program_id(2) == 0)
    def _():
        g_ref[...] = start_ref[...]

    @pl.when((pl.program_id(2) == 0) & (pl.program_id(1) == 0))
    def _():
        grate_ref[...] = jnp.zeros_like(grate_ref)

    def sums_out(at, bufs):
        _, _, adj_ref, rated_ref, dw_part = bufs
        rows = pl.ds(at * GROUP, GROUP)
        s1_ref[rows, :] = jnp.dot(write_ref[rows, :], adj_ref[...], preferred_element_type=f32)
        sums = jnp.dot(ones_ref[...], rated_ref[...], preferred_element_type=f32)
        s2_ref[rows, :] = sums[:GROUP]
        dw_ref[pl.ds(at, 1), :] = lax.dot_general(unit, dw_part[...], NT, preferred_element_type=f32)[:1]
        dr_ref[rows, :] = lax.dot_general(
            grad_ref[rows, :].astype(bf), hist_ref[pl.ds(n + at * GROUP * n, GROUP * n), :], NT,
            preferred_element_type=f32)
        return sums[GROUP:]

    def strips(values):
        parts = [values[:, k * 128 : (k + 1) * 128] for k in range(width // 128)]
        while len(parts) > 1:
            parts = [a + b for a, b in zip(parts[::2], parts[1::2])] + parts[len(parts) // 2 * 2 :]
        return parts[0]

    def walk(at, state, bufs):
        decay_ref, power_ref, adj_ref, rated_ref, dw_part = bufs
        slab = slab_ref[pl.ds(at * n, n), :]
        for place in reversed(range(GROUP)):
            t = at * GROUP + place
            here = pl.ds(place * n, n)
            read = across(slab, place, width)
            adjoint = state + grad_ref[pl.ds(t, 1), :] * read
            power = dte_ref[pl.ds(t, 1), :] * rate_ref[...]
            state = jnp.exp2(power) * adjoint
            low = adjoint.astype(bf)
            adj_ref[here, :] = low
            rated_ref[here, :] = state.astype(bf) * hist_ref[pl.ds(t * n, n), :] * power.astype(bf)
            dw_part[here, :] = strips(adjoint * dtx_ref[pl.ds(t, 1), :]).astype(bf)
        return state

    def pair(step, state):
        at = groups - 1 - 2 * step
        old = sums_out(jnp.minimum(at + 1, groups - 1), odd)
        state = walk(at, state, even)
        grate_ref[...] += jnp.where(step > 0, old, 0.0) + sums_out(at, even)
        return walk(at - 1, state, odd)
    g_ref[...] = lax.fori_loop(0, groups // 2, pair, g_ref[...])
    grate_ref[...] += sums_out(0, odd)


def bwd_full(dte, dtx, grad, hist, slabs, write, rate, start, seqs, width=512, block=256):
    tokens, chans = dte.shape
    n = rate.shape[0]
    width = min(width, chans)
    strips = chans // width
    blocks = tokens // seqs // block
    span = GROUP * n
    work = tokens * chans * n
    column = jnp.arange(span)
    ones = jnp.concatenate(
        [(column // n)[None, :] == jnp.arange(GROUP)[:, None], (column % n)[None, :] == jnp.arange(n)[:, None]]
    ).astype(jnp.bfloat16)
    here = lambda c, s, t: (s * blocks + blocks - 1 - t, c)
    rows = lambda c, s, t: (s * blocks + blocks - 1 - t, 0)
    strip = lambda c, s, t: (c * seqs * blocks + s * blocks + blocks - 1 - t, 0)
    f32 = jnp.float32
    s1, s2, grate, dw, dr = pl.pallas_call(
        bwd_full_body,
        grid=(strips, seqs, blocks),
        in_specs=[
            pl.BlockSpec((block, width), here),
            pl.BlockSpec((block, width), here),
            pl.BlockSpec((block, width), here),
            pl.BlockSpec(((block + 1) * n, width), here),
            pl.BlockSpec((block // GROUP * n, GROUP), rows),
            pl.BlockSpec((block, span), rows),
            pl.BlockSpec(ones.shape, lambda c, s, t: (0, 0)),
            pl.BlockSpec((n, width), lambda c, s, t: (0, c)),
            pl.BlockSpec((n, width), lambda c, s, t: (s, c)),
        ],
        out_specs=[
            pl.BlockSpec((block, width), here),
            pl.BlockSpec((block, width), here),
            pl.BlockSpec((n, width), lambda c, s, t: (0, c)),
            pl.BlockSpec((block // GROUP, span), strip),
            pl.BlockSpec((block, span), strip),
        ],
        out_shape=[
            jax.ShapeDtypeStruct((tokens, chans), f32),
            jax.ShapeDtypeStruct((tokens, chans), f32),
            jax.ShapeDtypeStruct((n, chans), f32),
            jax.ShapeDtypeStruct((strips * tokens // GROUP, span), f32),
            jax.ShapeDtypeStruct((strips * tokens, span), f32),
        ],
        scratch_shapes=[
            pltpu.VMEM((n, width), f32),
            *[
                pltpu.VMEM((span, width), f32),
                *[pltpu.VMEM((span, width), jnp.bfloat16)] * 3,
                pltpu.VMEM((span, 128), jnp.bfloat16),
            ] * 2,
        ],
        compiler_params=pltpu.CompilerParams(vmem_limit_bytes=VMEM_LIMIT),
        cost_estimate=pl.CostEstimate(flops=14 * work, transcendentals=work, bytes_accessed=2 * work),
        name="bwd_full",
    )(dte, dtx, grad, hist, slabs, write, ones, rate, start)
    dw = dw.reshape(strips, tokens, n).sum(0).T
    own = jnp.arange(tokens)[:, None] % GROUP == jnp.arange(GROUP)[None, :]
    dr = jnp.where(own[None, :, :, None], dr.reshape(strips, tokens, GROUP, n), 0).sum((0, 2)).T
    return s1, s2, grate, dw, dr


def slabs_of(values):
    n, tokens = values.shape
    return values.reshape(n, tokens // GROUP, GROUP).transpose(1, 0, 2).reshape(tokens // GROUP * n, GROUP)


def spread(values):
    n, tokens = values.shape
    own = jnp.arange(tokens)[:, None] % GROUP == jnp.arange(GROUP)[None, :]
    return jnp.where(own[:, :, None], values.T[:, None, :], 0).reshape(tokens, GROUP * n).astype(jnp.bfloat16)


MESH = pl.DeviceIdType.MESH


class Grid:
    def __init__(self, axis, size, inner):
        self.axis, self.inner, self.outer = axis, inner, size // inner
        me = lax.axis_index(axis)
        self.row, self.col = me // inner, me % inner

    def device(self, row, col):
        return {self.axis: row * self.inner + col}

    def neighbours(self):
        row, col = self.row, self.col
        found = []
        if self.outer > 1:
            found += [(row > 0, self.device(row - 1, col)), (row < self.outer - 1, self.device(row + 1, col))]
        if self.inner > 1:
            found += [(col > 0, self.device(row, col - 1)), (col < self.inner - 1, self.device(row, col + 1))]
        return found

    def everyone(self):
        size = self.inner * self.outer
        me = self.row * self.inner + self.col
        return [(me >= 0, {self.axis: (me + step) % size}) for step in range(1, size)]


def greet(grids, all_of=()):
    barrier = pltpu.get_barrier_semaphore()
    count = 0
    for grid in grids:
        for there, device in grid.everyone() if grid.axis in all_of else grid.neighbours():

            @pl.when(there)
            def _(device=device):
                pl.semaphore_signal(barrier, inc=1, device_id=device, device_id_type=MESH)

            count = count + there.astype(jnp.int32)
    pl.semaphore_wait(barrier, count)


def gather_steps(grid, whole_ref, out_ref, send_sem, recv_sem, own_sem, waits, chunk, chunks, across_too=True, ways=(True, True)):
    rows = whole_ref.shape[0]
    part = rows // chunks
    src_ref = whole_ref.at[pl.ds(chunk * part, part)]
    outer, inner = grid.outer, grid.inner if across_too else 1
    row, col = grid.row, grid.col

    def number(r, c):
        return r * inner + c if across_too else r

    def place(r, c):
        return pl.ds(pl.multiple_of(number(r, c) * rows + chunk * part, part), part)

    def send(there, way, r, c, device, source):
        copy = pltpu.make_async_remote_copy(
            src_ref=source, dst_ref=out_ref.at[place(r, c)], send_sem=send_sem.at[way, number(r, c)],
            recv_sem=recv_sem.at[number(r, c)], device_id=device, device_id_type=MESH)

        @pl.when(there)
        def _():
            copy.start()

        waits.append((there, copy))

    def across(there, r, c, source):
        if inner > 1:
            send(there & (c >= col) & (col > 0), 2, r, c, grid.device(row, col - 1), source)
            send(there & (c <= col) & (col < inner - 1), 3, r, c, grid.device(row, col + 1), source)

    def along(there, r, source):
        if outer > 1:
            if ways[0]:
                send(there & (r >= row) & (row > 0), 0, r, col, grid.device(row - 1, col), source)
            if ways[1]:
                send(there & (r <= row) & (row < outer - 1), 1, r, col, grid.device(row + 1, col), source)

    def arrive(there, r, c):
        copy = pltpu.make_async_remote_copy(
            src_ref=src_ref, dst_ref=out_ref.at[place(r, c)], send_sem=send_sem.at[0, 0],
            recv_sem=recv_sem.at[number(r, c)], device_id=grid.device(row, col), device_id_type=MESH)

        @pl.when(there)
        def _():
            copy.wait_recv()

    always = row >= 0
    along(always, row, src_ref)
    across(always, row, col, src_ref)
    own = pltpu.make_async_copy(src_ref, out_ref.at[place(row, col)], own_sem)
    own.start()
    waits.append((None, own))
    for _ in range(chunk + 1):
        yield

    def rows_at(distance):
        return [row - distance] * ways[1] + [row + distance] * ways[0]

    for distance in range(1, outer):
        for r in rows_at(distance):
            there = (r >= 0) & (r < outer)
            arrive(there, r, col)
            along(there, r, out_ref.at[place(r, col)])
            across(there, r, col, out_ref.at[place(r, col)])
        yield
    for step in range(1, inner):
        for distance in range(outer):
            for r in rows_at(distance) if distance else (row,):
                for c in (col - step, col + step):
                    there = (r >= 0) & (r < outer) & (c >= 0) & (c < inner)
                    arrive(there, r, c)
                    if step < inner - 1:
                        across(there, r, c, out_ref.at[place(r, c)])
            yield


def finish(waits):
    for there, copy in waits:
        if there is None:
            copy.wait()
        else:

            @pl.when(there)
            def _(copy=copy):
                copy.wait_send()


def in_turn(runs):
    runs = list(runs)
    while runs:
        left = []
        for run in runs:
            if next(run, run) is not run:
                left.append(run)
        runs = left


def link_gather(arrays, sizes, collective_id, ways=(True, True)):
    count = len(arrays)
    axes = sorted({entry[0] for entry in arrays})

    def kernel(*refs):
        sources, outs, sems = refs[:count], refs[count : 2 * count], refs[2 * count :]
        grids = {axis: Grid(axis, *sizes[axis]) for axis in axes}
        greet([grids[axis] for axis in axes])
        waits = []
        runs = []
        for i, (axis, _, chunks) in enumerate(arrays):
            for chunk in range(chunks):
                runs.append(gather_steps(grids[axis], sources[i], outs[i], *sems[:3], waits, chunk, chunks, ways=ways))
                sems = sems[3:]
        in_turn(runs)
        finish(waits)

    sems = []
    for axis, _, chunks in arrays:
        size = sizes[axis][0]
        sems += [pltpu.SemaphoreType.DMA((4, size)), pltpu.SemaphoreType.DMA((size,)), pltpu.SemaphoreType.DMA] * chunks
    return pl.pallas_call(
        kernel,
        in_specs=[pl.BlockSpec(memory_space=pl.ANY)] * count,
        out_specs=[pl.BlockSpec(memory_space=pl.ANY)] * count,
        out_shape=[
            jax.ShapeDtypeStruct((sizes[axis][0] * a.shape[0], *a.shape[1:]), a.dtype) for axis, a, _ in arrays],
        scratch_shapes=sems,
        compiler_params=pltpu.CompilerParams(collective_id=collective_id, has_side_effects=True),
        name="link_gather",
    )(*[a for _, a, _ in arrays])


def reduce_steps(grid, src_ref, out_ref, acc, inner_buf, outer_buf, sems, waits, chunk, chunks, share=None):
    outer, inner = grid.outer, grid.inner
    row, col = grid.row, grid.col
    rows, part = acc.shape[0] // (outer * inner), acc.shape[0] // (outer * inner * chunks)
    piece = min(part, 64)
    load_sem, inner_send, inner_recv, outer_send, outer_recv, out_sem = sems

    def place(r, c):
        return pl.ds(pl.multiple_of((r * inner + c) * rows + chunk * part, part), part)

    def add(r, c, buf):
        start = (r * inner + c) * rows + chunk * part

        @pl.loop(0, part // piece)
        def _(k):
            here = pl.ds(pl.multiple_of(start + k * piece, piece), piece)
            there = pl.ds(pl.multiple_of(k * piece, piece), piece)
            acc[here, :] = (acc[here, :].astype(jnp.float32) + buf[there, :].astype(jnp.float32)).astype(acc.dtype)

    def line(me, size, device, block, buf, send, recv):
        def hop(there, target, onward, slot):
            copy = pltpu.make_async_remote_copy(
                src_ref=acc.at[place(*block(target))], dst_ref=buf.at[slot], send_sem=send.at[target],
                recv_sem=recv.at[slot], device_id=device(onward), device_id_type=MESH)

            @pl.when(there)
            def _():
                copy.start()

            waits.append((there, copy))

        def from_low(target):
            return target if size > 2 else 0

        def from_high(target, owner):
            return jnp.where(target == owner, size, target) if size > 2 else 0

        def up(there, target):
            hop(there & (target > me), target, me + 1, from_low(target))

        def down(there, target):
            hop(there & (target < me), target, me - 1, from_high(target, me - 1))

        def arrive(there, target, slot):
            copy = pltpu.make_async_remote_copy(
                src_ref=acc.at[place(*block(target))], dst_ref=buf.at[slot], send_sem=send.at[target],
                recv_sem=recv.at[slot], device_id=device(me), device_id_type=MESH)

            @pl.when(there)
            def _():
                copy.wait_recv()
                add(*block(target), buf.at[slot])

        def begin(target):
            up(me == 0, target)
            down(me == size - 1, target)

        def go_on(target):
            arrive((me > 0) & (target >= me), target, from_low(target))
            arrive((me < size - 1) & (target <= me), target, from_high(target, me))
            up((me > 0) & (me < size - 1), target)
            down((me > 0) & (me < size - 1), target)

        return begin, go_on

    order = sorted(range(outer), key=lambda k: -abs(2 * k - outer + 1))
    lines = {}
    for r in order:
        loads = []
        for c in range(inner):
            load = pltpu.make_async_copy(src_ref.at[place(r, c)], acc.at[place(r, c)], load_sem.at[r * inner + c])
            load.start()
            loads.append(load)
        lines[r] = (loads, line(
            col, inner, lambda c: grid.device(row, c), lambda t, r=r: (r, t), inner_buf.at[r], inner_send.at[r],
            inner_recv.at[r]))
    for r in order:
        loads, (begin, _) = lines[r]
        for load in loads:
            load.wait()
        if inner > 1:
            for c in range(inner):
                begin(c)
    for _ in range(chunk + 1):
        yield
    begin_outer, go_on_outer = line(
        row, outer, lambda r: grid.device(r, col), lambda t: (t, col), outer_buf, outer_send, outer_recv)
    late = []
    for r in order:
        if inner > 1:
            for c in range(inner):
                lines[r][1][1](c)
        if outer > 1:
            begin_outer(r)
            yield
            for earlier in late:
                go_on_outer(earlier)
            late = [r]
        yield
    for earlier in late:
        go_on_outer(earlier)
    if share is None:
        last = pltpu.make_async_copy(acc.at[place(row, col)], out_ref.at[pl.ds(chunk * part, part)], out_sem)
        last.start()
        waits.append((None, last))
        return
    other, strip, send_sem, recv_sem = share
    count, me = other.outer * other.inner, other.row * other.inner + other.col
    take = rows // count
    strips = acc.shape[1] // strip
    first = (row * inner + col) * rows
    for step in range(count):
        mate = (me + step) % count
        source_rows = pl.ds(pl.multiple_of(first + mate * take, take), take)
        for k in range(strips):
            piece_ref = acc.at[source_rows, pl.ds(k * strip, strip)]
            target = out_ref.at[:, pl.ds(pl.multiple_of((k * count + me) * strip, strip), strip)]
            if step == 0:
                copy = pltpu.make_async_copy(piece_ref, target, send_sem.at[step, k])
                copy.start()
                waits.append((None, copy))
            else:
                copy = pltpu.make_async_remote_copy(
                    src_ref=piece_ref, dst_ref=target, send_sem=send_sem.at[step, k], recv_sem=recv_sem.at[step, k],
                    device_id={other.axis: mate}, device_id_type=MESH)
                copy.start()
                waits.append((me >= 0, copy))
    for step in range(1, count):
        mate = (me + count - step) % count
        for k in range(strips):
            copy = pltpu.make_async_remote_copy(
                src_ref=acc.at[pl.ds(0, take), pl.ds(k * strip, strip)],
                dst_ref=out_ref.at[:, pl.ds(pl.multiple_of((k * count + mate) * strip, strip), strip)],
                send_sem=send_sem.at[step, k], recv_sem=recv_sem.at[step, k], device_id={other.axis: me},
                device_id_type=MESH)
            copy.wait_recv()


def link_reduce(arrays, sizes, collective_id):
    count = len(arrays)

    def kernel(*refs):
        sources, outs, scratch = refs[:count], refs[count : 2 * count], refs[2 * count :]
        grids = {axis: Grid(axis, *sizes[axis]) for axis in ("seq", "stream")}
        greet(list(grids.values()), ("stream",))
        waits = []
        runs = []
        for i, (axis, _, chunks, strip) in enumerate(arrays):
            acc, scratch = scratch[0], scratch[1:]
            share = None
            if strip:
                share, scratch = (grids["stream"], strip, *scratch[:2]), scratch[2:]
            for chunk in range(chunks):
                inner_buf, outer_buf, sems, scratch = scratch[0], scratch[1], scratch[2:8], scratch[8:]
                runs.append(reduce_steps(
                    grids[axis], sources[i], outs[i], acc, inner_buf, outer_buf, sems, waits, chunk, chunks, share))
        in_turn(runs)
        finish(waits)

    scratch, shapes = [], []
    for axis, a, chunks, strip in arrays:
        size, inner = sizes[axis]
        outer = size // inner
        part = a.shape[0] // size // chunks
        slots = [n + 1 if n > 2 else 1 for n in (inner, outer)]
        dma = pltpu.SemaphoreType.DMA
        scratch.append(pltpu.VMEM(a.shape, a.dtype))
        if strip:
            mates = sizes["stream"][0]
            shapes.append(jax.ShapeDtypeStruct((a.shape[0] // size // mates, a.shape[1] * mates), a.dtype))
            scratch += [dma((mates, a.shape[1] // strip))] * 2
        else:
            shapes.append(jax.ShapeDtypeStruct((a.shape[0] // size, a.shape[1]), a.dtype))
        for _ in range(chunks):
            scratch += [
                pltpu.VMEM((outer, slots[0], part, a.shape[1]), a.dtype),
                pltpu.VMEM((slots[1], part, a.shape[1]), a.dtype),
                dma((size,)), dma((outer, inner)), dma((outer, slots[0])), dma((outer,)), dma((slots[1],)), dma]
    return pl.pallas_call(
        kernel,
        in_specs=[pl.BlockSpec(memory_space=pl.ANY)] * count,
        out_specs=[pl.BlockSpec(memory_space=pl.ANY)] * count,
        out_shape=shapes,
        scratch_shapes=scratch,
        compiler_params=pltpu.CompilerParams(
            collective_id=collective_id, has_side_effects=True, vmem_limit_bytes=VMEM_LIMIT),
        name="link_reduce",
    )(*[entry[1] for entry in arrays])


def link_sum(partial, sizes, collective_id):
    rows, width = partial.shape
    size, inner = sizes["stream"]
    outer = size // inner
    assert inner == 2
    half = rows // 2
    bf, f32 = jnp.bfloat16, jnp.float32
    dma = pltpu.SemaphoreType.DMA

    def kernel(own_ref, out_ref, mate_buf, pair_ref, terms_ref, total_ref, send, recv, line_send, line_recv, own_sem):
        grid = Grid("stream", size, inner)
        row, col = grid.row, grid.col
        greet([grid])
        mate = grid.device(row, 1 - col)
        mine = pl.ds(pl.multiple_of(col * half, half), half)
        swap = pltpu.make_async_remote_copy(
            src_ref=own_ref, dst_ref=mate_buf, send_sem=send.at[0], recv_sem=recv.at[0], device_id=mate,
            device_id_type=MESH)
        swap.start()
        swap.wait_recv()
        pair_ref[...] = (own_ref[mine, :].astype(f32) + mate_buf[mine, :].astype(f32)).astype(bf)
        waits = []
        line = Grid("stream", size, inner)
        in_turn([gather_steps(
            line, pair_ref, terms_ref, line_send, line_recv, own_sem, waits, 0, 1, across_too=False)])
        finish(waits)
        total = terms_ref[pl.ds(0, half), :].astype(f32)
        for r in range(1, outer):
            total = total + terms_ref[pl.ds(r * half, half), :].astype(f32)
        total_ref[...] = total
        out_ref[mine, :] = total
        swap_back = pltpu.make_async_remote_copy(
            src_ref=total_ref, dst_ref=out_ref.at[mine], send_sem=send.at[1], recv_sem=recv.at[1], device_id=mate,
            device_id_type=MESH)
        swap_back.start()
        theirs = pltpu.make_async_remote_copy(
            src_ref=total_ref, dst_ref=out_ref.at[pl.ds(pl.multiple_of((1 - col) * half, half), half)],
            send_sem=send.at[1], recv_sem=recv.at[1], device_id=mate, device_id_type=MESH)
        theirs.wait_recv()
        swap.wait_send()
        swap_back.wait_send()

    return pl.pallas_call(
        kernel,
        in_specs=[pl.BlockSpec(memory_space=pltpu.VMEM)],
        out_specs=pl.BlockSpec(memory_space=pltpu.VMEM),
        out_shape=jax.ShapeDtypeStruct((rows, width), f32),
        scratch_shapes=[
            pltpu.VMEM((rows, width), bf), pltpu.VMEM((half, width), bf), pltpu.VMEM((outer * half, width), bf),
            pltpu.VMEM((half, width), f32), dma((2,)), dma((2,)), dma((2, outer)), dma((outer,)), dma],
        compiler_params=pltpu.CompilerParams(
            collective_id=collective_id, has_side_effects=True, vmem_limit_bytes=VMEM_LIMIT),
        name="link_sum",
    )(partial.astype(bf))


def link_open(conv, gate, arrays, sizes, collective_id):
    count = len(arrays)
    mates = sizes["stream"][0]
    take = conv.shape[0] // mates
    dma = pltpu.SemaphoreType.DMA

    def kernel(conv_ref, gate_ref, *refs):
        sources, refs = refs[:count], refs[count:]
        conv_all, conv_own, gate_own, outs, refs = *refs[:3], refs[3 : 3 + count], refs[3 + count :]
        hand_send, hand_recv, sems = refs[0], refs[1], refs[2:]
        grids = {axis: Grid(axis, *sizes[axis]) for axis in ("seq", "stream")}
        greet(list(grids.values()), ("stream",))
        me = grids["stream"].row * grids["stream"].inner + grids["stream"].col
        waits = []

        def rows(mate):
            return pl.ds(pl.multiple_of(mate * take, take), take)

        def hand(kind, source, target):
            copy = pltpu.make_async_copy(source.at[rows(me)], target.at[rows(me)], hand_send.at[kind, 0])
            copy.start()
            waits_own = [copy]
            for step in range(1, mates):
                mate = (me + step) % mates
                copy = pltpu.make_async_remote_copy(
                    src_ref=source.at[rows(mate)], dst_ref=target.at[rows(me)], send_sem=hand_send.at[kind, step],
                    recv_sem=hand_recv.at[kind, step], device_id={"stream": mate}, device_id_type=MESH)
                copy.start()
                waits.append((me >= 0, copy))
            return waits_own

        def handed(kind, source, target, own):
            for copy in own:
                copy.wait()
            for step in range(1, mates):
                mate = (me + mates - step) % mates
                pltpu.make_async_remote_copy(
                    src_ref=source.at[rows(me)], dst_ref=target.at[rows(mate)], send_sem=hand_send.at[kind, step],
                    recv_sem=hand_recv.at[kind, step], device_id={"stream": me}, device_id_type=MESH).wait_recv()

        own = hand(0, conv_ref, conv_own)

        def main():
            for i, (axis, _, chunks) in enumerate(arrays):
                for chunk in range(chunks):
                    at = 3 * (1 + sum(entry[2] for entry in arrays[:i]) + chunk)
                    yield gather_steps(grids[axis], sources[i], outs[i], *sems[at : at + 3], waits, chunk, chunks)

        runs = list(main())
        for run in runs:
            next(run)
        own_gate = hand(1, gate_ref, gate_own)
        handed(0, conv_ref, conv_own, own)
        first = gather_steps(grids["seq"], conv_own, conv_all, *sems[:3], waits, 0, 1)
        next(first)
        in_turn([first, *runs])
        handed(1, gate_ref, gate_own, own_gate)
        finish(waits)

    entries = [("seq", conv, 1), *arrays]
    sems = []
    for axis, _, chunks in entries:
        size = sizes[axis][0]
        sems += [dma((4, size)), dma((size,)), dma] * chunks
    result = pl.pallas_call(
        kernel,
        in_specs=[pl.BlockSpec(memory_space=pl.ANY)] * (count + 2),
        out_specs=[pl.BlockSpec(memory_space=pl.ANY)] * (count + 3),
        out_shape=[
            jax.ShapeDtypeStruct((sizes["seq"][0] * conv.shape[0], conv.shape[1]), conv.dtype),
            jax.ShapeDtypeStruct(conv.shape, conv.dtype),
            jax.ShapeDtypeStruct(gate.shape, gate.dtype),
            *[jax.ShapeDtypeStruct((sizes[axis][0] * a.shape[0], *a.shape[1:]), a.dtype) for axis, a, _ in arrays]],
        scratch_shapes=[dma((2, mates)), dma((2, mates)), *sems],
        compiler_params=pltpu.CompilerParams(collective_id=collective_id, has_side_effects=True),
        name="link_open",
    )(conv, gate, *[a for _, a, _ in arrays])
    return result[0], result[2], *result[3:]


def passed_along(block, axis, distance):
    devices = range(lax.axis_size(axis))
    route = [(i - distance, i) for i in devices if i - distance in devices]
    return lax.ppermute(block, axis, route)


def silu_slope(values_in):
    sigmoid_v = jax.nn.sigmoid(values_in)
    return sigmoid_v * (1.0 + values_in * (1.0 - sigmoid_v))


def token_layout(lengths, first_pos, n_tokens):
    doc_ends = jnp.cumsum(lengths)
    begins = doc_ends - lengths
    positions = first_pos + jnp.arange(n_tokens, dtype=jnp.int32)
    live_slot = (lengths > 0)[None, :]
    doc_ids = jnp.sum(((begins[None, :] <= positions[:, None]) & live_slot).astype(jnp.int32), axis=1)
    start_flags = jnp.sum(((begins[None, :] == positions[:, None]) & live_slot).astype(jnp.float32), axis=1)
    valid_mask = (positions < doc_ends[-1]).astype(jnp.float32)
    return (doc_ids, start_flags, valid_mask)


def contract_rows(left_mat, right_mat):
    return lax.dot_general(left_mat, right_mat, (((0,), (0,)), ((), ())), preferred_element_type=jnp.float32)


def contract_cols(left_mat, right_mat):
    return lax.dot_general(left_mat, right_mat, NT, preferred_element_type=jnp.float32)


def padded_rows(array, rows):
    return jnp.pad(array, ((0, -array.shape[0] % rows), (0, 0)))


def carried(ends, step_sum, rate, backward, sizes, collective_id):
    seqs, chans = step_sum.shape
    n = rate.shape[0]
    high = step_sum.astype(jnp.bfloat16)
    low = (step_sum - high.astype(jnp.float32)).astype(jnp.bfloat16)
    sent = padded_rows(jnp.concatenate([ends.astype(jnp.bfloat16), high, low], axis=0), 16)
    (gathered,) = link_gather([("seq", sent, 1)], sizes, collective_id, (backward, not backward))
    gathered = gathered.reshape(-1, *sent.shape)
    count = lax.axis_size("seq")
    place = lax.axis_index("seq")
    state = jnp.zeros((seqs, n, chans), jnp.float32)
    for step in range(count - 1):
        source = count - 1 - step if backward else step
        block = gathered[source].astype(jnp.float32)
        total = block[seqs * n : seqs * (n + 1)] + block[seqs * (n + 1) : seqs * (n + 2)]
        joined = jnp.exp2(total[:, None, :] * rate[None]) * state + block[: seqs * n].reshape(seqs, n, chans)
        state = jnp.where(source > place if backward else source < place, joined, state)
    return state.reshape(seqs * n, chans)


def local(sizes, resid_in, out_grad, row_lengths, norm_gain, in_weight, conv_weight, conv_bias, xproj_weight, dt_weight,
          dt_bias, a_log, skip_gain, out_weight):
    bf, f32 = jnp.bfloat16, jnp.float32
    seqs = lax.axis_size("stream")
    parts = lax.axis_size("seq")
    own = conv_bias.shape[0]
    own_feats = norm_gain.shape[0]
    chans = own * parts
    rank_dim = dt_weight.shape[0]
    state_dim = a_log.shape[1]
    proj_dim = xproj_weight.shape[1]
    length, feats = resid_in.shape[1:]
    tokens = seqs * length

    gain = norm_gain.astype(f32)
    scaled = (in_weight.astype(f32) * gain[:, None]).astype(bf).reshape(own_feats, 2, parts, seqs, own)
    scaled = scaled.transpose(1, 3, 0, 2, 4).reshape(2, seqs * own_feats, chans)
    packed = jnp.concatenate(
        [xproj_weight, dt_weight.T, a_log, conv_weight.T, conv_bias[:, None], dt_bias[:, None], skip_gain[:, None]],
        axis=1)
    residual = resid_in[0].astype(f32)
    cotangent = out_grad[0]
    inv_rms = lax.rsqrt(jnp.mean(residual * residual, axis=-1, keepdims=True) + EPSILON)
    unit_own = residual * inv_rms
    slots = row_lengths.shape[1]
    arrays = [
        ("stream", jnp.pad(row_lengths, ((0, 7), (0, -slots % 128))), 1), ("stream", unit_own.astype(bf), 4),
        ("seq", jnp.pad(packed, ((0, 0), (0, -packed.shape[1] % 128))), 1)]
    if own_feats % 16:
        mine = lax.all_to_all(scaled, "stream", 1, 1, tiled=True)
        gate_own = mine[1]
        lengths, unit, packed, in_conv = link_gather([*arrays, ("seq", mine[0], 1)], sizes, 1)
    else:
        in_conv, gate_own, lengths, unit, packed = link_open(scaled[0], scaled[1], arrays, sizes, 1)
    lengths = lengths[::8, :slots]
    unit, gate_own, out_own, cot_own = lax.optimization_barrier((unit, gate_own, out_weight, cotangent))
    in_gate = lax.all_gather(gate_own, "seq", axis=0, tiled=True)
    out_full = lax.all_gather(out_own, "seq", axis=0, tiled=True)
    cot_all = lax.all_gather(cot_own, "stream", axis=0, tiled=True)
    xproj_full = packed[:, :proj_dim]
    dtw_cols = packed[:, proj_dim : proj_dim + rank_dim]
    at = proj_dim + rank_dim
    log_rates = packed[:, at : at + state_dim].astype(f32).T
    at += state_dim
    conv_taps = packed[:, at : at + CONV].astype(f32).T
    at += CONV
    conv_shift, dt_shift, skip_vec = (packed[:, at + i].astype(f32) for i in range(3))
    rate = -jnp.exp(log_rates) / LN2

    rim = CONV - 1
    first_pos = lax.axis_index("seq") * length
    doc_ids, start_flags, valid_mask = jax.vmap(
        lambda row: token_layout(row, first_pos - rim, length + 2 * rim))(lengths)
    own_ids = doc_ids[:, rim : rim + length]
    starts = start_flags[:, rim : rim + length].reshape(tokens, 1)
    valid = valid_mask[:, rim : rim + length].reshape(tokens, 1)
    matches = [(doc_ids[:, tap : tap + length] == own_ids).astype(f32)[:, :, None] for tap in range(CONV)]

    conv_in = jnp.dot(unit, in_conv, preferred_element_type=f32).reshape(seqs, length, chans)
    gate_in = jnp.dot(unit, in_gate, preferred_element_type=f32)
    earlier = passed_along(conv_in[:, length - rim :].astype(bf), "seq", 1).astype(f32)
    padded = jnp.concatenate([earlier, conv_in], axis=1)
    conv_out = conv_shift
    for tap in range(CONV):
        conv_out = conv_out + conv_taps[tap] * padded[:, tap : tap + length] * matches[tap]
    activated = jax.nn.silu(conv_out).astype(bf).reshape(tokens, chans)
    act_float = activated.astype(f32)
    projected = link_sum(
        lax.dot_general(xproj_full, activated, (((0,), (1,)), ((), ())), preferred_element_type=f32), sizes, 2)
    low_rank = projected[:rank_dim].astype(bf)
    write_in = projected[rank_dim : rank_dim + state_dim]
    readout = projected[rank_dim + state_dim :]
    dt_pre = lax.dot_general(low_rank, dtw_cols, (((0,), (1,)), ((), ())), preferred_element_type=f32) + dt_shift
    dt_step = jax.nn.softplus(dt_pre)
    dt_reset = jnp.where(starts > 0, RESET, dt_step)
    dt_act = dt_step * act_float
    write_slabs, read_slabs = slabs_of(write_in), slabs_of(readout)
    write_diag, read_diag = spread(write_in), spread(readout)

    step_sum = jnp.sum(dt_reset.reshape(seqs, length, chans), axis=1)
    ends = scan_end(fwd_end_body, dt_reset, dt_act, write_slabs, rate, seqs)
    start_state = carried(ends, step_sum, rate, False, sizes, 3)
    scanned, history = fwd_full(dt_reset, dt_act, write_slabs, read_diag, rate, start_state, seqs)
    ssm_out = scanned + skip_vec * act_float
    gate_act = jax.nn.silu(gate_in)
    gated = (ssm_out * gate_act * valid).astype(bf)
    product = jnp.dot(gated, out_full, preferred_element_type=f32).astype(bf)
    output = (residual + lax.psum_scatter(product, "stream", scatter_dimension=0, tiled=True).astype(f32)).astype(bf)

    d_gated = contract_cols(cot_all, out_full)
    g_out = lax.psum_scatter(contract_rows(gated, cot_all).astype(bf), "seq", scatter_dimension=0, tiled=True)
    d_masked = d_gated * valid
    d_ssm = d_masked * gate_act
    d_gate = (d_masked * ssm_out * silu_slope(gate_in)).astype(bf)
    g_in_gate = lax.psum_scatter(contract_rows(unit, d_gate).astype(bf), "seq", scatter_dimension=0, tiled=True)
    g_skip = jnp.sum(d_ssm * act_float, axis=0)
    back_ends = scan_end(bwd_end_body, dt_reset, d_ssm, read_slabs, rate, seqs)
    later_sum = carried(back_ends, step_sum, rate, True, sizes, 4)
    sum_write, sum_rate, g_log, d_write, d_read = bwd_full(
        dt_reset, dt_act, d_ssm, history, read_slabs, write_diag, rate, later_sum, seqs)
    per_step = jnp.where(dt_step > 1e-30, sum_rate * LN2 / jnp.maximum(dt_step, 1e-30), 0.0)
    d_step = per_step + act_float * sum_write
    d_pre = d_step * jax.nn.sigmoid(dt_pre)
    g_dt_bias = jnp.sum(d_pre, axis=0)
    d_pre_low = d_pre.astype(bf)
    g_dt = lax.dot_general(d_pre_low, low_rank, (((0,), (1,)), ((), ())), preferred_element_type=f32)
    d_low = lax.dot_general(dtw_cols, d_pre_low, (((0,), (1,)), ((), ())), preferred_element_type=f32)
    d_proj = link_sum(jnp.concatenate([d_low, d_write, d_read], axis=0), sizes, 5).astype(bf)
    g_xproj = lax.dot_general(activated, d_proj, (((0,), (1,)), ((), ())), preferred_element_type=f32)
    d_act = dt_step * sum_write + skip_vec * d_ssm + lax.dot_general(
        d_proj, xproj_full, (((0,), (1,)), ((), ())), preferred_element_type=f32)
    d_conv = d_act.reshape(seqs, length, chans) * silu_slope(conv_out)
    g_conv_bias = jnp.sum(d_conv, axis=(0, 1))
    g_conv = jnp.stack(
        [jnp.sum(d_conv * padded[:, tap : tap + length] * matches[tap], axis=(0, 1)) for tap in range(CONV)], axis=1)
    later = passed_along(d_conv[:, :rim].astype(bf), "seq", -1).astype(f32)
    d_ext = jnp.concatenate([d_conv, later], axis=1)
    d_conv_in = jnp.zeros_like(d_conv)
    for tap in range(CONV):
        offset = rim - tap
        match_back = (doc_ids[:, rim + offset : rim + offset + length] == own_ids).astype(f32)[:, :, None]
        d_conv_in = d_conv_in + conv_taps[tap] * d_ext[:, offset : offset + length] * match_back
    d_conv_in = d_conv_in.astype(bf).reshape(tokens, chans)
    g_in_conv = contract_rows(unit, d_conv_in).astype(bf)
    d_unit = (contract_cols(d_conv_in, in_conv) + contract_cols(d_gate, in_gate)).astype(bf)
    small = jnp.concatenate(
        [g_xproj, g_dt, g_log.T * LN2, g_conv, g_conv_bias[:, None], g_dt_bias[:, None], g_skip[:, None]], axis=1)
    small = jnp.pad(small, ((0, 0), (0, -small.shape[1] % 128))).astype(bf)
    g_in_conv, small, d_unit = link_reduce(
        [("seq", g_in_conv, 1, 0 if own_feats % 16 else own), ("seq", small, 1, 0), ("stream", d_unit, 4, 0)], sizes, 6)
    small = small.astype(f32)
    d_unit = d_unit.astype(f32)
    in_grad = cotangent.astype(f32) + inv_rms * (d_unit - unit_own * jnp.mean(d_unit * unit_own, axis=-1, keepdims=True))

    def in_rows(block):
        shared = lax.all_to_all(block, "stream", 0, 0, tiled=True).reshape(seqs, own_feats, parts, own)
        return shared.transpose(1, 2, 0, 3).reshape(own_feats, parts * seqs * own)

    g_in_conv = in_rows(g_in_conv) if own_feats % 16 else g_in_conv
    g_unit = jnp.concatenate([g_in_conv, in_rows(g_in_gate)], axis=1).astype(f32)
    at = proj_dim + rank_dim
    return (
        output[None],
        in_grad.astype(bf)[None],
        jnp.sum(g_unit * in_weight.astype(f32), axis=1),
        g_unit * gain[:, None],
        small[:, at + state_dim : at + state_dim + CONV].T,
        small[:, at + state_dim + CONV],
        small[:, :proj_dim],
        small[:, proj_dim:at].T,
        small[:, at + state_dim + CONV + 1],
        small[:, at : at + state_dim],
        small[:, at + state_dim + CONV + 2],
        g_out.astype(f32),
    )


def lines_of(mesh):
    devices = mesh.devices
    places = [getattr(device, "coords", None) for device in devices[:, 0]]
    seq = len(places)
    plane = 1
    if all(place is not None for place in places):
        plane = len({tuple(place)[1] for place in places})
    if seq % plane:
        plane = 1
    return {"seq": (seq, plane), "stream": (devices.shape[1], 1 if devices.shape[1] % 2 else 2)}


def solution(mesh):
    in_specs = (
        P("stream", "seq", None),
        P("stream", "seq", None),
        P("stream", None),
        P(("seq", "stream")),
        P(("seq", "stream"), None),
        P(None, ("seq", "stream")),
        P(("seq", "stream")),
        P(("seq", "stream"), None),
        P(None, ("seq", "stream")),
        P(("seq", "stream")),
        P(("seq", "stream"), None),
        P(("seq", "stream")),
        P(("seq", "stream"), None),
    )
    out_specs = (
        P("stream", "seq", None),
        P("stream", "seq", None),
        P(("seq", "stream")),
        P(("seq", "stream"), None),
        P(None, ("seq", "stream")),
        P(("seq", "stream")),
        P(("seq", "stream"), None),
        P(None, ("seq", "stream")),
        P(("seq", "stream")),
        P(("seq", "stream"), None),
        P(("seq", "stream")),
        P(("seq", "stream"), None),
    )
    return jax.shard_map(functools.partial(local, lines_of(mesh)), mesh=mesh, in_specs=in_specs, out_specs=out_specs, check_vma=False)
```

```python
import functools

import jax
import jax.numpy as jnp
from jax import lax
from jax.experimental import pallas as pl
from jax.experimental.pallas import tpu as pltpu
from jax.sharding import PartitionSpec as P

CONV = 4
EPSILON = 1e-05
RESET = 1e30
GROUP = 16
LN2 = 0.6931471805599453
NT = (((1,), (1,)), ((), ()))
VMEM_LIMIT = 56 << 20


def across(slab, place, width):
    return jnp.concatenate([jnp.broadcast_to(slab[:, place : place + 1], (slab.shape[0], 128))] * (width // 128), axis=1)


def decays(dte_ref, rate_ref, at, buf, power_buf=None):
    n = rate_ref.shape[0]
    for place in range(GROUP):
        power = dte_ref[pl.ds(at * GROUP + place, 1), :] * rate_ref[...]
        buf[pl.ds(place * n, n), :] = jnp.exp2(power)
        if power_buf is not None:
            power_buf[pl.ds(place * n, n), :] = power.astype(jnp.bfloat16)


def fwd_end_body(dte_ref, dtx_ref, slab_ref, rate_ref, end_ref, even_ref, odd_ref):
    n, width = rate_ref.shape
    groups = dte_ref.shape[0] // GROUP

    def walk(at, state, decay_ref):
        slab = slab_ref[pl.ds(at * n, n), :]
        for place in range(GROUP):
            write = across(slab, place, width)
            state = decay_ref[pl.ds(place * n, n), :] * state + dtx_ref[pl.ds(at * GROUP + place, 1), :] * write
        return state

    def pair(step, state):
        decays(dte_ref, rate_ref, 2 * step + 1, odd_ref)
        state = walk(2 * step, state, even_ref)
        decays(dte_ref, rate_ref, jnp.minimum(2 * step + 2, groups - 1), even_ref)
        return walk(2 * step + 1, state, odd_ref)

    decays(dte_ref, rate_ref, 0, even_ref)
    end_ref[...] = lax.fori_loop(0, groups // 2, pair, jnp.zeros_like(end_ref))


def bwd_end_body(dte_ref, grad_ref, slab_ref, rate_ref, end_ref, even_ref, odd_ref):
    n, width = rate_ref.shape
    groups = dte_ref.shape[0] // GROUP

    def walk(at, state, decay_ref):
        slab = slab_ref[pl.ds(at * n, n), :]
        for place in reversed(range(GROUP)):
            read = across(slab, place, width)
            state = decay_ref[pl.ds(place * n, n), :] * (state + grad_ref[pl.ds(at * GROUP + place, 1), :] * read)
        return state

    def pair(step, state):
        at = groups - 1 - 2 * step
        decays(dte_ref, rate_ref, at - 1, odd_ref)
        state = walk(at, state, even_ref)
        decays(dte_ref, rate_ref, jnp.maximum(at - 2, 0), even_ref)
        return walk(at - 1, state, odd_ref)

    decays(dte_ref, rate_ref, groups - 1, even_ref)
    end_ref[...] = lax.fori_loop(0, groups // 2, pair, jnp.zeros_like(end_ref))


def scan_end(body, dte, other, slabs, rate, seqs, width=512):
    tokens, chans = dte.shape
    length = tokens // seqs
    n = rate.shape[0]
    width = min(width, chans)
    work = tokens * chans * n
    return pl.pallas_call(
        body,
        grid=(seqs, chans // width),
        in_specs=[
            pl.BlockSpec((length, width), lambda s, c: (s, c)),
            pl.BlockSpec((length, width), lambda s, c: (s, c)),
            pl.BlockSpec((length // GROUP * n, GROUP), lambda s, c: (s, 0)),
            pl.BlockSpec((n, width), lambda s, c: (0, c)),
        ],
        out_specs=pl.BlockSpec((n, width), lambda s, c: (s, c)),
        out_shape=jax.ShapeDtypeStruct((seqs * n, chans), jnp.float32),
        scratch_shapes=[pltpu.VMEM((GROUP * n, width), jnp.float32)] * 2,
        compiler_params=pltpu.CompilerParams(vmem_limit_bytes=VMEM_LIMIT),
        cost_estimate=pl.CostEstimate(flops=4 * work, transcendentals=work, bytes_accessed=8 * tokens * chans),
        name=body.__name__[:7],
    )(dte, other, slabs, rate)


def fwd_full_body(dte_ref, dtx_ref, slab_ref, read_ref, rate_ref, start_ref, y_ref, hist_ref, h_ref, even_ref, odd_ref):
    block = dte_ref.shape[0]
    n, width = rate_ref.shape
    span = GROUP * n
    rate = rate_ref[...]

    @pl.when(pl.program_id(2) == 0)
    def _():
        h_ref[...] = start_ref[...]

    first = h_ref[...]
    hist_ref[pl.ds(0, n), :] = first.astype(jnp.bfloat16)

    def rows_out(at, buf):
        y_ref[pl.ds(at * GROUP, GROUP), :] = jnp.dot(
            read_ref[pl.ds(at * GROUP, GROUP), :], buf[...], preferred_element_type=jnp.float32)

    def group(at, state, buf):
        slab = slab_ref[pl.ds(at * n, n), :]
        for place in range(GROUP):
            t = at * GROUP + place
            write = across(slab, place, width)
            state = jnp.exp2(dte_ref[pl.ds(t, 1), :] * rate) * state + dtx_ref[pl.ds(t, 1), :] * write
            kept = state.astype(jnp.bfloat16)
            hist_ref[pl.ds((t + 1) * n, n), :] = kept
            buf[pl.ds(place * n, n), :] = kept
        return state

    def pair(step, state):
        at = 2 * step
        rows_out(jnp.maximum(at - 1, 0), odd_ref)
        state = group(at, state, even_ref)
        rows_out(at, even_ref)
        return group(at + 1, state, odd_ref)

    h_ref[...] = lax.fori_loop(0, block // GROUP // 2, pair, first)
    rows_out(block // GROUP - 1, odd_ref)


def fwd_full(dte, dtx, slabs, read, rate, start, seqs, width=512, block=256):
    tokens, chans = dte.shape
    n = rate.shape[0]
    width = min(width, chans)
    blocks = tokens // seqs // block
    work = tokens * chans * n
    here = lambda c, s, t: (s * blocks + t, c)
    rows = lambda c, s, t: (s * blocks + t, 0)
    return pl.pallas_call(
        fwd_full_body,
        grid=(chans // width, seqs, blocks),
        in_specs=[
            pl.BlockSpec((block, width), here),
            pl.BlockSpec((block, width), here),
            pl.BlockSpec((block // GROUP * n, GROUP), rows),
            pl.BlockSpec((block, read.shape[1]), rows),
            pl.BlockSpec((n, width), lambda c, s, t: (0, c)),
            pl.BlockSpec((n, width), lambda c, s, t: (s, c)),
        ],
        out_specs=[pl.BlockSpec((block, width), here), pl.BlockSpec(((block + 1) * n, width), here)],
        out_shape=[
            jax.ShapeDtypeStruct((tokens, chans), jnp.float32),
            jax.ShapeDtypeStruct((seqs * blocks * (block + 1) * n, chans), jnp.bfloat16),
        ],
        scratch_shapes=[pltpu.VMEM((n, width), jnp.float32)] + [pltpu.VMEM((GROUP * n, width), jnp.bfloat16)] * 2,
        compiler_params=pltpu.CompilerParams(vmem_limit_bytes=VMEM_LIMIT),
        cost_estimate=pl.CostEstimate(flops=8 * work, transcendentals=work, bytes_accessed=2 * work),
        name="fwd_full",
    )(dte, dtx, slabs, read, rate, start)


def bwd_full_body(dte_ref, dtx_ref, grad_ref, hist_ref, slab_ref, write_ref, ones_ref, rate_ref, start_ref,
                  s1_ref, s2_ref, grate_ref, dw_ref, dr_ref, g_ref, *scratch):
    block = dte_ref.shape[0]
    n, width = rate_ref.shape
    groups = block // GROUP
    bf, f32 = jnp.bfloat16, jnp.float32
    even, odd = scratch[:5], scratch[5:]
    unit = jnp.ones((GROUP, 128), bf)

    @pl.when(pl.program_id(2) == 0)
    def _():
        g_ref[...] = start_ref[...]

    @pl.when((pl.program_id(2) == 0) & (pl.program_id(1) == 0))
    def _():
        grate_ref[...] = jnp.zeros_like(grate_ref)

    def sums_out(at, bufs):
        _, _, adj_ref, rated_ref, dw_part = bufs
        rows = pl.ds(at * GROUP, GROUP)
        s1_ref[rows, :] = jnp.dot(write_ref[rows, :], adj_ref[...], preferred_element_type=f32)
        sums = jnp.dot(ones_ref[...], rated_ref[...], preferred_element_type=f32)
        s2_ref[rows, :] = sums[:GROUP]
        dw_ref[pl.ds(at, 1), :] = lax.dot_general(unit, dw_part[...], NT, preferred_element_type=f32)[:1]
        reads = lax.dot_general(
            grad_ref[rows, :].astype(bf), hist_ref[pl.ds(n + at * GROUP * n, GROUP * n), :], NT,
            preferred_element_type=f32)
        own = lax.broadcasted_iota(jnp.int32, reads.shape, 1) // n == lax.broadcasted_iota(jnp.int32, reads.shape, 0)
        dr_ref[pl.ds(at, 1), :] = jnp.sum(jnp.where(own, reads, 0.0), axis=0, keepdims=True)
        return sums[GROUP:]

    def strips(values):
        parts = [values[:, k * 128 : (k + 1) * 128] for k in range(width // 128)]
        while len(parts) > 1:
            parts = [a + b for a, b in zip(parts[::2], parts[1::2])] + parts[len(parts) // 2 * 2 :]
        return parts[0]

    def walk(at, state, bufs):
        decay_ref, power_ref, adj_ref, rated_ref, dw_part = bufs
        slab = slab_ref[pl.ds(at * n, n), :]
        for place in reversed(range(GROUP)):
            t = at * GROUP + place
            here = pl.ds(place * n, n)
            read = across(slab, place, width)
            adjoint = state + grad_ref[pl.ds(t, 1), :] * read
            power = dte_ref[pl.ds(t, 1), :] * rate_ref[...]
            state = jnp.exp2(power) * adjoint
            low = adjoint.astype(bf)
            adj_ref[here, :] = low
            rated_ref[here, :] = state.astype(bf) * hist_ref[pl.ds(t * n, n), :] * power.astype(bf)
            dw_part[here, :] = strips(adjoint * dtx_ref[pl.ds(t, 1), :]).astype(bf)
        return state

    def pair(step, state):
        at = groups - 1 - 2 * step
        old = sums_out(jnp.minimum(at + 1, groups - 1), odd)
        state = walk(at, state, even)
        grate_ref[...] += jnp.where(step > 0, old, 0.0) + sums_out(at, even)
        return walk(at - 1, state, odd)
    g_ref[...] = lax.fori_loop(0, groups // 2, pair, g_ref[...])
    grate_ref[...] += sums_out(0, odd)


def bwd_full(dte, dtx, grad, hist, slabs, write, rate, start, seqs, width=512, block=256):
    tokens, chans = dte.shape
    n = rate.shape[0]
    width = min(width, chans)
    strips = chans // width
    blocks = tokens // seqs // block
    span = GROUP * n
    work = tokens * chans * n
    column = jnp.arange(span)
    ones = jnp.concatenate(
        [(column // n)[None, :] == jnp.arange(GROUP)[:, None], (column % n)[None, :] == jnp.arange(n)[:, None]]
    ).astype(jnp.bfloat16)
    here = lambda c, s, t: (s * blocks + blocks - 1 - t, c)
    rows = lambda c, s, t: (s * blocks + blocks - 1 - t, 0)
    strip = lambda c, s, t: (c * seqs * blocks + s * blocks + blocks - 1 - t, 0)
    f32 = jnp.float32
    s1, s2, grate, dw, dr = pl.pallas_call(
        bwd_full_body,
        grid=(strips, seqs, blocks),
        in_specs=[
            pl.BlockSpec((block, width), here),
            pl.BlockSpec((block, width), here),
            pl.BlockSpec((block, width), here),
            pl.BlockSpec(((block + 1) * n, width), here),
            pl.BlockSpec((block // GROUP * n, GROUP), rows),
            pl.BlockSpec((block, span), rows),
            pl.BlockSpec(ones.shape, lambda c, s, t: (0, 0)),
            pl.BlockSpec((n, width), lambda c, s, t: (0, c)),
            pl.BlockSpec((n, width), lambda c, s, t: (s, c)),
        ],
        out_specs=[
            pl.BlockSpec((block, width), here),
            pl.BlockSpec((block, width), here),
            pl.BlockSpec((n, width), lambda c, s, t: (0, c)),
            pl.BlockSpec((block // GROUP, span), strip),
            pl.BlockSpec((block // GROUP, span), strip),
        ],
        out_shape=[
            jax.ShapeDtypeStruct((tokens, chans), f32),
            jax.ShapeDtypeStruct((tokens, chans), f32),
            jax.ShapeDtypeStruct((n, chans), f32),
            jax.ShapeDtypeStruct((strips * tokens // GROUP, span), f32),
            jax.ShapeDtypeStruct((strips * tokens // GROUP, span), f32),
        ],
        scratch_shapes=[
            pltpu.VMEM((n, width), f32),
            *[
                pltpu.VMEM((span, width), f32),
                *[pltpu.VMEM((span, width), jnp.bfloat16)] * 3,
                pltpu.VMEM((span, 128), jnp.bfloat16),
            ] * 2,
        ],
        compiler_params=pltpu.CompilerParams(vmem_limit_bytes=VMEM_LIMIT),
        cost_estimate=pl.CostEstimate(flops=14 * work, transcendentals=work, bytes_accessed=2 * work),
        name="bwd_full",
    )(dte, dtx, grad, hist, slabs, write, ones, rate, start)
    both = jnp.stack([part.reshape(strips, tokens // GROUP, span).sum(0) for part in (dw, dr)])
    both = both.reshape(2, tokens // GROUP, GROUP, n).transpose(0, 3, 1, 2).reshape(2, n, tokens)
    return s1, s2, grate, both[0], both[1]


def slabs_of(values):
    n, tokens = values.shape
    return values.reshape(n, tokens // GROUP, GROUP).transpose(1, 0, 2).reshape(tokens // GROUP * n, GROUP)


def spread(values):
    n, tokens = values.shape
    own = jnp.arange(tokens)[:, None] % GROUP == jnp.arange(GROUP)[None, :]
    return jnp.where(own[:, :, None], values.T[:, None, :], 0).reshape(tokens, GROUP * n).astype(jnp.bfloat16)


MESH = pl.DeviceIdType.MESH


class Grid:
    def __init__(self, axis, size, inner):
        self.axis, self.inner, self.outer = axis, inner, size // inner
        me = lax.axis_index(axis)
        self.row, self.col = me // inner, me % inner

    def device(self, row, col):
        return {self.axis: row * self.inner + col}

    def neighbours(self):
        row, col = self.row, self.col
        found = []
        if self.outer > 1:
            found += [(row > 0, self.device(row - 1, col)), (row < self.outer - 1, self.device(row + 1, col))]
        if self.inner > 1:
            found += [(col > 0, self.device(row, col - 1)), (col < self.inner - 1, self.device(row, col + 1))]
        return found

    def everyone(self):
        size = self.inner * self.outer
        me = self.row * self.inner + self.col
        return [(me >= 0, {self.axis: (me + step) % size}) for step in range(1, size)]


def greet(grids, all_of=()):
    barrier = pltpu.get_barrier_semaphore()
    count = 0
    for grid in grids:
        for there, device in grid.everyone() if grid.axis in all_of else grid.neighbours():

            @pl.when(there)
            def _(device=device):
                pl.semaphore_signal(barrier, inc=1, device_id=device, device_id_type=MESH)

            count = count + there.astype(jnp.int32)
    pl.semaphore_wait(barrier, count)


def gather_steps(grid, whole_ref, out_ref, send_sem, recv_sem, own, waits, chunk, chunks, across_too=True, ways=(True, True)):
    rows = whole_ref.shape[0]
    part = rows // chunks
    src_ref = whole_ref.at[pl.ds(chunk * part, part)]
    outer, inner = grid.outer, grid.inner if across_too else 1
    row, col = grid.row, grid.col

    def number(r, c):
        return r * inner + c if across_too else r

    def place(r, c):
        return pl.ds(pl.multiple_of(number(r, c) * rows + chunk * part, part), part)

    def send(there, way, r, c, device, source):
        copy = pltpu.make_async_remote_copy(
            src_ref=source, dst_ref=out_ref.at[place(r, c)], send_sem=send_sem.at[way, number(r, c)],
            recv_sem=recv_sem.at[number(r, c)], device_id=device, device_id_type=MESH)

        @pl.when(there)
        def _():
            copy.start()

        waits.append((there, copy))

    def across(there, r, c, source):
        if inner > 1:
            send(there & (c >= col) & (col > 0), 2, r, c, grid.device(row, col - 1), source)
            send(there & (c <= col) & (col < inner - 1), 3, r, c, grid.device(row, col + 1), source)

    def along(there, r, source):
        if outer > 1:
            if ways[0]:
                send(there & (r >= row) & (row > 0), 0, r, col, grid.device(row - 1, col), source)
            if ways[1]:
                send(there & (r <= row) & (row < outer - 1), 1, r, col, grid.device(row + 1, col), source)

    def arrive(there, r, c):
        copy = pltpu.make_async_remote_copy(
            src_ref=src_ref, dst_ref=out_ref.at[place(r, c)], send_sem=send_sem.at[0, 0],
            recv_sem=recv_sem.at[number(r, c)], device_id=grid.device(row, col), device_id_type=MESH)

        @pl.when(there)
        def _():
            copy.wait_recv()

    always = row >= 0
    along(always, row, src_ref)
    across(always, row, col, src_ref)
    own_sem, own_buf = own
    fetch = pltpu.make_async_copy(src_ref, own_buf, own_sem.at[0])
    fetch.start()
    for _ in range(chunk + 1):
        yield
    fetch.wait()
    keep = pltpu.make_async_copy(own_buf, out_ref.at[place(row, col)], own_sem.at[1])
    keep.start()
    waits.append((None, keep))

    def rows_at(distance):
        return [row - distance] * ways[1] + [row + distance] * ways[0]

    for distance in range(1, outer):
        for r in rows_at(distance):
            there = (r >= 0) & (r < outer)
            arrive(there, r, col)
            along(there, r, out_ref.at[place(r, col)])
            across(there, r, col, out_ref.at[place(r, col)])
        yield
    for step in range(1, inner):
        for distance in range(outer):
            for r in rows_at(distance) if distance else (row,):
                for c in (col - step, col + step):
                    there = (r >= 0) & (r < outer) & (c >= 0) & (c < inner)
                    arrive(there, r, c)
                    if step < inner - 1:
                        across(there, r, c, out_ref.at[place(r, c)])
            yield


def finish(waits):
    for there, copy in waits:
        if there is None:
            copy.wait()
        else:

            @pl.when(there)
            def _(copy=copy):
                if copy.is_remote:
                    copy.wait_send()
                else:
                    copy.wait()


def gather_scratch(size, array, chunks):
    dma = pltpu.SemaphoreType.DMA
    own = pltpu.VMEM((array.shape[0] // chunks, *array.shape[1:]), array.dtype)
    return [dma((4, size)), dma((size,)), dma((2,)), own] * chunks


def in_turn(runs):
    runs = list(runs)
    while runs:
        left = []
        for run in runs:
            if next(run, run) is not run:
                left.append(run)
        runs = left


def link_gather(arrays, sizes, collective_id, ways=(True, True)):
    count = len(arrays)
    axes = sorted({entry[0] for entry in arrays})

    def kernel(*refs):
        sources, outs, sems = refs[:count], refs[count : 2 * count], refs[2 * count :]
        grids = {axis: Grid(axis, *sizes[axis]) for axis in axes}
        greet([grids[axis] for axis in axes])
        waits = []
        runs = []
        for i, (axis, _, chunks) in enumerate(arrays):
            for chunk in range(chunks):
                runs.append(gather_steps(
                    grids[axis], sources[i], outs[i], sems[0], sems[1], sems[2:4], waits, chunk, chunks, ways=ways))
                sems = sems[4:]
        in_turn(runs)
        finish(waits)

    sems = []
    for axis, a, chunks in arrays:
        sems += gather_scratch(sizes[axis][0], a, chunks)
    return pl.pallas_call(
        kernel,
        in_specs=[pl.BlockSpec(memory_space=pl.ANY)] * count,
        out_specs=[pl.BlockSpec(memory_space=pl.ANY)] * count,
        out_shape=[
            jax.ShapeDtypeStruct((sizes[axis][0] * a.shape[0], *a.shape[1:]), a.dtype) for axis, a, _ in arrays],
        scratch_shapes=sems,
        compiler_params=pltpu.CompilerParams(
            collective_id=collective_id, has_side_effects=True, vmem_limit_bytes=VMEM_LIMIT),
        name="link_gather",
    )(*[a for _, a, _ in arrays])


def reduce_steps(grid, src_ref, out_ref, scratch, waits, chunks, share):
    acc, inner_buf, outer_buf, load_sem, inner_send, inner_recv, outer_send, outer_recv, out_sem = scratch[:9]
    outer, inner = grid.outer, grid.inner
    row, col = grid.row, grid.col
    rows = acc.shape[0] // (outer * inner)
    part = rows // chunks
    piece = min(part, 64)

    def start_of(chunk, r, c):
        return pl.multiple_of((r * inner + c) * rows + chunk * part, part)

    def line(me, size, device, block, buf, send, recv):
        def from_low(target):
            return target if size > 2 else 0

        def from_high(target, owner):
            return jnp.where(target == owner, size, target) if size > 2 else 0

        def hop(there, target, onward, slot):
            copy = pltpu.make_async_remote_copy(
                src_ref=acc.at[pl.ds(block(target), part)], dst_ref=buf.at[slot], send_sem=send.at[target],
                recv_sem=recv.at[slot], device_id=device(onward), device_id_type=MESH)

            @pl.when(there)
            def _():
                copy.start()

            waits.append((there, copy))

        def up(there, target):
            hop(there & (target > me), target, me + 1, from_low(target))

        def down(there, target):
            hop(there & (target < me), target, me - 1, from_high(target, me - 1))

        def arrive(there, target, slot):
            at = block(target)
            copy = pltpu.make_async_remote_copy(
                src_ref=acc.at[pl.ds(at, part)], dst_ref=buf.at[slot], send_sem=send.at[target],
                recv_sem=recv.at[slot], device_id=device(me), device_id_type=MESH)

            @pl.when(there)
            def _():
                copy.wait_recv()

                @pl.loop(0, part // piece)
                def _(k):
                    here = pl.ds(pl.multiple_of(at + k * piece, piece), piece)
                    there_rows = pl.ds(pl.multiple_of(k * piece, piece), piece)
                    total = acc[here, :].astype(jnp.float32) + buf[slot, there_rows, :].astype(jnp.float32)
                    acc[here, :] = total.astype(acc.dtype)

        def begin(target):
            up(me == 0, target)
            down(me == size - 1, target)

        def go_on(target):
            arrive((me > 0) & (target >= me), target, from_low(target))
            arrive((me < size - 1) & (target <= me), target, from_high(target, me))
            if size > 2:
                up((me > 0) & (me < size - 1), target)
                down((me > 0) & (me < size - 1), target)

        return begin, go_on

    order = sorted(range(outer), key=lambda k: -abs(2 * k - outer + 1))
    pieces = [(chunk, r) for chunk in range(chunks) for r in order]
    loads = {}
    for chunk, r in pieces:
        loads[chunk, r] = [
            pltpu.make_async_copy(
                src_ref.at[pl.ds(start_of(chunk, r, c), part)], acc.at[pl.ds(start_of(chunk, r, c), part)],
                load_sem.at[chunk, r * inner + c])
            for c in range(inner)]
        for load in loads[chunk, r]:
            load.start()

    def inner_line(chunk, r):
        return line(
            col, inner, lambda c: grid.device(row, c), lambda t: start_of(chunk, r, t), inner_buf.at[chunk, r],
            inner_send.at[chunk, r], inner_recv.at[chunk, r])

    def outer_line(chunk):
        return line(
            row, outer, lambda r: grid.device(r, col), lambda t: start_of(chunk, t, col), outer_buf.at[chunk],
            outer_send.at[chunk], outer_recv.at[chunk])

    def inner_start(k):
        if k < len(pieces):
            for load in loads[pieces[k]]:
                load.wait()
            if inner > 1:
                for c in range(inner):
                    inner_line(*pieces[k])[0](c)

    def outer_rest(k):
        if 0 <= k < len(pieces):
            chunk, r = pieces[k]
            if outer > 1:
                outer_line(chunk)[1](r)
            if r == order[-1]:
                give(chunk)

    def give(chunk):
        first = start_of(chunk, row, col)
        if share is None:
            last = pltpu.make_async_copy(
                acc.at[pl.ds(first, part)], out_ref.at[pl.ds(chunk * part, part)], out_sem.at[chunk])
            last.start()
            waits.append((None, last))
            return
        other, strip, send_sem, recv_sem = share
        count, me = other.outer * other.inner, other.row * other.inner + other.col
        take = rows // count
        for mate in range(chunk * part // take, (chunk + 1) * part // take):
            for k in range(acc.shape[1] // strip):
                source = acc.at[
                    pl.ds(pl.multiple_of((row * inner + col) * rows + mate * take, take), take),
                    pl.ds(k * strip, strip)]
                target = out_ref.at[:, pl.ds(pl.multiple_of((k * count + me) * strip, strip), strip)]
                own = pltpu.make_async_copy(source, target, send_sem.at[mate, k])
                sent = pltpu.make_async_remote_copy(
                    src_ref=source, dst_ref=target, send_sem=send_sem.at[mate, k], recv_sem=recv_sem.at[me, k],
                    device_id={other.axis: mate}, device_id_type=MESH)

                @pl.when(mate == me)
                def _(own=own):
                    own.start()

                @pl.when(mate != me)
                def _(sent=sent):
                    sent.start()

                waits.append((mate != me, sent))
                waits.append((mate == me, own))

    window = 2
    for k in range(window):
        inner_start(k)
    yield
    for k in range(len(pieces)):
        inner_start(k + window)
        chunk, r = pieces[k]
        if inner > 1:
            for c in range(inner):
                inner_line(chunk, r)[1](c)
        if outer > 1:
            outer_line(chunk)[0](r)
        yield
        outer_rest(k - window)
        yield
    for k in range(len(pieces) - window, len(pieces)):
        outer_rest(k)
        yield
    if share is not None:
        other, strip, send_sem, recv_sem = share
        count, me = other.outer * other.inner, other.row * other.inner + other.col
        take = rows // count
        for mate in range(count):
            for k in range(acc.shape[1] // strip):
                copy = pltpu.make_async_remote_copy(
                    src_ref=acc.at[pl.ds(0, take), pl.ds(k * strip, strip)],
                    dst_ref=out_ref.at[:, pl.ds((k * count + mate) * strip, strip)], send_sem=send_sem.at[mate, k],
                    recv_sem=recv_sem.at[mate, k], device_id={other.axis: me}, device_id_type=MESH)

                @pl.when(mate != me)
                def _(copy=copy):
                    copy.wait_recv()


def link_reduce(arrays, sizes, collective_id):
    count = len(arrays)

    def kernel(*refs):
        sources, outs, scratch = refs[:count], refs[count : 2 * count], refs[2 * count :]
        grids = {axis: Grid(axis, *sizes[axis]) for axis in ("seq", "stream")}
        greet(list(grids.values()), ("stream",))
        waits = []
        runs = []
        for i, (axis, _, chunks, strip) in enumerate(arrays):
            share = (grids["stream"], strip, scratch[9], scratch[10]) if strip else None
            runs.append(reduce_steps(grids[axis], sources[i], outs[i], scratch[:9], waits, chunks, share))
            scratch = scratch[11 if strip else 9 :]
        in_turn(runs)
        finish(waits)

    scratch, shapes = [], []
    for axis, a, chunks, strip in arrays:
        size, inner = sizes[axis]
        outer = size // inner
        part = a.shape[0] // size // chunks
        slots = [n + 1 if n > 2 else 1 for n in (inner, outer)]
        dma = pltpu.SemaphoreType.DMA
        scratch += [
            pltpu.VMEM(a.shape, a.dtype),
            pltpu.VMEM((chunks, outer, slots[0], part, a.shape[1]), a.dtype),
            pltpu.VMEM((chunks, slots[1], part, a.shape[1]), a.dtype),
            dma((chunks, size)), dma((chunks, outer, inner)), dma((chunks, outer, slots[0])), dma((chunks, outer)),
            dma((chunks, slots[1])), dma((chunks,))]
        if strip:
            mates = sizes["stream"][0]
            shapes.append(jax.ShapeDtypeStruct((a.shape[0] // size // mates, a.shape[1] * mates), a.dtype))
            scratch += [dma((mates, a.shape[1] // strip))] * 2
        else:
            shapes.append(jax.ShapeDtypeStruct((a.shape[0] // size, a.shape[1]), a.dtype))
    return pl.pallas_call(
        kernel,
        in_specs=[pl.BlockSpec(memory_space=pl.ANY)] * count,
        out_specs=[pl.BlockSpec(memory_space=pl.ANY)] * count,
        out_shape=shapes,
        scratch_shapes=scratch,
        compiler_params=pltpu.CompilerParams(
            collective_id=collective_id, has_side_effects=True, vmem_limit_bytes=VMEM_LIMIT),
        name="link_reduce",
    )(*[entry[1] for entry in arrays])


def link_sum(partial, sizes, collective_id):
    rows, width = partial.shape
    size, inner = sizes["stream"]
    outer = size // inner
    assert inner == 2
    half = rows // 2
    bf, f32 = jnp.bfloat16, jnp.float32
    dma = pltpu.SemaphoreType.DMA

    def kernel(own_ref, out_ref, mate_buf, pair_ref, terms_ref, total_ref, send, recv, line_send, line_recv, own_sem, own_buf):
        grid = Grid("stream", size, inner)
        row, col = grid.row, grid.col
        greet([grid])
        mate = grid.device(row, 1 - col)
        mine = pl.ds(pl.multiple_of(col * half, half), half)
        swap = pltpu.make_async_remote_copy(
            src_ref=own_ref, dst_ref=mate_buf, send_sem=send.at[0], recv_sem=recv.at[0], device_id=mate,
            device_id_type=MESH)
        swap.start()
        swap.wait_recv()
        pair_ref[...] = (own_ref[mine, :].astype(f32) + mate_buf[mine, :].astype(f32)).astype(bf)
        waits = []
        line = Grid("stream", size, inner)
        in_turn([gather_steps(
            line, pair_ref, terms_ref, line_send, line_recv, (own_sem, own_buf), waits, 0, 1, across_too=False)])
        finish(waits)
        total = terms_ref[pl.ds(0, half), :].astype(f32)
        for r in range(1, outer):
            total = total + terms_ref[pl.ds(r * half, half), :].astype(f32)
        total_ref[...] = total
        out_ref[mine, :] = total
        swap_back = pltpu.make_async_remote_copy(
            src_ref=total_ref, dst_ref=out_ref.at[mine], send_sem=send.at[1], recv_sem=recv.at[1], device_id=mate,
            device_id_type=MESH)
        swap_back.start()
        theirs = pltpu.make_async_remote_copy(
            src_ref=total_ref, dst_ref=out_ref.at[pl.ds(pl.multiple_of((1 - col) * half, half), half)],
            send_sem=send.at[1], recv_sem=recv.at[1], device_id=mate, device_id_type=MESH)
        theirs.wait_recv()
        swap.wait_send()
        swap_back.wait_send()

    return pl.pallas_call(
        kernel,
        in_specs=[pl.BlockSpec(memory_space=pltpu.VMEM)],
        out_specs=pl.BlockSpec(memory_space=pltpu.VMEM),
        out_shape=jax.ShapeDtypeStruct((rows, width), f32),
        scratch_shapes=[
            pltpu.VMEM((rows, width), bf), pltpu.VMEM((half, width), bf), pltpu.VMEM((outer * half, width), bf),
            pltpu.VMEM((half, width), f32), dma((2,)), dma((2,)), dma((4, outer)), dma((outer,)), dma((2,)),
            pltpu.VMEM((half, width), bf)],
        compiler_params=pltpu.CompilerParams(
            collective_id=collective_id, has_side_effects=True, vmem_limit_bytes=VMEM_LIMIT),
        name="link_sum",
    )(partial.astype(bf))


def link_open(conv, gate, arrays, sizes, collective_id):
    count = len(arrays)
    mates = sizes["stream"][0]
    take = conv.shape[0] // mates
    dma = pltpu.SemaphoreType.DMA

    def kernel(conv_ref, gate_ref, *refs):
        sources, refs = refs[:count], refs[count:]
        conv_all, conv_own, gate_own, outs, refs = *refs[:3], refs[3 : 3 + count], refs[3 + count :]
        hand_send, hand_recv, hand_buf, sems = refs[0], refs[1], refs[2], refs[3:]
        grids = {axis: Grid(axis, *sizes[axis]) for axis in ("seq", "stream")}
        greet(list(grids.values()), ("stream",))
        me = grids["stream"].row * grids["stream"].inner + grids["stream"].col
        waits = []

        def rows(mate):
            return pl.ds(pl.multiple_of(mate * take, take), take)

        def hand(kind, source, target):
            fetch = pltpu.make_async_copy(source.at[rows(me)], hand_buf.at[kind], hand_send.at[kind, 0])
            fetch.start()
            for step in range(1, mates):
                mate = (me + step) % mates
                copy = pltpu.make_async_remote_copy(
                    src_ref=source.at[rows(mate)], dst_ref=target.at[rows(me)], send_sem=hand_send.at[kind, step],
                    recv_sem=hand_recv.at[kind, step], device_id={"stream": mate}, device_id_type=MESH)
                copy.start()
                waits.append((me >= 0, copy))
            fetch.wait()
            keep = pltpu.make_async_copy(hand_buf.at[kind], target.at[rows(me)], hand_recv.at[kind, 0])
            keep.start()
            return keep

        def handed(kind, source, target, own):
            own.wait()
            for step in range(1, mates):
                mate = (me + mates - step) % mates
                pltpu.make_async_remote_copy(
                    src_ref=source.at[rows(me)], dst_ref=target.at[rows(mate)], send_sem=hand_send.at[kind, step],
                    recv_sem=hand_recv.at[kind, step], device_id={"stream": me}, device_id_type=MESH).wait_recv()

        own = hand(0, conv_ref, conv_own)

        def main():
            for i, (axis, _, chunks) in enumerate(arrays):
                for chunk in range(chunks):
                    at = 4 * (1 + sum(entry[2] for entry in arrays[:i]) + chunk)
                    yield gather_steps(
                        grids[axis], sources[i], outs[i], sems[at], sems[at + 1], sems[at + 2 : at + 4], waits, chunk,
                        chunks)

        runs = list(main())
        for run in runs:
            next(run)
        own_gate = hand(1, gate_ref, gate_own)
        handed(0, conv_ref, conv_own, own)
        first = gather_steps(grids["seq"], conv_own, conv_all, sems[0], sems[1], sems[2:4], waits, 0, 1)
        next(first)
        in_turn([first, *runs])
        handed(1, gate_ref, gate_own, own_gate)
        finish(waits)

    entries = [("seq", conv, 1), *arrays]
    sems = []
    for axis, a, chunks in entries:
        sems += gather_scratch(sizes[axis][0], a, chunks)
    result = pl.pallas_call(
        kernel,
        in_specs=[pl.BlockSpec(memory_space=pl.ANY)] * (count + 2),
        out_specs=[pl.BlockSpec(memory_space=pl.ANY)] * (count + 3),
        out_shape=[
            jax.ShapeDtypeStruct((sizes["seq"][0] * conv.shape[0], conv.shape[1]), conv.dtype),
            jax.ShapeDtypeStruct(conv.shape, conv.dtype),
            jax.ShapeDtypeStruct(gate.shape, gate.dtype),
            *[jax.ShapeDtypeStruct((sizes[axis][0] * a.shape[0], *a.shape[1:]), a.dtype) for axis, a, _ in arrays]],
        scratch_shapes=[
            dma((2, mates)), dma((2, mates)), pltpu.VMEM((2, take, conv.shape[1]), conv.dtype), *sems],
        compiler_params=pltpu.CompilerParams(
            collective_id=collective_id, has_side_effects=True, vmem_limit_bytes=VMEM_LIMIT),
        name="link_open",
    )(conv, gate, *[a for _, a, _ in arrays])
    return result[0], result[2], *result[3:]


def passed_along(block, axis, distance):
    devices = range(lax.axis_size(axis))
    route = [(i - distance, i) for i in devices if i - distance in devices]
    return lax.ppermute(block, axis, route)


def silu_slope(values_in):
    sigmoid_v = jax.nn.sigmoid(values_in)
    return sigmoid_v * (1.0 + values_in * (1.0 - sigmoid_v))


def token_layout(lengths, first_pos, n_tokens):
    doc_ends = jnp.cumsum(lengths)
    begins = doc_ends - lengths
    positions = first_pos + jnp.arange(n_tokens, dtype=jnp.int32)
    live_slot = (lengths > 0)[None, :]
    doc_ids = jnp.sum(((begins[None, :] <= positions[:, None]) & live_slot).astype(jnp.int32), axis=1)
    start_flags = jnp.sum(((begins[None, :] == positions[:, None]) & live_slot).astype(jnp.float32), axis=1)
    valid_mask = (positions < doc_ends[-1]).astype(jnp.float32)
    return (doc_ids, start_flags, valid_mask)


def contract_rows(left_mat, right_mat):
    return lax.dot_general(left_mat, right_mat, (((0,), (0,)), ((), ())), preferred_element_type=jnp.float32)


def contract_cols(left_mat, right_mat):
    return lax.dot_general(left_mat, right_mat, NT, preferred_element_type=jnp.float32)


def padded_rows(array, rows):
    return jnp.pad(array, ((0, -array.shape[0] % rows), (0, 0)))


def carried(ends, step_sum, rate, backward, sizes, collective_id):
    seqs, chans = step_sum.shape
    n = rate.shape[0]
    high = step_sum.astype(jnp.bfloat16)
    low = (step_sum - high.astype(jnp.float32)).astype(jnp.bfloat16)
    sent = padded_rows(jnp.concatenate([ends.astype(jnp.bfloat16), high, low], axis=0), 16)
    (gathered,) = link_gather([("seq", sent, 1)], sizes, collective_id, (backward, not backward))
    gathered = gathered.reshape(-1, *sent.shape)
    count = lax.axis_size("seq")
    place = lax.axis_index("seq")
    state = jnp.zeros((seqs, n, chans), jnp.float32)
    for step in range(count - 1):
        source = count - 1 - step if backward else step
        block = gathered[source].astype(jnp.float32)
        total = block[seqs * n : seqs * (n + 1)] + block[seqs * (n + 1) : seqs * (n + 2)]
        joined = jnp.exp2(total[:, None, :] * rate[None]) * state + block[: seqs * n].reshape(seqs, n, chans)
        state = jnp.where(source > place if backward else source < place, joined, state)
    return state.reshape(seqs * n, chans)


def local(sizes, resid_in, out_grad, row_lengths, norm_gain, in_weight, conv_weight, conv_bias, xproj_weight, dt_weight,
          dt_bias, a_log, skip_gain, out_weight):
    bf, f32 = jnp.bfloat16, jnp.float32
    seqs = lax.axis_size("stream")
    parts = lax.axis_size("seq")
    own = conv_bias.shape[0]
    own_feats = norm_gain.shape[0]
    chans = own * parts
    rank_dim = dt_weight.shape[0]
    state_dim = a_log.shape[1]
    proj_dim = xproj_weight.shape[1]
    length, feats = resid_in.shape[1:]
    tokens = seqs * length

    gain = norm_gain.astype(f32)
    scaled = (in_weight.astype(f32) * gain[:, None]).astype(bf).reshape(own_feats, 2, parts, seqs, own)
    scaled = scaled.transpose(1, 3, 0, 2, 4).reshape(2, seqs * own_feats, chans)
    packed = jnp.concatenate(
        [xproj_weight, dt_weight.T, a_log, conv_weight.T, conv_bias[:, None], dt_bias[:, None], skip_gain[:, None]],
        axis=1)
    residual = resid_in[0].astype(f32)
    cotangent = out_grad[0]
    inv_rms = lax.rsqrt(jnp.mean(residual * residual, axis=-1, keepdims=True) + EPSILON)
    unit_own = residual * inv_rms
    slots = row_lengths.shape[1]
    arrays = [
        ("stream", jnp.pad(row_lengths, ((0, 7), (0, -slots % 128))), 1), ("stream", unit_own.astype(bf), 4),
        ("seq", jnp.pad(packed, ((0, 0), (0, -packed.shape[1] % 128))), 1)]
    if own_feats % 16:
        mine = lax.all_to_all(scaled, "stream", 1, 1, tiled=True)
        gate_own = mine[1]
        lengths, unit, packed, in_conv = link_gather([*arrays, ("seq", mine[0], 1)], sizes, 1)
    else:
        in_conv, gate_own, lengths, unit, packed = link_open(scaled[0], scaled[1], arrays, sizes, 1)
    lengths = lengths[::8, :slots]
    unit, gate_own, out_own, cot_own = lax.optimization_barrier((unit, gate_own, out_weight, cotangent))
    in_gate = lax.all_gather(gate_own, "seq", axis=0, tiled=True)
    out_full = lax.all_gather(out_own, "seq", axis=0, tiled=True)
    cot_all = lax.all_gather(cot_own, "stream", axis=0, tiled=True)
    xproj_full = packed[:, :proj_dim]
    dtw_cols = packed[:, proj_dim : proj_dim + rank_dim]
    at = proj_dim + rank_dim
    log_rates = packed[:, at : at + state_dim].astype(f32).T
    at += state_dim
    conv_taps = packed[:, at : at + CONV].astype(f32).T
    at += CONV
    conv_shift, dt_shift, skip_vec = (packed[:, at + i].astype(f32) for i in range(3))
    rate = -jnp.exp(log_rates) / LN2

    rim = CONV - 1
    first_pos = lax.axis_index("seq") * length
    doc_ids, start_flags, valid_mask = jax.vmap(
        lambda row: token_layout(row, first_pos - rim, length + 2 * rim))(lengths)
    own_ids = doc_ids[:, rim : rim + length]
    starts = start_flags[:, rim : rim + length].reshape(tokens, 1)
    valid = valid_mask[:, rim : rim + length].reshape(tokens, 1)
    matches = [(doc_ids[:, tap : tap + length] == own_ids).astype(f32)[:, :, None] for tap in range(CONV)]

    conv_in = jnp.dot(unit, in_conv, preferred_element_type=f32).reshape(seqs, length, chans)
    gate_in = jnp.dot(unit, in_gate, preferred_element_type=f32)
    earlier = passed_along(conv_in[:, length - rim :].astype(bf), "seq", 1).astype(f32)
    padded = jnp.concatenate([earlier, conv_in], axis=1)
    conv_out = conv_shift
    for tap in range(CONV):
        conv_out = conv_out + conv_taps[tap] * padded[:, tap : tap + length] * matches[tap]
    activated = jax.nn.silu(conv_out).astype(bf).reshape(tokens, chans)
    act_float = activated.astype(f32)
    projected = link_sum(
        lax.dot_general(xproj_full, activated, (((0,), (1,)), ((), ())), preferred_element_type=f32), sizes, 2)
    low_rank = projected[:rank_dim].astype(bf)
    write_in = projected[rank_dim : rank_dim + state_dim]
    readout = projected[rank_dim + state_dim :]
    dt_pre = lax.dot_general(low_rank, dtw_cols, (((0,), (1,)), ((), ())), preferred_element_type=f32) + dt_shift
    dt_step = jax.nn.softplus(dt_pre)
    dt_reset = jnp.where(starts > 0, RESET, dt_step)
    dt_act = dt_step * act_float
    write_slabs, read_slabs = slabs_of(write_in), slabs_of(readout)
    write_diag, read_diag = spread(write_in), spread(readout)

    step_sum = jnp.sum(dt_reset.reshape(seqs, length, chans), axis=1)
    ends = scan_end(fwd_end_body, dt_reset, dt_act, write_slabs, rate, seqs)
    start_state = carried(ends, step_sum, rate, False, sizes, 3)
    scanned, history = fwd_full(dt_reset, dt_act, write_slabs, read_diag, rate, start_state, seqs)
    ssm_out = scanned + skip_vec * act_float
    gate_act = jax.nn.silu(gate_in)
    gated = (ssm_out * gate_act * valid).astype(bf)
    product = jnp.dot(gated, out_full, preferred_element_type=f32).astype(bf)
    output = (residual + lax.psum_scatter(product, "stream", scatter_dimension=0, tiled=True).astype(f32)).astype(bf)

    d_gated = contract_cols(cot_all, out_full)
    g_out = lax.psum_scatter(contract_rows(gated, cot_all).astype(bf), "seq", scatter_dimension=0, tiled=True)
    d_masked = d_gated * valid
    d_ssm = d_masked * gate_act
    d_gate = (d_masked * ssm_out * silu_slope(gate_in)).astype(bf)
    g_in_gate = lax.psum_scatter(contract_rows(unit, d_gate).astype(bf), "seq", scatter_dimension=0, tiled=True)
    g_skip = jnp.sum(d_ssm * act_float, axis=0)
    back_ends = scan_end(bwd_end_body, dt_reset, d_ssm, read_slabs, rate, seqs)
    later_sum = carried(back_ends, step_sum, rate, True, sizes, 4)
    sum_write, sum_rate, g_log, d_write, d_read = bwd_full(
        dt_reset, dt_act, d_ssm, history, read_slabs, write_diag, rate, later_sum, seqs)
    per_step = jnp.where(dt_step > 1e-30, sum_rate * LN2 / jnp.maximum(dt_step, 1e-30), 0.0)
    d_step = per_step + act_float * sum_write
    d_pre = d_step * jax.nn.sigmoid(dt_pre)
    g_dt_bias = jnp.sum(d_pre, axis=0)
    d_pre_low = d_pre.astype(bf)
    g_dt = lax.dot_general(d_pre_low, low_rank, (((0,), (1,)), ((), ())), preferred_element_type=f32)
    d_low = lax.dot_general(dtw_cols, d_pre_low, (((0,), (1,)), ((), ())), preferred_element_type=f32)
    d_proj = link_sum(jnp.concatenate([d_low, d_write, d_read], axis=0), sizes, 5).astype(bf)
    g_xproj = lax.dot_general(activated, d_proj, (((0,), (1,)), ((), ())), preferred_element_type=f32)
    d_act = dt_step * sum_write + skip_vec * d_ssm + lax.dot_general(
        d_proj, xproj_full, (((0,), (1,)), ((), ())), preferred_element_type=f32)
    d_conv = d_act.reshape(seqs, length, chans) * silu_slope(conv_out)
    g_conv_bias = jnp.sum(d_conv, axis=(0, 1))
    g_conv = jnp.stack(
        [jnp.sum(d_conv * padded[:, tap : tap + length] * matches[tap], axis=(0, 1)) for tap in range(CONV)], axis=1)
    later = passed_along(d_conv[:, :rim].astype(bf), "seq", -1).astype(f32)
    d_ext = jnp.concatenate([d_conv, later], axis=1)
    d_conv_in = jnp.zeros_like(d_conv)
    for tap in range(CONV):
        offset = rim - tap
        match_back = (doc_ids[:, rim + offset : rim + offset + length] == own_ids).astype(f32)[:, :, None]
        d_conv_in = d_conv_in + conv_taps[tap] * d_ext[:, offset : offset + length] * match_back
    d_conv_in = d_conv_in.astype(bf).reshape(tokens, chans)
    g_in_conv = contract_rows(unit, d_conv_in).astype(bf)
    d_unit = (contract_cols(d_conv_in, in_conv) + contract_cols(d_gate, in_gate)).astype(bf)
    def in_rows(block):
        shared = lax.all_to_all(block, "stream", 0, 0, tiled=True).reshape(seqs, own_feats, parts, own)
        return shared.transpose(1, 2, 0, 3).reshape(own_feats, parts * seqs * own)

    def padded_small(columns):
        joined = jnp.concatenate(columns, axis=1)
        return jnp.pad(joined, ((0, 0), (0, -joined.shape[1] % 128))).astype(bf)

    small = padded_small([g_xproj, g_dt, g_log.T * LN2, g_dt_bias[:, None], g_skip[:, None]])
    small = lax.psum_scatter(small, "seq", scatter_dimension=0, tiled=True).astype(f32)
    taps = padded_small([g_conv, g_conv_bias[:, None]])
    d_unit, g_in_gate = lax.optimization_barrier((d_unit, in_rows(g_in_gate)))
    g_in_conv, taps, d_unit = link_reduce(
        [("seq", g_in_conv, 2, 0 if own_feats % 16 else own), ("seq", taps, 1, 0), ("stream", d_unit, 4, 0)], sizes, 6)
    taps = taps.astype(f32)
    d_unit = d_unit.astype(f32)
    in_grad = cotangent.astype(f32) + inv_rms * (d_unit - unit_own * jnp.mean(d_unit * unit_own, axis=-1, keepdims=True))

    g_in_conv = in_rows(g_in_conv) if own_feats % 16 else g_in_conv
    g_unit = jnp.concatenate([g_in_conv, g_in_gate], axis=1).astype(f32)
    at = proj_dim + rank_dim
    return (
        output[None],
        in_grad.astype(bf)[None],
        jnp.sum(g_unit * in_weight.astype(f32), axis=1),
        g_unit * gain[:, None],
        taps[:, :CONV].T,
        taps[:, CONV],
        small[:, :proj_dim],
        small[:, proj_dim:at].T,
        small[:, at + state_dim],
        small[:, at : at + state_dim],
        small[:, at + state_dim + 1],
        g_out.astype(f32),
    )


def lines_of(mesh):
    devices = mesh.devices
    places = [getattr(device, "coords", None) for device in devices[:, 0]]
    seq = len(places)
    plane = 1
    if all(place is not None for place in places):
        plane = len({tuple(place)[1] for place in places})
    if seq % plane:
        plane = 1
    return {"seq": (seq, plane), "stream": (devices.shape[1], 1 if devices.shape[1] % 2 else 2)}


def solution(mesh):
    in_specs = (
        P("stream", "seq", None),
        P("stream", "seq", None),
        P("stream", None),
        P(("seq", "stream")),
        P(("seq", "stream"), None),
        P(None, ("seq", "stream")),
        P(("seq", "stream")),
        P(("seq", "stream"), None),
        P(None, ("seq", "stream")),
        P(("seq", "stream")),
        P(("seq", "stream"), None),
        P(("seq", "stream")),
        P(("seq", "stream"), None),
    )
    out_specs = (
        P("stream", "seq", None),
        P("stream", "seq", None),
        P(("seq", "stream")),
        P(("seq", "stream"), None),
        P(None, ("seq", "stream")),
        P(("seq", "stream")),
        P(("seq", "stream"), None),
        P(None, ("seq", "stream")),
        P(("seq", "stream")),
        P(("seq", "stream"), None),
        P(("seq", "stream")),
        P(("seq", "stream"), None),
    )
    return jax.shard_map(functools.partial(local, lines_of(mesh)), mesh=mesh, in_specs=in_specs, out_specs=out_specs, check_vma=False)
```

```python
import functools

import jax
import jax.numpy as jnp
from jax import lax
from jax.experimental import pallas as pl
from jax.experimental.pallas import tpu as pltpu
from jax.sharding import PartitionSpec as P

CONV = 4
EPSILON = 1e-05
RESET = 1e30
GROUP = 16
LN2 = 0.6931471805599453
NT = (((1,), (1,)), ((), ()))
VMEM_LIMIT = 56 << 20
LINK_COST = 20_000_000_000


def across(slab, place, width):
    return jnp.concatenate([jnp.broadcast_to(slab[:, place : place + 1], (slab.shape[0], 128))] * (width // 128), axis=1)


def decays(dte_ref, rate_ref, at, buf, power_buf=None):
    n = rate_ref.shape[0]
    for place in range(GROUP):
        power = dte_ref[pl.ds(at * GROUP + place, 1), :] * rate_ref[...]
        buf[pl.ds(place * n, n), :] = jnp.exp2(power)
        if power_buf is not None:
            power_buf[pl.ds(place * n, n), :] = power.astype(jnp.bfloat16)


def fwd_end_body(dte_ref, dtx_ref, slab_ref, rate_ref, end_ref, even_ref, odd_ref):
    n, width = rate_ref.shape
    groups = dte_ref.shape[0] // GROUP

    def walk(at, state, decay_ref):
        slab = slab_ref[pl.ds(at * n, n), :]
        for place in range(GROUP):
            write = across(slab, place, width)
            state = decay_ref[pl.ds(place * n, n), :] * state + dtx_ref[pl.ds(at * GROUP + place, 1), :] * write
        return state

    def pair(step, state):
        decays(dte_ref, rate_ref, 2 * step + 1, odd_ref)
        state = walk(2 * step, state, even_ref)
        decays(dte_ref, rate_ref, jnp.minimum(2 * step + 2, groups - 1), even_ref)
        return walk(2 * step + 1, state, odd_ref)

    decays(dte_ref, rate_ref, 0, even_ref)
    end_ref[...] = lax.fori_loop(0, groups // 2, pair, jnp.zeros_like(end_ref))


def bwd_end_body(dte_ref, grad_ref, slab_ref, rate_ref, end_ref, even_ref, odd_ref):
    n, width = rate_ref.shape
    groups = dte_ref.shape[0] // GROUP

    def walk(at, state, decay_ref):
        slab = slab_ref[pl.ds(at * n, n), :]
        for place in reversed(range(GROUP)):
            read = across(slab, place, width)
            state = decay_ref[pl.ds(place * n, n), :] * (state + grad_ref[pl.ds(at * GROUP + place, 1), :] * read)
        return state

    def pair(step, state):
        at = groups - 1 - 2 * step
        decays(dte_ref, rate_ref, at - 1, odd_ref)
        state = walk(at, state, even_ref)
        decays(dte_ref, rate_ref, jnp.maximum(at - 2, 0), even_ref)
        return walk(at - 1, state, odd_ref)

    decays(dte_ref, rate_ref, groups - 1, even_ref)
    end_ref[...] = lax.fori_loop(0, groups // 2, pair, jnp.zeros_like(end_ref))


def scan_end(body, dte, other, slabs, rate, seqs, width=512):
    tokens, chans = dte.shape
    length = tokens // seqs
    n = rate.shape[0]
    width = min(width, chans)
    work = tokens * chans * n
    return pl.pallas_call(
        body,
        grid=(seqs, chans // width),
        in_specs=[
            pl.BlockSpec((length, width), lambda s, c: (s, c)),
            pl.BlockSpec((length, width), lambda s, c: (s, c)),
            pl.BlockSpec((length // GROUP * n, GROUP), lambda s, c: (s, 0)),
            pl.BlockSpec((n, width), lambda s, c: (0, c)),
        ],
        out_specs=pl.BlockSpec((n, width), lambda s, c: (s, c)),
        out_shape=jax.ShapeDtypeStruct((seqs * n, chans), jnp.float32),
        scratch_shapes=[pltpu.VMEM((GROUP * n, width), jnp.float32)] * 2,
        compiler_params=pltpu.CompilerParams(vmem_limit_bytes=VMEM_LIMIT),
        cost_estimate=pl.CostEstimate(flops=1000 * work, transcendentals=work, bytes_accessed=8 * tokens * chans),
        name=body.__name__[:7],
    )(dte, other, slabs, rate)


def fwd_full_body(dte_ref, dtx_ref, slab_ref, read_ref, rate_ref, start_ref, y_ref, hist_ref, h_ref, even_ref, odd_ref):
    block = dte_ref.shape[0]
    n, width = rate_ref.shape
    span = GROUP * n
    rate = rate_ref[...]

    @pl.when(pl.program_id(2) == 0)
    def _():
        h_ref[...] = start_ref[...]

    first = h_ref[...]
    hist_ref[pl.ds(0, n), :] = first.astype(jnp.bfloat16)

    def rows_out(at, buf):
        y_ref[pl.ds(at * GROUP, GROUP), :] = jnp.dot(
            read_ref[pl.ds(at * GROUP, GROUP), :], buf[...], preferred_element_type=jnp.float32)

    def group(at, state, buf):
        slab = slab_ref[pl.ds(at * n, n), :]
        for place in range(GROUP):
            t = at * GROUP + place
            write = across(slab, place, width)
            state = jnp.exp2(dte_ref[pl.ds(t, 1), :] * rate) * state + dtx_ref[pl.ds(t, 1), :] * write
            kept = state.astype(jnp.bfloat16)
            hist_ref[pl.ds((t + 1) * n, n), :] = kept
            buf[pl.ds(place * n, n), :] = kept
        return state

    def pair(step, state):
        at = 2 * step
        rows_out(jnp.maximum(at - 1, 0), odd_ref)
        state = group(at, state, even_ref)
        rows_out(at, even_ref)
        return group(at + 1, state, odd_ref)

    h_ref[...] = lax.fori_loop(0, block // GROUP // 2, pair, first)
    rows_out(block // GROUP - 1, odd_ref)


def fwd_full(dte, dtx, slabs, read, rate, start, seqs, width=512, block=256):
    tokens, chans = dte.shape
    n = rate.shape[0]
    width = min(width, chans)
    blocks = tokens // seqs // block
    work = tokens * chans * n
    here = lambda c, s, t: (s * blocks + t, c)
    rows = lambda c, s, t: (s * blocks + t, 0)
    return pl.pallas_call(
        fwd_full_body,
        grid=(chans // width, seqs, blocks),
        in_specs=[
            pl.BlockSpec((block, width), here),
            pl.BlockSpec((block, width), here),
            pl.BlockSpec((block // GROUP * n, GROUP), rows),
            pl.BlockSpec((block, read.shape[1]), rows),
            pl.BlockSpec((n, width), lambda c, s, t: (0, c)),
            pl.BlockSpec((n, width), lambda c, s, t: (s, c)),
        ],
        out_specs=[pl.BlockSpec((block, width), here), pl.BlockSpec(((block + 1) * n, width), here)],
        out_shape=[
            jax.ShapeDtypeStruct((tokens, chans), jnp.float32),
            jax.ShapeDtypeStruct((seqs * blocks * (block + 1) * n, chans), jnp.bfloat16),
        ],
        scratch_shapes=[pltpu.VMEM((n, width), jnp.float32)] + [pltpu.VMEM((GROUP * n, width), jnp.bfloat16)] * 2,
        compiler_params=pltpu.CompilerParams(vmem_limit_bytes=VMEM_LIMIT),
        cost_estimate=pl.CostEstimate(flops=1400 * work, transcendentals=work, bytes_accessed=2 * work),
        name="fwd_full",
    )(dte, dtx, slabs, read, rate, start)


def bwd_full_body(dte_ref, dtx_ref, grad_ref, hist_ref, slab_ref, write_ref, ones_ref, rate_ref, start_ref,
                  s1_ref, s2_ref, grate_ref, dw_ref, dr_ref, g_ref, *scratch):
    block = dte_ref.shape[0]
    n, width = rate_ref.shape
    groups = block // GROUP
    bf, f32 = jnp.bfloat16, jnp.float32
    even, odd = scratch[:5], scratch[5:]
    unit = jnp.ones((GROUP, 128), bf)

    @pl.when(pl.program_id(2) == 0)
    def _():
        g_ref[...] = start_ref[...]

    @pl.when((pl.program_id(2) == 0) & (pl.program_id(1) == 0))
    def _():
        grate_ref[...] = jnp.zeros_like(grate_ref)

    def sums_out(at, bufs):
        _, _, adj_ref, rated_ref, dw_part = bufs
        rows = pl.ds(at * GROUP, GROUP)
        s1_ref[rows, :] = jnp.dot(write_ref[rows, :], adj_ref[...], preferred_element_type=f32)
        sums = jnp.dot(ones_ref[...], rated_ref[...], preferred_element_type=f32)
        s2_ref[rows, :] = sums[:GROUP]
        dw_ref[pl.ds(at, 1), :] = lax.dot_general(unit, dw_part[...], NT, preferred_element_type=f32)[:1]
        reads = lax.dot_general(
            grad_ref[rows, :].astype(bf), hist_ref[pl.ds(n + at * GROUP * n, GROUP * n), :], NT,
            preferred_element_type=f32)
        own = lax.broadcasted_iota(jnp.int32, reads.shape, 1) // n == lax.broadcasted_iota(jnp.int32, reads.shape, 0)
        dr_ref[pl.ds(at, 1), :] = jnp.sum(jnp.where(own, reads, 0.0), axis=0, keepdims=True)
        return sums[GROUP:]

    def strips(values):
        parts = [values[:, k * 128 : (k + 1) * 128] for k in range(width // 128)]
        while len(parts) > 1:
            parts = [a + b for a, b in zip(parts[::2], parts[1::2])] + parts[len(parts) // 2 * 2 :]
        return parts[0]

    def walk(at, state, bufs):
        decay_ref, power_ref, adj_ref, rated_ref, dw_part = bufs
        slab = slab_ref[pl.ds(at * n, n), :]
        for place in reversed(range(GROUP)):
            t = at * GROUP + place
            here = pl.ds(place * n, n)
            read = across(slab, place, width)
            adjoint = state + grad_ref[pl.ds(t, 1), :] * read
            power = dte_ref[pl.ds(t, 1), :] * rate_ref[...]
            state = jnp.exp2(power) * adjoint
            low = adjoint.astype(bf)
            adj_ref[here, :] = low
            rated_ref[here, :] = state.astype(bf) * hist_ref[pl.ds(t * n, n), :] * power.astype(bf)
            dw_part[here, :] = strips(adjoint * dtx_ref[pl.ds(t, 1), :]).astype(bf)
        return state

    def pair(step, state):
        at = groups - 1 - 2 * step
        old = sums_out(jnp.minimum(at + 1, groups - 1), odd)
        state = walk(at, state, even)
        grate_ref[...] += jnp.where(step > 0, old, 0.0) + sums_out(at, even)
        return walk(at - 1, state, odd)
    g_ref[...] = lax.fori_loop(0, groups // 2, pair, g_ref[...])
    grate_ref[...] += sums_out(0, odd)


def bwd_full(dte, dtx, grad, hist, slabs, write, rate, start, seqs, width=512, block=256):
    tokens, chans = dte.shape
    n = rate.shape[0]
    width = min(width, chans)
    strips = chans // width
    blocks = tokens // seqs // block
    span = GROUP * n
    work = tokens * chans * n
    column = jnp.arange(span)
    ones = jnp.concatenate(
        [(column // n)[None, :] == jnp.arange(GROUP)[:, None], (column % n)[None, :] == jnp.arange(n)[:, None]]
    ).astype(jnp.bfloat16)
    here = lambda c, s, t: (s * blocks + blocks - 1 - t, c)
    rows = lambda c, s, t: (s * blocks + blocks - 1 - t, 0)
    strip = lambda c, s, t: (c * seqs * blocks + s * blocks + blocks - 1 - t, 0)
    f32 = jnp.float32
    s1, s2, grate, dw, dr = pl.pallas_call(
        bwd_full_body,
        grid=(strips, seqs, blocks),
        in_specs=[
            pl.BlockSpec((block, width), here),
            pl.BlockSpec((block, width), here),
            pl.BlockSpec((block, width), here),
            pl.BlockSpec(((block + 1) * n, width), here),
            pl.BlockSpec((block // GROUP * n, GROUP), rows),
            pl.BlockSpec((block, span), rows),
            pl.BlockSpec(ones.shape, lambda c, s, t: (0, 0)),
            pl.BlockSpec((n, width), lambda c, s, t: (0, c)),
            pl.BlockSpec((n, width), lambda c, s, t: (s, c)),
        ],
        out_specs=[
            pl.BlockSpec((block, width), here),
            pl.BlockSpec((block, width), here),
            pl.BlockSpec((n, width), lambda c, s, t: (0, c)),
            pl.BlockSpec((block // GROUP, span), strip),
            pl.BlockSpec((block // GROUP, span), strip),
        ],
        out_shape=[
            jax.ShapeDtypeStruct((tokens, chans), f32),
            jax.ShapeDtypeStruct((tokens, chans), f32),
            jax.ShapeDtypeStruct((n, chans), f32),
            jax.ShapeDtypeStruct((strips * tokens // GROUP, span), f32),
            jax.ShapeDtypeStruct((strips * tokens // GROUP, span), f32),
        ],
        scratch_shapes=[
            pltpu.VMEM((n, width), f32),
            *[
                pltpu.VMEM((span, width), f32),
                *[pltpu.VMEM((span, width), jnp.bfloat16)] * 3,
                pltpu.VMEM((span, 128), jnp.bfloat16),
            ] * 2,
        ],
        compiler_params=pltpu.CompilerParams(vmem_limit_bytes=VMEM_LIMIT),
        cost_estimate=pl.CostEstimate(flops=3200 * work, transcendentals=work, bytes_accessed=2 * work),
        name="bwd_full",
    )(dte, dtx, grad, hist, slabs, write, ones, rate, start)
    both = jnp.stack([part.reshape(strips, tokens // GROUP, span).sum(0) for part in (dw, dr)])
    both = both.reshape(2, tokens // GROUP, GROUP, n).transpose(0, 3, 1, 2).reshape(2, n, tokens)
    return s1, s2, grate, both[0], both[1]


def slabs_of(values):
    n, tokens = values.shape
    return values.reshape(n, tokens // GROUP, GROUP).transpose(1, 0, 2).reshape(tokens // GROUP * n, GROUP)


def spread(values):
    n, tokens = values.shape
    own = jnp.arange(tokens)[:, None] % GROUP == jnp.arange(GROUP)[None, :]
    return jnp.where(own[:, :, None], values.T[:, None, :], 0).reshape(tokens, GROUP * n).astype(jnp.bfloat16)


MESH = pl.DeviceIdType.MESH


class Grid:
    def __init__(self, axis, size, inner):
        self.axis, self.inner, self.outer = axis, inner, size // inner
        me = lax.axis_index(axis)
        self.row, self.col = me // inner, me % inner

    def device(self, row, col):
        return {self.axis: row * self.inner + col}

    def neighbours(self):
        row, col = self.row, self.col
        found = []
        if self.outer > 1:
            found += [(row > 0, self.device(row - 1, col)), (row < self.outer - 1, self.device(row + 1, col))]
        if self.inner > 1:
            found += [(col > 0, self.device(row, col - 1)), (col < self.inner - 1, self.device(row, col + 1))]
        return found

    def everyone(self):
        size = self.inner * self.outer
        me = self.row * self.inner + self.col
        return [(me >= 0, {self.axis: (me + step) % size}) for step in range(1, size)]


def greet(grids, all_of=()):
    barrier = pltpu.get_barrier_semaphore()
    count = 0
    for grid in grids:
        for there, device in grid.everyone() if grid.axis in all_of else grid.neighbours():

            @pl.when(there)
            def _(device=device):
                pl.semaphore_signal(barrier, inc=1, device_id=device, device_id_type=MESH)

            count = count + there.astype(jnp.int32)
    pl.semaphore_wait(barrier, count)


def gather_steps(grid, whole_ref, out_ref, send_sem, recv_sem, own, waits, chunk, chunks, across_too=True, ways=(True, True)):
    rows = whole_ref.shape[0]
    part = rows // chunks
    src_ref = whole_ref.at[pl.ds(chunk * part, part)]
    outer, inner = grid.outer, grid.inner if across_too else 1
    row, col = grid.row, grid.col

    def number(r, c):
        return r * inner + c if across_too else r

    def place(r, c):
        return pl.ds(pl.multiple_of(number(r, c) * rows + chunk * part, part), part)

    def send(there, way, r, c, device, source):
        copy = pltpu.make_async_remote_copy(
            src_ref=source, dst_ref=out_ref.at[place(r, c)], send_sem=send_sem.at[way, number(r, c)],
            recv_sem=recv_sem.at[number(r, c)], device_id=device, device_id_type=MESH)

        @pl.when(there)
        def _():
            copy.start()

        waits.append((there, copy))

    def across(there, r, c, source):
        if inner > 1:
            send(there & (c >= col) & (col > 0), 2, r, c, grid.device(row, col - 1), source)
            send(there & (c <= col) & (col < inner - 1), 3, r, c, grid.device(row, col + 1), source)

    def along(there, r, source):
        if outer > 1:
            if ways[0]:
                send(there & (r >= row) & (row > 0), 0, r, col, grid.device(row - 1, col), source)
            if ways[1]:
                send(there & (r <= row) & (row < outer - 1), 1, r, col, grid.device(row + 1, col), source)

    def arrive(there, r, c):
        copy = pltpu.make_async_remote_copy(
            src_ref=src_ref, dst_ref=out_ref.at[place(r, c)], send_sem=send_sem.at[0, 0],
            recv_sem=recv_sem.at[number(r, c)], device_id=grid.device(row, col), device_id_type=MESH)

        @pl.when(there)
        def _():
            copy.wait_recv()

    always = row >= 0
    along(always, row, src_ref)
    across(always, row, col, src_ref)
    own_sem, own_buf = own
    fetch = pltpu.make_async_copy(src_ref, own_buf, own_sem.at[0])
    fetch.start()
    for _ in range(chunk + 1):
        yield
    fetch.wait()
    keep = pltpu.make_async_copy(own_buf, out_ref.at[place(row, col)], own_sem.at[1])
    keep.start()
    waits.append((None, keep))

    def rows_at(distance):
        return [row - distance] * ways[1] + [row + distance] * ways[0]

    for distance in range(1, outer):
        for r in rows_at(distance):
            there = (r >= 0) & (r < outer)
            arrive(there, r, col)
            along(there, r, out_ref.at[place(r, col)])
            across(there, r, col, out_ref.at[place(r, col)])
        yield
    for step in range(1, inner):
        for distance in range(outer):
            for r in rows_at(distance) if distance else (row,):
                for c in (col - step, col + step):
                    there = (r >= 0) & (r < outer) & (c >= 0) & (c < inner)
                    arrive(there, r, c)
                    if step < inner - 1:
                        across(there, r, c, out_ref.at[place(r, c)])
            yield


def finish(waits):
    for there, copy in waits:
        if there is None:
            copy.wait()
        else:

            @pl.when(there)
            def _(copy=copy):
                if copy.is_remote:
                    copy.wait_send()
                else:
                    copy.wait()


def gather_scratch(size, array, chunks):
    dma = pltpu.SemaphoreType.DMA
    own = pltpu.VMEM((array.shape[0] // chunks, *array.shape[1:]), array.dtype)
    return [dma((4, size)), dma((size,)), dma((2,)), own] * chunks


def in_turn(runs):
    runs = list(runs)
    while runs:
        left = []
        for run in runs:
            if next(run, run) is not run:
                left.append(run)
        runs = left


def link_gather(arrays, sizes, collective_id, ways=(True, True)):
    count = len(arrays)
    axes = sorted({entry[0] for entry in arrays})

    def kernel(*refs):
        sources, outs, sems = refs[:count], refs[count : 2 * count], refs[2 * count :]
        grids = {axis: Grid(axis, *sizes[axis]) for axis in axes}
        greet([grids[axis] for axis in axes])
        waits = []
        runs = []
        for i, (axis, _, chunks) in enumerate(arrays):
            for chunk in range(chunks):
                runs.append(gather_steps(
                    grids[axis], sources[i], outs[i], sems[0], sems[1], sems[2:4], waits, chunk, chunks, ways=ways))
                sems = sems[4:]
        in_turn(runs)
        finish(waits)

    sems = []
    for axis, a, chunks in arrays:
        sems += gather_scratch(sizes[axis][0], a, chunks)
    return pl.pallas_call(
        kernel,
        in_specs=[pl.BlockSpec(memory_space=pl.ANY)] * count,
        out_specs=[pl.BlockSpec(memory_space=pl.ANY)] * count,
        out_shape=[
            jax.ShapeDtypeStruct((sizes[axis][0] * a.shape[0], *a.shape[1:]), a.dtype) for axis, a, _ in arrays],
        scratch_shapes=sems,
        compiler_params=pltpu.CompilerParams(
            collective_id=collective_id, has_side_effects=True, vmem_limit_bytes=VMEM_LIMIT),
        cost_estimate=pl.CostEstimate(flops=LINK_COST, transcendentals=0, bytes_accessed=0),
        name="link_gather",
    )(*[a for _, a, _ in arrays])


def reduce_steps(grid, src_ref, out_ref, scratch, waits, chunks, share):
    acc, inner_buf, outer_buf, load_sem, inner_send, inner_recv, outer_send, outer_recv, out_sem = scratch[:9]
    outer, inner = grid.outer, grid.inner
    row, col = grid.row, grid.col
    rows = acc.shape[0] // (outer * inner)
    part = rows // chunks
    piece = min(part, 64)

    def start_of(chunk, r, c):
        return pl.multiple_of((r * inner + c) * rows + chunk * part, part)

    def line(me, size, device, block, buf, send, recv):
        def from_low(target):
            return target if size > 2 else 0

        def from_high(target, owner):
            return jnp.where(target == owner, size, target) if size > 2 else 0

        def hop(there, target, onward, slot):
            copy = pltpu.make_async_remote_copy(
                src_ref=acc.at[pl.ds(block(target), part)], dst_ref=buf.at[slot], send_sem=send.at[target],
                recv_sem=recv.at[slot], device_id=device(onward), device_id_type=MESH)

            @pl.when(there)
            def _():
                copy.start()

            waits.append((there, copy))

        def up(there, target):
            hop(there & (target > me), target, me + 1, from_low(target))

        def down(there, target):
            hop(there & (target < me), target, me - 1, from_high(target, me - 1))

        def arrive(there, target, slot):
            at = block(target)
            copy = pltpu.make_async_remote_copy(
                src_ref=acc.at[pl.ds(at, part)], dst_ref=buf.at[slot], send_sem=send.at[target],
                recv_sem=recv.at[slot], device_id=device(me), device_id_type=MESH)

            @pl.when(there)
            def _():
                copy.wait_recv()

                @pl.loop(0, part // piece)
                def _(k):
                    here = pl.ds(pl.multiple_of(at + k * piece, piece), piece)
                    there_rows = pl.ds(pl.multiple_of(k * piece, piece), piece)
                    total = acc[here, :].astype(jnp.float32) + buf[slot, there_rows, :].astype(jnp.float32)
                    acc[here, :] = total.astype(acc.dtype)

        def begin(target):
            up(me == 0, target)
            down(me == size - 1, target)

        def go_on(target):
            arrive((me > 0) & (target >= me), target, from_low(target))
            arrive((me < size - 1) & (target <= me), target, from_high(target, me))
            if size > 2:
                up((me > 0) & (me < size - 1), target)
                down((me > 0) & (me < size - 1), target)

        return begin, go_on

    order = sorted(range(outer), key=lambda k: -abs(2 * k - outer + 1))
    pieces = [(chunk, r) for chunk in range(chunks) for r in order]
    loads = {}
    for chunk, r in pieces:
        loads[chunk, r] = [
            pltpu.make_async_copy(
                src_ref.at[pl.ds(start_of(chunk, r, c), part)], acc.at[pl.ds(start_of(chunk, r, c), part)],
                load_sem.at[chunk, r * inner + c])
            for c in range(inner)]
        for load in loads[chunk, r]:
            load.start()

    def inner_line(chunk, r):
        return line(
            col, inner, lambda c: grid.device(row, c), lambda t: start_of(chunk, r, t), inner_buf.at[chunk, r],
            inner_send.at[chunk, r], inner_recv.at[chunk, r])

    def outer_line(chunk):
        return line(
            row, outer, lambda r: grid.device(r, col), lambda t: start_of(chunk, t, col), outer_buf.at[chunk],
            outer_send.at[chunk], outer_recv.at[chunk])

    def inner_start(k):
        if k < len(pieces):
            for load in loads[pieces[k]]:
                load.wait()
            if inner > 1:
                for c in range(inner):
                    inner_line(*pieces[k])[0](c)

    def outer_rest(k):
        if 0 <= k < len(pieces):
            chunk, r = pieces[k]
            if outer > 1:
                outer_line(chunk)[1](r)
            if r == order[-1]:
                give(chunk)

    def give(chunk):
        first = start_of(chunk, row, col)
        if share is None:
            last = pltpu.make_async_copy(
                acc.at[pl.ds(first, part)], out_ref.at[pl.ds(chunk * part, part)], out_sem.at[chunk])
            last.start()
            waits.append((None, last))
            return
        other, strip, send_sem, recv_sem = share
        count, me = other.outer * other.inner, other.row * other.inner + other.col
        take = rows // count
        for mate in range(chunk * part // take, (chunk + 1) * part // take):
            for k in range(acc.shape[1] // strip):
                source = acc.at[
                    pl.ds(pl.multiple_of((row * inner + col) * rows + mate * take, take), take),
                    pl.ds(k * strip, strip)]
                target = out_ref.at[:, pl.ds(pl.multiple_of((k * count + me) * strip, strip), strip)]
                own = pltpu.make_async_copy(source, target, send_sem.at[mate, k])
                sent = pltpu.make_async_remote_copy(
                    src_ref=source, dst_ref=target, send_sem=send_sem.at[mate, k], recv_sem=recv_sem.at[me, k],
                    device_id={other.axis: mate}, device_id_type=MESH)

                @pl.when(mate == me)
                def _(own=own):
                    own.start()

                @pl.when(mate != me)
                def _(sent=sent):
                    sent.start()

                waits.append((mate != me, sent))
                waits.append((mate == me, own))

    window = 2
    for k in range(window):
        inner_start(k)
    yield
    for k in range(len(pieces)):
        inner_start(k + window)
        chunk, r = pieces[k]
        if inner > 1:
            for c in range(inner):
                inner_line(chunk, r)[1](c)
        if outer > 1:
            outer_line(chunk)[0](r)
        yield
        outer_rest(k - window)
        yield
    for k in range(len(pieces) - window, len(pieces)):
        outer_rest(k)
        yield
    if share is not None:
        other, strip, send_sem, recv_sem = share
        count, me = other.outer * other.inner, other.row * other.inner + other.col
        take = rows // count
        for mate in range(count):
            for k in range(acc.shape[1] // strip):
                copy = pltpu.make_async_remote_copy(
                    src_ref=acc.at[pl.ds(0, take), pl.ds(k * strip, strip)],
                    dst_ref=out_ref.at[:, pl.ds((k * count + mate) * strip, strip)], send_sem=send_sem.at[mate, k],
                    recv_sem=recv_sem.at[mate, k], device_id={other.axis: me}, device_id_type=MESH)

                @pl.when(mate != me)
                def _(copy=copy):
                    copy.wait_recv()


def link_reduce(arrays, sizes, collective_id):
    count = len(arrays)

    def kernel(*refs):
        sources, outs, scratch = refs[:count], refs[count : 2 * count], refs[2 * count :]
        grids = {axis: Grid(axis, *sizes[axis]) for axis in ("seq", "stream")}
        greet(list(grids.values()), ("stream",))
        waits = []
        runs = []
        for i, (axis, _, chunks, strip) in enumerate(arrays):
            share = (grids["stream"], strip, scratch[9], scratch[10]) if strip else None
            runs.append(reduce_steps(grids[axis], sources[i], outs[i], scratch[:9], waits, chunks, share))
            scratch = scratch[11 if strip else 9 :]
        in_turn(runs)
        finish(waits)

    scratch, shapes = [], []
    for axis, a, chunks, strip in arrays:
        size, inner = sizes[axis]
        outer = size // inner
        part = a.shape[0] // size // chunks
        slots = [n + 1 if n > 2 else 1 for n in (inner, outer)]
        dma = pltpu.SemaphoreType.DMA
        scratch += [
            pltpu.VMEM(a.shape, a.dtype),
            pltpu.VMEM((chunks, outer, slots[0], part, a.shape[1]), a.dtype),
            pltpu.VMEM((chunks, slots[1], part, a.shape[1]), a.dtype),
            dma((chunks, size)), dma((chunks, outer, inner)), dma((chunks, outer, slots[0])), dma((chunks, outer)),
            dma((chunks, slots[1])), dma((chunks,))]
        if strip:
            mates = sizes["stream"][0]
            shapes.append(jax.ShapeDtypeStruct((a.shape[0] // size // mates, a.shape[1] * mates), a.dtype))
            scratch += [dma((mates, a.shape[1] // strip))] * 2
        else:
            shapes.append(jax.ShapeDtypeStruct((a.shape[0] // size, a.shape[1]), a.dtype))
    return pl.pallas_call(
        kernel,
        in_specs=[pl.BlockSpec(memory_space=pl.ANY)] * count,
        out_specs=[pl.BlockSpec(memory_space=pl.ANY)] * count,
        out_shape=shapes,
        scratch_shapes=scratch,
        compiler_params=pltpu.CompilerParams(
            collective_id=collective_id, has_side_effects=True, vmem_limit_bytes=VMEM_LIMIT),
        cost_estimate=pl.CostEstimate(flops=4 * LINK_COST, transcendentals=0, bytes_accessed=0),
        name="link_reduce",
    )(*[entry[1] for entry in arrays])


def link_sum(partial, sizes, collective_id):
    rows, width = partial.shape
    size, inner = sizes["stream"]
    outer = size // inner
    assert inner == 2
    half = rows // 2
    bf, f32 = jnp.bfloat16, jnp.float32
    dma = pltpu.SemaphoreType.DMA

    def kernel(own_ref, out_ref, mate_buf, pair_ref, terms_ref, total_ref, send, recv, line_send, line_recv, own_sem, own_buf):
        grid = Grid("stream", size, inner)
        row, col = grid.row, grid.col
        greet([grid])
        mate = grid.device(row, 1 - col)
        mine = pl.ds(pl.multiple_of(col * half, half), half)
        swap = pltpu.make_async_remote_copy(
            src_ref=own_ref, dst_ref=mate_buf, send_sem=send.at[0], recv_sem=recv.at[0], device_id=mate,
            device_id_type=MESH)
        swap.start()
        swap.wait_recv()
        pair_ref[...] = (own_ref[mine, :].astype(f32) + mate_buf[mine, :].astype(f32)).astype(bf)
        waits = []
        line = Grid("stream", size, inner)
        in_turn([gather_steps(
            line, pair_ref, terms_ref, line_send, line_recv, (own_sem, own_buf), waits, 0, 1, across_too=False)])
        finish(waits)
        total = terms_ref[pl.ds(0, half), :].astype(f32)
        for r in range(1, outer):
            total = total + terms_ref[pl.ds(r * half, half), :].astype(f32)
        total_ref[...] = total
        out_ref[mine, :] = total
        swap_back = pltpu.make_async_remote_copy(
            src_ref=total_ref, dst_ref=out_ref.at[mine], send_sem=send.at[1], recv_sem=recv.at[1], device_id=mate,
            device_id_type=MESH)
        swap_back.start()
        theirs = pltpu.make_async_remote_copy(
            src_ref=total_ref, dst_ref=out_ref.at[pl.ds(pl.multiple_of((1 - col) * half, half), half)],
            send_sem=send.at[1], recv_sem=recv.at[1], device_id=mate, device_id_type=MESH)
        theirs.wait_recv()
        swap.wait_send()
        swap_back.wait_send()

    return pl.pallas_call(
        kernel,
        in_specs=[pl.BlockSpec(memory_space=pltpu.VMEM)],
        out_specs=pl.BlockSpec(memory_space=pltpu.VMEM),
        out_shape=jax.ShapeDtypeStruct((rows, width), f32),
        scratch_shapes=[
            pltpu.VMEM((rows, width), bf), pltpu.VMEM((half, width), bf), pltpu.VMEM((outer * half, width), bf),
            pltpu.VMEM((half, width), f32), dma((2,)), dma((2,)), dma((4, outer)), dma((outer,)), dma((2,)),
            pltpu.VMEM((half, width), bf)],
        compiler_params=pltpu.CompilerParams(
            collective_id=collective_id, has_side_effects=True, vmem_limit_bytes=VMEM_LIMIT),
        cost_estimate=pl.CostEstimate(flops=LINK_COST, transcendentals=0, bytes_accessed=0),
        name="link_sum",
    )(partial.astype(bf))


def link_open(conv, gate, arrays, sizes, collective_id):
    count = len(arrays)
    mates = sizes["stream"][0]
    take = conv.shape[0] // mates
    dma = pltpu.SemaphoreType.DMA

    def kernel(conv_ref, gate_ref, *refs):
        sources, refs = refs[:count], refs[count:]
        conv_all, conv_own, gate_own, outs, refs = *refs[:3], refs[3 : 3 + count], refs[3 + count :]
        hand_send, hand_recv, hand_buf, sems = refs[0], refs[1], refs[2], refs[3:]
        grids = {axis: Grid(axis, *sizes[axis]) for axis in ("seq", "stream")}
        greet(list(grids.values()), ("stream",))
        me = grids["stream"].row * grids["stream"].inner + grids["stream"].col
        waits = []

        def rows(mate):
            return pl.ds(pl.multiple_of(mate * take, take), take)

        def hand(kind, source, target):
            fetch = pltpu.make_async_copy(source.at[rows(me)], hand_buf.at[kind], hand_send.at[kind, 0])
            fetch.start()
            for step in range(1, mates):
                mate = (me + step) % mates
                copy = pltpu.make_async_remote_copy(
                    src_ref=source.at[rows(mate)], dst_ref=target.at[rows(me)], send_sem=hand_send.at[kind, step],
                    recv_sem=hand_recv.at[kind, step], device_id={"stream": mate}, device_id_type=MESH)
                copy.start()
                waits.append((me >= 0, copy))
            fetch.wait()
            keep = pltpu.make_async_copy(hand_buf.at[kind], target.at[rows(me)], hand_recv.at[kind, 0])
            keep.start()
            return keep

        def handed(kind, source, target, own):
            own.wait()
            for step in range(1, mates):
                mate = (me + mates - step) % mates
                pltpu.make_async_remote_copy(
                    src_ref=source.at[rows(me)], dst_ref=target.at[rows(mate)], send_sem=hand_send.at[kind, step],
                    recv_sem=hand_recv.at[kind, step], device_id={"stream": me}, device_id_type=MESH).wait_recv()

        own = hand(0, conv_ref, conv_own)

        def main():
            for i, (axis, _, chunks) in enumerate(arrays):
                for chunk in range(chunks):
                    at = 4 * (1 + sum(entry[2] for entry in arrays[:i]) + chunk)
                    yield gather_steps(
                        grids[axis], sources[i], outs[i], sems[at], sems[at + 1], sems[at + 2 : at + 4], waits, chunk,
                        chunks)

        runs = list(main())
        for run in runs:
            next(run)
        own_gate = hand(1, gate_ref, gate_own)
        handed(0, conv_ref, conv_own, own)
        first = gather_steps(grids["seq"], conv_own, conv_all, sems[0], sems[1], sems[2:4], waits, 0, 1)
        next(first)
        in_turn([first, *runs])
        handed(1, gate_ref, gate_own, own_gate)
        finish(waits)

    entries = [("seq", conv, 1), *arrays]
    sems = []
    for axis, a, chunks in entries:
        sems += gather_scratch(sizes[axis][0], a, chunks)
    result = pl.pallas_call(
        kernel,
        in_specs=[pl.BlockSpec(memory_space=pl.ANY)] * (count + 2),
        out_specs=[pl.BlockSpec(memory_space=pl.ANY)] * (count + 3),
        out_shape=[
            jax.ShapeDtypeStruct((sizes["seq"][0] * conv.shape[0], conv.shape[1]), conv.dtype),
            jax.ShapeDtypeStruct(conv.shape, conv.dtype),
            jax.ShapeDtypeStruct(gate.shape, gate.dtype),
            *[jax.ShapeDtypeStruct((sizes[axis][0] * a.shape[0], *a.shape[1:]), a.dtype) for axis, a, _ in arrays]],
        scratch_shapes=[
            dma((2, mates)), dma((2, mates)), pltpu.VMEM((2, take, conv.shape[1]), conv.dtype), *sems],
        compiler_params=pltpu.CompilerParams(
            collective_id=collective_id, has_side_effects=True, vmem_limit_bytes=VMEM_LIMIT),
        cost_estimate=pl.CostEstimate(flops=4 * LINK_COST, transcendentals=0, bytes_accessed=0),
        name="link_open",
    )(conv, gate, *[a for _, a, _ in arrays])
    return result[0], result[2], *result[3:]


def passed_along(block, axis, distance):
    devices = range(lax.axis_size(axis))
    route = [(i - distance, i) for i in devices if i - distance in devices]
    return lax.ppermute(block, axis, route)


def silu_slope(values_in):
    sigmoid_v = jax.nn.sigmoid(values_in)
    return sigmoid_v * (1.0 + values_in * (1.0 - sigmoid_v))


def token_layout(lengths, first_pos, n_tokens):
    doc_ends = jnp.cumsum(lengths)
    begins = doc_ends - lengths
    positions = first_pos + jnp.arange(n_tokens, dtype=jnp.int32)
    live_slot = (lengths > 0)[None, :]
    doc_ids = jnp.sum(((begins[None, :] <= positions[:, None]) & live_slot).astype(jnp.int32), axis=1)
    start_flags = jnp.sum(((begins[None, :] == positions[:, None]) & live_slot).astype(jnp.float32), axis=1)
    valid_mask = (positions < doc_ends[-1]).astype(jnp.float32)
    return (doc_ids, start_flags, valid_mask)


def contract_rows(left_mat, right_mat):
    return lax.dot_general(left_mat, right_mat, (((0,), (0,)), ((), ())), preferred_element_type=jnp.float32)


def contract_cols(left_mat, right_mat):
    return lax.dot_general(left_mat, right_mat, NT, preferred_element_type=jnp.float32)


def padded_rows(array, rows):
    return jnp.pad(array, ((0, -array.shape[0] % rows), (0, 0)))


def carried(ends, step_sum, rate, backward, sizes, collective_id):
    seqs, chans = step_sum.shape
    n = rate.shape[0]
    high = step_sum.astype(jnp.bfloat16)
    low = (step_sum - high.astype(jnp.float32)).astype(jnp.bfloat16)
    sent = padded_rows(jnp.concatenate([ends.astype(jnp.bfloat16), high, low], axis=0), 16)
    (gathered,) = link_gather([("seq", sent, 1)], sizes, collective_id, (backward, not backward))
    gathered = gathered.reshape(-1, *sent.shape)
    count = lax.axis_size("seq")
    place = lax.axis_index("seq")
    state = jnp.zeros((seqs, n, chans), jnp.float32)
    for step in range(count - 1):
        source = count - 1 - step if backward else step
        block = gathered[source].astype(jnp.float32)
        total = block[seqs * n : seqs * (n + 1)] + block[seqs * (n + 1) : seqs * (n + 2)]
        joined = jnp.exp2(total[:, None, :] * rate[None]) * state + block[: seqs * n].reshape(seqs, n, chans)
        state = jnp.where(source > place if backward else source < place, joined, state)
    return state.reshape(seqs * n, chans)


def local(sizes, resid_in, out_grad, row_lengths, norm_gain, in_weight, conv_weight, conv_bias, xproj_weight, dt_weight,
          dt_bias, a_log, skip_gain, out_weight):
    bf, f32 = jnp.bfloat16, jnp.float32
    seqs = lax.axis_size("stream")
    parts = lax.axis_size("seq")
    own = conv_bias.shape[0]
    own_feats = norm_gain.shape[0]
    chans = own * parts
    rank_dim = dt_weight.shape[0]
    state_dim = a_log.shape[1]
    proj_dim = xproj_weight.shape[1]
    length, feats = resid_in.shape[1:]
    tokens = seqs * length

    gain = norm_gain.astype(f32)
    scaled = (in_weight.astype(f32) * gain[:, None]).astype(bf).reshape(own_feats, 2, parts, seqs, own)
    scaled = scaled.transpose(1, 3, 0, 2, 4).reshape(2, seqs * own_feats, chans)
    packed = jnp.concatenate(
        [xproj_weight, dt_weight.T, a_log, conv_weight.T, conv_bias[:, None], dt_bias[:, None], skip_gain[:, None]],
        axis=1)
    residual = resid_in[0].astype(f32)
    cotangent = out_grad[0]
    inv_rms = lax.rsqrt(jnp.mean(residual * residual, axis=-1, keepdims=True) + EPSILON)
    unit_own = residual * inv_rms
    slots = row_lengths.shape[1]
    arrays = [
        ("stream", jnp.pad(row_lengths, ((0, 7), (0, -slots % 128))), 1), ("stream", unit_own.astype(bf), 4),
        ("seq", jnp.pad(packed, ((0, 0), (0, -packed.shape[1] % 128))), 1)]
    if own_feats % 16:
        mine = lax.all_to_all(scaled, "stream", 1, 1, tiled=True)
        gate_own = mine[1]
        lengths, unit, packed, in_conv = link_gather([*arrays, ("seq", mine[0], 1)], sizes, 1)
    else:
        in_conv, gate_own, lengths, unit, packed = link_open(scaled[0], scaled[1], arrays, sizes, 1)
    lengths = lengths[::8, :slots]
    unit, gate_own, out_own, cot_own = lax.optimization_barrier((unit, gate_own, out_weight, cotangent))
    in_gate = lax.all_gather(gate_own, "seq", axis=0, tiled=True)
    out_full = lax.all_gather(out_own, "seq", axis=0, tiled=True)
    cot_all = lax.all_gather(cot_own, "stream", axis=0, tiled=True)
    xproj_full = packed[:, :proj_dim]
    dtw_cols = packed[:, proj_dim : proj_dim + rank_dim]
    at = proj_dim + rank_dim
    log_rates = packed[:, at : at + state_dim].astype(f32).T
    at += state_dim
    conv_taps = packed[:, at : at + CONV].astype(f32).T
    at += CONV
    conv_shift, dt_shift, skip_vec = (packed[:, at + i].astype(f32) for i in range(3))
    rate = -jnp.exp(log_rates) / LN2

    rim = CONV - 1
    first_pos = lax.axis_index("seq") * length
    doc_ids, start_flags, valid_mask = jax.vmap(
        lambda row: token_layout(row, first_pos - rim, length + 2 * rim))(lengths)
    own_ids = doc_ids[:, rim : rim + length]
    starts = start_flags[:, rim : rim + length].reshape(tokens, 1)
    valid = valid_mask[:, rim : rim + length].reshape(tokens, 1)
    matches = [(doc_ids[:, tap : tap + length] == own_ids).astype(f32)[:, :, None] for tap in range(CONV)]

    conv_in = jnp.dot(unit, in_conv, preferred_element_type=f32).reshape(seqs, length, chans)
    gate_in = jnp.dot(unit, in_gate, preferred_element_type=f32)
    earlier = passed_along(conv_in[:, length - rim :].astype(bf), "seq", 1).astype(f32)
    padded = jnp.concatenate([earlier, conv_in], axis=1)
    conv_out = conv_shift
    for tap in range(CONV):
        conv_out = conv_out + conv_taps[tap] * padded[:, tap : tap + length] * matches[tap]
    activated = jax.nn.silu(conv_out).astype(bf).reshape(tokens, chans)
    act_float = activated.astype(f32)
    projected = link_sum(
        lax.dot_general(xproj_full, activated, (((0,), (1,)), ((), ())), preferred_element_type=f32), sizes, 2)
    low_rank = projected[:rank_dim].astype(bf)
    write_in = projected[rank_dim : rank_dim + state_dim]
    readout = projected[rank_dim + state_dim :]
    dt_pre = lax.dot_general(low_rank, dtw_cols, (((0,), (1,)), ((), ())), preferred_element_type=f32) + dt_shift
    dt_step = jax.nn.softplus(dt_pre)
    dt_reset = jnp.where(starts > 0, RESET, dt_step)
    dt_act = dt_step * act_float
    write_slabs, read_slabs = slabs_of(write_in), slabs_of(readout)
    write_diag, read_diag = spread(write_in), spread(readout)

    step_sum = jnp.sum(dt_reset.reshape(seqs, length, chans), axis=1)
    ends = scan_end(fwd_end_body, dt_reset, dt_act, write_slabs, rate, seqs)
    start_state = carried(ends, step_sum, rate, False, sizes, 3)
    scanned, history = fwd_full(dt_reset, dt_act, write_slabs, read_diag, rate, start_state, seqs)
    ssm_out = scanned + skip_vec * act_float
    gate_act = jax.nn.silu(gate_in)
    gated = (ssm_out * gate_act * valid).astype(bf)
    product = jnp.dot(gated, out_full, preferred_element_type=f32).astype(bf)
    d_gated = contract_cols(cot_all, out_full)
    g_out = contract_rows(gated, cot_all).astype(bf)
    d_masked = d_gated * valid
    d_ssm = d_masked * gate_act
    d_gate = (d_masked * ssm_out * silu_slope(gate_in)).astype(bf)
    g_in_gate = contract_rows(unit, d_gate).astype(bf)
    d_ssm, product, g_out, g_in_gate = lax.optimization_barrier((d_ssm, product, g_out, g_in_gate))
    g_out = lax.psum_scatter(g_out, "seq", scatter_dimension=0, tiled=True)
    g_in_gate = lax.psum_scatter(g_in_gate, "seq", scatter_dimension=0, tiled=True)
    output = (residual + lax.psum_scatter(product, "stream", scatter_dimension=0, tiled=True).astype(f32)).astype(bf)
    g_skip = jnp.sum(d_ssm * act_float, axis=0)
    back_ends = scan_end(bwd_end_body, dt_reset, d_ssm, read_slabs, rate, seqs)
    later_sum = carried(back_ends, step_sum, rate, True, sizes, 4)
    sum_write, sum_rate, g_log, d_write, d_read = bwd_full(
        dt_reset, dt_act, d_ssm, history, read_slabs, write_diag, rate, later_sum, seqs)
    per_step = jnp.where(dt_step > 1e-30, sum_rate * LN2 / jnp.maximum(dt_step, 1e-30), 0.0)
    d_step = per_step + act_float * sum_write
    d_pre = d_step * jax.nn.sigmoid(dt_pre)
    g_dt_bias = jnp.sum(d_pre, axis=0)
    d_pre_low = d_pre.astype(bf)
    g_dt = lax.dot_general(d_pre_low, low_rank, (((0,), (1,)), ((), ())), preferred_element_type=f32)
    d_low = lax.dot_general(dtw_cols, d_pre_low, (((0,), (1,)), ((), ())), preferred_element_type=f32)
    d_proj = link_sum(jnp.concatenate([d_low, d_write, d_read], axis=0), sizes, 5).astype(bf)
    g_xproj = lax.dot_general(activated, d_proj, (((0,), (1,)), ((), ())), preferred_element_type=f32)
    d_act = dt_step * sum_write + skip_vec * d_ssm + lax.dot_general(
        d_proj, xproj_full, (((0,), (1,)), ((), ())), preferred_element_type=f32)
    d_conv = d_act.reshape(seqs, length, chans) * silu_slope(conv_out)
    g_conv_bias = jnp.sum(d_conv, axis=(0, 1))
    g_conv = jnp.stack(
        [jnp.sum(d_conv * padded[:, tap : tap + length] * matches[tap], axis=(0, 1)) for tap in range(CONV)], axis=1)
    later = passed_along(d_conv[:, :rim].astype(bf), "seq", -1).astype(f32)
    d_ext = jnp.concatenate([d_conv, later], axis=1)
    d_conv_in = jnp.zeros_like(d_conv)
    for tap in range(CONV):
        offset = rim - tap
        match_back = (doc_ids[:, rim + offset : rim + offset + length] == own_ids).astype(f32)[:, :, None]
        d_conv_in = d_conv_in + conv_taps[tap] * d_ext[:, offset : offset + length] * match_back
    d_conv_in = d_conv_in.astype(bf).reshape(tokens, chans)
    g_in_conv = contract_rows(unit, d_conv_in).astype(bf)
    d_unit = (contract_cols(d_conv_in, in_conv) + contract_cols(d_gate, in_gate)).astype(bf)
    def in_rows(block):
        shared = lax.all_to_all(block, "stream", 0, 0, tiled=True).reshape(seqs, own_feats, parts, own)
        return shared.transpose(1, 2, 0, 3).reshape(own_feats, parts * seqs * own)

    def padded_small(columns):
        joined = jnp.concatenate(columns, axis=1)
        return jnp.pad(joined, ((0, 0), (0, -joined.shape[1] % 128))).astype(bf)

    small = padded_small(
        [g_xproj, g_dt, g_log.T * LN2, g_dt_bias[:, None], g_skip[:, None], g_conv, g_conv_bias[:, None]])
    d_unit, g_in_gate, output, g_out = lax.optimization_barrier((d_unit, in_rows(g_in_gate), output, g_out))
    g_in_conv, small, d_unit = link_reduce(
        [("seq", g_in_conv, 2, 0 if own_feats % 16 else own), ("seq", small, 2, 0), ("stream", d_unit, 4, 0)], sizes, 6)
    small = small.astype(f32)
    d_unit = d_unit.astype(f32)
    in_grad = cotangent.astype(f32) + inv_rms * (d_unit - unit_own * jnp.mean(d_unit * unit_own, axis=-1, keepdims=True))

    g_in_conv = in_rows(g_in_conv) if own_feats % 16 else g_in_conv
    g_unit = jnp.concatenate([g_in_conv, g_in_gate], axis=1).astype(f32)
    at = proj_dim + rank_dim
    return (
        output[None],
        in_grad.astype(bf)[None],
        jnp.sum(g_unit * in_weight.astype(f32), axis=1),
        g_unit * gain[:, None],
        small[:, at + state_dim + 2 : at + state_dim + 2 + CONV].T,
        small[:, at + state_dim + 2 + CONV],
        small[:, :proj_dim],
        small[:, proj_dim:at].T,
        small[:, at + state_dim],
        small[:, at : at + state_dim],
        small[:, at + state_dim + 1],
        g_out.astype(f32),
    )


def lines_of(mesh):
    devices = mesh.devices
    places = [getattr(device, "coords", None) for device in devices[:, 0]]
    seq = len(places)
    plane = 1
    if all(place is not None for place in places):
        plane = len({tuple(place)[1] for place in places})
    if seq % plane:
        plane = 1
    return {"seq": (seq, plane), "stream": (devices.shape[1], 1 if devices.shape[1] % 2 else 2)}


def solution(mesh):
    in_specs = (
        P("stream", "seq", None),
        P("stream", "seq", None),
        P("stream", None),
        P(("seq", "stream")),
        P(("seq", "stream"), None),
        P(None, ("seq", "stream")),
        P(("seq", "stream")),
        P(("seq", "stream"), None),
        P(None, ("seq", "stream")),
        P(("seq", "stream")),
        P(("seq", "stream"), None),
        P(("seq", "stream")),
        P(("seq", "stream"), None),
    )
    out_specs = (
        P("stream", "seq", None),
        P("stream", "seq", None),
        P(("seq", "stream")),
        P(("seq", "stream"), None),
        P(None, ("seq", "stream")),
        P(("seq", "stream")),
        P(("seq", "stream"), None),
        P(None, ("seq", "stream")),
        P(("seq", "stream")),
        P(("seq", "stream"), None),
        P(("seq", "stream")),
        P(("seq", "stream"), None),
    )
    return jax.shard_map(functools.partial(local, lines_of(mesh)), mesh=mesh, in_specs=in_specs, out_specs=out_specs, check_vma=False)
```

```python
import functools

import jax
import jax.numpy as jnp
from jax import lax
from jax.experimental import pallas as pl
from jax.experimental.pallas import tpu as pltpu
from jax.sharding import PartitionSpec as P

CONV = 4
EPSILON = 1e-05
RESET = 1e30
GROUP = 16
LN2 = 0.6931471805599453
NT = (((1,), (1,)), ((), ()))
VMEM_LIMIT = 56 << 20
LINK_COST = 20_000_000_000


def across(slab, place, width):
    return jnp.concatenate([jnp.broadcast_to(slab[:, place : place + 1], (slab.shape[0], 128))] * (width // 128), axis=1)


def decays(dte_ref, rate_ref, at, buf, power_buf=None):
    n = rate_ref.shape[0]
    for place in range(GROUP):
        power = dte_ref[pl.ds(at * GROUP + place, 1), :] * rate_ref[...]
        buf[pl.ds(place * n, n), :] = jnp.exp2(power)
        if power_buf is not None:
            power_buf[pl.ds(place * n, n), :] = power.astype(jnp.bfloat16)


def fwd_end_body(dte_ref, dtx_ref, slab_ref, rate_ref, end_ref, even_ref, odd_ref):
    n, width = rate_ref.shape
    groups = dte_ref.shape[0] // GROUP

    def walk(at, state, decay_ref):
        slab = slab_ref[pl.ds(at * n, n), :]
        for place in range(GROUP):
            write = across(slab, place, width)
            state = decay_ref[pl.ds(place * n, n), :] * state + dtx_ref[pl.ds(at * GROUP + place, 1), :] * write
        return state

    def pair(step, state):
        decays(dte_ref, rate_ref, 2 * step + 1, odd_ref)
        state = walk(2 * step, state, even_ref)
        decays(dte_ref, rate_ref, jnp.minimum(2 * step + 2, groups - 1), even_ref)
        return walk(2 * step + 1, state, odd_ref)

    decays(dte_ref, rate_ref, 0, even_ref)
    end_ref[...] = lax.fori_loop(0, groups // 2, pair, jnp.zeros_like(end_ref))


def bwd_end_body(dte_ref, grad_ref, slab_ref, rate_ref, end_ref, even_ref, odd_ref):
    n, width = rate_ref.shape
    groups = dte_ref.shape[0] // GROUP

    def walk(at, state, decay_ref):
        slab = slab_ref[pl.ds(at * n, n), :]
        for place in reversed(range(GROUP)):
            read = across(slab, place, width)
            state = decay_ref[pl.ds(place * n, n), :] * (state + grad_ref[pl.ds(at * GROUP + place, 1), :] * read)
        return state

    def pair(step, state):
        at = groups - 1 - 2 * step
        decays(dte_ref, rate_ref, at - 1, odd_ref)
        state = walk(at, state, even_ref)
        decays(dte_ref, rate_ref, jnp.maximum(at - 2, 0), even_ref)
        return walk(at - 1, state, odd_ref)

    decays(dte_ref, rate_ref, groups - 1, even_ref)
    end_ref[...] = lax.fori_loop(0, groups // 2, pair, jnp.zeros_like(end_ref))


def scan_end(body, dte, other, slabs, rate, seqs, width=512):
    tokens, chans = dte.shape
    length = tokens // seqs
    n = rate.shape[0]
    width = min(width, chans)
    work = tokens * chans * n
    return pl.pallas_call(
        body,
        grid=(seqs, chans // width),
        in_specs=[
            pl.BlockSpec((length, width), lambda s, c: (s, c)),
            pl.BlockSpec((length, width), lambda s, c: (s, c)),
            pl.BlockSpec((length // GROUP * n, GROUP), lambda s, c: (s, 0)),
            pl.BlockSpec((n, width), lambda s, c: (0, c)),
        ],
        out_specs=pl.BlockSpec((n, width), lambda s, c: (s, c)),
        out_shape=jax.ShapeDtypeStruct((seqs * n, chans), jnp.float32),
        scratch_shapes=[pltpu.VMEM((GROUP * n, width), jnp.float32)] * 2,
        compiler_params=pltpu.CompilerParams(vmem_limit_bytes=VMEM_LIMIT),
        cost_estimate=pl.CostEstimate(flops=1000 * work, transcendentals=work, bytes_accessed=8 * tokens * chans),
        name=body.__name__[:7],
    )(dte, other, slabs, rate)


def fwd_full_body(dte_ref, dtx_ref, slab_ref, read_ref, rate_ref, start_ref, y_ref, hist_ref, h_ref, even_ref, odd_ref):
    block = dte_ref.shape[0]
    n, width = rate_ref.shape
    span = GROUP * n
    rate = rate_ref[...]

    @pl.when(pl.program_id(2) == 0)
    def _():
        h_ref[...] = start_ref[...]

    first = h_ref[...]
    hist_ref[pl.ds(0, n), :] = first.astype(jnp.bfloat16)

    def rows_out(at, buf):
        y_ref[pl.ds(at * GROUP, GROUP), :] = jnp.dot(
            read_ref[pl.ds(at * GROUP, GROUP), :], buf[...], preferred_element_type=jnp.float32)

    def group(at, state, buf):
        slab = slab_ref[pl.ds(at * n, n), :]
        for place in range(GROUP):
            t = at * GROUP + place
            write = across(slab, place, width)
            state = jnp.exp2(dte_ref[pl.ds(t, 1), :] * rate) * state + dtx_ref[pl.ds(t, 1), :] * write
            kept = state.astype(jnp.bfloat16)
            hist_ref[pl.ds((t + 1) * n, n), :] = kept
            buf[pl.ds(place * n, n), :] = kept
        return state

    def pair(step, state):
        at = 2 * step
        rows_out(jnp.maximum(at - 1, 0), odd_ref)
        state = group(at, state, even_ref)
        rows_out(at, even_ref)
        return group(at + 1, state, odd_ref)

    h_ref[...] = lax.fori_loop(0, block // GROUP // 2, pair, first)
    rows_out(block // GROUP - 1, odd_ref)


def fwd_full(dte, dtx, slabs, read, rate, start, seqs, width=512, block=256):
    tokens, chans = dte.shape
    n = rate.shape[0]
    width = min(width, chans)
    blocks = tokens // seqs // block
    work = tokens * chans * n
    here = lambda c, s, t: (s * blocks + t, c)
    rows = lambda c, s, t: (s * blocks + t, 0)
    return pl.pallas_call(
        fwd_full_body,
        grid=(chans // width, seqs, blocks),
        in_specs=[
            pl.BlockSpec((block, width), here),
            pl.BlockSpec((block, width), here),
            pl.BlockSpec((block // GROUP * n, GROUP), rows),
            pl.BlockSpec((block, read.shape[1]), rows),
            pl.BlockSpec((n, width), lambda c, s, t: (0, c)),
            pl.BlockSpec((n, width), lambda c, s, t: (s, c)),
        ],
        out_specs=[pl.BlockSpec((block, width), here), pl.BlockSpec(((block + 1) * n, width), here)],
        out_shape=[
            jax.ShapeDtypeStruct((tokens, chans), jnp.float32),
            jax.ShapeDtypeStruct((seqs * blocks * (block + 1) * n, chans), jnp.bfloat16),
        ],
        scratch_shapes=[pltpu.VMEM((n, width), jnp.float32)] + [pltpu.VMEM((GROUP * n, width), jnp.bfloat16)] * 2,
        compiler_params=pltpu.CompilerParams(vmem_limit_bytes=VMEM_LIMIT),
        cost_estimate=pl.CostEstimate(flops=1400 * work, transcendentals=work, bytes_accessed=2 * work),
        name="fwd_full",
    )(dte, dtx, slabs, read, rate, start)


def bwd_full_body(dte_ref, dtx_ref, grad_ref, hist_ref, slab_ref, write_ref, ones_ref, rate_ref, start_ref,
                  s1_ref, s2_ref, grate_ref, dw_ref, dr_ref, g_ref, *scratch):
    block = dte_ref.shape[0]
    n, width = rate_ref.shape
    groups = block // GROUP
    bf, f32 = jnp.bfloat16, jnp.float32
    even, odd = scratch[:5], scratch[5:]
    unit = jnp.ones((GROUP, 128), bf)

    @pl.when(pl.program_id(2) == 0)
    def _():
        g_ref[...] = start_ref[...]

    @pl.when((pl.program_id(2) == 0) & (pl.program_id(1) == 0))
    def _():
        grate_ref[...] = jnp.zeros_like(grate_ref)

    def sums_out(at, bufs):
        _, _, adj_ref, rated_ref, dw_part = bufs
        rows = pl.ds(at * GROUP, GROUP)
        s1_ref[rows, :] = jnp.dot(write_ref[rows, :], adj_ref[...], preferred_element_type=f32)
        sums = jnp.dot(ones_ref[...], rated_ref[...], preferred_element_type=f32)
        s2_ref[rows, :] = sums[:GROUP]
        dw_ref[pl.ds(at, 1), :] = lax.dot_general(unit, dw_part[...], NT, preferred_element_type=f32)[:1]
        reads = lax.dot_general(
            grad_ref[rows, :].astype(bf), hist_ref[pl.ds(n + at * GROUP * n, GROUP * n), :], NT,
            preferred_element_type=f32)
        own = lax.broadcasted_iota(jnp.int32, reads.shape, 1) // n == lax.broadcasted_iota(jnp.int32, reads.shape, 0)
        dr_ref[pl.ds(at, 1), :] = jnp.sum(jnp.where(own, reads, 0.0), axis=0, keepdims=True)
        return sums[GROUP:]

    def strips(values):
        parts = [values[:, k * 128 : (k + 1) * 128] for k in range(width // 128)]
        while len(parts) > 1:
            parts = [a + b for a, b in zip(parts[::2], parts[1::2])] + parts[len(parts) // 2 * 2 :]
        return parts[0]

    def walk(at, state, bufs):
        decay_ref, power_ref, adj_ref, rated_ref, dw_part = bufs
        slab = slab_ref[pl.ds(at * n, n), :]
        for place in reversed(range(GROUP)):
            t = at * GROUP + place
            here = pl.ds(place * n, n)
            read = across(slab, place, width)
            adjoint = state + grad_ref[pl.ds(t, 1), :] * read
            power = dte_ref[pl.ds(t, 1), :] * rate_ref[...]
            state = jnp.exp2(power) * adjoint
            low = adjoint.astype(bf)
            adj_ref[here, :] = low
            rated_ref[here, :] = state.astype(bf) * hist_ref[pl.ds(t * n, n), :] * power.astype(bf)
            dw_part[here, :] = strips(adjoint * dtx_ref[pl.ds(t, 1), :]).astype(bf)
        return state

    def pair(step, state):
        at = groups - 1 - 2 * step
        old = sums_out(jnp.minimum(at + 1, groups - 1), odd)
        state = walk(at, state, even)
        grate_ref[...] += jnp.where(step > 0, old, 0.0) + sums_out(at, even)
        return walk(at - 1, state, odd)
    g_ref[...] = lax.fori_loop(0, groups // 2, pair, g_ref[...])
    grate_ref[...] += sums_out(0, odd)


def bwd_full(dte, dtx, grad, hist, slabs, write, rate, start, seqs, width=512, block=256):
    tokens, chans = dte.shape
    n = rate.shape[0]
    width = min(width, chans)
    strips = chans // width
    blocks = tokens // seqs // block
    span = GROUP * n
    work = tokens * chans * n
    column = jnp.arange(span)
    ones = jnp.concatenate(
        [(column // n)[None, :] == jnp.arange(GROUP)[:, None], (column % n)[None, :] == jnp.arange(n)[:, None]]
    ).astype(jnp.bfloat16)
    here = lambda c, s, t: (s * blocks + blocks - 1 - t, c)
    rows = lambda c, s, t: (s * blocks + blocks - 1 - t, 0)
    strip = lambda c, s, t: (c * seqs * blocks + s * blocks + blocks - 1 - t, 0)
    f32 = jnp.float32
    s1, s2, grate, dw, dr = pl.pallas_call(
        bwd_full_body,
        grid=(strips, seqs, blocks),
        in_specs=[
            pl.BlockSpec((block, width), here),
            pl.BlockSpec((block, width), here),
            pl.BlockSpec((block, width), here),
            pl.BlockSpec(((block + 1) * n, width), here),
            pl.BlockSpec((block // GROUP * n, GROUP), rows),
            pl.BlockSpec((block, span), rows),
            pl.BlockSpec(ones.shape, lambda c, s, t: (0, 0)),
            pl.BlockSpec((n, width), lambda c, s, t: (0, c)),
            pl.BlockSpec((n, width), lambda c, s, t: (s, c)),
        ],
        out_specs=[
            pl.BlockSpec((block, width), here),
            pl.BlockSpec((block, width), here),
            pl.BlockSpec((n, width), lambda c, s, t: (0, c)),
            pl.BlockSpec((block // GROUP, span), strip),
            pl.BlockSpec((block // GROUP, span), strip),
        ],
        out_shape=[
            jax.ShapeDtypeStruct((tokens, chans), f32),
            jax.ShapeDtypeStruct((tokens, chans), f32),
            jax.ShapeDtypeStruct((n, chans), f32),
            jax.ShapeDtypeStruct((strips * tokens // GROUP, span), f32),
            jax.ShapeDtypeStruct((strips * tokens // GROUP, span), f32),
        ],
        scratch_shapes=[
            pltpu.VMEM((n, width), f32),
            *[
                pltpu.VMEM((span, width), f32),
                *[pltpu.VMEM((span, width), jnp.bfloat16)] * 3,
                pltpu.VMEM((span, 128), jnp.bfloat16),
            ] * 2,
        ],
        compiler_params=pltpu.CompilerParams(vmem_limit_bytes=VMEM_LIMIT),
        cost_estimate=pl.CostEstimate(flops=3200 * work, transcendentals=work, bytes_accessed=2 * work),
        name="bwd_full",
    )(dte, dtx, grad, hist, slabs, write, ones, rate, start)
    both = jnp.stack([part.reshape(strips, tokens // GROUP, span).sum(0) for part in (dw, dr)])
    both = both.reshape(2, tokens // GROUP, GROUP, n).transpose(0, 3, 1, 2).reshape(2, n, tokens)
    return s1, s2, grate, both[0], both[1]


def slabs_of(values):
    n, tokens = values.shape
    return values.reshape(n, tokens // GROUP, GROUP).transpose(1, 0, 2).reshape(tokens // GROUP * n, GROUP)


def spread(values):
    n, tokens = values.shape
    own = jnp.arange(tokens)[:, None] % GROUP == jnp.arange(GROUP)[None, :]
    return jnp.where(own[:, :, None], values.T[:, None, :], 0).reshape(tokens, GROUP * n).astype(jnp.bfloat16)


MESH = pl.DeviceIdType.MESH


class Grid:
    def __init__(self, axis, size, inner):
        self.axis, self.inner, self.outer = axis, inner, size // inner
        me = lax.axis_index(axis)
        self.row, self.col = me // inner, me % inner

    def device(self, row, col):
        return {self.axis: row * self.inner + col}

    def neighbours(self):
        row, col = self.row, self.col
        found = []
        if self.outer > 1:
            found += [(row > 0, self.device(row - 1, col)), (row < self.outer - 1, self.device(row + 1, col))]
        if self.inner > 1:
            found += [(col > 0, self.device(row, col - 1)), (col < self.inner - 1, self.device(row, col + 1))]
        return found

    def everyone(self):
        size = self.inner * self.outer
        me = self.row * self.inner + self.col
        return [(me >= 0, {self.axis: (me + step) % size}) for step in range(1, size)]


def greet(grids, all_of=()):
    barrier = pltpu.get_barrier_semaphore()
    count = 0
    for grid in grids:
        for there, device in grid.everyone() if grid.axis in all_of else grid.neighbours():

            @pl.when(there)
            def _(device=device):
                pl.semaphore_signal(barrier, inc=1, device_id=device, device_id_type=MESH)

            count = count + there.astype(jnp.int32)
    pl.semaphore_wait(barrier, count)


def gather_steps(grid, whole_ref, out_ref, send_sem, recv_sem, own, waits, chunk, chunks, across_too=True, ways=(True, True)):
    rows = whole_ref.shape[0]
    part = rows // chunks
    src_ref = whole_ref.at[pl.ds(chunk * part, part)]
    outer, inner = grid.outer, grid.inner if across_too else 1
    row, col = grid.row, grid.col

    def number(r, c):
        return r * inner + c if across_too else r

    def place(r, c):
        return pl.ds(pl.multiple_of(number(r, c) * rows + chunk * part, part), part)

    def send(there, way, r, c, device, source):
        copy = pltpu.make_async_remote_copy(
            src_ref=source, dst_ref=out_ref.at[place(r, c)], send_sem=send_sem.at[way, number(r, c)],
            recv_sem=recv_sem.at[number(r, c)], device_id=device, device_id_type=MESH)

        @pl.when(there)
        def _():
            copy.start()

        waits.append((there, copy))

    def across(there, r, c, source):
        if inner > 1:
            send(there & (c >= col) & (col > 0), 2, r, c, grid.device(row, col - 1), source)
            send(there & (c <= col) & (col < inner - 1), 3, r, c, grid.device(row, col + 1), source)

    def along(there, r, source):
        if outer > 1:
            if ways[0]:
                send(there & (r >= row) & (row > 0), 0, r, col, grid.device(row - 1, col), source)
            if ways[1]:
                send(there & (r <= row) & (row < outer - 1), 1, r, col, grid.device(row + 1, col), source)

    def arrive(there, r, c):
        copy = pltpu.make_async_remote_copy(
            src_ref=src_ref, dst_ref=out_ref.at[place(r, c)], send_sem=send_sem.at[0, 0],
            recv_sem=recv_sem.at[number(r, c)], device_id=grid.device(row, col), device_id_type=MESH)

        @pl.when(there)
        def _():
            copy.wait_recv()

    always = row >= 0
    along(always, row, src_ref)
    across(always, row, col, src_ref)
    own_sem, own_buf = own
    fetch = pltpu.make_async_copy(src_ref, own_buf, own_sem.at[0])
    fetch.start()
    for _ in range(chunk + 1):
        yield
    fetch.wait()
    keep = pltpu.make_async_copy(own_buf, out_ref.at[place(row, col)], own_sem.at[1])
    keep.start()
    waits.append((None, keep))

    def rows_at(distance):
        return [row - distance] * ways[1] + [row + distance] * ways[0]

    for distance in range(1, outer):
        for r in rows_at(distance):
            there = (r >= 0) & (r < outer)
            arrive(there, r, col)
            along(there, r, out_ref.at[place(r, col)])
            across(there, r, col, out_ref.at[place(r, col)])
        yield
    for step in range(1, inner):
        for distance in range(outer):
            for r in rows_at(distance) if distance else (row,):
                for c in (col - step, col + step):
                    there = (r >= 0) & (r < outer) & (c >= 0) & (c < inner)
                    arrive(there, r, c)
                    if step < inner - 1:
                        across(there, r, c, out_ref.at[place(r, c)])
            yield


def finish(waits):
    for there, copy in waits:
        if there is None:
            copy.wait()
        else:

            @pl.when(there)
            def _(copy=copy):
                if copy.is_remote:
                    copy.wait_send()
                else:
                    copy.wait()


def gather_scratch(size, array, chunks):
    dma = pltpu.SemaphoreType.DMA
    own = pltpu.VMEM((array.shape[0] // chunks, *array.shape[1:]), array.dtype)
    return [dma((4, size)), dma((size,)), dma((2,)), own] * chunks


def in_turn(runs):
    runs = list(runs)
    while runs:
        left = []
        for run in runs:
            if next(run, run) is not run:
                left.append(run)
        runs = left


def link_gather(arrays, sizes, collective_id, ways=(True, True)):
    count = len(arrays)
    axes = sorted({entry[0] for entry in arrays})

    def kernel(*refs):
        sources, outs, sems = refs[:count], refs[count : 2 * count], refs[2 * count :]
        grids = {axis: Grid(axis, *sizes[axis]) for axis in axes}
        greet([grids[axis] for axis in axes])
        waits = []
        runs = []
        for i, (axis, _, chunks) in enumerate(arrays):
            for chunk in range(chunks):
                runs.append(gather_steps(
                    grids[axis], sources[i], outs[i], sems[0], sems[1], sems[2:4], waits, chunk, chunks, ways=ways))
                sems = sems[4:]
        in_turn(runs)
        finish(waits)

    sems = []
    for axis, a, chunks in arrays:
        sems += gather_scratch(sizes[axis][0], a, chunks)
    return pl.pallas_call(
        kernel,
        in_specs=[pl.BlockSpec(memory_space=pl.ANY)] * count,
        out_specs=[pl.BlockSpec(memory_space=pl.ANY)] * count,
        out_shape=[
            jax.ShapeDtypeStruct((sizes[axis][0] * a.shape[0], *a.shape[1:]), a.dtype) for axis, a, _ in arrays],
        scratch_shapes=sems,
        compiler_params=pltpu.CompilerParams(
            collective_id=collective_id, has_side_effects=True, vmem_limit_bytes=VMEM_LIMIT),
        cost_estimate=pl.CostEstimate(flops=LINK_COST, transcendentals=0, bytes_accessed=0),
        name="link_gather",
    )(*[a for _, a, _ in arrays])


def reduce_steps(grid, src_ref, out_ref, scratch, waits, chunks, share):
    acc, inner_buf, outer_buf, load_sem, inner_send, inner_recv, outer_send, outer_recv, out_sem = scratch[:9]
    outer, inner = grid.outer, grid.inner
    row, col = grid.row, grid.col
    rows = acc.shape[0] // (outer * inner)
    part = rows // chunks
    piece = min(part, 64)

    def start_of(chunk, r, c):
        return pl.multiple_of((r * inner + c) * rows + chunk * part, part)

    def line(me, size, device, block, buf, send, recv):
        def from_low(target):
            return target if size > 2 else 0

        def from_high(target, owner):
            return jnp.where(target == owner, size, target) if size > 2 else 0

        def hop(there, target, onward, slot):
            copy = pltpu.make_async_remote_copy(
                src_ref=acc.at[pl.ds(block(target), part)], dst_ref=buf.at[slot], send_sem=send.at[target],
                recv_sem=recv.at[slot], device_id=device(onward), device_id_type=MESH)

            @pl.when(there)
            def _():
                copy.start()

            waits.append((there, copy))

        def up(there, target):
            hop(there & (target > me), target, me + 1, from_low(target))

        def down(there, target):
            hop(there & (target < me), target, me - 1, from_high(target, me - 1))

        def arrive(there, target, slot):
            at = block(target)
            copy = pltpu.make_async_remote_copy(
                src_ref=acc.at[pl.ds(at, part)], dst_ref=buf.at[slot], send_sem=send.at[target],
                recv_sem=recv.at[slot], device_id=device(me), device_id_type=MESH)

            @pl.when(there)
            def _():
                copy.wait_recv()

                @pl.loop(0, part // piece)
                def _(k):
                    here = pl.ds(pl.multiple_of(at + k * piece, piece), piece)
                    there_rows = pl.ds(pl.multiple_of(k * piece, piece), piece)
                    total = acc[here, :].astype(jnp.float32) + buf[slot, there_rows, :].astype(jnp.float32)
                    acc[here, :] = total.astype(acc.dtype)

        def begin(target):
            up(me == 0, target)
            down(me == size - 1, target)

        def go_on(target):
            arrive((me > 0) & (target >= me), target, from_low(target))
            arrive((me < size - 1) & (target <= me), target, from_high(target, me))
            if size > 2:
                up((me > 0) & (me < size - 1), target)
                down((me > 0) & (me < size - 1), target)

        return begin, go_on

    order = sorted(range(outer), key=lambda k: -abs(2 * k - outer + 1))
    pieces = [(chunk, r) for chunk in range(chunks) for r in order]
    loads = {}
    for chunk, r in pieces:
        loads[chunk, r] = [
            pltpu.make_async_copy(
                src_ref.at[pl.ds(start_of(chunk, r, c), part)], acc.at[pl.ds(start_of(chunk, r, c), part)],
                load_sem.at[chunk, r * inner + c])
            for c in range(inner)]
        for load in loads[chunk, r]:
            load.start()

    def inner_line(chunk, r):
        return line(
            col, inner, lambda c: grid.device(row, c), lambda t: start_of(chunk, r, t), inner_buf.at[chunk, r],
            inner_send.at[chunk, r], inner_recv.at[chunk, r])

    def outer_line(chunk):
        return line(
            row, outer, lambda r: grid.device(r, col), lambda t: start_of(chunk, t, col), outer_buf.at[chunk],
            outer_send.at[chunk], outer_recv.at[chunk])

    def inner_start(k):
        if k < len(pieces):
            for load in loads[pieces[k]]:
                load.wait()
            if inner > 1:
                for c in range(inner):
                    inner_line(*pieces[k])[0](c)

    def outer_rest(k):
        if 0 <= k < len(pieces):
            chunk, r = pieces[k]
            if outer > 1:
                outer_line(chunk)[1](r)
            if r == order[-1]:
                give(chunk)

    def give(chunk):
        first = start_of(chunk, row, col)
        if share is None:
            last = pltpu.make_async_copy(
                acc.at[pl.ds(first, part)], out_ref.at[pl.ds(chunk * part, part)], out_sem.at[chunk])
            last.start()
            waits.append((None, last))
            return
        other, strip, send_sem, recv_sem = share
        count, me = other.outer * other.inner, other.row * other.inner + other.col
        take = rows // count
        for mate in range(chunk * part // take, (chunk + 1) * part // take):
            for k in range(acc.shape[1] // strip):
                source = acc.at[
                    pl.ds(pl.multiple_of((row * inner + col) * rows + mate * take, take), take),
                    pl.ds(k * strip, strip)]
                target = out_ref.at[:, pl.ds(pl.multiple_of((k * count + me) * strip, strip), strip)]
                own = pltpu.make_async_copy(source, target, send_sem.at[mate, k])
                sent = pltpu.make_async_remote_copy(
                    src_ref=source, dst_ref=target, send_sem=send_sem.at[mate, k], recv_sem=recv_sem.at[me, k],
                    device_id={other.axis: mate}, device_id_type=MESH)

                @pl.when(mate == me)
                def _(own=own):
                    own.start()

                @pl.when(mate != me)
                def _(sent=sent):
                    sent.start()

                waits.append((mate != me, sent))
                waits.append((mate == me, own))

    window = 2
    for k in range(window):
        inner_start(k)
    yield
    for k in range(len(pieces)):
        inner_start(k + window)
        chunk, r = pieces[k]
        if inner > 1:
            for c in range(inner):
                inner_line(chunk, r)[1](c)
        if outer > 1:
            outer_line(chunk)[0](r)
        yield
        outer_rest(k - window)
        yield
    for k in range(len(pieces) - window, len(pieces)):
        outer_rest(k)
        yield
    if share is not None:
        other, strip, send_sem, recv_sem = share
        count, me = other.outer * other.inner, other.row * other.inner + other.col
        take = rows // count
        for mate in range(count):
            for k in range(acc.shape[1] // strip):
                copy = pltpu.make_async_remote_copy(
                    src_ref=acc.at[pl.ds(0, take), pl.ds(k * strip, strip)],
                    dst_ref=out_ref.at[:, pl.ds((k * count + mate) * strip, strip)], send_sem=send_sem.at[mate, k],
                    recv_sem=recv_sem.at[mate, k], device_id={other.axis: me}, device_id_type=MESH)

                @pl.when(mate != me)
                def _(copy=copy):
                    copy.wait_recv()


def link_reduce(arrays, sizes, collective_id):
    count = len(arrays)

    def kernel(*refs):
        sources, outs, scratch = refs[:count], refs[count : 2 * count], refs[2 * count :]
        grids = {axis: Grid(axis, *sizes[axis]) for axis in ("seq", "stream")}
        greet(list(grids.values()), ("stream",))
        waits = []
        runs = []
        for i, (axis, _, chunks, strip) in enumerate(arrays):
            share = (grids["stream"], strip, scratch[9], scratch[10]) if strip else None
            runs.append(reduce_steps(grids[axis], sources[i], outs[i], scratch[:9], waits, chunks, share))
            scratch = scratch[11 if strip else 9 :]
        in_turn(runs)
        finish(waits)

    scratch, shapes = [], []
    for axis, a, chunks, strip in arrays:
        size, inner = sizes[axis]
        outer = size // inner
        part = a.shape[0] // size // chunks
        slots = [n + 1 if n > 2 else 1 for n in (inner, outer)]
        dma = pltpu.SemaphoreType.DMA
        scratch += [
            pltpu.VMEM(a.shape, a.dtype),
            pltpu.VMEM((chunks, outer, slots[0], part, a.shape[1]), a.dtype),
            pltpu.VMEM((chunks, slots[1], part, a.shape[1]), a.dtype),
            dma((chunks, size)), dma((chunks, outer, inner)), dma((chunks, outer, slots[0])), dma((chunks, outer)),
            dma((chunks, slots[1])), dma((chunks,))]
        if strip:
            mates = sizes["stream"][0]
            shapes.append(jax.ShapeDtypeStruct((a.shape[0] // size // mates, a.shape[1] * mates), a.dtype))
            scratch += [dma((mates, a.shape[1] // strip))] * 2
        else:
            shapes.append(jax.ShapeDtypeStruct((a.shape[0] // size, a.shape[1]), a.dtype))
    return pl.pallas_call(
        kernel,
        in_specs=[pl.BlockSpec(memory_space=pl.ANY)] * count,
        out_specs=[pl.BlockSpec(memory_space=pl.ANY)] * count,
        out_shape=shapes,
        scratch_shapes=scratch,
        compiler_params=pltpu.CompilerParams(
            collective_id=collective_id, has_side_effects=True, vmem_limit_bytes=VMEM_LIMIT),
        cost_estimate=pl.CostEstimate(flops=4 * LINK_COST, transcendentals=0, bytes_accessed=0),
        name="link_reduce",
    )(*[entry[1] for entry in arrays])


def link_sum(partial, sizes, collective_id):
    rows, width = partial.shape
    size, inner = sizes["stream"]
    outer = size // inner
    assert inner == 2
    half = rows // 2
    bf, f32 = jnp.bfloat16, jnp.float32
    dma = pltpu.SemaphoreType.DMA

    def kernel(own_ref, out_ref, mate_buf, pair_ref, terms_ref, total_ref, send, recv, line_send, line_recv, own_sem, own_buf):
        grid = Grid("stream", size, inner)
        row, col = grid.row, grid.col
        greet([grid])
        mate = grid.device(row, 1 - col)
        mine = pl.ds(pl.multiple_of(col * half, half), half)
        swap = pltpu.make_async_remote_copy(
            src_ref=own_ref, dst_ref=mate_buf, send_sem=send.at[0], recv_sem=recv.at[0], device_id=mate,
            device_id_type=MESH)
        swap.start()
        swap.wait_recv()
        pair_ref[...] = (own_ref[mine, :].astype(f32) + mate_buf[mine, :].astype(f32)).astype(bf)
        waits = []
        line = Grid("stream", size, inner)
        in_turn([gather_steps(
            line, pair_ref, terms_ref, line_send, line_recv, (own_sem, own_buf), waits, 0, 1, across_too=False)])
        finish(waits)
        total = terms_ref[pl.ds(0, half), :].astype(f32)
        for r in range(1, outer):
            total = total + terms_ref[pl.ds(r * half, half), :].astype(f32)
        total_ref[...] = total
        out_ref[mine, :] = total
        swap_back = pltpu.make_async_remote_copy(
            src_ref=total_ref, dst_ref=out_ref.at[mine], send_sem=send.at[1], recv_sem=recv.at[1], device_id=mate,
            device_id_type=MESH)
        swap_back.start()
        theirs = pltpu.make_async_remote_copy(
            src_ref=total_ref, dst_ref=out_ref.at[pl.ds(pl.multiple_of((1 - col) * half, half), half)],
            send_sem=send.at[1], recv_sem=recv.at[1], device_id=mate, device_id_type=MESH)
        theirs.wait_recv()
        swap.wait_send()
        swap_back.wait_send()

    return pl.pallas_call(
        kernel,
        in_specs=[pl.BlockSpec(memory_space=pltpu.VMEM)],
        out_specs=pl.BlockSpec(memory_space=pltpu.VMEM),
        out_shape=jax.ShapeDtypeStruct((rows, width), f32),
        scratch_shapes=[
            pltpu.VMEM((rows, width), bf), pltpu.VMEM((half, width), bf), pltpu.VMEM((outer * half, width), bf),
            pltpu.VMEM((half, width), f32), dma((2,)), dma((2,)), dma((4, outer)), dma((outer,)), dma((2,)),
            pltpu.VMEM((half, width), bf)],
        compiler_params=pltpu.CompilerParams(
            collective_id=collective_id, has_side_effects=True, vmem_limit_bytes=VMEM_LIMIT),
        cost_estimate=pl.CostEstimate(flops=LINK_COST, transcendentals=0, bytes_accessed=0),
        name="link_sum",
    )(partial.astype(bf))


def link_open(conv, gate, arrays, sizes, collective_id):
    count = len(arrays)
    mates = sizes["stream"][0]
    take = conv.shape[0] // mates
    dma = pltpu.SemaphoreType.DMA

    def kernel(conv_ref, gate_ref, *refs):
        sources, refs = refs[:count], refs[count:]
        conv_all, conv_own, gate_own, outs, refs = *refs[:3], refs[3 : 3 + count], refs[3 + count :]
        hand_send, hand_recv, hand_buf, sems = refs[0], refs[1], refs[2], refs[3:]
        grids = {axis: Grid(axis, *sizes[axis]) for axis in ("seq", "stream")}
        greet(list(grids.values()), ("stream",))
        me = grids["stream"].row * grids["stream"].inner + grids["stream"].col
        waits = []

        def rows(mate):
            return pl.ds(pl.multiple_of(mate * take, take), take)

        def hand(kind, source, target):
            fetch = pltpu.make_async_copy(source.at[rows(me)], hand_buf.at[kind], hand_send.at[kind, 0])
            fetch.start()
            for step in range(1, mates):
                mate = (me + step) % mates
                copy = pltpu.make_async_remote_copy(
                    src_ref=source.at[rows(mate)], dst_ref=target.at[rows(me)], send_sem=hand_send.at[kind, step],
                    recv_sem=hand_recv.at[kind, step], device_id={"stream": mate}, device_id_type=MESH)
                copy.start()
                waits.append((me >= 0, copy))
            fetch.wait()
            keep = pltpu.make_async_copy(hand_buf.at[kind], target.at[rows(me)], hand_recv.at[kind, 0])
            keep.start()
            return keep

        def handed(kind, source, target, own):
            own.wait()
            for step in range(1, mates):
                mate = (me + mates - step) % mates
                pltpu.make_async_remote_copy(
                    src_ref=source.at[rows(me)], dst_ref=target.at[rows(mate)], send_sem=hand_send.at[kind, step],
                    recv_sem=hand_recv.at[kind, step], device_id={"stream": me}, device_id_type=MESH).wait_recv()

        own = hand(0, conv_ref, conv_own)

        def main():
            for i, (axis, _, chunks) in enumerate(arrays):
                for chunk in range(chunks):
                    at = 4 * (1 + sum(entry[2] for entry in arrays[:i]) + chunk)
                    yield gather_steps(
                        grids[axis], sources[i], outs[i], sems[at], sems[at + 1], sems[at + 2 : at + 4], waits, chunk,
                        chunks)

        runs = list(main())
        for run in runs:
            next(run)
        own_gate = hand(1, gate_ref, gate_own)
        handed(0, conv_ref, conv_own, own)
        first = gather_steps(grids["seq"], conv_own, conv_all, sems[0], sems[1], sems[2:4], waits, 0, 1)
        next(first)
        in_turn([first, *runs])
        handed(1, gate_ref, gate_own, own_gate)
        finish(waits)

    entries = [("seq", conv, 1), *arrays]
    sems = []
    for axis, a, chunks in entries:
        sems += gather_scratch(sizes[axis][0], a, chunks)
    result = pl.pallas_call(
        kernel,
        in_specs=[pl.BlockSpec(memory_space=pl.ANY)] * (count + 2),
        out_specs=[pl.BlockSpec(memory_space=pl.ANY)] * (count + 3),
        out_shape=[
            jax.ShapeDtypeStruct((sizes["seq"][0] * conv.shape[0], conv.shape[1]), conv.dtype),
            jax.ShapeDtypeStruct(conv.shape, conv.dtype),
            jax.ShapeDtypeStruct(gate.shape, gate.dtype),
            *[jax.ShapeDtypeStruct((sizes[axis][0] * a.shape[0], *a.shape[1:]), a.dtype) for axis, a, _ in arrays]],
        scratch_shapes=[
            dma((2, mates)), dma((2, mates)), pltpu.VMEM((2, take, conv.shape[1]), conv.dtype), *sems],
        compiler_params=pltpu.CompilerParams(
            collective_id=collective_id, has_side_effects=True, vmem_limit_bytes=VMEM_LIMIT),
        cost_estimate=pl.CostEstimate(flops=4 * LINK_COST, transcendentals=0, bytes_accessed=0),
        name="link_open",
    )(conv, gate, *[a for _, a, _ in arrays])
    return result[0], result[2], *result[3:]


ROWS = 128


def conv_fwd_body(x_ref, early_ref, masks_ref, taps_ref, act_ref, slope_ref, ext_ref):
    length = x_ref.shape[0]
    ext_ref[pl.ds(0, 8), :] = early_ref[...]

    @pl.loop(0, length // ROWS)
    def _(k):
        here = pl.ds(pl.multiple_of(k * ROWS, ROWS), ROWS)
        ext_ref[pl.ds(pl.multiple_of(k * ROWS + 8, 8), ROWS), :] = x_ref[here, :]
        window = ext_ref[pl.ds(pl.multiple_of(k * ROWS, ROWS), ROWS + 8), :]
        masks = masks_ref[here, :]
        total = taps_ref[CONV : CONV + 1, :] + taps_ref[CONV - 1 : CONV, :] * window[8:]
        for tap in range(CONV - 1):
            shift = 8 - (CONV - 1) + tap
            total = total + taps_ref[tap : tap + 1, :] * (window[shift : shift + ROWS] * masks[:, tap : tap + 1])
        gate = jax.nn.sigmoid(total)
        act_ref[here, :] = (total * gate).astype(act_ref.dtype)
        slope_ref[here, :] = (gate * (1.0 + total * (1.0 - gate))).astype(slope_ref.dtype)


def conv_bwd_body(grad_ref, slope_ref, late_ref, x_ref, masks_ref, taps_ref, out_ref, sums_ref, ext_ref):
    length, width = x_ref.shape
    ext_ref[pl.ds(length, 8), :] = late_ref[...]

    @pl.loop(0, length // ROWS)
    def _(k):
        here = pl.ds(pl.multiple_of(k * ROWS, ROWS), ROWS)
        ext_ref[here, :] = grad_ref[here, :] * slope_ref[here, :].astype(jnp.float32)

    def some(k, sums):
        start = pl.multiple_of(k * ROWS, ROWS)
        here = pl.ds(start, ROWS)
        window = ext_ref[pl.ds(start, ROWS + 8), :]
        masks = masks_ref[here, :]
        x = x_ref[here, :]
        total = jnp.zeros((ROWS, width), jnp.float32)
        parts = []
        for tap in range(CONV):
            ahead = CONV - 1 - tap
            term = window[ahead : ahead + ROWS]
            if ahead:
                term = term * masks[:, CONV - 2 + ahead : CONV - 1 + ahead]
            total = total + taps_ref[tap : tap + 1, :] * term
            parts.append((term * x).reshape(ROWS // 8, 8, width).sum(0))
        parts.append(window[:ROWS].reshape(ROWS // 8, 8, width).sum(0))
        out_ref[here, :] = total.astype(out_ref.dtype)
        return tuple(a + b for a, b in zip(sums, parts))

    sums = lax.fori_loop(0, length // ROWS, some, (jnp.zeros((8, width), jnp.float32),) * (CONV + 1))
    for tap in range(CONV + 1):
        sums_ref[tap : tap + 1, :] = jnp.sum(sums[tap], axis=0, keepdims=True)
    sums_ref[CONV + 1 :, :] = jnp.zeros((7 - CONV, width), jnp.float32)


def conv_fwd(x, early, masks, taps, seqs, width=1024):
    tokens, chans = x.shape
    width = min(width, chans)
    length = tokens // seqs
    block = pl.BlockSpec((length, width), lambda s, c: (s, c))
    return pl.pallas_call(
        conv_fwd_body,
        grid=(seqs, chans // width),
        in_specs=[
            block, pl.BlockSpec((8, width), lambda s, c: (s, c)), pl.BlockSpec((length, 8), lambda s, c: (s, 0)),
            pl.BlockSpec((8, width), lambda s, c: (0, c))],
        out_specs=[block, block],
        out_shape=[jax.ShapeDtypeStruct((tokens, chans), jnp.bfloat16)] * 2,
        scratch_shapes=[pltpu.VMEM((length + 8, width), jnp.float32)],
        compiler_params=pltpu.CompilerParams(vmem_limit_bytes=VMEM_LIMIT),
        cost_estimate=pl.CostEstimate(
            flops=4000 * tokens * chans, transcendentals=tokens * chans, bytes_accessed=8 * tokens * chans),
        name="conv_fwd",
    )(x, early, masks, taps)


def conv_bwd(grad, slope, late, x, masks, taps, seqs, width=512):
    tokens, chans = x.shape
    width = min(width, chans)
    length = tokens // seqs
    block = pl.BlockSpec((length, width), lambda s, c: (s, c))
    rim = pl.BlockSpec((8, width), lambda s, c: (s, c))
    return pl.pallas_call(
        conv_bwd_body,
        grid=(seqs, chans // width),
        in_specs=[
            block, block, rim, block, pl.BlockSpec((length, 8), lambda s, c: (s, 0)),
            pl.BlockSpec((8, width), lambda s, c: (0, c))],
        out_specs=[block, rim],
        out_shape=[
            jax.ShapeDtypeStruct((tokens, chans), jnp.bfloat16), jax.ShapeDtypeStruct((seqs * 8, chans), jnp.float32)],
        scratch_shapes=[pltpu.VMEM((length + 8, width), jnp.float32)],
        compiler_params=pltpu.CompilerParams(vmem_limit_bytes=VMEM_LIMIT),
        cost_estimate=pl.CostEstimate(
            flops=5000 * tokens * chans, transcendentals=0, bytes_accessed=12 * tokens * chans),
        name="conv_bwd",
    )(grad, slope, late, x, masks, taps)


def passed_along(block, axis, distance):
    devices = range(lax.axis_size(axis))
    route = [(i - distance, i) for i in devices if i - distance in devices]
    return lax.ppermute(block, axis, route)


def silu_slope(values_in):
    sigmoid_v = jax.nn.sigmoid(values_in)
    return sigmoid_v * (1.0 + values_in * (1.0 - sigmoid_v))


def token_layout(lengths, first_pos, n_tokens):
    doc_ends = jnp.cumsum(lengths)
    begins = doc_ends - lengths
    positions = first_pos + jnp.arange(n_tokens, dtype=jnp.int32)
    live_slot = (lengths > 0)[None, :]
    doc_ids = jnp.sum(((begins[None, :] <= positions[:, None]) & live_slot).astype(jnp.int32), axis=1)
    start_flags = jnp.sum(((begins[None, :] == positions[:, None]) & live_slot).astype(jnp.float32), axis=1)
    valid_mask = (positions < doc_ends[-1]).astype(jnp.float32)
    return (doc_ids, start_flags, valid_mask)


def contract_rows(left_mat, right_mat):
    return lax.dot_general(left_mat, right_mat, (((0,), (0,)), ((), ())), preferred_element_type=jnp.float32)


def contract_cols(left_mat, right_mat):
    return lax.dot_general(left_mat, right_mat, NT, preferred_element_type=jnp.float32)


def padded_rows(array, rows):
    return jnp.pad(array, ((0, -array.shape[0] % rows), (0, 0)))


def carried(ends, step_sum, rate, backward, sizes, collective_id):
    seqs, chans = step_sum.shape
    n = rate.shape[0]
    high = step_sum.astype(jnp.bfloat16)
    low = (step_sum - high.astype(jnp.float32)).astype(jnp.bfloat16)
    sent = padded_rows(jnp.concatenate([ends.astype(jnp.bfloat16), high, low], axis=0), 16)
    (gathered,) = link_gather([("seq", sent, 1)], sizes, collective_id, (backward, not backward))
    gathered = gathered.reshape(-1, *sent.shape)
    count = lax.axis_size("seq")
    place = lax.axis_index("seq")
    state = jnp.zeros((seqs, n, chans), jnp.float32)
    for step in range(count - 1):
        source = count - 1 - step if backward else step
        block = gathered[source].astype(jnp.float32)
        total = block[seqs * n : seqs * (n + 1)] + block[seqs * (n + 1) : seqs * (n + 2)]
        joined = jnp.exp2(total[:, None, :] * rate[None]) * state + block[: seqs * n].reshape(seqs, n, chans)
        state = jnp.where(source > place if backward else source < place, joined, state)
    return state.reshape(seqs * n, chans)


def local(sizes, resid_in, out_grad, row_lengths, norm_gain, in_weight, conv_weight, conv_bias, xproj_weight, dt_weight,
          dt_bias, a_log, skip_gain, out_weight):
    bf, f32 = jnp.bfloat16, jnp.float32
    seqs = lax.axis_size("stream")
    parts = lax.axis_size("seq")
    own = conv_bias.shape[0]
    own_feats = norm_gain.shape[0]
    chans = own * parts
    rank_dim = dt_weight.shape[0]
    state_dim = a_log.shape[1]
    proj_dim = xproj_weight.shape[1]
    length, feats = resid_in.shape[1:]
    tokens = seqs * length

    gain = norm_gain.astype(f32)
    scaled = (in_weight.astype(f32) * gain[:, None]).astype(bf).reshape(own_feats, 2, parts, seqs, own)
    scaled = scaled.transpose(1, 3, 0, 2, 4).reshape(2, seqs * own_feats, chans)
    packed = jnp.concatenate(
        [xproj_weight, dt_weight.T, a_log, conv_weight.T, conv_bias[:, None], dt_bias[:, None], skip_gain[:, None]],
        axis=1)
    residual = resid_in[0].astype(f32)
    cotangent = out_grad[0]
    inv_rms = lax.rsqrt(jnp.mean(residual * residual, axis=-1, keepdims=True) + EPSILON)
    unit_own = residual * inv_rms
    slots = row_lengths.shape[1]
    arrays = [
        ("stream", jnp.pad(row_lengths, ((0, 7), (0, -slots % 128))), 1), ("stream", unit_own.astype(bf), 4),
        ("seq", jnp.pad(packed, ((0, 0), (0, -packed.shape[1] % 128))), 1)]
    if own_feats % 16:
        mine = lax.all_to_all(scaled, "stream", 1, 1, tiled=True)
        gate_own = mine[1]
        lengths, unit, packed, in_conv = link_gather([*arrays, ("seq", mine[0], 1)], sizes, 1)
    else:
        in_conv, gate_own, lengths, unit, packed = link_open(scaled[0], scaled[1], arrays, sizes, 1)
    lengths = lengths[::8, :slots]
    unit, gate_own, out_own, cot_own = lax.optimization_barrier((unit, gate_own, out_weight, cotangent))
    in_gate = lax.all_gather(gate_own, "seq", axis=0, tiled=True)
    out_full = lax.all_gather(out_own, "seq", axis=0, tiled=True)
    cot_all = lax.all_gather(cot_own, "stream", axis=0, tiled=True)
    xproj_full = packed[:, :proj_dim]
    dtw_cols = packed[:, proj_dim : proj_dim + rank_dim]
    at = proj_dim + rank_dim
    log_rates = packed[:, at : at + state_dim].astype(f32).T
    at += state_dim
    conv_taps = packed[:, at : at + CONV].astype(f32).T
    at += CONV
    conv_shift, dt_shift, skip_vec = (packed[:, at + i].astype(f32) for i in range(3))
    rate = -jnp.exp(log_rates) / LN2

    rim = CONV - 1
    first_pos = lax.axis_index("seq") * length
    doc_ids, start_flags, valid_mask = jax.vmap(
        lambda row: token_layout(row, first_pos - rim, length + 2 * rim))(lengths)
    own_ids = doc_ids[:, rim : rim + length]
    starts = start_flags[:, rim : rim + length].reshape(tokens, 1)
    valid = valid_mask[:, rim : rim + length].reshape(tokens, 1)
    near = [doc_ids[:, tap : tap + length] == own_ids for tap in range(2 * rim + 1) if tap != rim]
    masks = jnp.pad(jnp.stack(near, axis=-1).astype(f32), ((0, 0), (0, 0), (0, 8 - 2 * rim))).reshape(tokens, 8)

    conv_in = jnp.dot(unit, in_conv, preferred_element_type=f32)
    gate_in = jnp.dot(unit, in_gate, preferred_element_type=f32)
    earlier = passed_along(conv_in.reshape(seqs, length, chans)[:, length - rim :].astype(bf), "seq", 1).astype(f32)
    earlier = jnp.pad(earlier, ((0, 0), (8 - rim, 0), (0, 0))).reshape(seqs * 8, chans)
    taps = jnp.pad(jnp.concatenate([conv_taps, conv_shift[None]]), ((0, 7 - CONV), (0, 0)))
    activated, slope = conv_fwd(conv_in, earlier, masks, taps, seqs)
    act_float = activated.astype(f32)
    projected = link_sum(
        lax.dot_general(xproj_full, activated, (((0,), (1,)), ((), ())), preferred_element_type=f32), sizes, 2)
    low_rank = projected[:rank_dim].astype(bf)
    write_in = projected[rank_dim : rank_dim + state_dim]
    readout = projected[rank_dim + state_dim :]
    dt_pre = lax.dot_general(low_rank, dtw_cols, (((0,), (1,)), ((), ())), preferred_element_type=f32) + dt_shift
    dt_step = jax.nn.softplus(dt_pre)
    dt_reset = jnp.where(starts > 0, RESET, dt_step)
    dt_act = dt_step * act_float
    write_slabs, read_slabs = slabs_of(write_in), slabs_of(readout)
    write_diag, read_diag = spread(write_in), spread(readout)

    step_sum = jnp.sum(dt_reset.reshape(seqs, length, chans), axis=1)
    ends = scan_end(fwd_end_body, dt_reset, dt_act, write_slabs, rate, seqs)
    start_state = carried(ends, step_sum, rate, False, sizes, 3)
    scanned, history = fwd_full(dt_reset, dt_act, write_slabs, read_diag, rate, start_state, seqs)
    ssm_out = scanned + skip_vec * act_float
    gate_act = jax.nn.silu(gate_in)
    gated = (ssm_out * gate_act * valid).astype(bf)
    product = jnp.dot(gated, out_full, preferred_element_type=f32).astype(bf)
    d_gated = contract_cols(cot_all, out_full)
    d_masked = d_gated * valid
    d_ssm = d_masked * gate_act
    d_gate = (d_masked * ssm_out * silu_slope(gate_in)).astype(bf)
    g_out = contract_rows(gated, cot_all).astype(bf)
    g_in_gate = contract_rows(unit, d_gate).astype(bf)
    d_ssm, product, g_out, g_in_gate = lax.optimization_barrier((d_ssm, product, g_out, g_in_gate))
    g_out = lax.psum_scatter(g_out, "seq", scatter_dimension=0, tiled=True)
    g_in_gate = lax.psum_scatter(g_in_gate, "seq", scatter_dimension=0, tiled=True)
    output = (residual + lax.psum_scatter(product, "stream", scatter_dimension=0, tiled=True).astype(f32)).astype(bf)
    g_skip = jnp.sum(d_ssm * act_float, axis=0)
    back_ends = scan_end(bwd_end_body, dt_reset, d_ssm, read_slabs, rate, seqs)
    later_sum = carried(back_ends, step_sum, rate, True, sizes, 4)
    sum_write, sum_rate, g_log, d_write, d_read = bwd_full(
        dt_reset, dt_act, d_ssm, history, read_slabs, write_diag, rate, later_sum, seqs)
    per_step = jnp.where(dt_step > 1e-30, sum_rate * LN2 / jnp.maximum(dt_step, 1e-30), 0.0)
    d_step = per_step + act_float * sum_write
    d_pre = d_step * jax.nn.sigmoid(dt_pre)
    g_dt_bias = jnp.sum(d_pre, axis=0)
    d_pre_low = d_pre.astype(bf)
    g_dt = lax.dot_general(d_pre_low, low_rank, (((0,), (1,)), ((), ())), preferred_element_type=f32)
    d_low = lax.dot_general(dtw_cols, d_pre_low, (((0,), (1,)), ((), ())), preferred_element_type=f32)
    d_proj = link_sum(jnp.concatenate([d_low, d_write, d_read], axis=0), sizes, 5).astype(bf)
    d_proj, g_out, g_in_gate = lax.optimization_barrier((d_proj, g_out, g_in_gate))
    g_xproj = lax.dot_general(activated, d_proj, (((0,), (1,)), ((), ())), preferred_element_type=f32)
    d_act = dt_step * sum_write + skip_vec * d_ssm + lax.dot_general(
        d_proj, xproj_full, (((0,), (1,)), ((), ())), preferred_element_type=f32)
    first = (d_act.reshape(seqs, length, chans)[:, :rim] * slope.reshape(seqs, length, chans)[:, :rim].astype(f32))
    later = passed_along(first.astype(bf), "seq", -1).astype(f32)
    later = jnp.pad(later, ((0, 0), (0, 8 - rim), (0, 0))).reshape(seqs * 8, chans)
    d_conv_in, sums = conv_bwd(d_act, slope, later, conv_in, masks, taps, seqs)
    sums = sums.reshape(seqs, 8, chans).sum(0)
    g_conv, g_conv_bias = sums[:CONV].T, sums[CONV]
    g_in_conv = contract_rows(unit, d_conv_in).astype(bf)
    d_unit = (contract_cols(d_conv_in, in_conv) + contract_cols(d_gate, in_gate)).astype(bf)
    def in_rows(block):
        shared = lax.all_to_all(block, "stream", 0, 0, tiled=True).reshape(seqs, own_feats, parts, own)
        return shared.transpose(1, 2, 0, 3).reshape(own_feats, parts * seqs * own)

    def padded_small(columns):
        joined = jnp.concatenate(columns, axis=1)
        return jnp.pad(joined, ((0, 0), (0, -joined.shape[1] % 128))).astype(bf)

    small = padded_small(
        [g_xproj, g_dt, g_log.T * LN2, g_dt_bias[:, None], g_skip[:, None], g_conv, g_conv_bias[:, None]])
    d_unit, g_in_gate, output, g_out = lax.optimization_barrier((d_unit, in_rows(g_in_gate), output, g_out))
    g_in_conv, small, d_unit = link_reduce(
        [("seq", g_in_conv, 2, 0 if own_feats % 16 else own), ("seq", small, 2, 0), ("stream", d_unit, 4, 0)], sizes, 6)
    small = small.astype(f32)
    d_unit = d_unit.astype(f32)
    in_grad = cotangent.astype(f32) + inv_rms * (d_unit - unit_own * jnp.mean(d_unit * unit_own, axis=-1, keepdims=True))

    g_in_conv = in_rows(g_in_conv) if own_feats % 16 else g_in_conv
    g_unit = jnp.concatenate([g_in_conv, g_in_gate], axis=1).astype(f32)
    at = proj_dim + rank_dim
    return (
        output[None],
        in_grad.astype(bf)[None],
        jnp.sum(g_unit * in_weight.astype(f32), axis=1),
        g_unit * gain[:, None],
        small[:, at + state_dim + 2 : at + state_dim + 2 + CONV].T,
        small[:, at + state_dim + 2 + CONV],
        small[:, :proj_dim],
        small[:, proj_dim:at].T,
        small[:, at + state_dim],
        small[:, at : at + state_dim],
        small[:, at + state_dim + 1],
        g_out.astype(f32),
    )


def lines_of(mesh):
    devices = mesh.devices
    places = [getattr(device, "coords", None) for device in devices[:, 0]]
    seq = len(places)
    plane = 1
    if all(place is not None for place in places):
        plane = len({tuple(place)[1] for place in places})
    if seq % plane:
        plane = 1
    return {"seq": (seq, plane), "stream": (devices.shape[1], 1 if devices.shape[1] % 2 else 2)}


def solution(mesh):
    in_specs = (
        P("stream", "seq", None),
        P("stream", "seq", None),
        P("stream", None),
        P(("seq", "stream")),
        P(("seq", "stream"), None),
        P(None, ("seq", "stream")),
        P(("seq", "stream")),
        P(("seq", "stream"), None),
        P(None, ("seq", "stream")),
        P(("seq", "stream")),
        P(("seq", "stream"), None),
        P(("seq", "stream")),
        P(("seq", "stream"), None),
    )
    out_specs = (
        P("stream", "seq", None),
        P("stream", "seq", None),
        P(("seq", "stream")),
        P(("seq", "stream"), None),
        P(None, ("seq", "stream")),
        P(("seq", "stream")),
        P(("seq", "stream"), None),
        P(None, ("seq", "stream")),
        P(("seq", "stream")),
        P(("seq", "stream"), None),
        P(("seq", "stream")),
        P(("seq", "stream"), None),
    )
    return jax.shard_map(functools.partial(local, lines_of(mesh)), mesh=mesh, in_specs=in_specs, out_specs=out_specs, check_vma=False)
```

```python
import functools

import jax
import jax.numpy as jnp
from jax import lax
from jax.experimental import pallas as pl
from jax.experimental.pallas import tpu as pltpu
from jax.sharding import PartitionSpec as P

CONV = 4
EPSILON = 1e-05
RESET = 1e30
GROUP = 16
LN2 = 0.6931471805599453
NT = (((1,), (1,)), ((), ()))
VMEM_LIMIT = 56 << 20
LINK_COST = 20_000_000_000


def across(slab, place, width):
    return jnp.concatenate([jnp.broadcast_to(slab[:, place : place + 1], (slab.shape[0], 128))] * (width // 128), axis=1)


def decays(dte_ref, rate_ref, at, buf, power_buf=None):
    n = rate_ref.shape[0]
    for place in range(GROUP):
        power = dte_ref[pl.ds(at * GROUP + place, 1), :] * rate_ref[...]
        buf[pl.ds(place * n, n), :] = jnp.exp2(power)
        if power_buf is not None:
            power_buf[pl.ds(place * n, n), :] = power.astype(jnp.bfloat16)


def fwd_end_body(dte_ref, dtx_ref, slab_ref, rate_ref, end_ref, even_ref, odd_ref):
    n, width = rate_ref.shape
    groups = dte_ref.shape[0] // GROUP

    def walk(at, state, decay_ref):
        slab = slab_ref[pl.ds(at * n, n), :]
        for place in range(GROUP):
            write = across(slab, place, width)
            state = decay_ref[pl.ds(place * n, n), :] * state + dtx_ref[pl.ds(at * GROUP + place, 1), :] * write
        return state

    def pair(step, state):
        decays(dte_ref, rate_ref, 2 * step + 1, odd_ref)
        state = walk(2 * step, state, even_ref)
        decays(dte_ref, rate_ref, jnp.minimum(2 * step + 2, groups - 1), even_ref)
        return walk(2 * step + 1, state, odd_ref)

    decays(dte_ref, rate_ref, 0, even_ref)
    end_ref[...] = lax.fori_loop(0, groups // 2, pair, jnp.zeros_like(end_ref))


def bwd_end_body(dte_ref, grad_ref, slab_ref, rate_ref, end_ref, even_ref, odd_ref):
    n, width = rate_ref.shape
    groups = dte_ref.shape[0] // GROUP

    def walk(at, state, decay_ref):
        slab = slab_ref[pl.ds(at * n, n), :]
        for place in reversed(range(GROUP)):
            read = across(slab, place, width)
            state = decay_ref[pl.ds(place * n, n), :] * (state + grad_ref[pl.ds(at * GROUP + place, 1), :] * read)
        return state

    def pair(step, state):
        at = groups - 1 - 2 * step
        decays(dte_ref, rate_ref, at - 1, odd_ref)
        state = walk(at, state, even_ref)
        decays(dte_ref, rate_ref, jnp.maximum(at - 2, 0), even_ref)
        return walk(at - 1, state, odd_ref)

    decays(dte_ref, rate_ref, groups - 1, even_ref)
    end_ref[...] = lax.fori_loop(0, groups // 2, pair, jnp.zeros_like(end_ref))


def scan_end(body, dte, other, slabs, rate, seqs, width=512):
    tokens, chans = dte.shape
    length = tokens // seqs
    n = rate.shape[0]
    width = min(width, chans)
    work = tokens * chans * n
    return pl.pallas_call(
        body,
        grid=(seqs, chans // width),
        in_specs=[
            pl.BlockSpec((length, width), lambda s, c: (s, c)),
            pl.BlockSpec((length, width), lambda s, c: (s, c)),
            pl.BlockSpec((length // GROUP * n, GROUP), lambda s, c: (s, 0)),
            pl.BlockSpec((n, width), lambda s, c: (0, c)),
        ],
        out_specs=pl.BlockSpec((n, width), lambda s, c: (s, c)),
        out_shape=jax.ShapeDtypeStruct((seqs * n, chans), jnp.float32),
        scratch_shapes=[pltpu.VMEM((GROUP * n, width), jnp.float32)] * 2,
        compiler_params=pltpu.CompilerParams(vmem_limit_bytes=VMEM_LIMIT),
        cost_estimate=pl.CostEstimate(flops=1000 * work, transcendentals=work, bytes_accessed=8 * tokens * chans),
        name=body.__name__[:7],
    )(dte, other, slabs, rate)


def fwd_full_body(dte_ref, dtx_ref, slab_ref, read_ref, rate_ref, start_ref, y_ref, hist_ref, h_ref, even_ref, odd_ref):
    block = dte_ref.shape[0]
    n, width = rate_ref.shape
    span = GROUP * n
    rate = rate_ref[...]

    @pl.when(pl.program_id(2) == 0)
    def _():
        h_ref[...] = start_ref[...]

    first = h_ref[...]
    hist_ref[pl.ds(0, n), :] = first.astype(jnp.bfloat16)

    def rows_out(at, buf):
        y_ref[pl.ds(at * GROUP, GROUP), :] = jnp.dot(
            read_ref[pl.ds(at * GROUP, GROUP), :], buf[...], preferred_element_type=jnp.float32)

    def group(at, state, buf):
        slab = slab_ref[pl.ds(at * n, n), :]
        for place in range(GROUP):
            t = at * GROUP + place
            write = across(slab, place, width)
            state = jnp.exp2(dte_ref[pl.ds(t, 1), :] * rate) * state + dtx_ref[pl.ds(t, 1), :] * write
            kept = state.astype(jnp.bfloat16)
            hist_ref[pl.ds((t + 1) * n, n), :] = kept
            buf[pl.ds(place * n, n), :] = kept
        return state

    def pair(step, state):
        at = 2 * step
        rows_out(jnp.maximum(at - 1, 0), odd_ref)
        state = group(at, state, even_ref)
        rows_out(at, even_ref)
        return group(at + 1, state, odd_ref)

    h_ref[...] = lax.fori_loop(0, block // GROUP // 2, pair, first)
    rows_out(block // GROUP - 1, odd_ref)


def fwd_full(dte, dtx, slabs, read, rate, start, seqs, width=512, block=256):
    tokens, chans = dte.shape
    n = rate.shape[0]
    width = min(width, chans)
    blocks = tokens // seqs // block
    work = tokens * chans * n
    here = lambda c, s, t: (s * blocks + t, c)
    rows = lambda c, s, t: (s * blocks + t, 0)
    return pl.pallas_call(
        fwd_full_body,
        grid=(chans // width, seqs, blocks),
        in_specs=[
            pl.BlockSpec((block, width), here),
            pl.BlockSpec((block, width), here),
            pl.BlockSpec((block // GROUP * n, GROUP), rows),
            pl.BlockSpec((block, read.shape[1]), rows),
            pl.BlockSpec((n, width), lambda c, s, t: (0, c)),
            pl.BlockSpec((n, width), lambda c, s, t: (s, c)),
        ],
        out_specs=[pl.BlockSpec((block, width), here), pl.BlockSpec(((block + 1) * n, width), here)],
        out_shape=[
            jax.ShapeDtypeStruct((tokens, chans), jnp.float32),
            jax.ShapeDtypeStruct((seqs * blocks * (block + 1) * n, chans), jnp.bfloat16),
        ],
        scratch_shapes=[pltpu.VMEM((n, width), jnp.float32)] + [pltpu.VMEM((GROUP * n, width), jnp.bfloat16)] * 2,
        compiler_params=pltpu.CompilerParams(vmem_limit_bytes=VMEM_LIMIT),
        cost_estimate=pl.CostEstimate(flops=1400 * work, transcendentals=work, bytes_accessed=2 * work),
        name="fwd_full",
    )(dte, dtx, slabs, read, rate, start)


def bwd_full_body(dte_ref, dtx_ref, grad_ref, hist_ref, slab_ref, write_ref, ones_ref, rate_ref, start_ref,
                  s1_ref, s2_ref, grate_ref, dw_ref, dr_ref, g_ref, *scratch):
    block = dte_ref.shape[0]
    n, width = rate_ref.shape
    groups = block // GROUP
    bf, f32 = jnp.bfloat16, jnp.float32
    even, odd = scratch[:5], scratch[5:]
    unit = jnp.ones((GROUP, 128), bf)

    @pl.when(pl.program_id(2) == 0)
    def _():
        g_ref[...] = start_ref[...]

    @pl.when((pl.program_id(2) == 0) & (pl.program_id(1) == 0))
    def _():
        grate_ref[...] = jnp.zeros_like(grate_ref)

    def sums_out(at, bufs):
        _, _, adj_ref, rated_ref, dw_part = bufs
        rows = pl.ds(at * GROUP, GROUP)
        s1_ref[rows, :] = jnp.dot(write_ref[rows, :], adj_ref[...], preferred_element_type=f32)
        sums = jnp.dot(ones_ref[...], rated_ref[...], preferred_element_type=f32)
        s2_ref[rows, :] = sums[:GROUP]
        dw_ref[pl.ds(at, 1), :] = lax.dot_general(unit, dw_part[...], NT, preferred_element_type=f32)[:1]
        reads = lax.dot_general(
            grad_ref[rows, :].astype(bf), hist_ref[pl.ds(n + at * GROUP * n, GROUP * n), :], NT,
            preferred_element_type=f32)
        own = lax.broadcasted_iota(jnp.int32, reads.shape, 1) // n == lax.broadcasted_iota(jnp.int32, reads.shape, 0)
        dr_ref[pl.ds(at, 1), :] = jnp.sum(jnp.where(own, reads, 0.0), axis=0, keepdims=True)
        return sums[GROUP:]

    def strips(values):
        parts = [values[:, k * 128 : (k + 1) * 128] for k in range(width // 128)]
        while len(parts) > 1:
            parts = [a + b for a, b in zip(parts[::2], parts[1::2])] + parts[len(parts) // 2 * 2 :]
        return parts[0]

    def walk(at, state, bufs):
        decay_ref, power_ref, adj_ref, rated_ref, dw_part = bufs
        slab = slab_ref[pl.ds(at * n, n), :]
        for place in reversed(range(GROUP)):
            t = at * GROUP + place
            here = pl.ds(place * n, n)
            read = across(slab, place, width)
            adjoint = state + grad_ref[pl.ds(t, 1), :] * read
            power = dte_ref[pl.ds(t, 1), :] * rate_ref[...]
            state = jnp.exp2(power) * adjoint
            low = adjoint.astype(bf)
            adj_ref[here, :] = low
            rated_ref[here, :] = state.astype(bf) * hist_ref[pl.ds(t * n, n), :] * power.astype(bf)
            dw_part[here, :] = strips(adjoint * dtx_ref[pl.ds(t, 1), :]).astype(bf)
        return state

    def pair(step, state):
        at = groups - 1 - 2 * step
        old = sums_out(jnp.minimum(at + 1, groups - 1), odd)
        state = walk(at, state, even)
        grate_ref[...] += jnp.where(step > 0, old, 0.0) + sums_out(at, even)
        return walk(at - 1, state, odd)
    g_ref[...] = lax.fori_loop(0, groups // 2, pair, g_ref[...])
    grate_ref[...] += sums_out(0, odd)


def bwd_full(dte, dtx, grad, hist, slabs, write, rate, start, seqs, width=512, block=256):
    tokens, chans = dte.shape
    n = rate.shape[0]
    width = min(width, chans)
    strips = chans // width
    blocks = tokens // seqs // block
    span = GROUP * n
    work = tokens * chans * n
    column = jnp.arange(span)
    ones = jnp.concatenate(
        [(column // n)[None, :] == jnp.arange(GROUP)[:, None], (column % n)[None, :] == jnp.arange(n)[:, None]]
    ).astype(jnp.bfloat16)
    here = lambda c, s, t: (s * blocks + blocks - 1 - t, c)
    rows = lambda c, s, t: (s * blocks + blocks - 1 - t, 0)
    strip = lambda c, s, t: (c * seqs * blocks + s * blocks + blocks - 1 - t, 0)
    f32 = jnp.float32
    s1, s2, grate, dw, dr = pl.pallas_call(
        bwd_full_body,
        grid=(strips, seqs, blocks),
        in_specs=[
            pl.BlockSpec((block, width), here),
            pl.BlockSpec((block, width), here),
            pl.BlockSpec((block, width), here),
            pl.BlockSpec(((block + 1) * n, width), here),
            pl.BlockSpec((block // GROUP * n, GROUP), rows),
            pl.BlockSpec((block, span), rows),
            pl.BlockSpec(ones.shape, lambda c, s, t: (0, 0)),
            pl.BlockSpec((n, width), lambda c, s, t: (0, c)),
            pl.BlockSpec((n, width), lambda c, s, t: (s, c)),
        ],
        out_specs=[
            pl.BlockSpec((block, width), here),
            pl.BlockSpec((block, width), here),
            pl.BlockSpec((n, width), lambda c, s, t: (0, c)),
            pl.BlockSpec((block // GROUP, span), strip),
            pl.BlockSpec((block // GROUP, span), strip),
        ],
        out_shape=[
            jax.ShapeDtypeStruct((tokens, chans), f32),
            jax.ShapeDtypeStruct((tokens, chans), f32),
            jax.ShapeDtypeStruct((n, chans), f32),
            jax.ShapeDtypeStruct((strips * tokens // GROUP, span), f32),
            jax.ShapeDtypeStruct((strips * tokens // GROUP, span), f32),
        ],
        scratch_shapes=[
            pltpu.VMEM((n, width), f32),
            *[
                pltpu.VMEM((span, width), f32),
                *[pltpu.VMEM((span, width), jnp.bfloat16)] * 3,
                pltpu.VMEM((span, 128), jnp.bfloat16),
            ] * 2,
        ],
        compiler_params=pltpu.CompilerParams(vmem_limit_bytes=VMEM_LIMIT),
        cost_estimate=pl.CostEstimate(flops=3200 * work, transcendentals=work, bytes_accessed=2 * work),
        name="bwd_full",
    )(dte, dtx, grad, hist, slabs, write, ones, rate, start)
    both = jnp.stack([part.reshape(strips, tokens // GROUP, span).sum(0) for part in (dw, dr)])
    both = both.reshape(2, tokens // GROUP, GROUP, n).transpose(0, 3, 1, 2).reshape(2, n, tokens)
    return s1, s2, grate, both[0], both[1]


def slabs_of(values):
    n, tokens = values.shape
    return values.reshape(n, tokens // GROUP, GROUP).transpose(1, 0, 2).reshape(tokens // GROUP * n, GROUP)


def spread(values):
    n, tokens = values.shape
    own = jnp.arange(tokens)[:, None] % GROUP == jnp.arange(GROUP)[None, :]
    return jnp.where(own[:, :, None], values.T[:, None, :], 0).reshape(tokens, GROUP * n).astype(jnp.bfloat16)


MESH = pl.DeviceIdType.MESH


class Grid:
    def __init__(self, axis, size, inner):
        self.axis, self.inner, self.outer = axis, inner, size // inner
        me = lax.axis_index(axis)
        self.row, self.col = me // inner, me % inner

    def device(self, row, col):
        return {self.axis: row * self.inner + col}

    def neighbours(self):
        row, col = self.row, self.col
        found = []
        if self.outer > 1:
            found += [(row > 0, self.device(row - 1, col)), (row < self.outer - 1, self.device(row + 1, col))]
        if self.inner > 1:
            found += [(col > 0, self.device(row, col - 1)), (col < self.inner - 1, self.device(row, col + 1))]
        return found

    def everyone(self):
        size = self.inner * self.outer
        me = self.row * self.inner + self.col
        return [(me >= 0, {self.axis: (me + step) % size}) for step in range(1, size)]


def greet(grids, all_of=()):
    barrier = pltpu.get_barrier_semaphore()
    count = 0
    for grid in grids:
        for there, device in grid.everyone() if grid.axis in all_of else grid.neighbours():

            @pl.when(there)
            def _(device=device):
                pl.semaphore_signal(barrier, inc=1, device_id=device, device_id_type=MESH)

            count = count + there.astype(jnp.int32)
    pl.semaphore_wait(barrier, count)


def gather_steps(grid, whole_ref, out_ref, send_sem, recv_sem, own, waits, chunk, chunks, across_too=True, ways=(True, True)):
    rows = whole_ref.shape[0]
    part = rows // chunks
    src_ref = whole_ref.at[pl.ds(chunk * part, part)]
    outer, inner = grid.outer, grid.inner if across_too else 1
    row, col = grid.row, grid.col

    def number(r, c):
        return r * inner + c if across_too else r

    def place(r, c):
        return pl.ds(pl.multiple_of(number(r, c) * rows + chunk * part, part), part)

    def send(there, way, r, c, device, source):
        copy = pltpu.make_async_remote_copy(
            src_ref=source, dst_ref=out_ref.at[place(r, c)], send_sem=send_sem.at[way, number(r, c)],
            recv_sem=recv_sem.at[number(r, c)], device_id=device, device_id_type=MESH)

        @pl.when(there)
        def _():
            copy.start()

        waits.append((there, copy))

    def across(there, r, c, source):
        if inner > 1:
            send(there & (c >= col) & (col > 0), 2, r, c, grid.device(row, col - 1), source)
            send(there & (c <= col) & (col < inner - 1), 3, r, c, grid.device(row, col + 1), source)

    def along(there, r, source):
        if outer > 1:
            if ways[0]:
                send(there & (r >= row) & (row > 0), 0, r, col, grid.device(row - 1, col), source)
            if ways[1]:
                send(there & (r <= row) & (row < outer - 1), 1, r, col, grid.device(row + 1, col), source)

    def arrive(there, r, c):
        copy = pltpu.make_async_remote_copy(
            src_ref=src_ref, dst_ref=out_ref.at[place(r, c)], send_sem=send_sem.at[0, 0],
            recv_sem=recv_sem.at[number(r, c)], device_id=grid.device(row, col), device_id_type=MESH)

        @pl.when(there)
        def _():
            copy.wait_recv()

    always = row >= 0
    along(always, row, src_ref)
    across(always, row, col, src_ref)
    own_sem, own_buf = own
    fetch = pltpu.make_async_copy(src_ref, own_buf, own_sem.at[0])
    fetch.start()
    for _ in range(chunk + 1):
        yield
    fetch.wait()
    keep = pltpu.make_async_copy(own_buf, out_ref.at[place(row, col)], own_sem.at[1])
    keep.start()
    waits.append((None, keep))

    def rows_at(distance):
        return [row - distance] * ways[1] + [row + distance] * ways[0]

    for distance in range(1, outer):
        for r in rows_at(distance):
            there = (r >= 0) & (r < outer)
            arrive(there, r, col)
            along(there, r, out_ref.at[place(r, col)])
            across(there, r, col, out_ref.at[place(r, col)])
        yield
    for step in range(1, inner):
        for distance in range(outer):
            for r in rows_at(distance) if distance else (row,):
                for c in (col - step, col + step):
                    there = (r >= 0) & (r < outer) & (c >= 0) & (c < inner)
                    arrive(there, r, c)
                    if step < inner - 1:
                        across(there, r, c, out_ref.at[place(r, c)])
            yield


def finish(waits):
    for there, copy in waits:
        if there is None:
            copy.wait()
        else:

            @pl.when(there)
            def _(copy=copy):
                if copy.is_remote:
                    copy.wait_send()
                else:
                    copy.wait()


def gather_scratch(size, array, chunks):
    dma = pltpu.SemaphoreType.DMA
    own = pltpu.VMEM((array.shape[0] // chunks, *array.shape[1:]), array.dtype)
    return [dma((4, size)), dma((size,)), dma((2,)), own] * chunks


def in_turn(runs):
    runs = list(runs)
    while runs:
        left = []
        for run in runs:
            if next(run, run) is not run:
                left.append(run)
        runs = left


def link_gather(arrays, sizes, collective_id, ways=(True, True)):
    count = len(arrays)
    axes = sorted({entry[0] for entry in arrays})

    def kernel(*refs):
        sources, outs, sems = refs[:count], refs[count : 2 * count], refs[2 * count :]
        grids = {axis: Grid(axis, *sizes[axis]) for axis in axes}
        greet([grids[axis] for axis in axes])
        waits = []
        runs = []
        for i, (axis, _, chunks) in enumerate(arrays):
            for chunk in range(chunks):
                runs.append(gather_steps(
                    grids[axis], sources[i], outs[i], sems[0], sems[1], sems[2:4], waits, chunk, chunks, ways=ways))
                sems = sems[4:]
        in_turn(runs)
        finish(waits)

    sems = []
    for axis, a, chunks in arrays:
        sems += gather_scratch(sizes[axis][0], a, chunks)
    return pl.pallas_call(
        kernel,
        in_specs=[pl.BlockSpec(memory_space=pl.ANY)] * count,
        out_specs=[pl.BlockSpec(memory_space=pl.ANY)] * count,
        out_shape=[
            jax.ShapeDtypeStruct((sizes[axis][0] * a.shape[0], *a.shape[1:]), a.dtype) for axis, a, _ in arrays],
        scratch_shapes=sems,
        compiler_params=pltpu.CompilerParams(
            collective_id=collective_id, has_side_effects=True, vmem_limit_bytes=VMEM_LIMIT),
        cost_estimate=pl.CostEstimate(flops=LINK_COST, transcendentals=0, bytes_accessed=0),
        name="link_gather",
    )(*[a for _, a, _ in arrays])


def reduce_steps(grid, src_ref, out_ref, scratch, waits, chunks, share):
    acc, inner_buf, outer_buf, load_sem, inner_send, inner_recv, outer_send, outer_recv, out_sem = scratch[:9]
    outer, inner = grid.outer, grid.inner
    row, col = grid.row, grid.col
    rows = acc.shape[0] // (outer * inner)
    part = rows // chunks
    piece = min(part, 64)

    def start_of(chunk, r, c):
        return pl.multiple_of((r * inner + c) * rows + chunk * part, part)

    def line(me, size, device, block, buf, send, recv):
        def from_low(target):
            return target if size > 2 else 0

        def from_high(target, owner):
            return jnp.where(target == owner, size, target) if size > 2 else 0

        def hop(there, target, onward, slot):
            copy = pltpu.make_async_remote_copy(
                src_ref=acc.at[pl.ds(block(target), part)], dst_ref=buf.at[slot], send_sem=send.at[target],
                recv_sem=recv.at[slot], device_id=device(onward), device_id_type=MESH)

            @pl.when(there)
            def _():
                copy.start()

            waits.append((there, copy))

        def up(there, target):
            hop(there & (target > me), target, me + 1, from_low(target))

        def down(there, target):
            hop(there & (target < me), target, me - 1, from_high(target, me - 1))

        def arrive(there, target, slot):
            at = block(target)
            copy = pltpu.make_async_remote_copy(
                src_ref=acc.at[pl.ds(at, part)], dst_ref=buf.at[slot], send_sem=send.at[target],
                recv_sem=recv.at[slot], device_id=device(me), device_id_type=MESH)

            @pl.when(there)
            def _():
                copy.wait_recv()

                @pl.loop(0, part // piece)
                def _(k):
                    here = pl.ds(pl.multiple_of(at + k * piece, piece), piece)
                    there_rows = pl.ds(pl.multiple_of(k * piece, piece), piece)
                    total = acc[here, :].astype(jnp.float32) + buf[slot, there_rows, :].astype(jnp.float32)
                    acc[here, :] = total.astype(acc.dtype)

        def begin(target):
            up(me == 0, target)
            down(me == size - 1, target)

        def go_on(target):
            arrive((me > 0) & (target >= me), target, from_low(target))
            arrive((me < size - 1) & (target <= me), target, from_high(target, me))
            if size > 2:
                up((me > 0) & (me < size - 1), target)
                down((me > 0) & (me < size - 1), target)

        return begin, go_on

    order = sorted(range(outer), key=lambda k: -abs(2 * k - outer + 1))
    pieces = [(chunk, r) for chunk in range(chunks) for r in order]
    loads = {}
    for chunk, r in pieces:
        loads[chunk, r] = [
            pltpu.make_async_copy(
                src_ref.at[pl.ds(start_of(chunk, r, c), part)], acc.at[pl.ds(start_of(chunk, r, c), part)],
                load_sem.at[chunk, r * inner + c])
            for c in range(inner)]
        for load in loads[chunk, r]:
            load.start()

    def inner_line(chunk, r):
        return line(
            col, inner, lambda c: grid.device(row, c), lambda t: start_of(chunk, r, t), inner_buf.at[chunk, r],
            inner_send.at[chunk, r], inner_recv.at[chunk, r])

    def outer_line(chunk):
        return line(
            row, outer, lambda r: grid.device(r, col), lambda t: start_of(chunk, t, col), outer_buf.at[chunk],
            outer_send.at[chunk], outer_recv.at[chunk])

    def inner_start(k):
        if k < len(pieces):
            for load in loads[pieces[k]]:
                load.wait()
            if inner > 1:
                for c in range(inner):
                    inner_line(*pieces[k])[0](c)

    def outer_rest(k):
        if 0 <= k < len(pieces):
            chunk, r = pieces[k]
            if outer > 1:
                outer_line(chunk)[1](r)
            if r == order[-1]:
                give(chunk)

    def give(chunk):
        first = start_of(chunk, row, col)
        if share is None:
            last = pltpu.make_async_copy(
                acc.at[pl.ds(first, part)], out_ref.at[pl.ds(chunk * part, part)], out_sem.at[chunk])
            last.start()
            waits.append((None, last))
            return
        other, strip, send_sem, recv_sem = share
        count, me = other.outer * other.inner, other.row * other.inner + other.col
        take = rows // count
        for mate in range(chunk * part // take, (chunk + 1) * part // take):
            for k in range(acc.shape[1] // strip):
                source = acc.at[
                    pl.ds(pl.multiple_of((row * inner + col) * rows + mate * take, take), take),
                    pl.ds(k * strip, strip)]
                target = out_ref.at[:, pl.ds(pl.multiple_of((k * count + me) * strip, strip), strip)]
                own = pltpu.make_async_copy(source, target, send_sem.at[mate, k])
                sent = pltpu.make_async_remote_copy(
                    src_ref=source, dst_ref=target, send_sem=send_sem.at[mate, k], recv_sem=recv_sem.at[me, k],
                    device_id={other.axis: mate}, device_id_type=MESH)

                @pl.when(mate == me)
                def _(own=own):
                    own.start()

                @pl.when(mate != me)
                def _(sent=sent):
                    sent.start()

                waits.append((mate != me, sent))
                waits.append((mate == me, own))

    window = 2
    for k in range(window):
        inner_start(k)
    yield
    for k in range(len(pieces)):
        inner_start(k + window)
        chunk, r = pieces[k]
        if inner > 1:
            for c in range(inner):
                inner_line(chunk, r)[1](c)
        if outer > 1:
            outer_line(chunk)[0](r)
        yield
        outer_rest(k - window)
        yield
    for k in range(len(pieces) - window, len(pieces)):
        outer_rest(k)
        yield
    if share is not None:
        other, strip, send_sem, recv_sem = share
        count, me = other.outer * other.inner, other.row * other.inner + other.col
        take = rows // count
        for mate in range(count):
            for k in range(acc.shape[1] // strip):
                copy = pltpu.make_async_remote_copy(
                    src_ref=acc.at[pl.ds(0, take), pl.ds(k * strip, strip)],
                    dst_ref=out_ref.at[:, pl.ds((k * count + mate) * strip, strip)], send_sem=send_sem.at[mate, k],
                    recv_sem=recv_sem.at[mate, k], device_id={other.axis: me}, device_id_type=MESH)

                @pl.when(mate != me)
                def _(copy=copy):
                    copy.wait_recv()


def link_reduce(arrays, sizes, collective_id):
    count = len(arrays)

    def kernel(*refs):
        sources, outs, scratch = refs[:count], refs[count : 2 * count], refs[2 * count :]
        grids = {axis: Grid(axis, *sizes[axis]) for axis in ("seq", "stream")}
        greet(list(grids.values()), ("stream",))
        waits = []
        runs = []
        for i, (axis, _, chunks, strip) in enumerate(arrays):
            share = (grids["stream"], strip, scratch[9], scratch[10]) if strip else None
            runs.append(reduce_steps(grids[axis], sources[i], outs[i], scratch[:9], waits, chunks, share))
            scratch = scratch[11 if strip else 9 :]
        in_turn(runs)
        finish(waits)

    scratch, shapes = [], []
    for axis, a, chunks, strip in arrays:
        size, inner = sizes[axis]
        outer = size // inner
        part = a.shape[0] // size // chunks
        slots = [n + 1 if n > 2 else 1 for n in (inner, outer)]
        dma = pltpu.SemaphoreType.DMA
        scratch += [
            pltpu.VMEM(a.shape, a.dtype),
            pltpu.VMEM((chunks, outer, slots[0], part, a.shape[1]), a.dtype),
            pltpu.VMEM((chunks, slots[1], part, a.shape[1]), a.dtype),
            dma((chunks, size)), dma((chunks, outer, inner)), dma((chunks, outer, slots[0])), dma((chunks, outer)),
            dma((chunks, slots[1])), dma((chunks,))]
        if strip:
            mates = sizes["stream"][0]
            shapes.append(jax.ShapeDtypeStruct((a.shape[0] // size // mates, a.shape[1] * mates), a.dtype))
            scratch += [dma((mates, a.shape[1] // strip))] * 2
        else:
            shapes.append(jax.ShapeDtypeStruct((a.shape[0] // size, a.shape[1]), a.dtype))
    return pl.pallas_call(
        kernel,
        in_specs=[pl.BlockSpec(memory_space=pl.ANY)] * count,
        out_specs=[pl.BlockSpec(memory_space=pl.ANY)] * count,
        out_shape=shapes,
        scratch_shapes=scratch,
        compiler_params=pltpu.CompilerParams(
            collective_id=collective_id, has_side_effects=True, vmem_limit_bytes=VMEM_LIMIT),
        cost_estimate=pl.CostEstimate(flops=4 * LINK_COST, transcendentals=0, bytes_accessed=0),
        name="link_reduce",
    )(*[entry[1] for entry in arrays])


def link_sum(partial, sizes, collective_id):
    rows, width = partial.shape
    size, inner = sizes["stream"]
    outer = size // inner
    assert inner == 2
    half = rows // 2
    bf, f32 = jnp.bfloat16, jnp.float32
    dma = pltpu.SemaphoreType.DMA

    def kernel(own_ref, out_ref, mate_buf, pair_ref, terms_ref, total_ref, send, recv, line_send, line_recv, own_sem, own_buf):
        grid = Grid("stream", size, inner)
        row, col = grid.row, grid.col
        greet([grid])
        mate = grid.device(row, 1 - col)
        mine = pl.ds(pl.multiple_of(col * half, half), half)
        swap = pltpu.make_async_remote_copy(
            src_ref=own_ref, dst_ref=mate_buf, send_sem=send.at[0], recv_sem=recv.at[0], device_id=mate,
            device_id_type=MESH)
        swap.start()
        swap.wait_recv()
        pair_ref[...] = (own_ref[mine, :].astype(f32) + mate_buf[mine, :].astype(f32)).astype(bf)
        waits = []
        line = Grid("stream", size, inner)
        in_turn([gather_steps(
            line, pair_ref, terms_ref, line_send, line_recv, (own_sem, own_buf), waits, 0, 1, across_too=False)])
        finish(waits)
        total = terms_ref[pl.ds(0, half), :].astype(f32)
        for r in range(1, outer):
            total = total + terms_ref[pl.ds(r * half, half), :].astype(f32)
        total_ref[...] = total
        out_ref[mine, :] = total
        swap_back = pltpu.make_async_remote_copy(
            src_ref=total_ref, dst_ref=out_ref.at[mine], send_sem=send.at[1], recv_sem=recv.at[1], device_id=mate,
            device_id_type=MESH)
        swap_back.start()
        theirs = pltpu.make_async_remote_copy(
            src_ref=total_ref, dst_ref=out_ref.at[pl.ds(pl.multiple_of((1 - col) * half, half), half)],
            send_sem=send.at[1], recv_sem=recv.at[1], device_id=mate, device_id_type=MESH)
        theirs.wait_recv()
        swap.wait_send()
        swap_back.wait_send()

    return pl.pallas_call(
        kernel,
        in_specs=[pl.BlockSpec(memory_space=pltpu.VMEM)],
        out_specs=pl.BlockSpec(memory_space=pltpu.VMEM),
        out_shape=jax.ShapeDtypeStruct((rows, width), f32),
        scratch_shapes=[
            pltpu.VMEM((rows, width), bf), pltpu.VMEM((half, width), bf), pltpu.VMEM((outer * half, width), bf),
            pltpu.VMEM((half, width), f32), dma((2,)), dma((2,)), dma((4, outer)), dma((outer,)), dma((2,)),
            pltpu.VMEM((half, width), bf)],
        compiler_params=pltpu.CompilerParams(
            collective_id=collective_id, has_side_effects=True, vmem_limit_bytes=VMEM_LIMIT),
        cost_estimate=pl.CostEstimate(flops=LINK_COST, transcendentals=0, bytes_accessed=0),
        name="link_sum",
    )(partial.astype(bf))


def link_open(conv, gate, arrays, sizes, collective_id):
    count = len(arrays)
    mates = sizes["stream"][0]
    take = conv.shape[0] // mates
    dma = pltpu.SemaphoreType.DMA

    def kernel(conv_ref, gate_ref, *refs):
        sources, refs = refs[:count], refs[count:]
        conv_all, conv_own, gate_own, outs, refs = *refs[:3], refs[3 : 3 + count], refs[3 + count :]
        hand_send, hand_recv, hand_buf, sems = refs[0], refs[1], refs[2], refs[3:]
        grids = {axis: Grid(axis, *sizes[axis]) for axis in ("seq", "stream")}
        greet(list(grids.values()), ("stream",))
        me = grids["stream"].row * grids["stream"].inner + grids["stream"].col
        waits = []

        def rows(mate):
            return pl.ds(pl.multiple_of(mate * take, take), take)

        def hand(kind, source, target):
            fetch = pltpu.make_async_copy(source.at[rows(me)], hand_buf.at[kind], hand_send.at[kind, 0])
            fetch.start()
            for step in range(1, mates):
                mate = (me + step) % mates
                copy = pltpu.make_async_remote_copy(
                    src_ref=source.at[rows(mate)], dst_ref=target.at[rows(me)], send_sem=hand_send.at[kind, step],
                    recv_sem=hand_recv.at[kind, step], device_id={"stream": mate}, device_id_type=MESH)
                copy.start()
                waits.append((me >= 0, copy))
            fetch.wait()
            keep = pltpu.make_async_copy(hand_buf.at[kind], target.at[rows(me)], hand_recv.at[kind, 0])
            keep.start()
            return keep

        def handed(kind, source, target, own):
            own.wait()
            for step in range(1, mates):
                mate = (me + mates - step) % mates
                pltpu.make_async_remote_copy(
                    src_ref=source.at[rows(me)], dst_ref=target.at[rows(mate)], send_sem=hand_send.at[kind, step],
                    recv_sem=hand_recv.at[kind, step], device_id={"stream": me}, device_id_type=MESH).wait_recv()

        own = hand(0, conv_ref, conv_own)

        def main():
            for i, (axis, _, chunks) in enumerate(arrays):
                for chunk in range(chunks):
                    at = 4 * (1 + sum(entry[2] for entry in arrays[:i]) + chunk)
                    yield gather_steps(
                        grids[axis], sources[i], outs[i], sems[at], sems[at + 1], sems[at + 2 : at + 4], waits, chunk,
                        chunks)

        runs = list(main())
        for run in runs:
            next(run)
        own_gate = hand(1, gate_ref, gate_own)
        handed(0, conv_ref, conv_own, own)
        first = gather_steps(grids["seq"], conv_own, conv_all, sems[0], sems[1], sems[2:4], waits, 0, 1)
        next(first)
        in_turn([first, *runs])
        handed(1, gate_ref, gate_own, own_gate)
        finish(waits)

    entries = [("seq", conv, 1), *arrays]
    sems = []
    for axis, a, chunks in entries:
        sems += gather_scratch(sizes[axis][0], a, chunks)
    result = pl.pallas_call(
        kernel,
        in_specs=[pl.BlockSpec(memory_space=pl.ANY)] * (count + 2),
        out_specs=[pl.BlockSpec(memory_space=pl.ANY)] * (count + 3),
        out_shape=[
            jax.ShapeDtypeStruct((sizes["seq"][0] * conv.shape[0], conv.shape[1]), conv.dtype),
            jax.ShapeDtypeStruct(conv.shape, conv.dtype),
            jax.ShapeDtypeStruct(gate.shape, gate.dtype),
            *[jax.ShapeDtypeStruct((sizes[axis][0] * a.shape[0], *a.shape[1:]), a.dtype) for axis, a, _ in arrays]],
        scratch_shapes=[
            dma((2, mates)), dma((2, mates)), pltpu.VMEM((2, take, conv.shape[1]), conv.dtype), *sems],
        compiler_params=pltpu.CompilerParams(
            collective_id=collective_id, has_side_effects=True, vmem_limit_bytes=VMEM_LIMIT),
        cost_estimate=pl.CostEstimate(flops=4 * LINK_COST, transcendentals=0, bytes_accessed=0),
        name="link_open",
    )(conv, gate, *[a for _, a, _ in arrays])
    return result[0], result[2], *result[3:]


ROWS = 128


def conv_fwd_body(x_ref, early_ref, masks_ref, taps_ref, act_ref, slope_ref, ext_ref):
    length = x_ref.shape[0]
    ext_ref[pl.ds(0, 8), :] = early_ref[...]

    @pl.loop(0, length // ROWS)
    def _(k):
        here = pl.ds(pl.multiple_of(k * ROWS, ROWS), ROWS)
        ext_ref[pl.ds(pl.multiple_of(k * ROWS + 8, 8), ROWS), :] = x_ref[here, :]
        window = ext_ref[pl.ds(pl.multiple_of(k * ROWS, ROWS), ROWS + 8), :]
        masks = masks_ref[here, :]
        total = taps_ref[CONV : CONV + 1, :] + taps_ref[CONV - 1 : CONV, :] * window[8:]
        for tap in range(CONV - 1):
            shift = 8 - (CONV - 1) + tap
            total = total + taps_ref[tap : tap + 1, :] * (window[shift : shift + ROWS] * masks[:, tap : tap + 1])
        gate = jax.nn.sigmoid(total)
        act_ref[here, :] = (total * gate).astype(act_ref.dtype)
        slope_ref[here, :] = (gate * (1.0 + total * (1.0 - gate))).astype(slope_ref.dtype)


def conv_bwd_body(grad_ref, slope_ref, late_ref, x_ref, masks_ref, taps_ref, out_ref, sums_ref, ext_ref):
    length, width = x_ref.shape
    ext_ref[pl.ds(length, 8), :] = late_ref[...]

    @pl.loop(0, length // ROWS)
    def _(k):
        here = pl.ds(pl.multiple_of(k * ROWS, ROWS), ROWS)
        ext_ref[here, :] = grad_ref[here, :] * slope_ref[here, :].astype(jnp.float32)

    def some(k, sums):
        start = pl.multiple_of(k * ROWS, ROWS)
        here = pl.ds(start, ROWS)
        window = ext_ref[pl.ds(start, ROWS + 8), :]
        masks = masks_ref[here, :]
        x = x_ref[here, :]
        total = jnp.zeros((ROWS, width), jnp.float32)
        parts = []
        for tap in range(CONV):
            ahead = CONV - 1 - tap
            term = window[ahead : ahead + ROWS]
            if ahead:
                term = term * masks[:, CONV - 2 + ahead : CONV - 1 + ahead]
            total = total + taps_ref[tap : tap + 1, :] * term
            parts.append((term * x).reshape(ROWS // 8, 8, width).sum(0))
        parts.append(window[:ROWS].reshape(ROWS // 8, 8, width).sum(0))
        out_ref[here, :] = total.astype(out_ref.dtype)
        return tuple(a + b for a, b in zip(sums, parts))

    sums = lax.fori_loop(0, length // ROWS, some, (jnp.zeros((8, width), jnp.float32),) * (CONV + 1))
    for tap in range(CONV + 1):
        sums_ref[tap : tap + 1, :] = jnp.sum(sums[tap], axis=0, keepdims=True)
    sums_ref[CONV + 1 :, :] = jnp.zeros((7 - CONV, width), jnp.float32)


def conv_fwd(x, early, masks, taps, seqs, width=1024):
    tokens, chans = x.shape
    width = min(width, chans)
    length = tokens // seqs
    block = pl.BlockSpec((length, width), lambda s, c: (s, c))
    return pl.pallas_call(
        conv_fwd_body,
        grid=(seqs, chans // width),
        in_specs=[
            block, pl.BlockSpec((8, width), lambda s, c: (s, c)), pl.BlockSpec((length, 8), lambda s, c: (s, 0)),
            pl.BlockSpec((8, width), lambda s, c: (0, c))],
        out_specs=[block, block],
        out_shape=[jax.ShapeDtypeStruct((tokens, chans), jnp.bfloat16)] * 2,
        scratch_shapes=[pltpu.VMEM((length + 8, width), jnp.float32)],
        compiler_params=pltpu.CompilerParams(vmem_limit_bytes=VMEM_LIMIT),
        cost_estimate=pl.CostEstimate(
            flops=4000 * tokens * chans, transcendentals=tokens * chans, bytes_accessed=8 * tokens * chans),
        name="conv_fwd",
    )(x, early, masks, taps)


def conv_bwd(grad, slope, late, x, masks, taps, seqs, width=512):
    tokens, chans = x.shape
    width = min(width, chans)
    length = tokens // seqs
    block = pl.BlockSpec((length, width), lambda s, c: (s, c))
    rim = pl.BlockSpec((8, width), lambda s, c: (s, c))
    return pl.pallas_call(
        conv_bwd_body,
        grid=(seqs, chans // width),
        in_specs=[
            block, block, rim, block, pl.BlockSpec((length, 8), lambda s, c: (s, 0)),
            pl.BlockSpec((8, width), lambda s, c: (0, c))],
        out_specs=[block, rim],
        out_shape=[
            jax.ShapeDtypeStruct((tokens, chans), jnp.bfloat16), jax.ShapeDtypeStruct((seqs * 8, chans), jnp.float32)],
        scratch_shapes=[pltpu.VMEM((length + 8, width), jnp.float32)],
        compiler_params=pltpu.CompilerParams(vmem_limit_bytes=VMEM_LIMIT),
        cost_estimate=pl.CostEstimate(
            flops=5000 * tokens * chans, transcendentals=0, bytes_accessed=12 * tokens * chans),
        name="conv_bwd",
    )(grad, slope, late, x, masks, taps)


def passed_along(block, axis, distance):
    devices = range(lax.axis_size(axis))
    route = [(i - distance, i) for i in devices if i - distance in devices]
    return lax.ppermute(block, axis, route)


def silu_slope(values_in):
    sigmoid_v = jax.nn.sigmoid(values_in)
    return sigmoid_v * (1.0 + values_in * (1.0 - sigmoid_v))


def token_layout(lengths, first_pos, n_tokens):
    doc_ends = jnp.cumsum(lengths)
    begins = doc_ends - lengths
    positions = first_pos + jnp.arange(n_tokens, dtype=jnp.int32)
    live_slot = (lengths > 0)[None, :]
    doc_ids = jnp.sum(((begins[None, :] <= positions[:, None]) & live_slot).astype(jnp.int32), axis=1)
    start_flags = jnp.sum(((begins[None, :] == positions[:, None]) & live_slot).astype(jnp.float32), axis=1)
    valid_mask = (positions < doc_ends[-1]).astype(jnp.float32)
    return (doc_ids, start_flags, valid_mask)


def contract_rows(left_mat, right_mat):
    return lax.dot_general(left_mat, right_mat, (((0,), (0,)), ((), ())), preferred_element_type=jnp.float32)


def contract_cols(left_mat, right_mat):
    return lax.dot_general(left_mat, right_mat, NT, preferred_element_type=jnp.float32)


def padded_rows(array, rows):
    return jnp.pad(array, ((0, -array.shape[0] % rows), (0, 0)))


def carried(ends, step_sum, rate, backward, sizes, collective_id):
    seqs, chans = step_sum.shape
    n = rate.shape[0]
    high = step_sum.astype(jnp.bfloat16)
    low = (step_sum - high.astype(jnp.float32)).astype(jnp.bfloat16)
    sent = padded_rows(jnp.concatenate([ends.astype(jnp.bfloat16), high, low], axis=0), 16)
    (gathered,) = link_gather([("seq", sent, 1)], sizes, collective_id, (backward, not backward))
    gathered = gathered.reshape(-1, *sent.shape)
    count = lax.axis_size("seq")
    place = lax.axis_index("seq")
    state = jnp.zeros((seqs, n, chans), jnp.float32)
    for step in range(count - 1):
        source = count - 1 - step if backward else step
        block = gathered[source].astype(jnp.float32)
        total = block[seqs * n : seqs * (n + 1)] + block[seqs * (n + 1) : seqs * (n + 2)]
        joined = jnp.exp2(total[:, None, :] * rate[None]) * state + block[: seqs * n].reshape(seqs, n, chans)
        state = jnp.where(source > place if backward else source < place, joined, state)
    return state.reshape(seqs * n, chans)


def local(sizes, resid_in, out_grad, row_lengths, norm_gain, in_weight, conv_weight, conv_bias, xproj_weight, dt_weight,
          dt_bias, a_log, skip_gain, out_weight):
    bf, f32 = jnp.bfloat16, jnp.float32
    seqs = lax.axis_size("stream")
    parts = lax.axis_size("seq")
    own = conv_bias.shape[0]
    own_feats = norm_gain.shape[0]
    chans = own * parts
    rank_dim = dt_weight.shape[0]
    state_dim = a_log.shape[1]
    proj_dim = xproj_weight.shape[1]
    length, feats = resid_in.shape[1:]
    tokens = seqs * length

    gain = norm_gain.astype(f32)
    scaled = (in_weight.astype(f32) * gain[:, None]).astype(bf).reshape(own_feats, 2, parts, seqs, own)
    scaled = scaled.transpose(1, 3, 0, 2, 4).reshape(2, seqs * own_feats, chans)
    packed = jnp.concatenate(
        [xproj_weight, dt_weight.T, a_log, conv_weight.T, conv_bias[:, None], dt_bias[:, None], skip_gain[:, None]],
        axis=1)
    residual = resid_in[0].astype(f32)
    cotangent = out_grad[0]
    inv_rms = lax.rsqrt(jnp.mean(residual * residual, axis=-1, keepdims=True) + EPSILON)
    unit_own = residual * inv_rms
    slots = row_lengths.shape[1]
    arrays = [
        ("stream", jnp.pad(row_lengths, ((0, 7), (0, -slots % 128))), 1), ("stream", unit_own.astype(bf), 4),
        ("seq", jnp.pad(packed, ((0, 0), (0, -packed.shape[1] % 128))), 1)]
    if own_feats % 16:
        mine = lax.all_to_all(scaled, "stream", 1, 1, tiled=True)
        gate_own = mine[1]
        lengths, unit, packed, in_conv = link_gather([*arrays, ("seq", mine[0], 1)], sizes, 1)
    else:
        in_conv, gate_own, lengths, unit, packed = link_open(scaled[0], scaled[1], arrays, sizes, 1)
    lengths = lengths[::8, :slots]
    unit, gate_own, out_own, cot_own = lax.optimization_barrier((unit, gate_own, out_weight, cotangent))
    in_gate = lax.all_gather(gate_own, "seq", axis=0, tiled=True)
    out_full = lax.all_gather(out_own, "seq", axis=0, tiled=True)
    cot_all = lax.all_gather(cot_own, "stream", axis=0, tiled=True)
    xproj_full = packed[:, :proj_dim]
    dtw_cols = packed[:, proj_dim : proj_dim + rank_dim]
    at = proj_dim + rank_dim
    log_rates = packed[:, at : at + state_dim].astype(f32).T
    at += state_dim
    conv_taps = packed[:, at : at + CONV].astype(f32).T
    at += CONV
    conv_shift, dt_shift, skip_vec = (packed[:, at + i].astype(f32) for i in range(3))
    rate = -jnp.exp(log_rates) / LN2

    rim = CONV - 1
    first_pos = lax.axis_index("seq") * length
    doc_ids, start_flags, valid_mask = jax.vmap(
        lambda row: token_layout(row, first_pos - rim, length + 2 * rim))(lengths)
    own_ids = doc_ids[:, rim : rim + length]
    starts = start_flags[:, rim : rim + length].reshape(tokens, 1)
    valid = valid_mask[:, rim : rim + length].reshape(tokens, 1)
    near = [doc_ids[:, tap : tap + length] == own_ids for tap in range(2 * rim + 1) if tap != rim]
    masks = jnp.pad(jnp.stack(near, axis=-1).astype(f32), ((0, 0), (0, 0), (0, 8 - 2 * rim))).reshape(tokens, 8)

    last_rows = unit.reshape(seqs, length, feats)[:, length - 16 :].reshape(seqs * 16, feats)
    last_rows = jnp.dot(last_rows, in_conv, preferred_element_type=f32).reshape(seqs, 16, chans)[:, 16 - rim :]
    last_rows, unit_main = lax.optimization_barrier((last_rows.astype(bf), unit))
    earlier = passed_along(last_rows, "seq", 1).astype(f32)
    conv_in = jnp.dot(unit_main, in_conv, preferred_element_type=f32)
    gate_in = jnp.dot(unit, in_gate, preferred_element_type=f32)
    earlier = jnp.pad(earlier, ((0, 0), (8 - rim, 0), (0, 0))).reshape(seqs * 8, chans)
    taps = jnp.pad(jnp.concatenate([conv_taps, conv_shift[None]]), ((0, 7 - CONV), (0, 0)))
    activated, slope = conv_fwd(conv_in, earlier, masks, taps, seqs)
    act_float = activated.astype(f32)
    projected = link_sum(
        lax.dot_general(xproj_full, activated, (((0,), (1,)), ((), ())), preferred_element_type=f32), sizes, 2)
    low_rank = projected[:rank_dim].astype(bf)
    write_in = projected[rank_dim : rank_dim + state_dim]
    readout = projected[rank_dim + state_dim :]
    dt_pre = lax.dot_general(low_rank, dtw_cols, (((0,), (1,)), ((), ())), preferred_element_type=f32) + dt_shift
    dt_step = jax.nn.softplus(dt_pre)
    dt_reset = jnp.where(starts > 0, RESET, dt_step)
    dt_act = dt_step * act_float
    write_slabs, read_slabs = slabs_of(write_in), slabs_of(readout)
    write_diag, read_diag = spread(write_in), spread(readout)

    step_sum = jnp.sum(dt_reset.reshape(seqs, length, chans), axis=1)
    ends = scan_end(fwd_end_body, dt_reset, dt_act, write_slabs, rate, seqs)
    start_state = carried(ends, step_sum, rate, False, sizes, 3)
    scanned, history = fwd_full(dt_reset, dt_act, write_slabs, read_diag, rate, start_state, seqs)
    ssm_out = scanned + skip_vec * act_float
    gate_act = jax.nn.silu(gate_in)
    gated = (ssm_out * gate_act * valid).astype(bf)
    product = jnp.dot(gated, out_full, preferred_element_type=f32).astype(bf)
    d_gated = contract_cols(cot_all, out_full)
    d_masked = d_gated * valid
    d_ssm = d_masked * gate_act
    d_gate = (d_masked * ssm_out * silu_slope(gate_in)).astype(bf)
    g_out = contract_rows(gated, cot_all).astype(bf)
    g_in_gate = contract_rows(unit, d_gate).astype(bf)
    d_ssm, product, g_out, g_in_gate = lax.optimization_barrier((d_ssm, product, g_out, g_in_gate))
    g_out = lax.psum_scatter(g_out, "seq", scatter_dimension=0, tiled=True)
    g_in_gate = lax.psum_scatter(g_in_gate, "seq", scatter_dimension=0, tiled=True)
    output = (residual + lax.psum_scatter(product, "stream", scatter_dimension=0, tiled=True).astype(f32)).astype(bf)
    g_skip = jnp.sum(d_ssm * act_float, axis=0)
    back_ends = scan_end(bwd_end_body, dt_reset, d_ssm, read_slabs, rate, seqs)
    later_sum = carried(back_ends, step_sum, rate, True, sizes, 4)
    sum_write, sum_rate, g_log, d_write, d_read = bwd_full(
        dt_reset, dt_act, d_ssm, history, read_slabs, write_diag, rate, later_sum, seqs)
    per_step = jnp.where(dt_step > 1e-30, sum_rate * LN2 / jnp.maximum(dt_step, 1e-30), 0.0)
    d_step = per_step + act_float * sum_write
    d_pre = d_step * jax.nn.sigmoid(dt_pre)
    g_dt_bias = jnp.sum(d_pre, axis=0)
    d_pre_low = d_pre.astype(bf)
    g_dt = lax.dot_general(d_pre_low, low_rank, (((0,), (1,)), ((), ())), preferred_element_type=f32)
    d_low = lax.dot_general(dtw_cols, d_pre_low, (((0,), (1,)), ((), ())), preferred_element_type=f32)
    d_proj = link_sum(jnp.concatenate([d_low, d_write, d_read], axis=0), sizes, 5).astype(bf)
    d_proj, g_out, g_in_gate = lax.optimization_barrier((d_proj, g_out, g_in_gate))
    g_xproj = lax.dot_general(activated, d_proj, (((0,), (1,)), ((), ())), preferred_element_type=f32)
    d_act = dt_step * sum_write + skip_vec * d_ssm + lax.dot_general(
        d_proj, xproj_full, (((0,), (1,)), ((), ())), preferred_element_type=f32)
    first = (d_act.reshape(seqs, length, chans)[:, :rim] * slope.reshape(seqs, length, chans)[:, :rim].astype(f32))
    later = passed_along(first.astype(bf), "seq", -1).astype(f32)
    later, gate_part = lax.optimization_barrier((later, contract_cols(d_gate, in_gate)))
    later = jnp.pad(later, ((0, 0), (0, 8 - rim), (0, 0))).reshape(seqs * 8, chans)
    d_conv_in, sums = conv_bwd(d_act, slope, later, conv_in, masks, taps, seqs)
    sums = sums.reshape(seqs, 8, chans).sum(0)
    g_conv, g_conv_bias = sums[:CONV].T, sums[CONV]
    g_in_conv = contract_rows(unit, d_conv_in).astype(bf)
    d_unit = (contract_cols(d_conv_in, in_conv) + gate_part).astype(bf)
    def in_rows(block):
        shared = lax.all_to_all(block, "stream", 0, 0, tiled=True).reshape(seqs, own_feats, parts, own)
        return shared.transpose(1, 2, 0, 3).reshape(own_feats, parts * seqs * own)

    def padded_small(columns):
        joined = jnp.concatenate(columns, axis=1)
        return jnp.pad(joined, ((0, 0), (0, -joined.shape[1] % 128))).astype(bf)

    small = padded_small(
        [g_xproj, g_dt, g_log.T * LN2, g_dt_bias[:, None], g_skip[:, None], g_conv, g_conv_bias[:, None]])
    d_unit, g_in_gate, output, g_out = lax.optimization_barrier((d_unit, in_rows(g_in_gate), output, g_out))
    g_in_conv, small, d_unit = link_reduce(
        [("seq", g_in_conv, 2, 0 if own_feats % 16 else own), ("seq", small, 2, 0), ("stream", d_unit, 4, 0)], sizes, 6)
    small = small.astype(f32)
    d_unit = d_unit.astype(f32)
    in_grad = cotangent.astype(f32) + inv_rms * (d_unit - unit_own * jnp.mean(d_unit * unit_own, axis=-1, keepdims=True))

    g_in_conv = in_rows(g_in_conv) if own_feats % 16 else g_in_conv
    g_unit = jnp.concatenate([g_in_conv, g_in_gate], axis=1).astype(f32)
    at = proj_dim + rank_dim
    return (
        output[None],
        in_grad.astype(bf)[None],
        jnp.sum(g_unit * in_weight.astype(f32), axis=1),
        g_unit * gain[:, None],
        small[:, at + state_dim + 2 : at + state_dim + 2 + CONV].T,
        small[:, at + state_dim + 2 + CONV],
        small[:, :proj_dim],
        small[:, proj_dim:at].T,
        small[:, at + state_dim],
        small[:, at : at + state_dim],
        small[:, at + state_dim + 1],
        g_out.astype(f32),
    )


def lines_of(mesh):
    devices = mesh.devices
    places = [getattr(device, "coords", None) for device in devices[:, 0]]
    seq = len(places)
    plane = 1
    if all(place is not None for place in places):
        plane = len({tuple(place)[1] for place in places})
    if seq % plane:
        plane = 1
    return {"seq": (seq, plane), "stream": (devices.shape[1], 1 if devices.shape[1] % 2 else 2)}


def solution(mesh):
    in_specs = (
        P("stream", "seq", None),
        P("stream", "seq", None),
        P("stream", None),
        P(("seq", "stream")),
        P(("seq", "stream"), None),
        P(None, ("seq", "stream")),
        P(("seq", "stream")),
        P(("seq", "stream"), None),
        P(None, ("seq", "stream")),
        P(("seq", "stream")),
        P(("seq", "stream"), None),
        P(("seq", "stream")),
        P(("seq", "stream"), None),
    )
    out_specs = (
        P("stream", "seq", None),
        P("stream", "seq", None),
        P(("seq", "stream")),
        P(("seq", "stream"), None),
        P(None, ("seq", "stream")),
        P(("seq", "stream")),
        P(("seq", "stream"), None),
        P(None, ("seq", "stream")),
        P(("seq", "stream")),
        P(("seq", "stream"), None),
        P(("seq", "stream")),
        P(("seq", "stream"), None),
    )
    return jax.shard_map(functools.partial(local, lines_of(mesh)), mesh=mesh, in_specs=in_specs, out_specs=out_specs, check_vma=False)
```

```python
import functools

import jax
import jax.numpy as jnp
from jax import lax
from jax.experimental import pallas as pl
from jax.experimental.pallas import tpu as pltpu
from jax.sharding import PartitionSpec as P

CONV = 4
EPSILON = 1e-05
RESET = 1e30
GROUP = 16
LN2 = 0.6931471805599453
NT = (((1,), (1,)), ((), ()))
VMEM_LIMIT = 56 << 20
LINK_COST = 20_000_000_000


def across(slab, place, width):
    return jnp.concatenate([jnp.broadcast_to(slab[:, place : place + 1], (slab.shape[0], 128))] * (width // 128), axis=1)


def decays(dte_ref, rate_ref, at, buf, power_buf=None):
    n = rate_ref.shape[0]
    for place in range(GROUP):
        power = dte_ref[pl.ds(at * GROUP + place, 1), :] * rate_ref[...]
        buf[pl.ds(place * n, n), :] = jnp.exp2(power)
        if power_buf is not None:
            power_buf[pl.ds(place * n, n), :] = power.astype(jnp.bfloat16)


def fwd_end_body(dte_ref, dtx_ref, slab_ref, rate_ref, end_ref, even_ref, odd_ref):
    n, width = rate_ref.shape
    groups = dte_ref.shape[0] // GROUP

    def walk(at, state, decay_ref):
        slab = slab_ref[pl.ds(at * n, n), :]
        for place in range(GROUP):
            write = across(slab, place, width)
            state = decay_ref[pl.ds(place * n, n), :] * state + dtx_ref[pl.ds(at * GROUP + place, 1), :] * write
        return state

    def pair(step, state):
        decays(dte_ref, rate_ref, 2 * step + 1, odd_ref)
        state = walk(2 * step, state, even_ref)
        decays(dte_ref, rate_ref, jnp.minimum(2 * step + 2, groups - 1), even_ref)
        return walk(2 * step + 1, state, odd_ref)

    decays(dte_ref, rate_ref, 0, even_ref)
    end_ref[...] = lax.fori_loop(0, groups // 2, pair, jnp.zeros_like(end_ref))


def bwd_end_body(dte_ref, grad_ref, slab_ref, rate_ref, end_ref, even_ref, odd_ref):
    n, width = rate_ref.shape
    groups = dte_ref.shape[0] // GROUP

    def walk(at, state, decay_ref):
        slab = slab_ref[pl.ds(at * n, n), :]
        for place in reversed(range(GROUP)):
            read = across(slab, place, width)
            state = decay_ref[pl.ds(place * n, n), :] * (state + grad_ref[pl.ds(at * GROUP + place, 1), :] * read)
        return state

    def pair(step, state):
        at = groups - 1 - 2 * step
        decays(dte_ref, rate_ref, at - 1, odd_ref)
        state = walk(at, state, even_ref)
        decays(dte_ref, rate_ref, jnp.maximum(at - 2, 0), even_ref)
        return walk(at - 1, state, odd_ref)

    decays(dte_ref, rate_ref, groups - 1, even_ref)
    end_ref[...] = lax.fori_loop(0, groups // 2, pair, jnp.zeros_like(end_ref))


def scan_end(body, dte, other, slabs, rate, seqs, width=512):
    tokens, chans = dte.shape
    length = tokens // seqs
    n = rate.shape[0]
    width = min(width, chans)
    work = tokens * chans * n
    return pl.pallas_call(
        body,
        grid=(seqs, chans // width),
        in_specs=[
            pl.BlockSpec((length, width), lambda s, c: (s, c)),
            pl.BlockSpec((length, width), lambda s, c: (s, c)),
            pl.BlockSpec((length // GROUP * n, GROUP), lambda s, c: (s, 0)),
            pl.BlockSpec((n, width), lambda s, c: (0, c)),
        ],
        out_specs=pl.BlockSpec((n, width), lambda s, c: (s, c)),
        out_shape=jax.ShapeDtypeStruct((seqs * n, chans), jnp.float32),
        scratch_shapes=[pltpu.VMEM((GROUP * n, width), jnp.float32)] * 2,
        compiler_params=pltpu.CompilerParams(vmem_limit_bytes=VMEM_LIMIT),
        cost_estimate=pl.CostEstimate(flops=1000 * work, transcendentals=work, bytes_accessed=8 * tokens * chans),
        name=body.__name__[:7],
    )(dte, other, slabs, rate)


def fwd_full_body(dte_ref, dtx_ref, slab_ref, read_ref, rate_ref, start_ref, y_ref, hist_ref, h_ref, even_ref, odd_ref):
    block = dte_ref.shape[0]
    n, width = rate_ref.shape
    span = GROUP * n
    rate = rate_ref[...]

    @pl.when(pl.program_id(2) == 0)
    def _():
        h_ref[...] = start_ref[...]

    first = h_ref[...]
    hist_ref[pl.ds(0, n), :] = first.astype(jnp.bfloat16)

    def rows_out(at, buf):
        y_ref[pl.ds(at * GROUP, GROUP), :] = jnp.dot(
            read_ref[pl.ds(at * GROUP, GROUP), :], buf[...], preferred_element_type=jnp.float32)

    def group(at, state, buf):
        slab = slab_ref[pl.ds(at * n, n), :]
        for place in range(GROUP):
            t = at * GROUP + place
            write = across(slab, place, width)
            state = jnp.exp2(dte_ref[pl.ds(t, 1), :] * rate) * state + dtx_ref[pl.ds(t, 1), :] * write
            kept = state.astype(jnp.bfloat16)
            hist_ref[pl.ds((t + 1) * n, n), :] = kept
            buf[pl.ds(place * n, n), :] = kept
        return state

    def pair(step, state):
        at = 2 * step
        rows_out(jnp.maximum(at - 1, 0), odd_ref)
        state = group(at, state, even_ref)
        rows_out(at, even_ref)
        return group(at + 1, state, odd_ref)

    h_ref[...] = lax.fori_loop(0, block // GROUP // 2, pair, first)
    rows_out(block // GROUP - 1, odd_ref)


def fwd_full(dte, dtx, slabs, read, rate, start, seqs, width=512, block=256):
    tokens, chans = dte.shape
    n = rate.shape[0]
    width = min(width, chans)
    blocks = tokens // seqs // block
    work = tokens * chans * n
    here = lambda c, s, t: (s * blocks + t, c)
    rows = lambda c, s, t: (s * blocks + t, 0)
    return pl.pallas_call(
        fwd_full_body,
        grid=(chans // width, seqs, blocks),
        in_specs=[
            pl.BlockSpec((block, width), here),
            pl.BlockSpec((block, width), here),
            pl.BlockSpec((block // GROUP * n, GROUP), rows),
            pl.BlockSpec((block, read.shape[1]), rows),
            pl.BlockSpec((n, width), lambda c, s, t: (0, c)),
            pl.BlockSpec((n, width), lambda c, s, t: (s, c)),
        ],
        out_specs=[pl.BlockSpec((block, width), here), pl.BlockSpec(((block + 1) * n, width), here)],
        out_shape=[
            jax.ShapeDtypeStruct((tokens, chans), jnp.float32),
            jax.ShapeDtypeStruct((seqs * blocks * (block + 1) * n, chans), jnp.bfloat16),
        ],
        scratch_shapes=[pltpu.VMEM((n, width), jnp.float32)] + [pltpu.VMEM((GROUP * n, width), jnp.bfloat16)] * 2,
        compiler_params=pltpu.CompilerParams(vmem_limit_bytes=VMEM_LIMIT),
        cost_estimate=pl.CostEstimate(flops=1400 * work, transcendentals=work, bytes_accessed=2 * work),
        name="fwd_full",
    )(dte, dtx, slabs, read, rate, start)


def bwd_full_body(dte_ref, dtx_ref, grad_ref, hist_ref, slab_ref, write_ref, ones_ref, rate_ref, start_ref,
                  s1_ref, s2_ref, grate_ref, dw_ref, dr_ref, g_ref, *scratch):
    block = dte_ref.shape[0]
    n, width = rate_ref.shape
    groups = block // GROUP
    bf, f32 = jnp.bfloat16, jnp.float32
    even, odd = scratch[:5], scratch[5:]
    unit = jnp.ones((GROUP, 128), bf)

    @pl.when(pl.program_id(2) == 0)
    def _():
        g_ref[...] = start_ref[...]

    @pl.when((pl.program_id(2) == 0) & (pl.program_id(1) == 0))
    def _():
        grate_ref[...] = jnp.zeros_like(grate_ref)

    def sums_out(at, bufs):
        _, _, adj_ref, rated_ref, dw_part = bufs
        rows = pl.ds(at * GROUP, GROUP)
        s1_ref[rows, :] = jnp.dot(write_ref[rows, :], adj_ref[...], preferred_element_type=f32)
        sums = jnp.dot(ones_ref[...], rated_ref[...], preferred_element_type=f32)
        s2_ref[rows, :] = sums[:GROUP]
        dw_ref[pl.ds(at, 1), :] = lax.dot_general(unit, dw_part[...], NT, preferred_element_type=f32)[:1]
        reads = lax.dot_general(
            grad_ref[rows, :].astype(bf), hist_ref[pl.ds(n + at * GROUP * n, GROUP * n), :], NT,
            preferred_element_type=f32)
        own = lax.broadcasted_iota(jnp.int32, reads.shape, 1) // n == lax.broadcasted_iota(jnp.int32, reads.shape, 0)
        dr_ref[pl.ds(at, 1), :] = jnp.sum(jnp.where(own, reads, 0.0), axis=0, keepdims=True)
        return sums[GROUP:]

    def strips(values):
        parts = [values[:, k * 128 : (k + 1) * 128] for k in range(width // 128)]
        while len(parts) > 1:
            parts = [a + b for a, b in zip(parts[::2], parts[1::2])] + parts[len(parts) // 2 * 2 :]
        return parts[0]

    def walk(at, state, bufs):
        decay_ref, power_ref, adj_ref, rated_ref, dw_part = bufs
        slab = slab_ref[pl.ds(at * n, n), :]
        for place in reversed(range(GROUP)):
            t = at * GROUP + place
            here = pl.ds(place * n, n)
            read = across(slab, place, width)
            adjoint = state + grad_ref[pl.ds(t, 1), :] * read
            power = dte_ref[pl.ds(t, 1), :] * rate_ref[...]
            state = jnp.exp2(power) * adjoint
            low = adjoint.astype(bf)
            adj_ref[here, :] = low
            rated_ref[here, :] = state.astype(bf) * hist_ref[pl.ds(t * n, n), :] * power.astype(bf)
            dw_part[here, :] = strips(adjoint * dtx_ref[pl.ds(t, 1), :]).astype(bf)
        return state

    def pair(step, state):
        at = groups - 1 - 2 * step
        old = sums_out(jnp.minimum(at + 1, groups - 1), odd)
        state = walk(at, state, even)
        grate_ref[...] += jnp.where(step > 0, old, 0.0) + sums_out(at, even)
        return walk(at - 1, state, odd)
    g_ref[...] = lax.fori_loop(0, groups // 2, pair, g_ref[...])
    grate_ref[...] += sums_out(0, odd)


def bwd_full(dte, dtx, grad, hist, slabs, write, rate, start, seqs, width=512, block=256):
    tokens, chans = dte.shape
    n = rate.shape[0]
    width = min(width, chans)
    strips = chans // width
    blocks = tokens // seqs // block
    span = GROUP * n
    work = tokens * chans * n
    column = jnp.arange(span)
    ones = jnp.concatenate(
        [(column // n)[None, :] == jnp.arange(GROUP)[:, None], (column % n)[None, :] == jnp.arange(n)[:, None]]
    ).astype(jnp.bfloat16)
    here = lambda c, s, t: (s * blocks + blocks - 1 - t, c)
    rows = lambda c, s, t: (s * blocks + blocks - 1 - t, 0)
    strip = lambda c, s, t: (c * seqs * blocks + s * blocks + blocks - 1 - t, 0)
    f32 = jnp.float32
    s1, s2, grate, dw, dr = pl.pallas_call(
        bwd_full_body,
        grid=(strips, seqs, blocks),
        in_specs=[
            pl.BlockSpec((block, width), here),
            pl.BlockSpec((block, width), here),
            pl.BlockSpec((block, width), here),
            pl.BlockSpec(((block + 1) * n, width), here),
            pl.BlockSpec((block // GROUP * n, GROUP), rows),
            pl.BlockSpec((block, span), rows),
            pl.BlockSpec(ones.shape, lambda c, s, t: (0, 0)),
            pl.BlockSpec((n, width), lambda c, s, t: (0, c)),
            pl.BlockSpec((n, width), lambda c, s, t: (s, c)),
        ],
        out_specs=[
            pl.BlockSpec((block, width), here),
            pl.BlockSpec((block, width), here),
            pl.BlockSpec((n, width), lambda c, s, t: (0, c)),
            pl.BlockSpec((block // GROUP, span), strip),
            pl.BlockSpec((block // GROUP, span), strip),
        ],
        out_shape=[
            jax.ShapeDtypeStruct((tokens, chans), f32),
            jax.ShapeDtypeStruct((tokens, chans), f32),
            jax.ShapeDtypeStruct((n, chans), f32),
            jax.ShapeDtypeStruct((strips * tokens // GROUP, span), f32),
            jax.ShapeDtypeStruct((strips * tokens // GROUP, span), f32),
        ],
        scratch_shapes=[
            pltpu.VMEM((n, width), f32),
            *[
                pltpu.VMEM((span, width), f32),
                *[pltpu.VMEM((span, width), jnp.bfloat16)] * 3,
                pltpu.VMEM((span, 128), jnp.bfloat16),
            ] * 2,
        ],
        compiler_params=pltpu.CompilerParams(vmem_limit_bytes=VMEM_LIMIT),
        cost_estimate=pl.CostEstimate(flops=3200 * work, transcendentals=work, bytes_accessed=2 * work),
        name="bwd_full",
    )(dte, dtx, grad, hist, slabs, write, ones, rate, start)
    both = jnp.stack([part.reshape(strips, tokens // GROUP, span).sum(0) for part in (dw, dr)])
    both = both.reshape(2, tokens // GROUP, GROUP, n).transpose(0, 3, 1, 2).reshape(2, n, tokens)
    return s1, s2, grate, both[0], both[1]


def slabs_of(values):
    n, tokens = values.shape
    return values.reshape(n, tokens // GROUP, GROUP).transpose(1, 0, 2).reshape(tokens // GROUP * n, GROUP)


def spread(values):
    n, tokens = values.shape
    own = jnp.arange(tokens)[:, None] % GROUP == jnp.arange(GROUP)[None, :]
    return jnp.where(own[:, :, None], values.T[:, None, :], 0).reshape(tokens, GROUP * n).astype(jnp.bfloat16)


MESH = pl.DeviceIdType.MESH


class Grid:
    def __init__(self, axis, size, inner):
        self.axis, self.inner, self.outer = axis, inner, size // inner
        me = lax.axis_index(axis)
        self.row, self.col = me // inner, me % inner

    def device(self, row, col):
        return {self.axis: row * self.inner + col}

    def neighbours(self):
        row, col = self.row, self.col
        found = []
        if self.outer > 1:
            found += [(row > 0, self.device(row - 1, col)), (row < self.outer - 1, self.device(row + 1, col))]
        if self.inner > 1:
            found += [(col > 0, self.device(row, col - 1)), (col < self.inner - 1, self.device(row, col + 1))]
        return found

    def everyone(self):
        size = self.inner * self.outer
        me = self.row * self.inner + self.col
        return [(me >= 0, {self.axis: (me + step) % size}) for step in range(1, size)]


def greet(grids, all_of=()):
    barrier = pltpu.get_barrier_semaphore()
    count = 0
    for grid in grids:
        for there, device in grid.everyone() if grid.axis in all_of else grid.neighbours():

            @pl.when(there)
            def _(device=device):
                pl.semaphore_signal(barrier, inc=1, device_id=device, device_id_type=MESH)

            count = count + there.astype(jnp.int32)
    pl.semaphore_wait(barrier, count)


def gather_steps(grid, whole_ref, out_ref, send_sem, recv_sem, own, waits, chunk, chunks, across_too=True, ways=(True, True)):
    rows = whole_ref.shape[0]
    part = rows // chunks
    src_ref = whole_ref.at[pl.ds(chunk * part, part)]
    outer, inner = grid.outer, grid.inner if across_too else 1
    row, col = grid.row, grid.col

    def number(r, c):
        return r * inner + c if across_too else r

    def place(r, c):
        return pl.ds(pl.multiple_of(number(r, c) * rows + chunk * part, part), part)

    def send(there, way, r, c, device, source):
        copy = pltpu.make_async_remote_copy(
            src_ref=source, dst_ref=out_ref.at[place(r, c)], send_sem=send_sem.at[way, number(r, c)],
            recv_sem=recv_sem.at[number(r, c)], device_id=device, device_id_type=MESH)

        @pl.when(there)
        def _():
            copy.start()

        waits.append((there, copy))

    def across(there, r, c, source):
        if inner > 1:
            send(there & (c >= col) & (col > 0), 2, r, c, grid.device(row, col - 1), source)
            send(there & (c <= col) & (col < inner - 1), 3, r, c, grid.device(row, col + 1), source)

    def along(there, r, source):
        if outer > 1:
            if ways[0]:
                send(there & (r >= row) & (row > 0), 0, r, col, grid.device(row - 1, col), source)
            if ways[1]:
                send(there & (r <= row) & (row < outer - 1), 1, r, col, grid.device(row + 1, col), source)

    def arrive(there, r, c):
        copy = pltpu.make_async_remote_copy(
            src_ref=src_ref, dst_ref=out_ref.at[place(r, c)], send_sem=send_sem.at[0, 0],
            recv_sem=recv_sem.at[number(r, c)], device_id=grid.device(row, col), device_id_type=MESH)

        @pl.when(there)
        def _():
            copy.wait_recv()

    always = row >= 0
    along(always, row, src_ref)
    across(always, row, col, src_ref)
    own_sem, own_buf = own
    fetch = pltpu.make_async_copy(src_ref, own_buf, own_sem.at[0])
    fetch.start()
    for _ in range(chunk + 1):
        yield
    fetch.wait()
    keep = pltpu.make_async_copy(own_buf, out_ref.at[place(row, col)], own_sem.at[1])
    keep.start()
    waits.append((None, keep))

    def rows_at(distance):
        return [row - distance] * ways[1] + [row + distance] * ways[0]

    for distance in range(1, outer):
        for r in rows_at(distance):
            there = (r >= 0) & (r < outer)
            arrive(there, r, col)
            along(there, r, out_ref.at[place(r, col)])
            across(there, r, col, out_ref.at[place(r, col)])
        yield
    for step in range(1, inner):
        for distance in range(outer):
            for r in rows_at(distance) if distance else (row,):
                for c in (col - step, col + step):
                    there = (r >= 0) & (r < outer) & (c >= 0) & (c < inner)
                    arrive(there, r, c)
                    if step < inner - 1:
                        across(there, r, c, out_ref.at[place(r, c)])
            yield


def finish(waits):
    for there, copy in waits:
        if there is None:
            copy.wait()
        else:

            @pl.when(there)
            def _(copy=copy):
                if copy.is_remote:
                    copy.wait_send()
                else:
                    copy.wait()


def gather_scratch(size, array, chunks):
    dma = pltpu.SemaphoreType.DMA
    own = pltpu.VMEM((array.shape[0] // chunks, *array.shape[1:]), array.dtype)
    return [dma((4, size)), dma((size,)), dma((2,)), own] * chunks


def in_turn(runs):
    runs = list(runs)
    while runs:
        left = []
        for run in runs:
            if next(run, run) is not run:
                left.append(run)
        runs = left


def link_gather(arrays, sizes, collective_id, ways=(True, True)):
    count = len(arrays)
    axes = sorted({entry[0] for entry in arrays})

    def kernel(*refs):
        sources, outs, sems = refs[:count], refs[count : 2 * count], refs[2 * count :]
        grids = {axis: Grid(axis, *sizes[axis]) for axis in axes}
        greet([grids[axis] for axis in axes])
        waits = []
        runs = []
        for i, (axis, _, chunks) in enumerate(arrays):
            for chunk in range(chunks):
                runs.append(gather_steps(
                    grids[axis], sources[i], outs[i], sems[0], sems[1], sems[2:4], waits, chunk, chunks, ways=ways))
                sems = sems[4:]
        in_turn(runs)
        finish(waits)

    sems = []
    for axis, a, chunks in arrays:
        sems += gather_scratch(sizes[axis][0], a, chunks)
    return pl.pallas_call(
        kernel,
        in_specs=[pl.BlockSpec(memory_space=pl.ANY)] * count,
        out_specs=[pl.BlockSpec(memory_space=pl.ANY)] * count,
        out_shape=[
            jax.ShapeDtypeStruct((sizes[axis][0] * a.shape[0], *a.shape[1:]), a.dtype) for axis, a, _ in arrays],
        scratch_shapes=sems,
        compiler_params=pltpu.CompilerParams(
            collective_id=collective_id, has_side_effects=True, vmem_limit_bytes=VMEM_LIMIT),
        cost_estimate=pl.CostEstimate(flops=LINK_COST, transcendentals=0, bytes_accessed=0),
        name="link_gather",
    )(*[a for _, a, _ in arrays])


def reduce_steps(grid, src_ref, out_ref, scratch, waits, chunks, share):
    acc, inner_buf, outer_buf, load_sem, inner_send, inner_recv, outer_send, outer_recv, out_sem = scratch[:9]
    outer, inner = grid.outer, grid.inner
    row, col = grid.row, grid.col
    rows = acc.shape[0] // (outer * inner)
    part = rows // chunks
    piece = min(part, 64)

    def start_of(chunk, r, c):
        return pl.multiple_of((r * inner + c) * rows + chunk * part, part)

    def line(me, size, device, block, buf, send, recv):
        def from_low(target):
            return target if size > 2 else 0

        def from_high(target, owner):
            return jnp.where(target == owner, size, target) if size > 2 else 0

        def hop(there, target, onward, slot):
            copy = pltpu.make_async_remote_copy(
                src_ref=acc.at[pl.ds(block(target), part)], dst_ref=buf.at[slot], send_sem=send.at[target],
                recv_sem=recv.at[slot], device_id=device(onward), device_id_type=MESH)

            @pl.when(there)
            def _():
                copy.start()

            waits.append((there, copy))

        def up(there, target):
            hop(there & (target > me), target, me + 1, from_low(target))

        def down(there, target):
            hop(there & (target < me), target, me - 1, from_high(target, me - 1))

        def arrive(there, target, slot):
            at = block(target)
            copy = pltpu.make_async_remote_copy(
                src_ref=acc.at[pl.ds(at, part)], dst_ref=buf.at[slot], send_sem=send.at[target],
                recv_sem=recv.at[slot], device_id=device(me), device_id_type=MESH)

            @pl.when(there)
            def _():
                copy.wait_recv()

                @pl.loop(0, part // piece)
                def _(k):
                    here = pl.ds(pl.multiple_of(at + k * piece, piece), piece)
                    there_rows = pl.ds(pl.multiple_of(k * piece, piece), piece)
                    total = acc[here, :].astype(jnp.float32) + buf[slot, there_rows, :].astype(jnp.float32)
                    acc[here, :] = total.astype(acc.dtype)

        def begin(target):
            up(me == 0, target)
            down(me == size - 1, target)

        def go_on(target):
            arrive((me > 0) & (target >= me), target, from_low(target))
            arrive((me < size - 1) & (target <= me), target, from_high(target, me))
            if size > 2:
                up((me > 0) & (me < size - 1), target)
                down((me > 0) & (me < size - 1), target)

        return begin, go_on

    order = sorted(range(outer), key=lambda k: -abs(2 * k - outer + 1))
    pieces = [(chunk, r) for chunk in range(chunks) for r in order]
    loads = {}
    for chunk, r in pieces:
        loads[chunk, r] = [
            pltpu.make_async_copy(
                src_ref.at[pl.ds(start_of(chunk, r, c), part)], acc.at[pl.ds(start_of(chunk, r, c), part)],
                load_sem.at[chunk, r * inner + c])
            for c in range(inner)]
        for load in loads[chunk, r]:
            load.start()

    def inner_line(chunk, r):
        return line(
            col, inner, lambda c: grid.device(row, c), lambda t: start_of(chunk, r, t), inner_buf.at[chunk, r],
            inner_send.at[chunk, r], inner_recv.at[chunk, r])

    def outer_line(chunk):
        return line(
            row, outer, lambda r: grid.device(r, col), lambda t: start_of(chunk, t, col), outer_buf.at[chunk],
            outer_send.at[chunk], outer_recv.at[chunk])

    def inner_start(k):
        if k < len(pieces):
            for load in loads[pieces[k]]:
                load.wait()
            if inner > 1:
                for c in range(inner):
                    inner_line(*pieces[k])[0](c)

    def outer_rest(k):
        if 0 <= k < len(pieces):
            chunk, r = pieces[k]
            if outer > 1:
                outer_line(chunk)[1](r)
            if r == order[-1]:
                give(chunk)

    def give(chunk):
        first = start_of(chunk, row, col)
        if share is None:
            last = pltpu.make_async_copy(
                acc.at[pl.ds(first, part)], out_ref.at[pl.ds(chunk * part, part)], out_sem.at[chunk])
            last.start()
            waits.append((None, last))
            return
        other, strip, send_sem, recv_sem = share
        count, me = other.outer * other.inner, other.row * other.inner + other.col
        take = rows // count
        for mate in range(chunk * part // take, (chunk + 1) * part // take):
            for k in range(acc.shape[1] // strip):
                source = acc.at[
                    pl.ds(pl.multiple_of((row * inner + col) * rows + mate * take, take), take),
                    pl.ds(k * strip, strip)]
                target = out_ref.at[:, pl.ds(pl.multiple_of((k * count + me) * strip, strip), strip)]
                own = pltpu.make_async_copy(source, target, send_sem.at[mate, k])
                sent = pltpu.make_async_remote_copy(
                    src_ref=source, dst_ref=target, send_sem=send_sem.at[mate, k], recv_sem=recv_sem.at[me, k],
                    device_id={other.axis: mate}, device_id_type=MESH)

                @pl.when(mate == me)
                def _(own=own):
                    own.start()

                @pl.when(mate != me)
                def _(sent=sent):
                    sent.start()

                waits.append((mate != me, sent))
                waits.append((mate == me, own))

    window = 2
    for k in range(window):
        inner_start(k)
    yield
    for k in range(len(pieces)):
        inner_start(k + window)
        chunk, r = pieces[k]
        if inner > 1:
            for c in range(inner):
                inner_line(chunk, r)[1](c)
        if outer > 1:
            outer_line(chunk)[0](r)
        yield
        outer_rest(k - window)
        yield
    for k in range(len(pieces) - window, len(pieces)):
        outer_rest(k)
        yield
    if share is not None:
        other, strip, send_sem, recv_sem = share
        count, me = other.outer * other.inner, other.row * other.inner + other.col
        take = rows // count
        for mate in range(count):
            for k in range(acc.shape[1] // strip):
                copy = pltpu.make_async_remote_copy(
                    src_ref=acc.at[pl.ds(0, take), pl.ds(k * strip, strip)],
                    dst_ref=out_ref.at[:, pl.ds((k * count + mate) * strip, strip)], send_sem=send_sem.at[mate, k],
                    recv_sem=recv_sem.at[mate, k], device_id={other.axis: me}, device_id_type=MESH)

                @pl.when(mate != me)
                def _(copy=copy):
                    copy.wait_recv()


def link_reduce(arrays, sizes, collective_id):
    count = len(arrays)

    def kernel(*refs):
        sources, outs, scratch = refs[:count], refs[count : 2 * count], refs[2 * count :]
        grids = {axis: Grid(axis, *sizes[axis]) for axis in ("seq", "stream")}
        greet(list(grids.values()), ("stream",))
        waits = []
        runs = []
        for i, (axis, _, chunks, strip) in enumerate(arrays):
            share = (grids["stream"], strip, scratch[9], scratch[10]) if strip else None
            runs.append(reduce_steps(grids[axis], sources[i], outs[i], scratch[:9], waits, chunks, share))
            scratch = scratch[11 if strip else 9 :]
        in_turn(runs)
        finish(waits)

    scratch, shapes = [], []
    for axis, a, chunks, strip in arrays:
        size, inner = sizes[axis]
        outer = size // inner
        part = a.shape[0] // size // chunks
        slots = [n + 1 if n > 2 else 1 for n in (inner, outer)]
        dma = pltpu.SemaphoreType.DMA
        scratch += [
            pltpu.VMEM(a.shape, a.dtype),
            pltpu.VMEM((chunks, outer, slots[0], part, a.shape[1]), a.dtype),
            pltpu.VMEM((chunks, slots[1], part, a.shape[1]), a.dtype),
            dma((chunks, size)), dma((chunks, outer, inner)), dma((chunks, outer, slots[0])), dma((chunks, outer)),
            dma((chunks, slots[1])), dma((chunks,))]
        if strip:
            mates = sizes["stream"][0]
            shapes.append(jax.ShapeDtypeStruct((a.shape[0] // size // mates, a.shape[1] * mates), a.dtype))
            scratch += [dma((mates, a.shape[1] // strip))] * 2
        else:
            shapes.append(jax.ShapeDtypeStruct((a.shape[0] // size, a.shape[1]), a.dtype))
    return pl.pallas_call(
        kernel,
        in_specs=[pl.BlockSpec(memory_space=pl.ANY)] * count,
        out_specs=[pl.BlockSpec(memory_space=pl.ANY)] * count,
        out_shape=shapes,
        scratch_shapes=scratch,
        compiler_params=pltpu.CompilerParams(
            collective_id=collective_id, has_side_effects=True, vmem_limit_bytes=VMEM_LIMIT),
        cost_estimate=pl.CostEstimate(flops=4 * LINK_COST, transcendentals=0, bytes_accessed=0),
        name="link_reduce",
    )(*[entry[1] for entry in arrays])


def link_sum(partial, sizes, collective_id):
    rows, width = partial.shape
    size, inner = sizes["stream"]
    outer = size // inner
    assert inner == 2
    half = rows // 2
    bf, f32 = jnp.bfloat16, jnp.float32
    dma = pltpu.SemaphoreType.DMA

    def kernel(own_ref, out_ref, mate_buf, pair_ref, terms_ref, total_ref, send, recv, line_send, line_recv, own_sem, own_buf):
        grid = Grid("stream", size, inner)
        row, col = grid.row, grid.col
        greet([grid])
        mate = grid.device(row, 1 - col)
        mine = pl.ds(pl.multiple_of(col * half, half), half)
        swap = pltpu.make_async_remote_copy(
            src_ref=own_ref, dst_ref=mate_buf, send_sem=send.at[0], recv_sem=recv.at[0], device_id=mate,
            device_id_type=MESH)
        swap.start()
        swap.wait_recv()
        pair_ref[...] = (own_ref[mine, :].astype(f32) + mate_buf[mine, :].astype(f32)).astype(bf)
        waits = []
        line = Grid("stream", size, inner)
        in_turn([gather_steps(
            line, pair_ref, terms_ref, line_send, line_recv, (own_sem, own_buf), waits, 0, 1, across_too=False)])
        finish(waits)
        total = terms_ref[pl.ds(0, half), :].astype(f32)
        for r in range(1, outer):
            total = total + terms_ref[pl.ds(r * half, half), :].astype(f32)
        total_ref[...] = total
        out_ref[mine, :] = total
        swap_back = pltpu.make_async_remote_copy(
            src_ref=total_ref, dst_ref=out_ref.at[mine], send_sem=send.at[1], recv_sem=recv.at[1], device_id=mate,
            device_id_type=MESH)
        swap_back.start()
        theirs = pltpu.make_async_remote_copy(
            src_ref=total_ref, dst_ref=out_ref.at[pl.ds(pl.multiple_of((1 - col) * half, half), half)],
            send_sem=send.at[1], recv_sem=recv.at[1], device_id=mate, device_id_type=MESH)
        theirs.wait_recv()
        swap.wait_send()
        swap_back.wait_send()

    return pl.pallas_call(
        kernel,
        in_specs=[pl.BlockSpec(memory_space=pltpu.VMEM)],
        out_specs=pl.BlockSpec(memory_space=pltpu.VMEM),
        out_shape=jax.ShapeDtypeStruct((rows, width), f32),
        scratch_shapes=[
            pltpu.VMEM((rows, width), bf), pltpu.VMEM((half, width), bf), pltpu.VMEM((outer * half, width), bf),
            pltpu.VMEM((half, width), f32), dma((2,)), dma((2,)), dma((4, outer)), dma((outer,)), dma((2,)),
            pltpu.VMEM((half, width), bf)],
        compiler_params=pltpu.CompilerParams(
            collective_id=collective_id, has_side_effects=True, vmem_limit_bytes=VMEM_LIMIT),
        cost_estimate=pl.CostEstimate(flops=LINK_COST, transcendentals=0, bytes_accessed=0),
        name="link_sum",
    )(partial.astype(bf))


def link_open(conv, gate, arrays, sizes, collective_id):
    count = len(arrays)
    mates = sizes["stream"][0]
    take = conv.shape[0] // mates
    dma = pltpu.SemaphoreType.DMA

    def kernel(conv_ref, gate_ref, *refs):
        sources, refs = refs[:count], refs[count:]
        conv_all, conv_own, gate_own, outs, refs = *refs[:3], refs[3 : 3 + count], refs[3 + count :]
        hand_send, hand_recv, hand_buf, sems = refs[0], refs[1], refs[2], refs[3:]
        grids = {axis: Grid(axis, *sizes[axis]) for axis in ("seq", "stream")}
        greet(list(grids.values()), ("stream",))
        me = grids["stream"].row * grids["stream"].inner + grids["stream"].col
        waits = []

        def rows(mate):
            return pl.ds(pl.multiple_of(mate * take, take), take)

        def hand(kind, source, target):
            fetch = pltpu.make_async_copy(source.at[rows(me)], hand_buf.at[kind], hand_send.at[kind, 0])
            fetch.start()
            for step in range(1, mates):
                mate = (me + step) % mates
                copy = pltpu.make_async_remote_copy(
                    src_ref=source.at[rows(mate)], dst_ref=target.at[rows(me)], send_sem=hand_send.at[kind, step],
                    recv_sem=hand_recv.at[kind, step], device_id={"stream": mate}, device_id_type=MESH)
                copy.start()
                waits.append((me >= 0, copy))
            fetch.wait()
            keep = pltpu.make_async_copy(hand_buf.at[kind], target.at[rows(me)], hand_recv.at[kind, 0])
            keep.start()
            return keep

        def handed(kind, source, target, own):
            own.wait()
            for step in range(1, mates):
                mate = (me + mates - step) % mates
                pltpu.make_async_remote_copy(
                    src_ref=source.at[rows(me)], dst_ref=target.at[rows(mate)], send_sem=hand_send.at[kind, step],
                    recv_sem=hand_recv.at[kind, step], device_id={"stream": me}, device_id_type=MESH).wait_recv()

        own = hand(0, conv_ref, conv_own)

        def main():
            for i, (axis, _, chunks) in enumerate(arrays):
                for chunk in range(chunks):
                    at = 4 * (1 + sum(entry[2] for entry in arrays[:i]) + chunk)
                    yield gather_steps(
                        grids[axis], sources[i], outs[i], sems[at], sems[at + 1], sems[at + 2 : at + 4], waits, chunk,
                        chunks)

        runs = list(main())
        for run in runs:
            next(run)
        own_gate = hand(1, gate_ref, gate_own)
        handed(0, conv_ref, conv_own, own)
        first = gather_steps(grids["seq"], conv_own, conv_all, sems[0], sems[1], sems[2:4], waits, 0, 1)
        next(first)
        in_turn([first, *runs])
        handed(1, gate_ref, gate_own, own_gate)
        finish(waits)

    entries = [("seq", conv, 1), *arrays]
    sems = []
    for axis, a, chunks in entries:
        sems += gather_scratch(sizes[axis][0], a, chunks)
    result = pl.pallas_call(
        kernel,
        in_specs=[pl.BlockSpec(memory_space=pl.ANY)] * (count + 2),
        out_specs=[pl.BlockSpec(memory_space=pl.ANY)] * (count + 3),
        out_shape=[
            jax.ShapeDtypeStruct((sizes["seq"][0] * conv.shape[0], conv.shape[1]), conv.dtype),
            jax.ShapeDtypeStruct(conv.shape, conv.dtype),
            jax.ShapeDtypeStruct(gate.shape, gate.dtype),
            *[jax.ShapeDtypeStruct((sizes[axis][0] * a.shape[0], *a.shape[1:]), a.dtype) for axis, a, _ in arrays]],
        scratch_shapes=[
            dma((2, mates)), dma((2, mates)), pltpu.VMEM((2, take, conv.shape[1]), conv.dtype), *sems],
        compiler_params=pltpu.CompilerParams(
            collective_id=collective_id, has_side_effects=True, vmem_limit_bytes=VMEM_LIMIT),
        cost_estimate=pl.CostEstimate(flops=4 * LINK_COST, transcendentals=0, bytes_accessed=0),
        name="link_open",
    )(conv, gate, *[a for _, a, _ in arrays])
    return result[0], result[2], *result[3:]


ROWS = 128


def conv_fwd_body(x_ref, early_ref, masks_ref, taps_ref, act_ref, slope_ref, ext_ref):
    length = x_ref.shape[0]
    ext_ref[pl.ds(0, 8), :] = early_ref[...]

    @pl.loop(0, length // ROWS)
    def _(k):
        here = pl.ds(pl.multiple_of(k * ROWS, ROWS), ROWS)
        ext_ref[pl.ds(pl.multiple_of(k * ROWS + 8, 8), ROWS), :] = x_ref[here, :]
        window = ext_ref[pl.ds(pl.multiple_of(k * ROWS, ROWS), ROWS + 8), :]
        masks = masks_ref[here, :]
        total = taps_ref[CONV : CONV + 1, :] + taps_ref[CONV - 1 : CONV, :] * window[8:]
        for tap in range(CONV - 1):
            shift = 8 - (CONV - 1) + tap
            total = total + taps_ref[tap : tap + 1, :] * (window[shift : shift + ROWS] * masks[:, tap : tap + 1])
        gate = jax.nn.sigmoid(total)
        act_ref[here, :] = (total * gate).astype(act_ref.dtype)
        slope_ref[here, :] = (gate * (1.0 + total * (1.0 - gate))).astype(slope_ref.dtype)


def conv_bwd_body(grad_ref, slope_ref, late_ref, x_ref, masks_ref, taps_ref, out_ref, sums_ref, ext_ref):
    length, width = x_ref.shape
    ext_ref[pl.ds(length, 8), :] = late_ref[...]

    @pl.loop(0, length // ROWS)
    def _(k):
        here = pl.ds(pl.multiple_of(k * ROWS, ROWS), ROWS)
        ext_ref[here, :] = grad_ref[here, :] * slope_ref[here, :].astype(jnp.float32)

    def some(k, sums):
        start = pl.multiple_of(k * ROWS, ROWS)
        here = pl.ds(start, ROWS)
        window = ext_ref[pl.ds(start, ROWS + 8), :]
        masks = masks_ref[here, :]
        x = x_ref[here, :]
        total = jnp.zeros((ROWS, width), jnp.float32)
        parts = []
        for tap in range(CONV):
            ahead = CONV - 1 - tap
            term = window[ahead : ahead + ROWS]
            if ahead:
                term = term * masks[:, CONV - 2 + ahead : CONV - 1 + ahead]
            total = total + taps_ref[tap : tap + 1, :] * term
            parts.append((term * x).reshape(ROWS // 8, 8, width).sum(0))
        parts.append(window[:ROWS].reshape(ROWS // 8, 8, width).sum(0))
        out_ref[here, :] = total.astype(out_ref.dtype)
        return tuple(a + b for a, b in zip(sums, parts))

    sums = lax.fori_loop(0, length // ROWS, some, (jnp.zeros((8, width), jnp.float32),) * (CONV + 1))
    for tap in range(CONV + 1):
        sums_ref[tap : tap + 1, :] = jnp.sum(sums[tap], axis=0, keepdims=True)
    sums_ref[CONV + 1 :, :] = jnp.zeros((7 - CONV, width), jnp.float32)


def conv_fwd(x, early, masks, taps, seqs, width=1024):
    tokens, chans = x.shape
    width = min(width, chans)
    length = tokens // seqs
    block = pl.BlockSpec((length, width), lambda s, c: (s, c))
    return pl.pallas_call(
        conv_fwd_body,
        grid=(seqs, chans // width),
        in_specs=[
            block, pl.BlockSpec((8, width), lambda s, c: (s, c)), pl.BlockSpec((length, 8), lambda s, c: (s, 0)),
            pl.BlockSpec((8, width), lambda s, c: (0, c))],
        out_specs=[block, block],
        out_shape=[jax.ShapeDtypeStruct((tokens, chans), jnp.bfloat16)] * 2,
        scratch_shapes=[pltpu.VMEM((length + 8, width), jnp.float32)],
        compiler_params=pltpu.CompilerParams(vmem_limit_bytes=VMEM_LIMIT),
        cost_estimate=pl.CostEstimate(
            flops=4000 * tokens * chans, transcendentals=tokens * chans, bytes_accessed=8 * tokens * chans),
        name="conv_fwd",
    )(x, early, masks, taps)


def conv_bwd(grad, slope, late, x, masks, taps, seqs, width=512):
    tokens, chans = x.shape
    width = min(width, chans)
    length = tokens // seqs
    block = pl.BlockSpec((length, width), lambda s, c: (s, c))
    rim = pl.BlockSpec((8, width), lambda s, c: (s, c))
    return pl.pallas_call(
        conv_bwd_body,
        grid=(seqs, chans // width),
        in_specs=[
            block, block, rim, block, pl.BlockSpec((length, 8), lambda s, c: (s, 0)),
            pl.BlockSpec((8, width), lambda s, c: (0, c))],
        out_specs=[block, rim],
        out_shape=[
            jax.ShapeDtypeStruct((tokens, chans), jnp.bfloat16), jax.ShapeDtypeStruct((seqs * 8, chans), jnp.float32)],
        scratch_shapes=[pltpu.VMEM((length + 8, width), jnp.float32)],
        compiler_params=pltpu.CompilerParams(vmem_limit_bytes=VMEM_LIMIT),
        cost_estimate=pl.CostEstimate(
            flops=5000 * tokens * chans, transcendentals=0, bytes_accessed=12 * tokens * chans),
        name="conv_bwd",
    )(grad, slope, late, x, masks, taps)


def passed_along(block, axis, distance):
    devices = range(lax.axis_size(axis))
    route = [(i - distance, i) for i in devices if i - distance in devices]
    return lax.ppermute(block, axis, route)


def silu_slope(values_in):
    sigmoid_v = jax.nn.sigmoid(values_in)
    return sigmoid_v * (1.0 + values_in * (1.0 - sigmoid_v))


def token_layout(lengths, first_pos, n_tokens):
    doc_ends = jnp.cumsum(lengths)
    begins = doc_ends - lengths
    positions = first_pos + jnp.arange(n_tokens, dtype=jnp.int32)
    live_slot = (lengths > 0)[None, :]
    doc_ids = jnp.sum(((begins[None, :] <= positions[:, None]) & live_slot).astype(jnp.int32), axis=1)
    start_flags = jnp.sum(((begins[None, :] == positions[:, None]) & live_slot).astype(jnp.float32), axis=1)
    valid_mask = (positions < doc_ends[-1]).astype(jnp.float32)
    return (doc_ids, start_flags, valid_mask)


def contract_rows(left_mat, right_mat):
    return lax.dot_general(left_mat, right_mat, (((0,), (0,)), ((), ())), preferred_element_type=jnp.float32)


def contract_cols(left_mat, right_mat):
    return lax.dot_general(left_mat, right_mat, NT, preferred_element_type=jnp.float32)


def padded_rows(array, rows):
    return jnp.pad(array, ((0, -array.shape[0] % rows), (0, 0)))


def carried(ends, step_sum, rate, backward, sizes, collective_id):
    seqs, chans = step_sum.shape
    n = rate.shape[0]
    high = step_sum.astype(jnp.bfloat16)
    low = (step_sum - high.astype(jnp.float32)).astype(jnp.bfloat16)
    sent = padded_rows(jnp.concatenate([ends.astype(jnp.bfloat16), high, low], axis=0), 16)
    (gathered,) = link_gather([("seq", sent, 1)], sizes, collective_id, (backward, not backward))
    gathered = gathered.reshape(-1, *sent.shape)
    count = lax.axis_size("seq")
    place = lax.axis_index("seq")
    state = jnp.zeros((seqs, n, chans), jnp.float32)
    for step in range(count - 1):
        source = count - 1 - step if backward else step
        block = gathered[source].astype(jnp.float32)
        total = block[seqs * n : seqs * (n + 1)] + block[seqs * (n + 1) : seqs * (n + 2)]
        joined = jnp.exp2(total[:, None, :] * rate[None]) * state + block[: seqs * n].reshape(seqs, n, chans)
        state = jnp.where(source > place if backward else source < place, joined, state)
    return state.reshape(seqs * n, chans)


def local(sizes, resid_in, out_grad, row_lengths, norm_gain, in_weight, conv_weight, conv_bias, xproj_weight, dt_weight,
          dt_bias, a_log, skip_gain, out_weight):
    bf, f32 = jnp.bfloat16, jnp.float32
    seqs = lax.axis_size("stream")
    parts = lax.axis_size("seq")
    own = conv_bias.shape[0]
    own_feats = norm_gain.shape[0]
    chans = own * parts
    rank_dim = dt_weight.shape[0]
    state_dim = a_log.shape[1]
    proj_dim = xproj_weight.shape[1]
    length, feats = resid_in.shape[1:]
    tokens = seqs * length

    gain = norm_gain.astype(f32)
    scaled = (in_weight.astype(f32) * gain[:, None]).astype(bf).reshape(own_feats, 2, parts, seqs, own)
    scaled = scaled.transpose(1, 3, 0, 2, 4).reshape(2, seqs * own_feats, chans)
    packed = jnp.concatenate(
        [xproj_weight, dt_weight.T, a_log, conv_weight.T, conv_bias[:, None], dt_bias[:, None], skip_gain[:, None]],
        axis=1)
    residual = resid_in[0].astype(f32)
    cotangent = out_grad[0]
    inv_rms = lax.rsqrt(jnp.mean(residual * residual, axis=-1, keepdims=True) + EPSILON)
    unit_own = residual * inv_rms
    slots = row_lengths.shape[1]
    arrays = [
        ("stream", jnp.pad(row_lengths, ((0, 7), (0, -slots % 128))), 1), ("stream", unit_own.astype(bf), 4),
        ("seq", jnp.pad(packed, ((0, 0), (0, -packed.shape[1] % 128))), 1)]
    if own_feats % 16:
        mine = lax.all_to_all(scaled, "stream", 1, 1, tiled=True)
        gate_own = mine[1]
        lengths, unit, packed, in_conv = link_gather([*arrays, ("seq", mine[0], 1)], sizes, 1)
    else:
        in_conv, gate_own, lengths, unit, packed = link_open(scaled[0], scaled[1], arrays, sizes, 1)
    lengths = lengths[::8, :slots]
    unit, gate_own, out_own, cot_own = lax.optimization_barrier((unit, gate_own, out_weight, cotangent))
    in_gate = lax.all_gather(gate_own, "seq", axis=0, tiled=True)
    out_full = lax.all_gather(out_own, "seq", axis=0, tiled=True)
    cot_all = lax.all_gather(cot_own, "stream", axis=0, tiled=True)
    xproj_full = packed[:, :proj_dim]
    dtw_cols = packed[:, proj_dim : proj_dim + rank_dim]
    at = proj_dim + rank_dim
    log_rates = packed[:, at : at + state_dim].astype(f32).T
    at += state_dim
    conv_taps = packed[:, at : at + CONV].astype(f32).T
    at += CONV
    conv_shift, dt_shift, skip_vec = (packed[:, at + i].astype(f32) for i in range(3))
    rate = -jnp.exp(log_rates) / LN2

    rim = CONV - 1
    first_pos = lax.axis_index("seq") * length
    doc_ids, start_flags, valid_mask = jax.vmap(
        lambda row: token_layout(row, first_pos - rim, length + 2 * rim))(lengths)
    own_ids = doc_ids[:, rim : rim + length]
    starts = start_flags[:, rim : rim + length].reshape(tokens, 1)
    valid = valid_mask[:, rim : rim + length].reshape(tokens, 1)
    near = [doc_ids[:, tap : tap + length] == own_ids for tap in range(2 * rim + 1) if tap != rim]
    masks = jnp.pad(jnp.stack(near, axis=-1).astype(f32), ((0, 0), (0, 0), (0, 8 - 2 * rim))).reshape(tokens, 8)

    conv_in = jnp.dot(unit, in_conv, preferred_element_type=f32)
    gate_in = jnp.dot(unit, in_gate, preferred_element_type=f32)
    earlier = passed_along(conv_in.reshape(seqs, length, chans)[:, length - rim :].astype(bf), "seq", 1).astype(f32)
    earlier = jnp.pad(earlier, ((0, 0), (8 - rim, 0), (0, 0))).reshape(seqs * 8, chans)
    taps = jnp.pad(jnp.concatenate([conv_taps, conv_shift[None]]), ((0, 7 - CONV), (0, 0)))
    activated, slope = conv_fwd(conv_in, earlier, masks, taps, seqs)
    act_float = activated.astype(f32)
    projected = link_sum(
        lax.dot_general(xproj_full, activated, (((0,), (1,)), ((), ())), preferred_element_type=f32), sizes, 2)
    low_rank = projected[:rank_dim].astype(bf)
    write_in = projected[rank_dim : rank_dim + state_dim]
    readout = projected[rank_dim + state_dim :]
    dt_pre = lax.dot_general(low_rank, dtw_cols, (((0,), (1,)), ((), ())), preferred_element_type=f32) + dt_shift
    dt_step = jax.nn.softplus(dt_pre)
    dt_reset = jnp.where(starts > 0, RESET, dt_step)
    dt_act = dt_step * act_float
    write_slabs, read_slabs = slabs_of(write_in), slabs_of(readout)
    write_diag, read_diag = spread(write_in), spread(readout)

    step_sum = jnp.sum(dt_reset.reshape(seqs, length, chans), axis=1)
    ends = scan_end(fwd_end_body, dt_reset, dt_act, write_slabs, rate, seqs)
    start_state = carried(ends, step_sum, rate, False, sizes, 3)
    scanned, history = fwd_full(dt_reset, dt_act, write_slabs, read_diag, rate, start_state, seqs)
    ssm_out = scanned + skip_vec * act_float
    gate_act = jax.nn.silu(gate_in)
    gated = (ssm_out * gate_act * valid).astype(bf)
    product = jnp.dot(gated, out_full, preferred_element_type=f32).astype(bf)
    d_gated = contract_cols(cot_all, out_full)
    d_masked = d_gated * valid
    d_ssm = d_masked * gate_act
    d_gate = (d_masked * ssm_out * silu_slope(gate_in)).astype(bf)
    product, d_ssm, gated, d_gate = lax.optimization_barrier((product, d_ssm, gated, d_gate))
    product = lax.psum_scatter(product, "stream", scatter_dimension=0, tiled=True)
    g_out = contract_rows(gated, cot_all).astype(bf)
    g_in_gate = contract_rows(unit, d_gate).astype(bf)
    d_ssm, g_out, g_in_gate = lax.optimization_barrier((d_ssm, g_out, g_in_gate))
    g_skip = jnp.sum(d_ssm * act_float, axis=0)
    back_ends = scan_end(bwd_end_body, dt_reset, d_ssm, read_slabs, rate, seqs)
    later_sum = carried(back_ends, step_sum, rate, True, sizes, 4)
    later_sum, product, g_out, g_in_gate = lax.optimization_barrier((later_sum, product, g_out, g_in_gate))
    output = (residual + product.astype(f32)).astype(bf)
    g_out = lax.psum_scatter(g_out, "seq", scatter_dimension=0, tiled=True)
    g_in_gate = lax.psum_scatter(g_in_gate, "seq", scatter_dimension=0, tiled=True)
    sum_write, sum_rate, g_log, d_write, d_read = bwd_full(
        dt_reset, dt_act, d_ssm, history, read_slabs, write_diag, rate, later_sum, seqs)
    per_step = jnp.where(dt_step > 1e-30, sum_rate * LN2 / jnp.maximum(dt_step, 1e-30), 0.0)
    d_step = per_step + act_float * sum_write
    d_pre = d_step * jax.nn.sigmoid(dt_pre)
    g_dt_bias = jnp.sum(d_pre, axis=0)
    d_pre_low = d_pre.astype(bf)
    g_dt = lax.dot_general(d_pre_low, low_rank, (((0,), (1,)), ((), ())), preferred_element_type=f32)
    d_low = lax.dot_general(dtw_cols, d_pre_low, (((0,), (1,)), ((), ())), preferred_element_type=f32)
    d_proj = link_sum(jnp.concatenate([d_low, d_write, d_read], axis=0), sizes, 5).astype(bf)
    d_proj, g_out = lax.optimization_barrier((d_proj, g_out))
    g_xproj = lax.dot_general(activated, d_proj, (((0,), (1,)), ((), ())), preferred_element_type=f32)
    d_act = dt_step * sum_write + skip_vec * d_ssm + lax.dot_general(
        d_proj, xproj_full, (((0,), (1,)), ((), ())), preferred_element_type=f32)
    first = (d_act.reshape(seqs, length, chans)[:, :rim] * slope.reshape(seqs, length, chans)[:, :rim].astype(f32))
    later = passed_along(first.astype(bf), "seq", -1).astype(f32)
    later = jnp.pad(later, ((0, 0), (0, 8 - rim), (0, 0))).reshape(seqs * 8, chans)
    d_conv_in, sums = conv_bwd(d_act, slope, later, conv_in, masks, taps, seqs)
    d_conv_in, g_in_gate = lax.optimization_barrier((d_conv_in, g_in_gate))
    sums = sums.reshape(seqs, 8, chans).sum(0)
    g_conv, g_conv_bias = sums[:CONV].T, sums[CONV]
    g_in_conv = contract_rows(unit, d_conv_in).astype(bf)
    d_unit = (contract_cols(d_conv_in, in_conv) + contract_cols(d_gate, in_gate)).astype(bf)
    def in_rows(block):
        shared = lax.all_to_all(block, "stream", 0, 0, tiled=True).reshape(seqs, own_feats, parts, own)
        return shared.transpose(1, 2, 0, 3).reshape(own_feats, parts * seqs * own)

    def padded_small(columns):
        joined = jnp.concatenate(columns, axis=1)
        return jnp.pad(joined, ((0, 0), (0, -joined.shape[1] % 128))).astype(bf)

    small = padded_small(
        [g_xproj, g_dt, g_log.T * LN2, g_dt_bias[:, None], g_skip[:, None], g_conv, g_conv_bias[:, None]])
    d_unit, g_in_gate, output, g_out = lax.optimization_barrier((d_unit, in_rows(g_in_gate), output, g_out))
    g_in_conv, small, d_unit = link_reduce(
        [("seq", g_in_conv, 2, 0 if own_feats % 16 else own), ("seq", small, 2, 0), ("stream", d_unit, 4, 0)], sizes, 6)
    small = small.astype(f32)
    d_unit = d_unit.astype(f32)
    in_grad = cotangent.astype(f32) + inv_rms * (d_unit - unit_own * jnp.mean(d_unit * unit_own, axis=-1, keepdims=True))

    g_in_conv = in_rows(g_in_conv) if own_feats % 16 else g_in_conv
    g_unit = jnp.concatenate([g_in_conv, g_in_gate], axis=1).astype(f32)
    at = proj_dim + rank_dim
    return (
        output[None],
        in_grad.astype(bf)[None],
        jnp.sum(g_unit * in_weight.astype(f32), axis=1),
        g_unit * gain[:, None],
        small[:, at + state_dim + 2 : at + state_dim + 2 + CONV].T,
        small[:, at + state_dim + 2 + CONV],
        small[:, :proj_dim],
        small[:, proj_dim:at].T,
        small[:, at + state_dim],
        small[:, at : at + state_dim],
        small[:, at + state_dim + 1],
        g_out.astype(f32),
    )


def lines_of(mesh):
    devices = mesh.devices
    places = [getattr(device, "coords", None) for device in devices[:, 0]]
    seq = len(places)
    plane = 1
    if all(place is not None for place in places):
        plane = len({tuple(place)[1] for place in places})
    if seq % plane:
        plane = 1
    return {"seq": (seq, plane), "stream": (devices.shape[1], 1 if devices.shape[1] % 2 else 2)}


def solution(mesh):
    in_specs = (
        P("stream", "seq", None),
        P("stream", "seq", None),
        P("stream", None),
        P(("seq", "stream")),
        P(("seq", "stream"), None),
        P(None, ("seq", "stream")),
        P(("seq", "stream")),
        P(("seq", "stream"), None),
        P(None, ("seq", "stream")),
        P(("seq", "stream")),
        P(("seq", "stream"), None),
        P(("seq", "stream")),
        P(("seq", "stream"), None),
    )
    out_specs = (
        P("stream", "seq", None),
        P("stream", "seq", None),
        P(("seq", "stream")),
        P(("seq", "stream"), None),
        P(None, ("seq", "stream")),
        P(("seq", "stream")),
        P(("seq", "stream"), None),
        P(None, ("seq", "stream")),
        P(("seq", "stream")),
        P(("seq", "stream"), None),
        P(("seq", "stream")),
        P(("seq", "stream"), None),
    )
    return jax.shard_map(functools.partial(local, lines_of(mesh)), mesh=mesh, in_specs=in_specs, out_specs=out_specs, check_vma=False)
```

```python
import functools

import jax
import jax.numpy as jnp
from jax import lax
from jax.experimental import pallas as pl
from jax.experimental.pallas import tpu as pltpu
from jax.sharding import PartitionSpec as P

CONV = 4
EPSILON = 1e-05
RESET = 1e30
GROUP = 16
LN2 = 0.6931471805599453
NT = (((1,), (1,)), ((), ()))
VMEM_LIMIT = 56 << 20
LINK_COST = 20_000_000_000


def across(slab, place, width):
    return jnp.concatenate([jnp.broadcast_to(slab[:, place : place + 1], (slab.shape[0], 128))] * (width // 128), axis=1)


def decays(dte_ref, rate_ref, at, buf, power_buf=None):
    n = rate_ref.shape[0]
    for place in range(GROUP):
        power = dte_ref[pl.ds(at * GROUP + place, 1), :] * rate_ref[...]
        buf[pl.ds(place * n, n), :] = jnp.exp2(power)
        if power_buf is not None:
            power_buf[pl.ds(place * n, n), :] = power.astype(jnp.bfloat16)


def fwd_end_body(dte_ref, dtx_ref, slab_ref, rate_ref, end_ref, even_ref, odd_ref):
    n, width = rate_ref.shape
    groups = dte_ref.shape[0] // GROUP

    def walk(at, state, decay_ref):
        slab = slab_ref[pl.ds(at * n, n), :]
        for place in range(GROUP):
            write = across(slab, place, width)
            state = decay_ref[pl.ds(place * n, n), :] * state + dtx_ref[pl.ds(at * GROUP + place, 1), :] * write
        return state

    def pair(step, state):
        decays(dte_ref, rate_ref, 2 * step + 1, odd_ref)
        state = walk(2 * step, state, even_ref)
        decays(dte_ref, rate_ref, jnp.minimum(2 * step + 2, groups - 1), even_ref)
        return walk(2 * step + 1, state, odd_ref)

    decays(dte_ref, rate_ref, 0, even_ref)
    end_ref[...] = lax.fori_loop(0, groups // 2, pair, jnp.zeros_like(end_ref))


def bwd_end_body(dte_ref, grad_ref, slab_ref, rate_ref, end_ref, even_ref, odd_ref):
    n, width = rate_ref.shape
    groups = dte_ref.shape[0] // GROUP

    def walk(at, state, decay_ref):
        slab = slab_ref[pl.ds(at * n, n), :]
        for place in reversed(range(GROUP)):
            read = across(slab, place, width)
            state = decay_ref[pl.ds(place * n, n), :] * (state + grad_ref[pl.ds(at * GROUP + place, 1), :] * read)
        return state

    def pair(step, state):
        at = groups - 1 - 2 * step
        decays(dte_ref, rate_ref, at - 1, odd_ref)
        state = walk(at, state, even_ref)
        decays(dte_ref, rate_ref, jnp.maximum(at - 2, 0), even_ref)
        return walk(at - 1, state, odd_ref)

    decays(dte_ref, rate_ref, groups - 1, even_ref)
    end_ref[...] = lax.fori_loop(0, groups // 2, pair, jnp.zeros_like(end_ref))


def scan_end(body, dte, other, slabs, rate, seqs, width=512):
    tokens, chans = dte.shape
    length = tokens // seqs
    n = rate.shape[0]
    width = min(width, chans)
    work = tokens * chans * n
    return pl.pallas_call(
        body,
        grid=(seqs, chans // width),
        in_specs=[
            pl.BlockSpec((length, width), lambda s, c: (s, c)),
            pl.BlockSpec((length, width), lambda s, c: (s, c)),
            pl.BlockSpec((length // GROUP * n, GROUP), lambda s, c: (s, 0)),
            pl.BlockSpec((n, width), lambda s, c: (0, c)),
        ],
        out_specs=pl.BlockSpec((n, width), lambda s, c: (s, c)),
        out_shape=jax.ShapeDtypeStruct((seqs * n, chans), jnp.float32),
        scratch_shapes=[pltpu.VMEM((GROUP * n, width), jnp.float32)] * 2,
        compiler_params=pltpu.CompilerParams(vmem_limit_bytes=VMEM_LIMIT),
        cost_estimate=pl.CostEstimate(flops=1000 * work, transcendentals=work, bytes_accessed=8 * tokens * chans),
        name=body.__name__[:7],
    )(dte, other, slabs, rate)


def fwd_full_body(dte_ref, dtx_ref, slab_ref, read_ref, rate_ref, start_ref, y_ref, hist_ref, h_ref, even_ref, odd_ref):
    block = dte_ref.shape[0]
    n, width = rate_ref.shape
    span = GROUP * n
    rate = rate_ref[...]

    @pl.when(pl.program_id(2) == 0)
    def _():
        h_ref[...] = start_ref[...]

    first = h_ref[...]
    hist_ref[pl.ds(0, n), :] = first.astype(jnp.bfloat16)

    def rows_out(at, buf):
        y_ref[pl.ds(at * GROUP, GROUP), :] = jnp.dot(
            read_ref[pl.ds(at * GROUP, GROUP), :], buf[...], preferred_element_type=jnp.float32)

    def group(at, state, buf):
        slab = slab_ref[pl.ds(at * n, n), :]
        for place in range(GROUP):
            t = at * GROUP + place
            write = across(slab, place, width)
            state = jnp.exp2(dte_ref[pl.ds(t, 1), :] * rate) * state + dtx_ref[pl.ds(t, 1), :] * write
            kept = state.astype(jnp.bfloat16)
            hist_ref[pl.ds((t + 1) * n, n), :] = kept
            buf[pl.ds(place * n, n), :] = kept
        return state

    def pair(step, state):
        at = 2 * step
        rows_out(jnp.maximum(at - 1, 0), odd_ref)
        state = group(at, state, even_ref)
        rows_out(at, even_ref)
        return group(at + 1, state, odd_ref)

    h_ref[...] = lax.fori_loop(0, block // GROUP // 2, pair, first)
    rows_out(block // GROUP - 1, odd_ref)


def fwd_full(dte, dtx, slabs, read, rate, start, seqs, width=512, block=256):
    tokens, chans = dte.shape
    n = rate.shape[0]
    width = min(width, chans)
    blocks = tokens // seqs // block
    work = tokens * chans * n
    here = lambda c, s, t: (s * blocks + t, c)
    rows = lambda c, s, t: (s * blocks + t, 0)
    return pl.pallas_call(
        fwd_full_body,
        grid=(chans // width, seqs, blocks),
        in_specs=[
            pl.BlockSpec((block, width), here),
            pl.BlockSpec((block, width), here),
            pl.BlockSpec((block // GROUP * n, GROUP), rows),
            pl.BlockSpec((block, read.shape[1]), rows),
            pl.BlockSpec((n, width), lambda c, s, t: (0, c)),
            pl.BlockSpec((n, width), lambda c, s, t: (s, c)),
        ],
        out_specs=[pl.BlockSpec((block, width), here), pl.BlockSpec(((block + 1) * n, width), here)],
        out_shape=[
            jax.ShapeDtypeStruct((tokens, chans), jnp.float32),
            jax.ShapeDtypeStruct((seqs * blocks * (block + 1) * n, chans), jnp.bfloat16),
        ],
        scratch_shapes=[pltpu.VMEM((n, width), jnp.float32)] + [pltpu.VMEM((GROUP * n, width), jnp.bfloat16)] * 2,
        compiler_params=pltpu.CompilerParams(vmem_limit_bytes=VMEM_LIMIT),
        cost_estimate=pl.CostEstimate(flops=1400 * work, transcendentals=work, bytes_accessed=2 * work),
        name="fwd_full",
    )(dte, dtx, slabs, read, rate, start)


def bwd_full_body(dte_ref, dtx_ref, grad_ref, hist_ref, slab_ref, write_ref, ones_ref, rate_ref, start_ref,
                  s1_ref, s2_ref, grate_ref, dw_ref, dr_ref, g_ref, *scratch):
    block = dte_ref.shape[0]
    n, width = rate_ref.shape
    groups = block // GROUP
    bf, f32 = jnp.bfloat16, jnp.float32
    even, odd = scratch[:5], scratch[5:]
    unit = jnp.ones((GROUP, 128), bf)

    @pl.when(pl.program_id(2) == 0)
    def _():
        g_ref[...] = start_ref[...]

    @pl.when((pl.program_id(2) == 0) & (pl.program_id(1) == 0))
    def _():
        grate_ref[...] = jnp.zeros_like(grate_ref)

    def sums_out(at, bufs):
        _, _, adj_ref, rated_ref, dw_part = bufs
        rows = pl.ds(at * GROUP, GROUP)
        s1_ref[rows, :] = jnp.dot(write_ref[rows, :], adj_ref[...], preferred_element_type=f32)
        sums = jnp.dot(ones_ref[...], rated_ref[...], preferred_element_type=f32)
        s2_ref[rows, :] = sums[:GROUP]
        dw_ref[pl.ds(at, 1), :] = lax.dot_general(unit, dw_part[...], NT, preferred_element_type=f32)[:1]
        reads = lax.dot_general(
            grad_ref[rows, :].astype(bf), hist_ref[pl.ds(n + at * GROUP * n, GROUP * n), :], NT,
            preferred_element_type=f32)
        own = lax.broadcasted_iota(jnp.int32, reads.shape, 1) // n == lax.broadcasted_iota(jnp.int32, reads.shape, 0)
        dr_ref[pl.ds(at, 1), :] = jnp.sum(jnp.where(own, reads, 0.0), axis=0, keepdims=True)
        return sums[GROUP:]

    def strips(values):
        parts = [values[:, k * 128 : (k + 1) * 128] for k in range(width // 128)]
        while len(parts) > 1:
            parts = [a + b for a, b in zip(parts[::2], parts[1::2])] + parts[len(parts) // 2 * 2 :]
        return parts[0]

    def walk(at, state, bufs):
        decay_ref, power_ref, adj_ref, rated_ref, dw_part = bufs
        slab = slab_ref[pl.ds(at * n, n), :]
        for place in reversed(range(GROUP)):
            t = at * GROUP + place
            here = pl.ds(place * n, n)
            read = across(slab, place, width)
            adjoint = state + grad_ref[pl.ds(t, 1), :] * read
            power = dte_ref[pl.ds(t, 1), :] * rate_ref[...]
            state = jnp.exp2(power) * adjoint
            low = adjoint.astype(bf)
            adj_ref[here, :] = low
            rated_ref[here, :] = state.astype(bf) * hist_ref[pl.ds(t * n, n), :] * power.astype(bf)
            dw_part[here, :] = strips(adjoint * dtx_ref[pl.ds(t, 1), :]).astype(bf)
        return state

    def pair(step, state):
        at = groups - 1 - 2 * step
        old = sums_out(jnp.minimum(at + 1, groups - 1), odd)
        state = walk(at, state, even)
        grate_ref[...] += jnp.where(step > 0, old, 0.0) + sums_out(at, even)
        return walk(at - 1, state, odd)
    g_ref[...] = lax.fori_loop(0, groups // 2, pair, g_ref[...])
    grate_ref[...] += sums_out(0, odd)


def bwd_full(dte, dtx, grad, hist, slabs, write, rate, start, seqs, width=512, block=256):
    tokens, chans = dte.shape
    n = rate.shape[0]
    width = min(width, chans)
    strips = chans // width
    blocks = tokens // seqs // block
    span = GROUP * n
    work = tokens * chans * n
    column = jnp.arange(span)
    ones = jnp.concatenate(
        [(column // n)[None, :] == jnp.arange(GROUP)[:, None], (column % n)[None, :] == jnp.arange(n)[:, None]]
    ).astype(jnp.bfloat16)
    here = lambda c, s, t: (s * blocks + blocks - 1 - t, c)
    rows = lambda c, s, t: (s * blocks + blocks - 1 - t, 0)
    strip = lambda c, s, t: (c * seqs * blocks + s * blocks + blocks - 1 - t, 0)
    f32 = jnp.float32
    s1, s2, grate, dw, dr = pl.pallas_call(
        bwd_full_body,
        grid=(strips, seqs, blocks),
        in_specs=[
            pl.BlockSpec((block, width), here),
            pl.BlockSpec((block, width), here),
            pl.BlockSpec((block, width), here),
            pl.BlockSpec(((block + 1) * n, width), here),
            pl.BlockSpec((block // GROUP * n, GROUP), rows),
            pl.BlockSpec((block, span), rows),
            pl.BlockSpec(ones.shape, lambda c, s, t: (0, 0)),
            pl.BlockSpec((n, width), lambda c, s, t: (0, c)),
            pl.BlockSpec((n, width), lambda c, s, t: (s, c)),
        ],
        out_specs=[
            pl.BlockSpec((block, width), here),
            pl.BlockSpec((block, width), here),
            pl.BlockSpec((n, width), lambda c, s, t: (0, c)),
            pl.BlockSpec((block // GROUP, span), strip),
            pl.BlockSpec((block // GROUP, span), strip),
        ],
        out_shape=[
            jax.ShapeDtypeStruct((tokens, chans), f32),
            jax.ShapeDtypeStruct((tokens, chans), f32),
            jax.ShapeDtypeStruct((n, chans), f32),
            jax.ShapeDtypeStruct((strips * tokens // GROUP, span), f32),
            jax.ShapeDtypeStruct((strips * tokens // GROUP, span), f32),
        ],
        scratch_shapes=[
            pltpu.VMEM((n, width), f32),
            *[
                pltpu.VMEM((span, width), f32),
                *[pltpu.VMEM((span, width), jnp.bfloat16)] * 3,
                pltpu.VMEM((span, 128), jnp.bfloat16),
            ] * 2,
        ],
        compiler_params=pltpu.CompilerParams(vmem_limit_bytes=VMEM_LIMIT),
        cost_estimate=pl.CostEstimate(flops=3200 * work, transcendentals=work, bytes_accessed=2 * work),
        name="bwd_full",
    )(dte, dtx, grad, hist, slabs, write, ones, rate, start)
    both = jnp.stack([part.reshape(strips, tokens // GROUP, span).sum(0) for part in (dw, dr)])
    both = both.reshape(2, tokens // GROUP, GROUP, n).transpose(0, 3, 1, 2).reshape(2, n, tokens)
    return s1, s2, grate, both[0], both[1]


def slabs_of(values):
    n, tokens = values.shape
    return values.reshape(n, tokens // GROUP, GROUP).transpose(1, 0, 2).reshape(tokens // GROUP * n, GROUP)


def spread(values):
    n, tokens = values.shape
    own = jnp.arange(tokens)[:, None] % GROUP == jnp.arange(GROUP)[None, :]
    return jnp.where(own[:, :, None], values.T[:, None, :], 0).reshape(tokens, GROUP * n).astype(jnp.bfloat16)


MESH = pl.DeviceIdType.MESH


class Grid:
    def __init__(self, axis, size, inner):
        self.axis, self.inner, self.outer = axis, inner, size // inner
        me = lax.axis_index(axis)
        self.row, self.col = me // inner, me % inner

    def device(self, row, col):
        return {self.axis: row * self.inner + col}

    def neighbours(self):
        row, col = self.row, self.col
        found = []
        if self.outer > 1:
            found += [(row > 0, self.device(row - 1, col)), (row < self.outer - 1, self.device(row + 1, col))]
        if self.inner > 1:
            found += [(col > 0, self.device(row, col - 1)), (col < self.inner - 1, self.device(row, col + 1))]
        return found

    def everyone(self):
        size = self.inner * self.outer
        me = self.row * self.inner + self.col
        return [(me >= 0, {self.axis: (me + step) % size}) for step in range(1, size)]


def greet(grids, all_of=()):
    barrier = pltpu.get_barrier_semaphore()
    count = 0
    for grid in grids:
        for there, device in grid.everyone() if grid.axis in all_of else grid.neighbours():

            @pl.when(there)
            def _(device=device):
                pl.semaphore_signal(barrier, inc=1, device_id=device, device_id_type=MESH)

            count = count + there.astype(jnp.int32)
    pl.semaphore_wait(barrier, count)


def gather_steps(grid, whole_ref, out_ref, send_sem, recv_sem, own, waits, chunk, chunks, across_too=True, ways=(True, True)):
    rows = whole_ref.shape[0]
    part = rows // chunks
    src_ref = whole_ref.at[pl.ds(chunk * part, part)]
    outer, inner = grid.outer, grid.inner if across_too else 1
    row, col = grid.row, grid.col

    def number(r, c):
        return r * inner + c if across_too else r

    def place(r, c):
        return pl.ds(pl.multiple_of(number(r, c) * rows + chunk * part, part), part)

    def send(there, way, r, c, device, source):
        copy = pltpu.make_async_remote_copy(
            src_ref=source, dst_ref=out_ref.at[place(r, c)], send_sem=send_sem.at[way, number(r, c)],
            recv_sem=recv_sem.at[number(r, c)], device_id=device, device_id_type=MESH)

        @pl.when(there)
        def _():
            copy.start()

        waits.append((there, copy))

    def across(there, r, c, source):
        if inner > 1:
            send(there & (c >= col) & (col > 0), 2, r, c, grid.device(row, col - 1), source)
            send(there & (c <= col) & (col < inner - 1), 3, r, c, grid.device(row, col + 1), source)

    def along(there, r, source):
        if outer > 1:
            if ways[0]:
                send(there & (r >= row) & (row > 0), 0, r, col, grid.device(row - 1, col), source)
            if ways[1]:
                send(there & (r <= row) & (row < outer - 1), 1, r, col, grid.device(row + 1, col), source)

    def arrive(there, r, c):
        copy = pltpu.make_async_remote_copy(
            src_ref=src_ref, dst_ref=out_ref.at[place(r, c)], send_sem=send_sem.at[0, 0],
            recv_sem=recv_sem.at[number(r, c)], device_id=grid.device(row, col), device_id_type=MESH)

        @pl.when(there)
        def _():
            copy.wait_recv()

    always = row >= 0
    along(always, row, src_ref)
    across(always, row, col, src_ref)
    own_sem, own_buf = own
    fetch = pltpu.make_async_copy(src_ref, own_buf, own_sem.at[0])
    fetch.start()
    for _ in range(chunk + 1):
        yield
    fetch.wait()
    keep = pltpu.make_async_copy(own_buf, out_ref.at[place(row, col)], own_sem.at[1])
    keep.start()
    waits.append((None, keep))

    def rows_at(distance):
        return [row - distance] * ways[1] + [row + distance] * ways[0]

    for distance in range(1, outer):
        for r in rows_at(distance):
            there = (r >= 0) & (r < outer)
            arrive(there, r, col)
            along(there, r, out_ref.at[place(r, col)])
            across(there, r, col, out_ref.at[place(r, col)])
        yield
    for step in range(1, inner):
        for distance in range(outer):
            for r in rows_at(distance) if distance else (row,):
                for c in (col - step, col + step):
                    there = (r >= 0) & (r < outer) & (c >= 0) & (c < inner)
                    arrive(there, r, c)
                    if step < inner - 1:
                        across(there, r, c, out_ref.at[place(r, c)])
            yield


def finish(waits):
    for there, copy in waits:
        if there is None:
            copy.wait()
        else:

            @pl.when(there)
            def _(copy=copy):
                if copy.is_remote:
                    copy.wait_send()
                else:
                    copy.wait()


def gather_scratch(size, array, chunks):
    dma = pltpu.SemaphoreType.DMA
    own = pltpu.VMEM((array.shape[0] // chunks, *array.shape[1:]), array.dtype)
    return [dma((4, size)), dma((size,)), dma((2,)), own] * chunks


def in_turn(runs):
    runs = list(runs)
    while runs:
        left = []
        for run in runs:
            if next(run, run) is not run:
                left.append(run)
        runs = left


def link_gather(arrays, sizes, collective_id, ways=(True, True)):
    count = len(arrays)
    axes = sorted({entry[0] for entry in arrays})

    def kernel(*refs):
        sources, outs, sems = refs[:count], refs[count : 2 * count], refs[2 * count :]
        grids = {axis: Grid(axis, *sizes[axis]) for axis in axes}
        greet([grids[axis] for axis in axes])
        waits = []
        runs = []
        for i, (axis, _, chunks) in enumerate(arrays):
            for chunk in range(chunks):
                runs.append(gather_steps(
                    grids[axis], sources[i], outs[i], sems[0], sems[1], sems[2:4], waits, chunk, chunks, ways=ways))
                sems = sems[4:]
        in_turn(runs)
        finish(waits)

    sems = []
    for axis, a, chunks in arrays:
        sems += gather_scratch(sizes[axis][0], a, chunks)
    return pl.pallas_call(
        kernel,
        in_specs=[pl.BlockSpec(memory_space=pl.ANY)] * count,
        out_specs=[pl.BlockSpec(memory_space=pl.ANY)] * count,
        out_shape=[
            jax.ShapeDtypeStruct((sizes[axis][0] * a.shape[0], *a.shape[1:]), a.dtype) for axis, a, _ in arrays],
        scratch_shapes=sems,
        compiler_params=pltpu.CompilerParams(
            collective_id=collective_id, has_side_effects=True, vmem_limit_bytes=VMEM_LIMIT),
        cost_estimate=pl.CostEstimate(flops=LINK_COST, transcendentals=0, bytes_accessed=0),
        name="link_gather",
    )(*[a for _, a, _ in arrays])


def reduce_steps(grid, src_ref, out_ref, scratch, waits, chunks, share):
    acc, inner_buf, outer_buf, load_sem, inner_send, inner_recv, outer_send, outer_recv, out_sem = scratch[:9]
    outer, inner = grid.outer, grid.inner
    row, col = grid.row, grid.col
    rows = acc.shape[0] // (outer * inner)
    part = rows // chunks
    piece = min(part, 64)

    def start_of(chunk, r, c):
        return pl.multiple_of((r * inner + c) * rows + chunk * part, part)

    def line(me, size, device, block, buf, send, recv):
        def from_low(target):
            return target if size > 2 else 0

        def from_high(target, owner):
            return jnp.where(target == owner, size, target) if size > 2 else 0

        def hop(there, target, onward, slot):
            copy = pltpu.make_async_remote_copy(
                src_ref=acc.at[pl.ds(block(target), part)], dst_ref=buf.at[slot], send_sem=send.at[target],
                recv_sem=recv.at[slot], device_id=device(onward), device_id_type=MESH)

            @pl.when(there)
            def _():
                copy.start()

            waits.append((there, copy))

        def up(there, target):
            hop(there & (target > me), target, me + 1, from_low(target))

        def down(there, target):
            hop(there & (target < me), target, me - 1, from_high(target, me - 1))

        def arrive(there, target, slot):
            at = block(target)
            copy = pltpu.make_async_remote_copy(
                src_ref=acc.at[pl.ds(at, part)], dst_ref=buf.at[slot], send_sem=send.at[target],
                recv_sem=recv.at[slot], device_id=device(me), device_id_type=MESH)

            @pl.when(there)
            def _():
                copy.wait_recv()

                @pl.loop(0, part // piece)
                def _(k):
                    here = pl.ds(pl.multiple_of(at + k * piece, piece), piece)
                    there_rows = pl.ds(pl.multiple_of(k * piece, piece), piece)
                    total = acc[here, :].astype(jnp.float32) + buf[slot, there_rows, :].astype(jnp.float32)
                    acc[here, :] = total.astype(acc.dtype)

        def begin(target):
            up(me == 0, target)
            down(me == size - 1, target)

        def go_on(target):
            arrive((me > 0) & (target >= me), target, from_low(target))
            arrive((me < size - 1) & (target <= me), target, from_high(target, me))
            if size > 2:
                up((me > 0) & (me < size - 1), target)
                down((me > 0) & (me < size - 1), target)

        return begin, go_on

    order = sorted(range(outer), key=lambda k: -abs(2 * k - outer + 1))
    pieces = [(chunk, r) for chunk in range(chunks) for r in order]
    loads = {}
    for chunk, r in pieces:
        loads[chunk, r] = [
            pltpu.make_async_copy(
                src_ref.at[pl.ds(start_of(chunk, r, c), part)], acc.at[pl.ds(start_of(chunk, r, c), part)],
                load_sem.at[chunk, r * inner + c])
            for c in range(inner)]
        for load in loads[chunk, r]:
            load.start()

    def inner_line(chunk, r):
        return line(
            col, inner, lambda c: grid.device(row, c), lambda t: start_of(chunk, r, t), inner_buf.at[chunk, r],
            inner_send.at[chunk, r], inner_recv.at[chunk, r])

    def outer_line(chunk):
        return line(
            row, outer, lambda r: grid.device(r, col), lambda t: start_of(chunk, t, col), outer_buf.at[chunk],
            outer_send.at[chunk], outer_recv.at[chunk])

    def inner_start(k):
        if k < len(pieces):
            for load in loads[pieces[k]]:
                load.wait()
            if inner > 1:
                for c in range(inner):
                    inner_line(*pieces[k])[0](c)

    def outer_rest(k):
        if 0 <= k < len(pieces):
            chunk, r = pieces[k]
            if outer > 1:
                outer_line(chunk)[1](r)
            if r == order[-1]:
                give(chunk)

    def give(chunk):
        first = start_of(chunk, row, col)
        if share is None:
            last = pltpu.make_async_copy(
                acc.at[pl.ds(first, part)], out_ref.at[pl.ds(chunk * part, part)], out_sem.at[chunk])
            last.start()
            waits.append((None, last))
            return
        other, strip, send_sem, recv_sem = share
        count, me = other.outer * other.inner, other.row * other.inner + other.col
        take = rows // count
        for mate in range(chunk * part // take, (chunk + 1) * part // take):
            for k in range(acc.shape[1] // strip):
                source = acc.at[
                    pl.ds(pl.multiple_of((row * inner + col) * rows + mate * take, take), take),
                    pl.ds(k * strip, strip)]
                target = out_ref.at[:, pl.ds(pl.multiple_of((k * count + me) * strip, strip), strip)]
                own = pltpu.make_async_copy(source, target, send_sem.at[mate, k])
                sent = pltpu.make_async_remote_copy(
                    src_ref=source, dst_ref=target, send_sem=send_sem.at[mate, k], recv_sem=recv_sem.at[me, k],
                    device_id={other.axis: mate}, device_id_type=MESH)

                @pl.when(mate == me)
                def _(own=own):
                    own.start()

                @pl.when(mate != me)
                def _(sent=sent):
                    sent.start()

                waits.append((mate != me, sent))
                waits.append((mate == me, own))

    window = 2
    for k in range(window):
        inner_start(k)
    yield
    for k in range(len(pieces)):
        inner_start(k + window)
        chunk, r = pieces[k]
        if inner > 1:
            for c in range(inner):
                inner_line(chunk, r)[1](c)
        if outer > 1:
            outer_line(chunk)[0](r)
        yield
        outer_rest(k - window)
        yield
    for k in range(len(pieces) - window, len(pieces)):
        outer_rest(k)
        yield
    if share is not None:
        other, strip, send_sem, recv_sem = share
        count, me = other.outer * other.inner, other.row * other.inner + other.col
        take = rows // count
        for mate in range(count):
            for k in range(acc.shape[1] // strip):
                copy = pltpu.make_async_remote_copy(
                    src_ref=acc.at[pl.ds(0, take), pl.ds(k * strip, strip)],
                    dst_ref=out_ref.at[:, pl.ds((k * count + mate) * strip, strip)], send_sem=send_sem.at[mate, k],
                    recv_sem=recv_sem.at[mate, k], device_id={other.axis: me}, device_id_type=MESH)

                @pl.when(mate != me)
                def _(copy=copy):
                    copy.wait_recv()


def link_reduce(arrays, sizes, collective_id):
    count = len(arrays)

    def kernel(*refs):
        sources, outs, scratch = refs[:count], refs[count : 2 * count], refs[2 * count :]
        grids = {axis: Grid(axis, *sizes[axis]) for axis in ("seq", "stream")}
        greet(list(grids.values()), ("stream",))
        waits = []
        runs = []
        for i, (axis, _, chunks, strip) in enumerate(arrays):
            share = (grids["stream"], strip, scratch[9], scratch[10]) if strip else None
            runs.append(reduce_steps(grids[axis], sources[i], outs[i], scratch[:9], waits, chunks, share))
            scratch = scratch[11 if strip else 9 :]
        in_turn(runs)
        finish(waits)

    scratch, shapes = [], []
    for axis, a, chunks, strip in arrays:
        size, inner = sizes[axis]
        outer = size // inner
        part = a.shape[0] // size // chunks
        slots = [n + 1 if n > 2 else 1 for n in (inner, outer)]
        dma = pltpu.SemaphoreType.DMA
        scratch += [
            pltpu.VMEM(a.shape, a.dtype),
            pltpu.VMEM((chunks, outer, slots[0], part, a.shape[1]), a.dtype),
            pltpu.VMEM((chunks, slots[1], part, a.shape[1]), a.dtype),
            dma((chunks, size)), dma((chunks, outer, inner)), dma((chunks, outer, slots[0])), dma((chunks, outer)),
            dma((chunks, slots[1])), dma((chunks,))]
        if strip:
            mates = sizes["stream"][0]
            shapes.append(jax.ShapeDtypeStruct((a.shape[0] // size // mates, a.shape[1] * mates), a.dtype))
            scratch += [dma((mates, a.shape[1] // strip))] * 2
        else:
            shapes.append(jax.ShapeDtypeStruct((a.shape[0] // size, a.shape[1]), a.dtype))
    return pl.pallas_call(
        kernel,
        in_specs=[pl.BlockSpec(memory_space=pl.ANY)] * count,
        out_specs=[pl.BlockSpec(memory_space=pl.ANY)] * count,
        out_shape=shapes,
        scratch_shapes=scratch,
        compiler_params=pltpu.CompilerParams(
            collective_id=collective_id, has_side_effects=True, vmem_limit_bytes=VMEM_LIMIT),
        cost_estimate=pl.CostEstimate(flops=4 * LINK_COST, transcendentals=0, bytes_accessed=0),
        name="link_reduce",
    )(*[entry[1] for entry in arrays])


def link_sum(partial, sizes, collective_id):
    rows, width = partial.shape
    size, inner = sizes["stream"]
    outer = size // inner
    assert inner == 2
    half = rows // 2
    bf, f32 = jnp.bfloat16, jnp.float32
    dma = pltpu.SemaphoreType.DMA

    def kernel(own_ref, out_ref, mate_buf, pair_ref, terms_ref, total_ref, send, recv, line_send, line_recv, own_sem, own_buf):
        grid = Grid("stream", size, inner)
        row, col = grid.row, grid.col
        greet([grid])
        mate = grid.device(row, 1 - col)
        mine = pl.ds(pl.multiple_of(col * half, half), half)
        swap = pltpu.make_async_remote_copy(
            src_ref=own_ref, dst_ref=mate_buf, send_sem=send.at[0], recv_sem=recv.at[0], device_id=mate,
            device_id_type=MESH)
        swap.start()
        swap.wait_recv()
        pair_ref[...] = (own_ref[mine, :].astype(f32) + mate_buf[mine, :].astype(f32)).astype(bf)
        waits = []
        line = Grid("stream", size, inner)
        in_turn([gather_steps(
            line, pair_ref, terms_ref, line_send, line_recv, (own_sem, own_buf), waits, 0, 1, across_too=False)])
        finish(waits)
        total = terms_ref[pl.ds(0, half), :].astype(f32)
        for r in range(1, outer):
            total = total + terms_ref[pl.ds(r * half, half), :].astype(f32)
        total_ref[...] = total
        out_ref[mine, :] = total
        swap_back = pltpu.make_async_remote_copy(
            src_ref=total_ref, dst_ref=out_ref.at[mine], send_sem=send.at[1], recv_sem=recv.at[1], device_id=mate,
            device_id_type=MESH)
        swap_back.start()
        theirs = pltpu.make_async_remote_copy(
            src_ref=total_ref, dst_ref=out_ref.at[pl.ds(pl.multiple_of((1 - col) * half, half), half)],
            send_sem=send.at[1], recv_sem=recv.at[1], device_id=mate, device_id_type=MESH)
        theirs.wait_recv()
        swap.wait_send()
        swap_back.wait_send()

    return pl.pallas_call(
        kernel,
        in_specs=[pl.BlockSpec(memory_space=pltpu.VMEM)],
        out_specs=pl.BlockSpec(memory_space=pltpu.VMEM),
        out_shape=jax.ShapeDtypeStruct((rows, width), f32),
        scratch_shapes=[
            pltpu.VMEM((rows, width), bf), pltpu.VMEM((half, width), bf), pltpu.VMEM((outer * half, width), bf),
            pltpu.VMEM((half, width), f32), dma((2,)), dma((2,)), dma((4, outer)), dma((outer,)), dma((2,)),
            pltpu.VMEM((half, width), bf)],
        compiler_params=pltpu.CompilerParams(
            collective_id=collective_id, has_side_effects=True, vmem_limit_bytes=VMEM_LIMIT),
        cost_estimate=pl.CostEstimate(flops=LINK_COST, transcendentals=0, bytes_accessed=0),
        name="link_sum",
    )(partial.astype(bf))


def link_open(conv, gate, arrays, sizes, collective_id):
    count = len(arrays)
    mates = sizes["stream"][0]
    take = conv.shape[0] // mates
    dma = pltpu.SemaphoreType.DMA

    def kernel(conv_ref, gate_ref, *refs):
        sources, refs = refs[:count], refs[count:]
        conv_all, conv_own, gate_own, outs, refs = *refs[:3], refs[3 : 3 + count], refs[3 + count :]
        hand_send, hand_recv, hand_buf, sems = refs[0], refs[1], refs[2], refs[3:]
        grids = {axis: Grid(axis, *sizes[axis]) for axis in ("seq", "stream")}
        greet(list(grids.values()), ("stream",))
        me = grids["stream"].row * grids["stream"].inner + grids["stream"].col
        waits = []

        def rows(mate):
            return pl.ds(pl.multiple_of(mate * take, take), take)

        def hand(kind, source, target):
            fetch = pltpu.make_async_copy(source.at[rows(me)], hand_buf.at[kind], hand_send.at[kind, 0])
            fetch.start()
            for step in range(1, mates):
                mate = (me + step) % mates
                copy = pltpu.make_async_remote_copy(
                    src_ref=source.at[rows(mate)], dst_ref=target.at[rows(me)], send_sem=hand_send.at[kind, step],
                    recv_sem=hand_recv.at[kind, step], device_id={"stream": mate}, device_id_type=MESH)
                copy.start()
                waits.append((me >= 0, copy))
            fetch.wait()
            keep = pltpu.make_async_copy(hand_buf.at[kind], target.at[rows(me)], hand_recv.at[kind, 0])
            keep.start()
            return keep

        def handed(kind, source, target, own):
            own.wait()
            for step in range(1, mates):
                mate = (me + mates - step) % mates
                pltpu.make_async_remote_copy(
                    src_ref=source.at[rows(me)], dst_ref=target.at[rows(mate)], send_sem=hand_send.at[kind, step],
                    recv_sem=hand_recv.at[kind, step], device_id={"stream": me}, device_id_type=MESH).wait_recv()

        own = hand(0, conv_ref, conv_own)

        def main():
            for i, (axis, _, chunks) in enumerate(arrays):
                for chunk in range(chunks):
                    at = 4 * (1 + sum(entry[2] for entry in arrays[:i]) + chunk)
                    yield gather_steps(
                        grids[axis], sources[i], outs[i], sems[at], sems[at + 1], sems[at + 2 : at + 4], waits, chunk,
                        chunks)

        runs = list(main())
        for run in runs:
            next(run)
        own_gate = hand(1, gate_ref, gate_own)
        handed(0, conv_ref, conv_own, own)
        first = gather_steps(grids["seq"], conv_own, conv_all, sems[0], sems[1], sems[2:4], waits, 0, 1)
        next(first)
        in_turn([first, *runs])
        handed(1, gate_ref, gate_own, own_gate)
        finish(waits)

    entries = [("seq", conv, 1), *arrays]
    sems = []
    for axis, a, chunks in entries:
        sems += gather_scratch(sizes[axis][0], a, chunks)
    result = pl.pallas_call(
        kernel,
        in_specs=[pl.BlockSpec(memory_space=pl.ANY)] * (count + 2),
        out_specs=[pl.BlockSpec(memory_space=pl.ANY)] * (count + 3),
        out_shape=[
            jax.ShapeDtypeStruct((sizes["seq"][0] * conv.shape[0], conv.shape[1]), conv.dtype),
            jax.ShapeDtypeStruct(conv.shape, conv.dtype),
            jax.ShapeDtypeStruct(gate.shape, gate.dtype),
            *[jax.ShapeDtypeStruct((sizes[axis][0] * a.shape[0], *a.shape[1:]), a.dtype) for axis, a, _ in arrays]],
        scratch_shapes=[
            dma((2, mates)), dma((2, mates)), pltpu.VMEM((2, take, conv.shape[1]), conv.dtype), *sems],
        compiler_params=pltpu.CompilerParams(
            collective_id=collective_id, has_side_effects=True, vmem_limit_bytes=VMEM_LIMIT),
        cost_estimate=pl.CostEstimate(flops=4 * LINK_COST, transcendentals=0, bytes_accessed=0),
        name="link_open",
    )(conv, gate, *[a for _, a, _ in arrays])
    return result[0], result[2], *result[3:]


ROWS = 128


def conv_fwd_body(x_ref, early_ref, masks_ref, taps_ref, act_ref, slope_ref, ext_ref):
    length = x_ref.shape[0]
    ext_ref[pl.ds(0, 8), :] = early_ref[...]

    @pl.loop(0, length // ROWS)
    def _(k):
        here = pl.ds(pl.multiple_of(k * ROWS, ROWS), ROWS)
        ext_ref[pl.ds(pl.multiple_of(k * ROWS + 8, 8), ROWS), :] = x_ref[here, :]
        window = ext_ref[pl.ds(pl.multiple_of(k * ROWS, ROWS), ROWS + 8), :]
        masks = masks_ref[here, :]
        total = taps_ref[CONV : CONV + 1, :] + taps_ref[CONV - 1 : CONV, :] * window[8:]
        for tap in range(CONV - 1):
            shift = 8 - (CONV - 1) + tap
            total = total + taps_ref[tap : tap + 1, :] * (window[shift : shift + ROWS] * masks[:, tap : tap + 1])
        gate = jax.nn.sigmoid(total)
        act_ref[here, :] = (total * gate).astype(act_ref.dtype)
        slope_ref[here, :] = (gate * (1.0 + total * (1.0 - gate))).astype(slope_ref.dtype)


def conv_bwd_body(grad_ref, slope_ref, late_ref, x_ref, masks_ref, taps_ref, out_ref, sums_ref, ext_ref):
    length, width = x_ref.shape
    ext_ref[pl.ds(length, 8), :] = late_ref[...]

    @pl.loop(0, length // ROWS)
    def _(k):
        here = pl.ds(pl.multiple_of(k * ROWS, ROWS), ROWS)
        ext_ref[here, :] = grad_ref[here, :] * slope_ref[here, :].astype(jnp.float32)

    def some(k, sums):
        start = pl.multiple_of(k * ROWS, ROWS)
        here = pl.ds(start, ROWS)
        window = ext_ref[pl.ds(start, ROWS + 8), :]
        masks = masks_ref[here, :]
        x = x_ref[here, :]
        total = jnp.zeros((ROWS, width), jnp.float32)
        parts = []
        for tap in range(CONV):
            ahead = CONV - 1 - tap
            term = window[ahead : ahead + ROWS]
            if ahead:
                term = term * masks[:, CONV - 2 + ahead : CONV - 1 + ahead]
            total = total + taps_ref[tap : tap + 1, :] * term
            parts.append((term * x).reshape(ROWS // 8, 8, width).sum(0))
        parts.append(window[:ROWS].reshape(ROWS // 8, 8, width).sum(0))
        out_ref[here, :] = total.astype(out_ref.dtype)
        return tuple(a + b for a, b in zip(sums, parts))

    sums = lax.fori_loop(0, length // ROWS, some, (jnp.zeros((8, width), jnp.float32),) * (CONV + 1))
    for tap in range(CONV + 1):
        sums_ref[tap : tap + 1, :] = jnp.sum(sums[tap], axis=0, keepdims=True)
    sums_ref[CONV + 1 :, :] = jnp.zeros((7 - CONV, width), jnp.float32)


def conv_fwd(x, early, masks, taps, seqs, width=1024):
    tokens, chans = x.shape
    width = min(width, chans)
    length = tokens // seqs
    block = pl.BlockSpec((length, width), lambda s, c: (s, c))
    return pl.pallas_call(
        conv_fwd_body,
        grid=(seqs, chans // width),
        in_specs=[
            block, pl.BlockSpec((8, width), lambda s, c: (s, c)), pl.BlockSpec((length, 8), lambda s, c: (s, 0)),
            pl.BlockSpec((8, width), lambda s, c: (0, c))],
        out_specs=[block, block],
        out_shape=[jax.ShapeDtypeStruct((tokens, chans), jnp.bfloat16)] * 2,
        scratch_shapes=[pltpu.VMEM((length + 8, width), jnp.float32)],
        compiler_params=pltpu.CompilerParams(vmem_limit_bytes=VMEM_LIMIT),
        cost_estimate=pl.CostEstimate(
            flops=4000 * tokens * chans, transcendentals=tokens * chans, bytes_accessed=8 * tokens * chans),
        name="conv_fwd",
    )(x, early, masks, taps)


def conv_bwd(grad, slope, late, x, masks, taps, seqs, width=512):
    tokens, chans = x.shape
    width = min(width, chans)
    length = tokens // seqs
    block = pl.BlockSpec((length, width), lambda s, c: (s, c))
    rim = pl.BlockSpec((8, width), lambda s, c: (s, c))
    return pl.pallas_call(
        conv_bwd_body,
        grid=(seqs, chans // width),
        in_specs=[
            block, block, rim, block, pl.BlockSpec((length, 8), lambda s, c: (s, 0)),
            pl.BlockSpec((8, width), lambda s, c: (0, c))],
        out_specs=[block, rim],
        out_shape=[
            jax.ShapeDtypeStruct((tokens, chans), jnp.bfloat16), jax.ShapeDtypeStruct((seqs * 8, chans), jnp.float32)],
        scratch_shapes=[pltpu.VMEM((length + 8, width), jnp.float32)],
        compiler_params=pltpu.CompilerParams(vmem_limit_bytes=VMEM_LIMIT),
        cost_estimate=pl.CostEstimate(
            flops=5000 * tokens * chans, transcendentals=0, bytes_accessed=12 * tokens * chans),
        name="conv_bwd",
    )(grad, slope, late, x, masks, taps)


def passed_along(block, axis, distance):
    devices = range(lax.axis_size(axis))
    route = [(i - distance, i) for i in devices if i - distance in devices]
    return lax.ppermute(block, axis, route)


def silu_slope(values_in):
    sigmoid_v = jax.nn.sigmoid(values_in)
    return sigmoid_v * (1.0 + values_in * (1.0 - sigmoid_v))


def token_layout(lengths, first_pos, n_tokens):
    doc_ends = jnp.cumsum(lengths)
    begins = doc_ends - lengths
    positions = first_pos + jnp.arange(n_tokens, dtype=jnp.int32)
    live_slot = (lengths > 0)[None, :]
    doc_ids = jnp.sum(((begins[None, :] <= positions[:, None]) & live_slot).astype(jnp.int32), axis=1)
    start_flags = jnp.sum(((begins[None, :] == positions[:, None]) & live_slot).astype(jnp.float32), axis=1)
    valid_mask = (positions < doc_ends[-1]).astype(jnp.float32)
    return (doc_ids, start_flags, valid_mask)


def contract_rows(left_mat, right_mat):
    return lax.dot_general(left_mat, right_mat, (((0,), (0,)), ((), ())), preferred_element_type=jnp.float32)


def contract_cols(left_mat, right_mat):
    return lax.dot_general(left_mat, right_mat, NT, preferred_element_type=jnp.float32)


def padded_rows(array, rows):
    return jnp.pad(array, ((0, -array.shape[0] % rows), (0, 0)))


def carried(ends, step_sum, rate, backward, sizes, collective_id):
    seqs, chans = step_sum.shape
    n = rate.shape[0]
    high = step_sum.astype(jnp.bfloat16)
    low = (step_sum - high.astype(jnp.float32)).astype(jnp.bfloat16)
    sent = padded_rows(jnp.concatenate([ends.astype(jnp.bfloat16), high, low], axis=0), 16)
    (gathered,) = link_gather([("seq", sent, 1)], sizes, collective_id, (backward, not backward))
    gathered = gathered.reshape(-1, *sent.shape)
    count = lax.axis_size("seq")
    place = lax.axis_index("seq")
    state = jnp.zeros((seqs, n, chans), jnp.float32)
    for step in range(count - 1):
        source = count - 1 - step if backward else step
        block = gathered[source].astype(jnp.float32)
        total = block[seqs * n : seqs * (n + 1)] + block[seqs * (n + 1) : seqs * (n + 2)]
        joined = jnp.exp2(total[:, None, :] * rate[None]) * state + block[: seqs * n].reshape(seqs, n, chans)
        state = jnp.where(source > place if backward else source < place, joined, state)
    return state.reshape(seqs * n, chans)


def local(sizes, resid_in, out_grad, row_lengths, norm_gain, in_weight, conv_weight, conv_bias, xproj_weight, dt_weight,
          dt_bias, a_log, skip_gain, out_weight):
    bf, f32 = jnp.bfloat16, jnp.float32
    seqs = lax.axis_size("stream")
    parts = lax.axis_size("seq")
    own = conv_bias.shape[0]
    own_feats = norm_gain.shape[0]
    chans = own * parts
    rank_dim = dt_weight.shape[0]
    state_dim = a_log.shape[1]
    proj_dim = xproj_weight.shape[1]
    length, feats = resid_in.shape[1:]
    tokens = seqs * length

    gain = norm_gain.astype(f32)
    scaled = (in_weight.astype(f32) * gain[:, None]).astype(bf).reshape(own_feats, 2, parts, seqs, own)
    scaled = scaled.transpose(1, 3, 0, 2, 4).reshape(2, seqs * own_feats, chans)
    packed = jnp.concatenate(
        [xproj_weight, dt_weight.T, a_log, conv_weight.T, conv_bias[:, None], dt_bias[:, None], skip_gain[:, None]],
        axis=1)
    residual = resid_in[0].astype(f32)
    cotangent = out_grad[0]
    inv_rms = lax.rsqrt(jnp.mean(residual * residual, axis=-1, keepdims=True) + EPSILON)
    unit_own = residual * inv_rms
    slots = row_lengths.shape[1]
    arrays = [
        ("stream", jnp.pad(row_lengths, ((0, 7), (0, -slots % 128))), 1), ("stream", unit_own.astype(bf), 4),
        ("seq", jnp.pad(packed, ((0, 0), (0, -packed.shape[1] % 128))), 1)]
    if own_feats % 16:
        mine = lax.all_to_all(scaled, "stream", 1, 1, tiled=True)
        gate_own = mine[1]
        lengths, unit, packed, in_conv = link_gather([*arrays, ("seq", mine[0], 1)], sizes, 1)
    else:
        in_conv, gate_own, lengths, unit, packed = link_open(scaled[0], scaled[1], arrays, sizes, 1)
    lengths = lengths[::8, :slots]
    unit, gate_own, out_own, cot_own = lax.optimization_barrier((unit, gate_own, out_weight, cotangent))
    in_gate = lax.all_gather(gate_own, "seq", axis=0, tiled=True)
    out_full = lax.all_gather(out_own, "seq", axis=0, tiled=True)
    if seqs == 4:
        core = lax.ppermute(cot_own, "stream", [(i, i ^ 1) for i in range(4)])
        far = lax.ppermute(cot_own, "stream", [(i, i ^ 2) for i in range(4)])
        both = lax.ppermute(far, "stream", [(i, i ^ 1) for i in range(4)])
        stacked = jnp.stack([cot_own, core, far, both])
        me = lax.axis_index("stream")
        cot_all = jnp.concatenate([lax.dynamic_index_in_dim(stacked, me ^ i, 0, False) for i in range(4)])
    else:
        cot_all = lax.all_gather(cot_own, "stream", axis=0, tiled=True)
    xproj_full = packed[:, :proj_dim]
    dtw_cols = packed[:, proj_dim : proj_dim + rank_dim]
    at = proj_dim + rank_dim
    log_rates = packed[:, at : at + state_dim].astype(f32).T
    at += state_dim
    conv_taps = packed[:, at : at + CONV].astype(f32).T
    at += CONV
    conv_shift, dt_shift, skip_vec = (packed[:, at + i].astype(f32) for i in range(3))
    rate = -jnp.exp(log_rates) / LN2

    rim = CONV - 1
    first_pos = lax.axis_index("seq") * length
    doc_ids, start_flags, valid_mask = jax.vmap(
        lambda row: token_layout(row, first_pos - rim, length + 2 * rim))(lengths)
    own_ids = doc_ids[:, rim : rim + length]
    starts = start_flags[:, rim : rim + length].reshape(tokens, 1)
    valid = valid_mask[:, rim : rim + length].reshape(tokens, 1)
    near = [doc_ids[:, tap : tap + length] == own_ids for tap in range(2 * rim + 1) if tap != rim]
    masks = jnp.pad(jnp.stack(near, axis=-1).astype(f32), ((0, 0), (0, 0), (0, 8 - 2 * rim))).reshape(tokens, 8)

    conv_in = jnp.dot(unit, in_conv, preferred_element_type=f32)
    gate_in = jnp.dot(unit, in_gate, preferred_element_type=f32)
    earlier = passed_along(conv_in.reshape(seqs, length, chans)[:, length - rim :].astype(bf), "seq", 1).astype(f32)
    earlier = jnp.pad(earlier, ((0, 0), (8 - rim, 0), (0, 0))).reshape(seqs * 8, chans)
    taps = jnp.pad(jnp.concatenate([conv_taps, conv_shift[None]]), ((0, 7 - CONV), (0, 0)))
    activated, slope = conv_fwd(conv_in, earlier, masks, taps, seqs)
    act_float = activated.astype(f32)
    projected = link_sum(
        lax.dot_general(xproj_full, activated, (((0,), (1,)), ((), ())), preferred_element_type=f32), sizes, 2)
    low_rank = projected[:rank_dim].astype(bf)
    write_in = projected[rank_dim : rank_dim + state_dim]
    readout = projected[rank_dim + state_dim :]
    dt_pre = lax.dot_general(low_rank, dtw_cols, (((0,), (1,)), ((), ())), preferred_element_type=f32) + dt_shift
    dt_step = jax.nn.softplus(dt_pre)
    dt_reset = jnp.where(starts > 0, RESET, dt_step)
    dt_act = dt_step * act_float
    write_slabs, read_slabs = slabs_of(write_in), slabs_of(readout)
    write_diag, read_diag = spread(write_in), spread(readout)

    step_sum = jnp.sum(dt_reset.reshape(seqs, length, chans), axis=1)
    ends = scan_end(fwd_end_body, dt_reset, dt_act, write_slabs, rate, seqs)
    start_state = carried(ends, step_sum, rate, False, sizes, 3)
    scanned, history = fwd_full(dt_reset, dt_act, write_slabs, read_diag, rate, start_state, seqs)
    ssm_out = scanned + skip_vec * act_float
    gate_act = jax.nn.silu(gate_in)
    gated = (ssm_out * gate_act * valid).astype(bf)
    product = jnp.dot(gated, out_full, preferred_element_type=f32).astype(bf)
    d_gated = contract_cols(cot_all, out_full)
    d_masked = d_gated * valid
    d_ssm = d_masked * gate_act
    d_gate = (d_masked * ssm_out * silu_slope(gate_in)).astype(bf)
    product, d_ssm, gated, d_gate = lax.optimization_barrier((product, d_ssm, gated, d_gate))
    product = lax.psum_scatter(product, "stream", scatter_dimension=0, tiled=True)
    g_out = contract_rows(gated, cot_all).astype(bf)
    g_in_gate = contract_rows(unit, d_gate).astype(bf)
    d_ssm, g_out, g_in_gate = lax.optimization_barrier((d_ssm, g_out, g_in_gate))
    g_skip = jnp.sum(d_ssm * act_float, axis=0)
    back_ends = scan_end(bwd_end_body, dt_reset, d_ssm, read_slabs, rate, seqs)
    later_sum = carried(back_ends, step_sum, rate, True, sizes, 4)
    later_sum, product, g_out, g_in_gate = lax.optimization_barrier((later_sum, product, g_out, g_in_gate))
    output = (residual + product.astype(f32)).astype(bf)
    g_out = lax.psum_scatter(g_out, "seq", scatter_dimension=0, tiled=True)
    g_in_gate = lax.psum_scatter(g_in_gate, "seq", scatter_dimension=0, tiled=True)
    sum_write, sum_rate, g_log, d_write, d_read = bwd_full(
        dt_reset, dt_act, d_ssm, history, read_slabs, write_diag, rate, later_sum, seqs)
    per_step = jnp.where(dt_step > 1e-30, sum_rate * LN2 / jnp.maximum(dt_step, 1e-30), 0.0)
    d_step = per_step + act_float * sum_write
    d_pre = d_step * jax.nn.sigmoid(dt_pre)
    g_dt_bias = jnp.sum(d_pre, axis=0)
    d_pre_low = d_pre.astype(bf)
    g_dt = lax.dot_general(d_pre_low, low_rank, (((0,), (1,)), ((), ())), preferred_element_type=f32)
    d_low = lax.dot_general(dtw_cols, d_pre_low, (((0,), (1,)), ((), ())), preferred_element_type=f32)
    d_proj = link_sum(jnp.concatenate([d_low, d_write, d_read], axis=0), sizes, 5).astype(bf)
    d_proj, g_out = lax.optimization_barrier((d_proj, g_out))
    g_xproj = lax.dot_general(activated, d_proj, (((0,), (1,)), ((), ())), preferred_element_type=f32)
    d_act = dt_step * sum_write + skip_vec * d_ssm + lax.dot_general(
        d_proj, xproj_full, (((0,), (1,)), ((), ())), preferred_element_type=f32)
    first = (d_act.reshape(seqs, length, chans)[:, :rim] * slope.reshape(seqs, length, chans)[:, :rim].astype(f32))
    later = passed_along(first.astype(bf), "seq", -1).astype(f32)
    later = jnp.pad(later, ((0, 0), (0, 8 - rim), (0, 0))).reshape(seqs * 8, chans)
    d_conv_in, sums = conv_bwd(d_act, slope, later, conv_in, masks, taps, seqs)
    d_conv_in, g_in_gate = lax.optimization_barrier((d_conv_in, g_in_gate))
    sums = sums.reshape(seqs, 8, chans).sum(0)
    g_conv, g_conv_bias = sums[:CONV].T, sums[CONV]
    g_in_conv = contract_rows(unit, d_conv_in).astype(bf)
    d_unit = (contract_cols(d_conv_in, in_conv) + contract_cols(d_gate, in_gate)).astype(bf)
    def in_rows(block):
        shared = lax.all_to_all(block, "stream", 0, 0, tiled=True).reshape(seqs, own_feats, parts, own)
        return shared.transpose(1, 2, 0, 3).reshape(own_feats, parts * seqs * own)

    def padded_small(columns):
        joined = jnp.concatenate(columns, axis=1)
        return jnp.pad(joined, ((0, 0), (0, -joined.shape[1] % 128))).astype(bf)

    small = padded_small(
        [g_xproj, g_dt, g_log.T * LN2, g_dt_bias[:, None], g_skip[:, None], g_conv, g_conv_bias[:, None]])
    d_unit, g_in_gate, output, g_out = lax.optimization_barrier((d_unit, in_rows(g_in_gate), output, g_out))
    g_in_conv, small, d_unit = link_reduce(
        [("seq", g_in_conv, 2, 0 if own_feats % 16 else own), ("seq", small, 2, 0), ("stream", d_unit, 4, 0)], sizes, 6)
    small = small.astype(f32)
    d_unit = d_unit.astype(f32)
    in_grad = cotangent.astype(f32) + inv_rms * (d_unit - unit_own * jnp.mean(d_unit * unit_own, axis=-1, keepdims=True))

    g_in_conv = in_rows(g_in_conv) if own_feats % 16 else g_in_conv
    g_unit = jnp.concatenate([g_in_conv, g_in_gate], axis=1).astype(f32)
    at = proj_dim + rank_dim
    return (
        output[None],
        in_grad.astype(bf)[None],
        jnp.sum(g_unit * in_weight.astype(f32), axis=1),
        g_unit * gain[:, None],
        small[:, at + state_dim + 2 : at + state_dim + 2 + CONV].T,
        small[:, at + state_dim + 2 + CONV],
        small[:, :proj_dim],
        small[:, proj_dim:at].T,
        small[:, at + state_dim],
        small[:, at : at + state_dim],
        small[:, at + state_dim + 1],
        g_out.astype(f32),
    )


def lines_of(mesh):
    devices = mesh.devices
    places = [getattr(device, "coords", None) for device in devices[:, 0]]
    seq = len(places)
    plane = 1
    if all(place is not None for place in places):
        plane = len({tuple(place)[1] for place in places})
    if seq % plane:
        plane = 1
    return {"seq": (seq, plane), "stream": (devices.shape[1], 1 if devices.shape[1] % 2 else 2)}


def solution(mesh):
    in_specs = (
        P("stream", "seq", None),
        P("stream", "seq", None),
        P("stream", None),
        P(("seq", "stream")),
        P(("seq", "stream"), None),
        P(None, ("seq", "stream")),
        P(("seq", "stream")),
        P(("seq", "stream"), None),
        P(None, ("seq", "stream")),
        P(("seq", "stream")),
        P(("seq", "stream"), None),
        P(("seq", "stream")),
        P(("seq", "stream"), None),
    )
    out_specs = (
        P("stream", "seq", None),
        P("stream", "seq", None),
        P(("seq", "stream")),
        P(("seq", "stream"), None),
        P(None, ("seq", "stream")),
        P(("seq", "stream")),
        P(("seq", "stream"), None),
        P(None, ("seq", "stream")),
        P(("seq", "stream")),
        P(("seq", "stream"), None),
        P(("seq", "stream")),
        P(("seq", "stream"), None),
    )
    return jax.shard_map(functools.partial(local, lines_of(mesh)), mesh=mesh, in_specs=in_specs, out_specs=out_specs, check_vma=False)
```
